32 devices in a mesh: ctx: 8 (over y, x, core), head: 4 (over z).
Axes of the slice: x: 2, y: 2, z: 4, core: 2. Of those that a mesh axis runs over, the one named last changes fastest.
Arguments:
- queries: bfloat16 [2048, 4096], P('ctx', 'head'), may hold values from -6 to 6
- key_rows: bfloat16 [8192, 4096], P('ctx', 'head'), may hold values from -8 to 8
- value_rows: bfloat16 [8192, 4096], P('ctx', 'head'), may hold values from -4 to 4
- selected: int32 [2048, 4], P('ctx'), may hold values from 0 to 127, as said below
- out_grad: bfloat16 [2048, 4096], P('ctx', 'head'), may hold values from -6 to 6
- out_weight: bfloat16 [4096, 4096], P(None, 'head'), may hold values from -0.09375 to 0.09375
Outputs:
- query_grad: float32 [2048, 4096], P('ctx', 'head')
- key_grad: float32 [8192, 4096], P('ctx', 'head')
- value_grad: float32 [8192, 4096], P('ctx', 'head')
- weight_grad: float32 [4096, 4096], P('ctx', 'head')
The draws below stay inside these ranges and needn't reach their ends.
Inputs may be any that keep to these rules, and one draw needn't show every extreme that they name: `selected`: each query names 4 different blocks. Among the queries of one index of ctx no block is named more than 16 times, and some blocks are named exactly 16 times by the queries of every index of ctx.
All inputs are finite; a program needn't handle non-finite values.
Results may differ from the reference program's by a relative error of at most 0.015.
Values may be sent and summed in bfloat16 or wider, within the bound.
No kernel may reach another device: no remote copies, remote signals or barrier semaphores. Data moves between devices by JAX's collectives and lax.ppermute only.
A program may use at most 128 MiB of HBM per device.

```python
import jax
import jax.numpy as jnp
from jax import lax

D = 4096
HEADS = 32
HD = 128
BLOCK = 64
TOPK = 4
Q_DEV = 256
QUERIES = 2048
CONTEXT = 8192
BLOCKS = 128


def route_table(key):
    route_key = jax.random.fold_in(key, 7)
    requests = Q_DEV * TOPK
    capacity = 2 * requests // BLOCKS
    hot_count = BLOCKS // 4
    half_point = requests // 2
    global_order = jax.random.permutation(jax.random.fold_in(route_key, 0), BLOCKS).astype(jnp.int32)
    entries = jnp.arange(requests, dtype=jnp.int32)
    ranking = jnp.where(entries < half_point, entries // capacity, hot_count + 3 * (entries - half_point) // capacity)

    def one_device(device):
        local_key = jax.random.fold_in(route_key, device + 1)
        cold_key = jax.random.fold_in(local_key, 1)
        row_key = jax.random.fold_in(local_key, 2)
        column_key = jax.random.fold_in(local_key, 3)
        cold_order = jax.random.permutation(cold_key, BLOCKS - hot_count).astype(jnp.int32)
        device_order = jnp.concatenate([global_order[:hot_count], global_order[hot_count:][cold_order]])
        block_table = device_order[ranking].reshape(TOPK, Q_DEV).T
        block_table = block_table[jax.random.permutation(row_key, Q_DEV)]
        mixing = jax.random.randint(column_key, (Q_DEV, TOPK), 0, 1024, dtype=jnp.int32) * TOPK + jnp.arange(TOPK, dtype=jnp.int32)[None, :]
        return jnp.take_along_axis(block_table, jnp.argsort(mixing, axis=1), axis=1)
    device_total = QUERIES // Q_DEV
    return jax.vmap(one_device)(jnp.arange(device_total, dtype=jnp.int32)).reshape(QUERIES, TOPK).astype(jnp.int32)


def draw_selected(key, part):
    return route_table(key)


def draw_queries(key, part):
    query_key = jax.random.fold_in(key, 21)
    drawn = jax.random.truncated_normal(jax.random.fold_in(query_key, 2), -4.0, 4.0, (QUERIES, HEADS * HD))
    return drawn.astype(jnp.float32).astype(jnp.bfloat16)


def draw_key_rows(key, part):
    token_key = jax.random.fold_in(key, 41)
    drawn = jax.random.truncated_normal(jax.random.fold_in(token_key, 2), -4.0, 4.0, (CONTEXT, HEADS * HD))
    return drawn.astype(jnp.float32).astype(jnp.bfloat16)


def with_spikes(result, own_key, source, target, blocks, factor):
    def block_of(dim):
        return (jnp.arange(result.shape[dim]) // (result.shape[dim] // blocks)).reshape((-1,) + (1,) * (result.ndim - 1 - dim))

    one_side = jax.random.permutation(own_key, blocks)[block_of(target)]
    far = (block_of(target) + blocks // 2) % blocks
    return jnp.where((block_of(source) == one_side) | (block_of(source) == far), factor * result, result)


def steps_of(stream_key, extent, pieces, smallest, high):
    def one(dim, shards_of):
        heights = jax.random.uniform(jax.random.fold_in(jax.random.fold_in(stream_key, 6), dim), (shards_of,), jnp.float32, smallest / len(pieces), high / len(pieces))
        return jnp.repeat(jnp.exp(heights), extent[dim] // shards_of).reshape((-1,) + (1,) * (len(extent) - dim - 1))

    loudness = one(*pieces[0])
    for cut in pieces[1:]:
        loudness = loudness * one(*cut)
    return loudness


def centred(own_key, dims, width, reach, split=(), kind=jnp.bfloat16):
    level = steps_of(own_key, dims, split, -0.22, 0.18) if split else 1.0
    values = jax.random.normal(own_key, dims, jnp.float32) * width * level
    return jnp.minimum(jnp.maximum(values, -reach), reach).astype(kind)


def heavy_noise(rng, shape, deviation, reach, cuts, heavy, held_as=jnp.bfloat16):
    values = deviation * jax.random.normal(rng, shape, jnp.float32)
    if cuts:
        values = values * steps_of(rng, shape, cuts, -0.22, 0.18)
    return jnp.clip(with_spikes(values, jax.random.fold_in(rng, 3), *heavy), -reach, reach).astype(held_as)


def setup_inputs(seed: int = 0) -> dict:
    arg_keys = jax.random.split(jax.random.key(seed), 7)
    queries = draw_queries(jax.random.fold_in(arg_keys[6], 71), 0)
    key_rows = draw_key_rows(jax.random.fold_in(arg_keys[6], 71), 0)
    value_rows = centred(arg_keys[2], (CONTEXT, HEADS * HD), 1.0, 4.0, ((0, 8), (1, 4)))
    selected = draw_selected(jax.random.fold_in(arg_keys[6], 71), 0)
    out_grad = heavy_noise(arg_keys[4], (QUERIES, D), 1.0, 6.0, ((0, 8), (1, 4)), (0, 1, 8, 2.0))
    out_weight = centred(arg_keys[5], (D, HEADS * HD), (HEADS * HD) ** -0.5, 0.09375, ((1, 4),))
    return dict(queries=queries, key_rows=key_rows, value_rows=value_rows, selected=selected, out_grad=out_grad, out_weight=out_weight)


def head_pass(head_bundle, selected):
    query_head, key_head, value_head, grad_head = head_bundle
    score_scale = HD ** -0.5
    offsets = jnp.arange(BLOCK, dtype=jnp.int32)
    token_index = (selected[:, :, None] * BLOCK + offsets[None, None, :]).astype(jnp.int32)
    mark_index = (selected * BLOCK + (BLOCK - 1)).astype(jnp.int32)
    key_tiles = key_head[token_index].astype(jnp.float32)
    value_tiles = value_head[token_index].astype(jnp.float32)
    query_wide = query_head.astype(jnp.float32)
    mark_keys = key_head[mark_index].astype(jnp.float32)
    gate_logits = score_scale * jnp.einsum("qd,qtd->qt", query_wide, mark_keys)
    gate_probs = jax.nn.softmax(gate_logits, axis=-1)
    logits = score_scale * jnp.einsum("qd,qtjd->qtj", query_wide, key_tiles)
    attn_probs = jax.nn.softmax(logits, axis=-1)
    probs_low = attn_probs.astype(jnp.bfloat16)
    probs_wide = probs_low.astype(jnp.float32)
    block_out = jnp.einsum("qtj,qtjd->qtd", probs_wide, value_tiles).astype(jnp.bfloat16)
    block_wide = block_out.astype(jnp.float32)
    attn_head = jnp.sum(gate_probs[:, :, None] * block_wide, axis=1).astype(jnp.bfloat16)
    grad_wide = grad_head.astype(jnp.float32)
    pushed = (gate_probs[:, :, None] * grad_wide[:, None, :]).astype(jnp.bfloat16)
    pushed_wide = pushed.astype(jnp.float32)
    gate_diff = jnp.einsum("qd,qtd->qt", grad_wide, block_wide)
    gate_grad = gate_probs * (gate_diff - jnp.sum(gate_probs * gate_diff, axis=-1, keepdims=True))
    prob_grad = jnp.einsum("qtd,qtjd->qtj", pushed_wide, value_tiles)
    delta_term = jnp.sum(pushed_wide * block_wide, axis=-1)
    score_grad = (attn_probs * (prob_grad - delta_term[:, :, None])).astype(jnp.bfloat16)
    score_wide = score_grad.astype(jnp.float32)
    query_part = (score_scale * jnp.einsum("qtj,qtjd->qtd", score_wide, key_tiles)).astype(jnp.bfloat16)
    query_grad = jnp.sum(query_part.astype(jnp.float32), axis=1) + score_scale * jnp.einsum("qt,qtd->qd", gate_grad, mark_keys)
    flat_tokens = token_index.reshape(-1)
    value_terms = probs_wide[:, :, :, None] * pushed_wide[:, :, None, :]
    value_grad = jnp.zeros((key_head.shape[0], HD), jnp.float32).at[flat_tokens].add(value_terms.reshape(-1, HD))
    key_terms = score_scale * score_wide[:, :, :, None] * query_wide[:, None, None, :]
    key_grad = jnp.zeros((key_head.shape[0], HD), jnp.float32).at[flat_tokens].add(key_terms.reshape(-1, HD))
    mark_terms = score_scale * gate_grad[:, :, None] * query_wide[:, None, :]
    key_grad = key_grad.at[mark_index.reshape(-1)].add(mark_terms.reshape(-1, HD))
    return attn_head, query_grad, key_grad, value_grad


def split_heads(matrix):
    return jnp.transpose(matrix.reshape(matrix.shape[0], HEADS, HD), (1, 0, 2))


def merge_heads(stacked):
    return jnp.transpose(stacked, (1, 0, 2)).reshape(stacked.shape[1], HEADS * HD)


def reference(queries, key_rows, value_rows, selected, out_grad, out_weight):
    grad_attn = jnp.dot(out_grad, out_weight, preferred_element_type=jnp.float32).astype(jnp.bfloat16)
    bundle = (split_heads(queries), split_heads(key_rows), split_heads(value_rows), split_heads(grad_attn))
    attn_heads, query_heads, key_heads, value_heads = lax.map(lambda head_bundle: head_pass(head_bundle, selected), bundle)
    attn_out = merge_heads(attn_heads)
    weight_grad = jnp.dot(out_grad.T, attn_out, preferred_element_type=jnp.float32)
    return merge_heads(query_heads), merge_heads(key_heads), merge_heads(value_heads), weight_grad
```

```python
import functools

import jax
import jax.numpy as jnp
from jax import lax
from jax.experimental import pallas as pl
from jax.experimental.pallas import tpu as pltpu
from jax.sharding import PartitionSpec as P

HD = 128
BLOCK = 64
TOPK = 4
F32 = jnp.float32
BF16 = jnp.bfloat16
VMEM_LIMIT = 56 * 1024 * 1024
NN = (((1,), (0,)), ((), ()))
NT = (((1,), (1,)), ((), ()))
TN = (((0,), (0,)), ((), ()))


def mm(a, b, dims=NN):
    return lax.dot_general(a, b, dims, preferred_element_type=F32)


def joined(items, axis):
    return items[0] if len(items) == 1 else jnp.concatenate(items, axis=axis)


def forward_kernel(chunks, span, cap, me_ref, sel_ref, mark_ref, k_ref, v_ref, *refs):
    q_refs = refs[:chunks]
    part_refs = refs[chunks : 2 * chunks]
    qg_ref, p_ref, gate_ref, hot_ref = refs[2 * chunks : 2 * chunks + 4]
    mask_ref, out_ref = refs[2 * chunks + 4 :]
    block_count, _, width = k_ref.shape
    block_total = mark_ref.shape[0]
    heads = width // HD
    rows = q_refs[0].shape[0]
    group_rows = rows * span
    groups = chunks // span
    me = me_ref[0]
    scale = HD ** (-0.5)
    base = me * block_count

    before = lax.broadcasted_iota(jnp.int32, (group_rows, group_rows), 0)
    after = lax.broadcasted_iota(jnp.int32, (group_rows, group_rows), 1)
    earlier = (before < after).astype(BF16)
    for g in range(groups):
        picked = joined([sel_ref[me ^ (g * span + i)] for i in range(span)], 1)
        own_ids = base + lax.broadcasted_iota(jnp.int32, (block_count, group_rows), 0)
        all_ids = lax.broadcasted_iota(jnp.int32, (block_total, group_rows), 0)
        own = picked[0:1, :] == own_ids
        named = picked[0:1, :] == all_ids
        for t in range(1, TOPK):
            own = own | (picked[t : t + 1, :] == own_ids)
            named = named | (picked[t : t + 1, :] == all_ids)
        own = jnp.where(own, 1.0, 0.0)
        rank = mm(own.astype(BF16), earlier)
        rank = jnp.where(own > 0.5, rank, -1.0)
        place = lax.broadcasted_iota(jnp.int32, (cap, group_rows), 0).astype(F32)
        hot = jnp.concatenate(
            [jnp.where(rank[b : b + 1, :] == place, 1.0, 0.0) for b in range(block_count)], axis=0
        ).astype(BF16)
        hot_ref[g] = hot
        named = jnp.where(named, 1.0, 0.0).astype(BF16)
        mask_ref[:, g * cap : (g + 1) * cap, :] = mm(hot, named, NT).reshape(
            block_count, cap, block_total
        )
        q_group = joined([q_refs[g * span + i][...] for i in range(span)], 0)
        qg_ref[:, g * cap : (g + 1) * cap, :] = (
            mm(hot, q_group).astype(BF16).reshape(block_count, cap, width)
        )

    def one_block(b, carry):
        mask = mask_ref[b].T > 0.5
        gates = []
        for h in range(heads):
            cols = slice(h * HD, (h + 1) * HD)
            q = qg_ref[b, :, cols]
            marks = jnp.where(mask, scale * mm(mark_ref[:, cols], q, NT), -1e30)
            top = jnp.max(marks, axis=0, keepdims=True)
            total = jnp.sum(jnp.exp(marks - top), axis=0, keepdims=True)
            logits = scale * mm(k_ref[b, :, cols], q, NT)
            gate = jnp.exp(jnp.minimum(logits[BLOCK - 1 :, :] - top, 0.0)) / total
            weight = jnp.exp(logits - jnp.max(logits, axis=0, keepdims=True))
            probs = weight * (1.0 / jnp.sum(weight, axis=0, keepdims=True))
            p_ref[b, h] = probs.astype(BF16)
            gates.append(gate)
            gated = (probs * gate).T.astype(BF16)
            out_ref[b, :, cols] = mm(gated, v_ref[b, :, cols]).astype(BF16)
        gate_ref[b] = jnp.concatenate(gates, axis=0)
        return carry

    lax.fori_loop(0, block_count, one_block, 0)

    for g in range(groups):
        hot = hot_ref[g]
        slots = out_ref[:, g * cap : (g + 1) * cap, :].reshape(block_count * cap, width)
        part = mm(hot, slots, TN).astype(BF16)
        for i in range(span):
            part_refs[g * span + i][...] = part[i * rows : (i + 1) * rows]


def backward_kernel(chunks, span, cap, hot_ref, qg_ref, p_ref, gate_ref, k_ref, v_ref, *refs):
    ga_refs = refs[:chunks]
    part_refs = refs[chunks : 2 * chunks]
    dk_ref, dv_ref = refs[2 * chunks : 2 * chunks + 2]
    gag_ref, dq_ref = refs[2 * chunks + 2 :]
    block_count, _, width = k_ref.shape
    heads = width // HD
    rows = ga_refs[0].shape[0]
    groups = chunks // span
    scale = HD ** (-0.5)

    for g in range(groups):
        ga_group = joined([ga_refs[g * span + i][...] for i in range(span)], 0)
        gag_ref[:, g * cap : (g + 1) * cap, :] = (
            mm(hot_ref[g], ga_group).astype(BF16).reshape(block_count, cap, width + HD)
        )
    last = lax.broadcasted_iota(jnp.int32, (BLOCK, groups * cap), 0) == BLOCK - 1

    def one_block(b, carry):
        dots = gag_ref[b, :, width:].astype(F32).T
        dots = dots[:heads] + dots[heads : 2 * heads]
        gates = gate_ref[b]
        for h in range(heads):
            cols = slice(h * HD, (h + 1) * HD)
            q = qg_ref[b, :, cols]
            ga = gag_ref[b, :, cols]
            probs = p_ref[b, h].astype(F32)
            gate = gates[h : h + 1, :]
            prob_grad = mm(v_ref[b, :, cols], ga, NT)
            delta = jnp.sum(probs * prob_grad, axis=0, keepdims=True)
            gated = probs * gate
            score = gated * (prob_grad - delta)
            score = score + jnp.where(last, gate * (delta - dots[h : h + 1, :]), 0.0)
            dv_ref[b, :, cols] = mm(gated.astype(BF16), ga)
            dk_ref[b, :, cols] = scale * mm(score.astype(BF16), q)
            dq_ref[b, :, cols] = (scale * mm(score.T.astype(BF16), k_ref[b, :, cols])).astype(BF16)
        return carry

    lax.fori_loop(0, block_count, one_block, 0)

    for g in range(groups):
        slots = dq_ref[:, g * cap : (g + 1) * cap, :].reshape(block_count * cap, width)
        part = mm(hot_ref[g], slots, TN).astype(BF16)
        for i in range(span):
            part_refs[g * span + i][...] = part[i * rows : (i + 1) * rows]


def swap(x, bits):
    count = lax.axis_size("ctx")
    return lax.ppermute(x, "ctx", [(i, i ^ bits) for i in range(count)])


def spread(x):
    count = lax.axis_size("ctx")
    pieces = [None] * count
    for m in range(0, count, 2):
        pieces[m] = swap(x, m) if m else x
    for m in range(0, count, 2):
        pieces[m + 1] = swap(pieces[m], 1)
    return pieces


def collect(parts):
    count = lax.axis_size("ctx")
    total = None
    for m in range(0, count, 2):
        both = parts[m].astype(F32) + swap(parts[m + 1], 1).astype(F32)
        term = swap(both.astype(BF16), m).astype(F32) if m else both
        total = term if total is None else total + term
    return total


def body(queries, key_rows, value_rows, selected, out_grad, out_weight):
    chunks = lax.axis_size("ctx")
    rows, width = queries.shape
    heads = width // HD
    block_count = key_rows.shape[0] // BLOCK
    block_total = block_count * chunks
    capacity = 2 * rows * TOPK // block_total
    span = max(1, 16 // capacity)
    cap = capacity * span
    groups = chunks // span
    slots = groups * cap
    me = lax.axis_index("ctx").astype(jnp.int32).reshape(1)
    keys = key_rows.reshape(block_count, BLOCK, width)
    values = value_rows.reshape(block_count, BLOCK, width)
    vmem = pl.BlockSpec(memory_space=pltpu.VMEM)

    queries_all = spread(queries)
    grad_full = lax.all_gather(out_grad, "head", axis=1, tiled=True)
    sel_all = lax.all_gather(selected.T, "ctx", axis=0)
    mark_all = lax.all_gather(keys[:, BLOCK - 1], "ctx", axis=0, tiled=True)

    outs = pl.pallas_call(
        functools.partial(forward_kernel, chunks, span, cap),
        out_shape=[jax.ShapeDtypeStruct((rows, width), BF16)] * chunks
        + [
            jax.ShapeDtypeStruct((block_count, slots, width), BF16),
            jax.ShapeDtypeStruct((block_count, heads, BLOCK, slots), BF16),
            jax.ShapeDtypeStruct((block_count, heads, slots), F32),
            jax.ShapeDtypeStruct((groups, block_count * cap, rows * span), BF16),
        ],
        in_specs=[pl.BlockSpec(memory_space=pltpu.SMEM)] + [vmem] * (4 + chunks),
        out_specs=[vmem] * (chunks + 4),
        scratch_shapes=[
            pltpu.VMEM((block_count, slots, block_total), F32),
            pltpu.VMEM((block_count, slots, width), BF16),
        ],
        compiler_params=pltpu.CompilerParams(vmem_limit_bytes=VMEM_LIMIT),
        name="forward",
    )(me, sel_all, mark_all, keys, values, *queries_all)
    attn_parts = outs[:chunks]
    q_slots, probs, gates, hot = outs[chunks:]

    grad_attn = jnp.dot(grad_full, out_weight, preferred_element_type=F32).astype(BF16)
    columns = lax.all_to_all(grad_full, "ctx", split_axis=1, concat_axis=0, tiled=True)

    attn_out = collect(attn_parts).astype(BF16)
    dots = jnp.sum(
        (grad_attn.astype(F32) * attn_out.astype(F32)).reshape(rows, heads, HD), axis=2
    )
    dots_high = dots.astype(BF16)
    dots_low = (dots - dots_high.astype(F32)).astype(BF16)
    spare = jnp.zeros((rows, HD - 2 * heads), BF16)
    grad_all = spread(jnp.concatenate([grad_attn, dots_high, dots_low, spare], axis=1))
    attn_all = lax.all_gather(attn_out, "ctx", axis=0, tiled=True)

    outs = pl.pallas_call(
        functools.partial(backward_kernel, chunks, span, cap),
        out_shape=[jax.ShapeDtypeStruct((rows, width), BF16)] * chunks
        + [jax.ShapeDtypeStruct((block_count, BLOCK, width), F32)] * 2,
        in_specs=[vmem] * (6 + chunks),
        out_specs=[vmem] * (chunks + 2),
        scratch_shapes=[
            pltpu.VMEM((block_count, slots, width + HD), BF16),
            pltpu.VMEM((block_count, slots, width), BF16),
        ],
        compiler_params=pltpu.CompilerParams(vmem_limit_bytes=VMEM_LIMIT),
        name="backward",
    )(hot, q_slots, probs, gates, keys, values, *grad_all)
    query_grad = collect(outs[:chunks])
    key_grad, value_grad = outs[chunks:]

    weight_grad = jnp.einsum(
        "qd,qf->df",
        columns,
        attn_all,
        preferred_element_type=F32,
    )
    return (
        query_grad,
        key_grad.reshape(-1, width),
        value_grad.reshape(-1, width),
        weight_grad,
    )


def solution(mesh):
    return jax.shard_map(
        body,
        mesh=mesh,
        in_specs=(
            P("ctx", "head"),
            P("ctx", "head"),
            P("ctx", "head"),
            P("ctx", None),
            P("ctx", "head"),
            P(None, "head"),
        ),
        out_specs=(P("ctx", "head"), P("ctx", "head"), P("ctx", "head"), P("ctx", "head")),
        check_vma=False,
    )
```

```python
import functools

import jax
import jax.numpy as jnp
from jax import lax
from jax.experimental import pallas as pl
from jax.experimental.pallas import tpu as pltpu
from jax.sharding import PartitionSpec as P

HD = 128
BLOCK = 64
TOPK = 4
F32 = jnp.float32
BF16 = jnp.bfloat16
VMEM_LIMIT = 40 * 1024 * 1024
NN = (((1,), (0,)), ((), ()))
NT = (((1,), (1,)), ((), ()))
TN = (((0,), (0,)), ((), ()))


def mm(a, b, dims=NN):
    return lax.dot_general(a, b, dims, preferred_element_type=F32)


def joined(items, axis):
    return items[0] if len(items) == 1 else jnp.concatenate(items, axis=axis)


def diagonal(pair):
    zero = jnp.zeros((pair.shape[0], HD), pair.dtype)
    top = jnp.concatenate([pair[:, :HD], zero], axis=1)
    low = jnp.concatenate([zero, pair[:, HD:]], axis=1)
    return jnp.concatenate([top, low], axis=0)


def gate_kernel(sel_ref, mark_ref, q_ref, aux_ref):
    block_total, width = mark_ref.shape
    rows = q_ref.shape[0]
    heads = width // HD
    scale = HD ** (-0.5)
    ids = lax.broadcasted_iota(jnp.int32, (block_total, rows), 0)
    picks = [sel_ref[t : t + 1, :] == ids for t in range(TOPK)]
    chosen = picks[0]
    for t in range(1, TOPK):
        chosen = chosen | picks[t]
    bias = jnp.where(chosen, 0.0, -1e30)
    gates = [[None] * heads for _ in range(TOPK)]
    for h in range(heads):
        cols = slice(h * HD, (h + 1) * HD)
        logits = scale * mm(mark_ref[:, cols], q_ref[:, cols], NT) + bias
        weight = jnp.exp(logits - jnp.max(logits, axis=0, keepdims=True))
        inverse = 1.0 / jnp.sum(weight, axis=0, keepdims=True)
        for t in range(TOPK):
            gates[t][h] = inverse * jnp.sum(
                jnp.where(picks[t], weight, 0.0), axis=0, keepdims=True
            )
    high = (sel_ref[...] >> 4).astype(F32)
    low = (sel_ref[...] & 15).astype(F32)
    lines = [gates[t][h] for t in range(TOPK) for h in range(heads)] + [high, low]
    lines.append(jnp.zeros((HD - TOPK * heads - 2 * TOPK, rows), F32))
    aux_ref[...] = jnp.concatenate(lines, axis=0).astype(BF16)


def block_ids(aux, heads):
    at = TOPK * heads
    return 16.0 * aux[at : at + TOPK] + aux[at + TOPK : at + 2 * TOPK]


def forward_kernel(chunks, span, cap, me_ref, aux_ref, k_ref, v_ref, *refs):
    q_refs = refs[:chunks]
    even_refs = refs[chunks : chunks + chunks // 2]
    odd_ref, qg_ref, p_ref, gate_ref, hot_ref = refs[chunks + chunks // 2 : chunks + chunks // 2 + 5]
    auxg_ref, out_ref = refs[chunks + chunks // 2 + 5 :]
    block_count, _, width = k_ref.shape
    heads = width // HD
    rows = q_refs[0].shape[0]
    group_rows = rows * span
    groups = chunks // span
    me = me_ref[0]
    rate = HD ** (-0.5) * 1.4426950408889634
    base = me * block_count

    before = lax.broadcasted_iota(jnp.int32, (group_rows, group_rows), 0)
    after = lax.broadcasted_iota(jnp.int32, (group_rows, group_rows), 1)
    earlier = (before < after).astype(BF16)
    own_ids = (base + lax.broadcasted_iota(jnp.int32, (block_count, group_rows), 0)).astype(F32)
    place = lax.broadcasted_iota(jnp.int32, (cap, group_rows), 0).astype(F32)
    for g in range(groups):
        aux = joined([aux_ref[me ^ (g * span + i)] for i in range(span)], 1)
        picked = block_ids(aux.astype(F32), heads)
        own = picked[0:1, :] == own_ids
        for t in range(1, TOPK):
            own = own | (picked[t : t + 1, :] == own_ids)
        own = jnp.where(own, 1.0, 0.0)
        rank = jnp.where(own > 0.5, mm(own.astype(BF16), earlier), -1.0)
        hot = jnp.concatenate(
            [jnp.where(rank[b : b + 1, :] == place, 1.0, 0.0) for b in range(block_count)], axis=0
        ).astype(BF16)
        hot_ref[g] = hot
        auxg_ref[:, g * cap : (g + 1) * cap, :] = mm(hot, aux, NT).reshape(block_count, cap, HD)
        q_group = joined([q_refs[g * span + i][...] for i in range(span)], 0)
        qg_ref[:, g * cap : (g + 1) * cap, :] = (
            mm(hot, q_group).astype(BF16).reshape(block_count, cap, width)
        )

    def one_block(b, carry):
        pairs = [slice(p * 2 * HD, (p + 1) * 2 * HD) for p in range(heads // 2)]
        logits = [mm(diagonal(k_ref[b, :, cols]), qg_ref[b, :, cols], NT) for cols in pairs]
        wide = [diagonal(v_ref[b, :, cols]) for cols in pairs]
        aux = auxg_ref[b].T
        ids = block_ids(aux, heads)
        mine = (base + b).astype(F32)
        gates = jnp.where(ids[0:1] == mine, aux[:heads], 0.0)
        for t in range(1, TOPK):
            gates = gates + jnp.where(
                ids[t : t + 1] == mine, aux[t * heads : (t + 1) * heads], 0.0
            )
        probs, gated = [], []
        for p in range(heads // 2):
            for i in range(2):
                part = logits[p][i * BLOCK : (i + 1) * BLOCK]
                weight = jnp.exp2(rate * (part - jnp.max(part, axis=0, keepdims=True)))
                inverse = 1.0 / jnp.sum(weight, axis=0, keepdims=True)
                gate = gates[2 * p + i : 2 * p + i + 1, :]
                probs.append((weight * inverse).astype(BF16))
                gated.append((weight * (inverse * gate)).astype(BF16))
        outs = [
            mm(jnp.concatenate(gated[2 * p : 2 * p + 2], axis=0), wide[p], TN).astype(BF16)
            for p in range(heads // 2)
        ]
        gate_ref[b] = gates
        for p in range(heads // 2):
            p_ref[b, p] = jnp.concatenate(probs[2 * p : 2 * p + 2], axis=0)
            out_ref[b, :, pairs[p]] = outs[p]
        return carry

    lax.fori_loop(0, block_count, one_block, 0)

    for g in range(groups):
        slots = out_ref[:, g * cap : (g + 1) * cap, :].reshape(block_count * cap, width)
        part = mm(hot_ref[g], slots, TN).astype(BF16)
        for i in range(span):
            m = g * span + i
            target = odd_ref.at[m // 2] if m % 2 else even_refs[m // 2]
            target[...] = part[i * rows : (i + 1) * rows]


def finish_kernel(*refs):
    *term_refs, ga_ref, attn_ref, ext_ref = refs
    rows, width = ga_ref.shape
    heads = width // HD
    lane = lax.broadcasted_iota(jnp.int32, (rows, HD), 1)
    high = jnp.zeros((rows, HD), F32)
    low = jnp.zeros((rows, HD), F32)
    ext_ref[:, :width] = ga_ref[...]
    for h in range(heads):
        cols = slice(h * HD, (h + 1) * HD)
        total = term_refs[0][:, cols].astype(F32)
        for ref in term_refs[1:]:
            total = total + ref[:, cols].astype(F32)
        attn_ref[:, cols] = total.astype(BF16)
        dots = jnp.sum(total * ga_ref[:, cols].astype(F32), axis=1, keepdims=True)
        upper = dots.astype(BF16).astype(F32)
        high = jnp.where(lane == h, upper, high)
        low = jnp.where(lane == heads + h, dots - upper, low)
    ext_ref[:, width:] = (high + low).astype(BF16)


def backward_kernel(chunks, span, cap, hot_ref, qg_ref, p_ref, gate_ref, k_ref, v_ref, *refs):
    ga_refs = refs[:chunks]
    even_refs = refs[chunks : chunks + chunks // 2]
    odd_ref, dk_ref, dv_ref = refs[chunks + chunks // 2 : chunks + chunks // 2 + 3]
    gag_ref, dq_ref = refs[chunks + chunks // 2 + 3 :]
    block_count, _, width = k_ref.shape
    heads = width // HD
    rows = ga_refs[0].shape[0]
    groups = chunks // span
    scale = HD ** (-0.5)

    for g in range(groups):
        ga_group = joined([ga_refs[g * span + i][...] for i in range(span)], 0)
        gag_ref[:, g * cap : (g + 1) * cap, :] = (
            mm(hot_ref[g], ga_group).astype(BF16).reshape(block_count, cap, width + HD)
        )
    last = lax.broadcasted_iota(jnp.int32, (BLOCK, groups * cap), 0) == BLOCK - 1

    def one_block(b, carry):
        pairs = [slice(p * 2 * HD, (p + 1) * 2 * HD) for p in range(heads // 2)]
        q = [qg_ref[b, :, cols] for cols in pairs]
        ga = [gag_ref[b, :, cols] for cols in pairs]
        grads = [mm(diagonal(v_ref[b, :, cols]), ga[p], NT) for p, cols in enumerate(pairs)]
        wide = [diagonal(k_ref[b, :, cols]) for cols in pairs]
        probs = [p_ref[b, p].astype(F32) for p in range(heads // 2)]
        gates = gate_ref[b]
        dots = gag_ref[b, :, width:].astype(F32).T
        dots = dots[:heads] + dots[heads : 2 * heads]
        gated, score = [], []
        for p in range(heads // 2):
            for i in range(2):
                at = slice(i * BLOCK, (i + 1) * BLOCK)
                h = 2 * p + i
                gate = gates[h : h + 1, :]
                grad = grads[p][at]
                delta = jnp.sum(probs[p][at] * grad, axis=0, keepdims=True)
                weight = probs[p][at] * gate
                extra = jnp.where(last, scale * gate * (delta - dots[h : h + 1, :]), 0.0)
                score.append((weight * (scale * (grad - delta)) + extra).astype(BF16))
                gated.append(weight.astype(BF16))
        for p, cols in enumerate(pairs):
            both = jnp.concatenate(gated[2 * p : 2 * p + 2], axis=0)
            scores = jnp.concatenate(score[2 * p : 2 * p + 2], axis=0)
            dv = mm(both, ga[p])
            dk = mm(scores, q[p])
            dq = mm(scores, wide[p], TN).astype(BF16)
            dv_ref[b, :, cols] = jnp.concatenate([dv[:BLOCK, :HD], dv[BLOCK:, HD:]], axis=1)
            dk_ref[b, :, cols] = jnp.concatenate([dk[:BLOCK, :HD], dk[BLOCK:, HD:]], axis=1)
            dq_ref[b, :, cols] = dq
        return carry

    lax.fori_loop(0, block_count, one_block, 0)

    for g in range(groups):
        slots = dq_ref[:, g * cap : (g + 1) * cap, :].reshape(block_count * cap, width)
        part = mm(hot_ref[g], slots, TN).astype(BF16)
        for i in range(span):
            m = g * span + i
            target = odd_ref.at[m // 2] if m % 2 else even_refs[m // 2]
            target[...] = part[i * rows : (i + 1) * rows]


def weight_kernel(chips, me_ref, *refs):
    slabs, attns = refs[:chips], refs[chips : 2 * chips]
    own_ref, other_ref = refs[2 * chips :]
    half = own_ref.shape[0]
    core = me_ref[0] % 2
    attn = jnp.concatenate([ref[...] for ref in attns], axis=0)

    def side(which):
        cols = pl.ds(pl.multiple_of(which * half, half), half)
        return mm(jnp.concatenate([ref[:, cols] for ref in slabs], axis=0), attn, TN)

    own_ref[...] = side(core)
    other_ref[...] = side(1 - core).astype(BF16)


def swap(x, bits):
    count = lax.axis_size("ctx")
    return lax.ppermute(x, "ctx", [(i, i ^ bits) for i in range(count)])


def after(x, *others):
    return lax.optimization_barrier((x, *others))[0]


def chip_terms(evens, odd):
    received = swap(odd, 1)
    terms = [evens[0], received[0]]
    for j in range(1, len(evens)):
        both = evens[j].astype(F32) + received[j].astype(F32)
        terms.append(swap(both.astype(BF16), 2 * j))
    return terms


def body(queries, key_rows, value_rows, selected, out_grad, out_weight):
    chunks = lax.axis_size("ctx")
    chips = chunks // 2
    rows, width = queries.shape
    features = out_weight.shape[0]
    heads = width // HD
    block_count = key_rows.shape[0] // BLOCK
    block_total = block_count * chunks
    capacity = 2 * rows * TOPK // block_total
    span = max(1, 16 // capacity)
    cap = capacity * span
    groups = chunks // span
    slots = groups * cap
    index = lax.axis_index("ctx").astype(jnp.int32)
    me = index.reshape(1)
    keys = key_rows.reshape(block_count, BLOCK, width)
    values = value_rows.reshape(block_count, BLOCK, width)
    vmem = pl.BlockSpec(memory_space=pltpu.VMEM)
    smem = pl.BlockSpec(memory_space=pltpu.SMEM)
    params = pltpu.CompilerParams(vmem_limit_bytes=VMEM_LIMIT)

    def shaped(shape, kind=BF16):
        return jax.ShapeDtypeStruct(shape, kind)

    grad_full = lax.all_gather(out_grad, "head", axis=0)
    query_chips = [queries] + [swap(queries, 2 * j) for j in range(1, chips)]
    mark_all = lax.all_gather(keys[:, BLOCK - 1], "ctx", axis=0, tiled=True)
    aux = pl.pallas_call(
        gate_kernel,
        out_shape=shaped((HD, rows)),
        in_specs=[vmem] * 3,
        out_specs=vmem,
        compiler_params=params,
        name="gates",
    )(selected.T, mark_all, queries)
    aux_all = lax.all_gather(aux, "ctx", axis=0)
    query_all = []
    for piece in query_chips:
        query_all += [piece, swap(after(piece, aux_all), 1)]

    outs = pl.pallas_call(
        functools.partial(forward_kernel, chunks, span, cap),
        out_shape=[shaped((rows, width))] * chips
        + [
            shaped((chips, rows, width)),
            shaped((block_count, slots, width)),
            shaped((block_count, heads // 2, 2 * BLOCK, slots)),
            shaped((block_count, heads, slots), F32),
            shaped((groups, block_count * cap, rows * span)),
        ],
        in_specs=[smem] + [vmem] * (3 + chunks),
        out_specs=[vmem] * (chips + 5),
        scratch_shapes=[
            pltpu.VMEM((block_count, slots, HD), F32),
            pltpu.VMEM((block_count, slots, width), BF16),
        ],
        compiler_params=params,
        name="forward",
    )(me, aux_all, keys, values, *query_all)
    q_slots, probs, gates, hot = outs[chips + 1 :]

    grad_attn = jnp.einsum(
        "zqf,zfd->qd",
        grad_full,
        out_weight.reshape(features // width, width, width),
        preferred_element_type=F32,
    ).astype(BF16)
    terms = chip_terms(outs[:chips], outs[chips])
    attn_out, extended = pl.pallas_call(
        finish_kernel,
        out_shape=[shaped((rows, width)), shaped((rows, width + HD))],
        in_specs=[vmem] * (len(terms) + 1),
        out_specs=[vmem] * 2,
        compiler_params=params,
        name="finish",
    )(*terms, grad_attn)
    grad_chips = [extended] + [swap(extended, 2 * j) for j in range(1, chips)]
    grad_all = []
    for piece in grad_chips:
        grad_all += [piece, swap(piece, 1)]

    share = features // chips
    slabs, attns = [], [attn_out]
    for j in range(chips):
        first = ((index // 2) ^ j) * share
        slab = lax.dynamic_slice(
            grad_full, (first // width, 0, first % width), (1, rows, share)
        ).reshape(rows, share)
        slabs.append(swap(after(slab, *grad_chips), 2 * j) if j else slab)
    for j in range(1, chips):
        attns.append(swap(after(attn_out, *grad_chips), 2 * j))

    outs = pl.pallas_call(
        functools.partial(backward_kernel, chunks, span, cap),
        out_shape=[shaped((rows, width))] * chips
        + [shaped((chips, rows, width))]
        + [shaped((block_count, BLOCK, width), F32)] * 2,
        in_specs=[vmem] * (6 + chunks),
        out_specs=[vmem] * (chips + 3),
        scratch_shapes=[
            pltpu.VMEM((block_count, slots, width + HD), BF16),
            pltpu.VMEM((block_count, slots, width), BF16),
        ],
        compiler_params=params,
        name="backward",
    )(hot, q_slots, probs, gates, keys, values, *grad_all)
    key_grad, value_grad = outs[chips + 1 :]
    terms = chip_terms(outs[:chips], outs[chips])
    query_grad = terms[0].astype(F32)
    for term in terms[1:]:
        query_grad = query_grad + term.astype(F32)

    weight_own, weight_other = pl.pallas_call(
        functools.partial(weight_kernel, chips),
        out_shape=[shaped((share // 2, width), F32), shaped((share // 2, width))],
        in_specs=[smem] + [vmem] * (2 * chips),
        out_specs=[vmem] * 2,
        compiler_params=params,
        name="weight",
    )(me, *slabs, *attns)
    weight_grad = weight_own + swap(weight_other, 1).astype(F32)
    return (
        query_grad,
        key_grad.reshape(-1, width),
        value_grad.reshape(-1, width),
        weight_grad,
    )


def solution(mesh):
    return jax.shard_map(
        body,
        mesh=mesh,
        in_specs=(
            P("ctx", "head"),
            P("ctx", "head"),
            P("ctx", "head"),
            P("ctx", None),
            P("ctx", "head"),
            P(None, "head"),
        ),
        out_specs=(P("ctx", "head"), P("ctx", "head"), P("ctx", "head"), P("ctx", "head")),
        check_vma=False,
    )
```

```python
import functools

import jax
import jax.numpy as jnp
from jax import lax
from jax.experimental import pallas as pl
from jax.experimental.pallas import tpu as pltpu
from jax.sharding import PartitionSpec as P

HD = 128
BLOCK = 64
TOPK = 4
F32 = jnp.float32
BF16 = jnp.bfloat16
VMEM_LIMIT = 40 * 1024 * 1024
NN = (((1,), (0,)), ((), ()))
NT = (((1,), (1,)), ((), ()))
TN = (((0,), (0,)), ((), ()))


def mm(a, b, dims=NN):
    return lax.dot_general(a, b, dims, preferred_element_type=F32)


def joined(items, axis):
    return items[0] if len(items) == 1 else jnp.concatenate(items, axis=axis)


def dealt(refs, counts):
    lists, at = [], 0
    for count in counts:
        lists.append(refs[at : at + count])
        at += count
    return lists, refs[at:]


def whole(refs):
    return joined([ref[...] for ref in refs], 0)


def added(terms, cols):
    total = None
    for refs in terms:
        term = joined([ref[:, cols].astype(F32) for ref in refs], 0)
        total = term if total is None else total + term
    return total


def diagonal(pair):
    zero = jnp.zeros((pair.shape[0], HD), pair.dtype)
    top = jnp.concatenate([pair[:, :HD], zero], axis=1)
    low = jnp.concatenate([zero, pair[:, HD:]], axis=1)
    return jnp.concatenate([top, low], axis=0)


def gate_kernel(me_ref, sel_ref, mine_ref, other_ref, q_ref, aux_ref, mark_ref):
    chips, block_count, width = mine_ref.shape
    block_total = 2 * chips * block_count
    rows = q_ref.shape[0]
    me = me_ref[0]
    for j in range(chips):
        mark_ref[me ^ (2 * j)] = mine_ref[j]
        mark_ref[me ^ (2 * j + 1)] = other_ref[j]
    heads = width // HD
    scale = HD ** (-0.5)
    ids = lax.broadcasted_iota(jnp.int32, (block_total, rows), 0)
    picks = [sel_ref[t : t + 1, :] == ids for t in range(TOPK)]
    chosen = picks[0]
    for t in range(1, TOPK):
        chosen = chosen | picks[t]
    bias = jnp.where(chosen, 0.0, -1e30)
    gates = [[None] * heads for _ in range(TOPK)]
    for h in range(heads):
        cols = slice(h * HD, (h + 1) * HD)
        marks = mark_ref[:, :, cols].reshape(block_total, HD)
        logits = scale * mm(marks, q_ref[:, cols], NT) + bias
        weight = jnp.exp(logits - jnp.max(logits, axis=0, keepdims=True))
        inverse = 1.0 / jnp.sum(weight, axis=0, keepdims=True)
        for t in range(TOPK):
            gates[t][h] = inverse * jnp.sum(
                jnp.where(picks[t], weight, 0.0), axis=0, keepdims=True
            )
    high = (sel_ref[...] >> 4).astype(F32)
    low = (sel_ref[...] & 15).astype(F32)
    lines = [gates[t][h] for t in range(TOPK) for h in range(heads)] + [high, low]
    lines.append(jnp.zeros((HD - TOPK * heads - 2 * TOPK, rows), F32))
    aux_ref[...] = jnp.concatenate(lines, axis=0).astype(BF16)


def block_ids(aux, heads):
    at = TOPK * heads
    return 16.0 * aux[at : at + TOPK] + aux[at + TOPK : at + 2 * TOPK]


def forward_kernel(counts, span, cap, me_ref, mine_ref, other_ref, k_ref, v_ref, *refs):
    chunks = len(counts)
    q_refs, refs = dealt(refs, counts)
    part_refs, refs = refs[:chunks], refs[chunks:]
    qg_ref, p_ref, gate_ref, hot_ref, auxg_ref, out_ref = refs
    aux_refs = [(other_ref if m % 2 else mine_ref).at[m // 2] for m in range(chunks)]
    block_count, _, width = k_ref.shape
    heads = width // HD
    rows = part_refs[0].shape[0]
    group_rows = rows * span
    groups = chunks // span
    me = me_ref[0]
    rate = HD ** (-0.5) * 1.4426950408889634
    base = me * block_count

    before = lax.broadcasted_iota(jnp.int32, (group_rows, group_rows), 0)
    after = lax.broadcasted_iota(jnp.int32, (group_rows, group_rows), 1)
    earlier = (before < after).astype(BF16)
    own_ids = (base + lax.broadcasted_iota(jnp.int32, (block_count, group_rows), 0)).astype(F32)
    place = lax.broadcasted_iota(jnp.int32, (cap, group_rows), 0).astype(F32)
    for g in range(groups):
        aux = joined([aux_refs[g * span + i][...] for i in range(span)], 1)
        picked = block_ids(aux.astype(F32), heads)
        own = picked[0:1, :] == own_ids
        for t in range(1, TOPK):
            own = own | (picked[t : t + 1, :] == own_ids)
        own = jnp.where(own, 1.0, 0.0)
        rank = jnp.where(own > 0.5, mm(own.astype(BF16), earlier), -1.0)
        hot = jnp.concatenate(
            [jnp.where(rank[b : b + 1, :] == place, 1.0, 0.0) for b in range(block_count)], axis=0
        ).astype(BF16)
        hot_ref[g] = hot
        auxg_ref[:, g * cap : (g + 1) * cap, :] = mm(hot, aux, NT).reshape(block_count, cap, HD)
        q_group = joined([whole(q_refs[g * span + i]) for i in range(span)], 0)
        qg_ref[:, g * cap : (g + 1) * cap, :] = (
            mm(hot, q_group).astype(BF16).reshape(block_count, cap, width)
        )

    def one_block(b, carry):
        pairs = [slice(p * 2 * HD, (p + 1) * 2 * HD) for p in range(heads // 2)]
        logits = [mm(diagonal(k_ref[b, :, cols]), qg_ref[b, :, cols], NT) for cols in pairs]
        wide = [diagonal(v_ref[b, :, cols]) for cols in pairs]
        aux = auxg_ref[b].T
        ids = block_ids(aux, heads)
        mine = (base + b).astype(F32)
        gates = jnp.where(ids[0:1] == mine, aux[:heads], 0.0)
        for t in range(1, TOPK):
            gates = gates + jnp.where(
                ids[t : t + 1] == mine, aux[t * heads : (t + 1) * heads], 0.0
            )
        probs, gated = [], []
        for p in range(heads // 2):
            for i in range(2):
                part = logits[p][i * BLOCK : (i + 1) * BLOCK]
                weight = jnp.exp2(rate * (part - jnp.max(part, axis=0, keepdims=True)))
                inverse = 1.0 / jnp.sum(weight, axis=0, keepdims=True)
                gate = gates[2 * p + i : 2 * p + i + 1, :]
                probs.append((weight * inverse).astype(BF16))
                gated.append((weight * (inverse * gate)).astype(BF16))
        outs = [
            mm(jnp.concatenate(gated[2 * p : 2 * p + 2], axis=0), wide[p], TN).astype(BF16)
            for p in range(heads // 2)
        ]
        gate_ref[b] = gates
        for p in range(heads // 2):
            p_ref[b, p] = jnp.concatenate(probs[2 * p : 2 * p + 2], axis=0)
            out_ref[b, :, pairs[p]] = outs[p]
        return carry

    lax.fori_loop(0, block_count, one_block, 0)

    for g in range(groups):
        slots = out_ref[:, g * cap : (g + 1) * cap, :].reshape(block_count * cap, width)
        part = mm(hot_ref[g], slots, TN).astype(BF16)
        for i in range(span):
            part_refs[g * span + i][...] = part[i * rows : (i + 1) * rows]


def grad_kernel(lines, chips, at_ref, w_ref, *refs):
    own_ref, up_refs, down_refs = refs[0], refs[1:lines], refs[lines : 2 * lines - 1]
    ga_ref, slab_refs = refs[2 * lines - 1], refs[2 * lines : 2 * lines + chips]
    full_ref, w_buf, sems = refs[2 * lines + chips :]
    width = own_ref.shape[1]
    share = slab_refs[0].shape[1]
    line, chip = at_ref[0], at_ref[1]
    copies = [
        pltpu.make_async_copy(w_ref.at[pl.ds(i * width, width)], w_buf.at[i], sems.at[i])
        for i in range(lines)
    ]
    for copy in copies:
        copy.start()
    full_ref[line] = own_ref[...]
    for d in range(1, lines):

        @pl.when(line >= d)
        def _():
            full_ref[line - d] = up_refs[d - 1][...]

        @pl.when(line + d < lines)
        def _():
            full_ref[line + d] = down_refs[d - 1][...]

    for j in range(chips):
        first = (chip ^ j) * share
        cols = pl.ds(pl.multiple_of(first % width, HD), share)
        slab_refs[j][...] = full_ref[first // width, :, cols]
    total = None
    for i in range(lines):
        copies[i].wait()
        term = mm(full_ref[i], w_buf[i])
        total = term if total is None else total + term
    ga_ref[...] = total.astype(BF16)


def finish_kernel(counts, *refs):
    terms, (ga_ref, attn_ref, ext_ref) = dealt(refs, counts)
    rows, width = ga_ref.shape
    heads = width // HD
    lane = lax.broadcasted_iota(jnp.int32, (rows, HD), 1)
    high = jnp.zeros((rows, HD), F32)
    low = jnp.zeros((rows, HD), F32)
    ext_ref[:, :width] = ga_ref[...]
    for h in range(heads):
        cols = slice(h * HD, (h + 1) * HD)
        total = added(terms, cols)
        attn_ref[:, cols] = total.astype(BF16)
        dots = jnp.sum(total * ga_ref[:, cols].astype(F32), axis=1, keepdims=True)
        upper = dots.astype(BF16).astype(F32)
        high = jnp.where(lane == h, upper, high)
        low = jnp.where(lane == heads + h, dots - upper, low)
    ext_ref[:, width:] = (high + low).astype(BF16)


def total_kernel(counts, *refs):
    terms, (out_ref,) = dealt(refs, counts)
    for h in range(out_ref.shape[1] // HD):
        cols = slice(h * HD, (h + 1) * HD)
        out_ref[:, cols] = added(terms, cols)


def backward_kernel(counts, span, cap, hot_ref, qg_ref, p_ref, gate_ref, k_ref, v_ref, *refs):
    chunks = len(counts)
    ga_refs, refs = dealt(refs, counts)
    part_refs, refs = refs[:chunks], refs[chunks:]
    dk_ref, dv_ref, gag_ref, dq_ref = refs
    block_count, _, width = k_ref.shape
    heads = width // HD
    rows = part_refs[0].shape[0]
    groups = chunks // span
    scale = HD ** (-0.5)

    for g in range(groups):
        ga_group = joined([whole(ga_refs[g * span + i]) for i in range(span)], 0)
        gag_ref[:, g * cap : (g + 1) * cap, :] = (
            mm(hot_ref[g], ga_group).astype(BF16).reshape(block_count, cap, width + HD)
        )
    last = lax.broadcasted_iota(jnp.int32, (BLOCK, groups * cap), 0) == BLOCK - 1

    def one_block(b, carry):
        pairs = [slice(p * 2 * HD, (p + 1) * 2 * HD) for p in range(heads // 2)]
        q = [qg_ref[b, :, cols] for cols in pairs]
        ga = [gag_ref[b, :, cols] for cols in pairs]
        grads = [mm(diagonal(v_ref[b, :, cols]), ga[p], NT) for p, cols in enumerate(pairs)]
        wide = [diagonal(k_ref[b, :, cols]) for cols in pairs]
        probs = [p_ref[b, p].astype(F32) for p in range(heads // 2)]
        gates = gate_ref[b]
        dots = gag_ref[b, :, width:].astype(F32).T
        dots = dots[:heads] + dots[heads : 2 * heads]
        gated, score = [], []
        for p in range(heads // 2):
            for i in range(2):
                at = slice(i * BLOCK, (i + 1) * BLOCK)
                h = 2 * p + i
                gate = gates[h : h + 1, :]
                grad = grads[p][at]
                delta = jnp.sum(probs[p][at] * grad, axis=0, keepdims=True)
                weight = probs[p][at] * gate
                extra = jnp.where(last, scale * gate * (delta - dots[h : h + 1, :]), 0.0)
                score.append((weight * (scale * (grad - delta)) + extra).astype(BF16))
                gated.append(weight.astype(BF16))
        for p, cols in enumerate(pairs):
            both = jnp.concatenate(gated[2 * p : 2 * p + 2], axis=0)
            scores = jnp.concatenate(score[2 * p : 2 * p + 2], axis=0)
            dv = mm(both, ga[p])
            dk = mm(scores, q[p])
            dq = mm(scores, wide[p], TN).astype(BF16)
            dv_ref[b, :, cols] = jnp.concatenate([dv[:BLOCK, :HD], dv[BLOCK:, HD:]], axis=1)
            dk_ref[b, :, cols] = jnp.concatenate([dk[:BLOCK, :HD], dk[BLOCK:, HD:]], axis=1)
            dq_ref[b, :, cols] = dq
        return carry

    lax.fori_loop(0, block_count, one_block, 0)

    for g in range(groups):
        slots = dq_ref[:, g * cap : (g + 1) * cap, :].reshape(block_count * cap, width)
        part = mm(hot_ref[g], slots, TN).astype(BF16)
        for i in range(span):
            part_refs[g * span + i][...] = part[i * rows : (i + 1) * rows]


def weight_kernel(counts, me_ref, *refs):
    chips = len(counts)
    slabs = refs[:chips]
    attns, (own_ref, other_ref) = dealt(refs[chips:], counts)
    half = own_ref.shape[0]
    core = me_ref[0] % 2
    attn = joined([whole(pieces) for pieces in attns], 0)

    def side(which):
        cols = pl.ds(pl.multiple_of(which * half, half), half)
        return mm(joined([ref[:, cols] for ref in slabs], 0), attn, TN)

    own_ref[...] = side(core)
    other_ref[...] = side(1 - core).astype(BF16)


def swap(x, bits):
    count = lax.axis_size("ctx")
    return lax.ppermute(x, "ctx", [(i, i ^ bits) for i in range(count)])


def after(x, *others):
    return lax.optimization_barrier((x, *others))[0]


def flat(lists):
    return [x for pieces in lists for x in pieces]


def spread_chips(x):
    chips = lax.axis_size("ctx") // 2
    if chips != 4:
        return [[x]] + [[swap(x, 2 * j)] for j in range(1, chips)]
    half = x.shape[0] // 2
    top, low = x[:half], x[half:]
    x_top, y_low = swap(top, 2), swap(low, 4)
    x_low, y_top = swap(low, 2), swap(top, 4)
    return [[x], [x_top, x_low], [y_top, y_low], [swap(x_top, 4), swap(y_low, 2)]]


def collect_chips(parts):
    chips = len(parts) // 2
    received = [None] * chips
    for j in reversed(range(chips)):
        received[j] = swap(parts[2 * j + 1], 1)

    def both(j, rows, extra=None):
        total = parts[2 * j][rows].astype(F32) + received[j][rows].astype(F32)
        if extra is not None:
            total = total + extra.astype(F32)
        return total.astype(BF16)

    terms = [[parts[0]], [received[0]]]
    if chips != 4:
        return terms + [[swap(both(j, slice(None)), 2 * j)] for j in range(1, chips)]
    half = parts[0].shape[0] // 2
    top, low = slice(0, half), slice(half, None)
    x_far, y_far = swap(both(3, top), 2), swap(both(3, low), 4)
    x_top, y_low = swap(both(1, top), 2), swap(both(2, low), 4)
    x_low, y_top = swap(both(1, low, y_far), 2), swap(both(2, top, x_far), 4)
    return terms + [[x_top, x_low], [y_top, y_low]]


def spread_line(x):
    lines = lax.axis_size("head")
    ups, downs = [x], [x]
    for d in range(1, lines):
        ups.append(lax.ppermute(ups[-1], "head", [(i, i + 1) for i in range(d - 1, lines - 1)]))
        downs.append(lax.ppermute(downs[-1], "head", [(i, i - 1) for i in range(1, lines - d + 1)]))
    return ups[1:], downs[1:]


def body(queries, key_rows, value_rows, selected, out_grad, out_weight):
    chunks = lax.axis_size("ctx")
    chips = chunks // 2
    lines = lax.axis_size("head")
    rows, width = queries.shape
    features = out_weight.shape[0]
    share = features // chips
    heads = width // HD
    block_count = key_rows.shape[0] // BLOCK
    block_total = block_count * chunks
    capacity = 2 * rows * TOPK // block_total
    span = max(1, 16 // capacity)
    cap = capacity * span
    groups = chunks // span
    slots = groups * cap
    index = lax.axis_index("ctx").astype(jnp.int32)
    me = index.reshape(1)
    at = jnp.stack([lax.axis_index("head").astype(jnp.int32), index // 2])
    keys = key_rows.reshape(block_count, BLOCK, width)
    values = value_rows.reshape(block_count, BLOCK, width)
    vmem = pl.BlockSpec(memory_space=pltpu.VMEM)
    smem = pl.BlockSpec(memory_space=pltpu.SMEM)
    params = pltpu.CompilerParams(vmem_limit_bytes=VMEM_LIMIT)

    def shaped(shape, kind=BF16):
        return jax.ShapeDtypeStruct(shape, kind)

    marks = keys[:, BLOCK - 1]
    marks = jnp.stack([marks] + [swap(marks, 2 * j) for j in range(1, chips)])
    ups, downs = spread_line(out_grad)
    query_chips = spread_chips(queries)
    aux = pl.pallas_call(
        gate_kernel,
        out_shape=shaped((HD, rows)),
        in_specs=[smem] + [vmem] * 4,
        out_specs=vmem,
        scratch_shapes=[pltpu.VMEM((chunks, block_count, width), BF16)],
        compiler_params=params,
        name="gates",
    )(me, selected.T, marks, swap(marks, 1), queries)
    aux = jnp.stack([aux] + [swap(aux, 2 * j) for j in range(1, chips)])
    query_all = []
    for pieces in query_chips:
        query_all += [pieces, [swap(piece, 1) for piece in pieces]]

    outs = pl.pallas_call(
        functools.partial(forward_kernel, [len(pieces) for pieces in query_all], span, cap),
        out_shape=[shaped((rows, width))] * chunks
        + [
            shaped((block_count, slots, width)),
            shaped((block_count, heads // 2, 2 * BLOCK, slots)),
            shaped((block_count, heads, slots), F32),
            shaped((groups, block_count * cap, rows * span)),
        ],
        in_specs=[smem] + [vmem] * (4 + len(flat(query_all))),
        out_specs=[vmem] * (chunks + 4),
        scratch_shapes=[
            pltpu.VMEM((block_count, slots, HD), F32),
            pltpu.VMEM((block_count, slots, width), BF16),
        ],
        compiler_params=params,
        name="forward",
    )(me, aux, swap(aux, 1), keys, values, *flat(query_all))
    q_slots, probs, gates, hot = outs[chunks:]

    grad_attn, *slabs = pl.pallas_call(
        functools.partial(grad_kernel, lines, chips),
        out_shape=[shaped((rows, width))] + [shaped((rows, share))] * chips,
        in_specs=[smem, pl.BlockSpec(memory_space=pl.ANY)] + [vmem] * (2 * lines - 1),
        out_specs=[vmem] * (1 + chips),
        scratch_shapes=[
            pltpu.VMEM((lines, rows, width), BF16),
            pltpu.VMEM((lines, width, width), BF16),
            pltpu.SemaphoreType.DMA((lines,)),
        ],
        compiler_params=params,
        name="grad",
    )(at, out_weight, out_grad, *ups, *downs)
    terms = collect_chips(outs[:chunks])
    attn_out, extended = pl.pallas_call(
        functools.partial(finish_kernel, [len(pieces) for pieces in terms]),
        out_shape=[shaped((rows, width)), shaped((rows, width + HD))],
        in_specs=[vmem] * (len(flat(terms)) + 1),
        out_specs=[vmem] * 2,
        compiler_params=params,
        name="finish",
    )(*flat(terms), grad_attn)
    grad_chips = spread_chips(extended)
    grad_all = []
    for pieces in grad_chips:
        grad_all += [pieces, [swap(piece, 1) for piece in pieces]]

    arrived = flat(grad_chips)
    attns = spread_chips(after(attn_out, *arrived))
    slabs = [slabs[0]] + [swap(after(slabs[j], *arrived), 2 * j) for j in range(1, chips)]

    outs = pl.pallas_call(
        functools.partial(backward_kernel, [len(pieces) for pieces in grad_all], span, cap),
        out_shape=[shaped((rows, width))] * chunks
        + [shaped((block_count, BLOCK, width), F32)] * 2,
        in_specs=[vmem] * (6 + len(flat(grad_all))),
        out_specs=[vmem] * (chunks + 2),
        scratch_shapes=[
            pltpu.VMEM((block_count, slots, width + HD), BF16),
            pltpu.VMEM((block_count, slots, width), BF16),
        ],
        compiler_params=params,
        name="backward",
    )(hot, q_slots, probs, gates, keys, values, *flat(grad_all))
    key_grad, value_grad = outs[chunks:]
    terms = collect_chips(outs[:chunks])
    query_grad = pl.pallas_call(
        functools.partial(total_kernel, [len(pieces) for pieces in terms]),
        out_shape=shaped((rows, width), F32),
        in_specs=[vmem] * len(flat(terms)),
        out_specs=vmem,
        compiler_params=params,
        name="total",
    )(*flat(terms))

    weight_own, weight_other = pl.pallas_call(
        functools.partial(weight_kernel, [len(pieces) for pieces in attns]),
        out_shape=[shaped((share // 2, width), F32), shaped((share // 2, width))],
        in_specs=[smem] + [vmem] * (chips + len(flat(attns))),
        out_specs=[vmem] * 2,
        compiler_params=params,
        name="weight",
    )(me, *slabs, *flat(attns))
    weight_grad = weight_own + swap(weight_other, 1).astype(F32)
    return (
        query_grad,
        key_grad.reshape(-1, width),
        value_grad.reshape(-1, width),
        weight_grad,
    )


def solution(mesh):
    return jax.shard_map(
        body,
        mesh=mesh,
        in_specs=(
            P("ctx", "head"),
            P("ctx", "head"),
            P("ctx", "head"),
            P("ctx", None),
            P("ctx", "head"),
            P(None, "head"),
        ),
        out_specs=(P("ctx", "head"), P("ctx", "head"), P("ctx", "head"), P("ctx", "head")),
        check_vma=False,
    )
```

```python
import functools

import jax
import jax.numpy as jnp
from jax import lax
from jax.experimental import pallas as pl
from jax.experimental.pallas import tpu as pltpu
from jax.sharding import PartitionSpec as P

HD = 128
BLOCK = 64
TOPK = 4
F32 = jnp.float32
BF16 = jnp.bfloat16
MIB = 1024 * 1024
NN = (((1,), (0,)), ((), ()))
NT = (((1,), (1,)), ((), ()))
TN = (((0,), (0,)), ((), ()))


def mm(a, b, dims=NN):
    return lax.dot_general(a, b, dims, preferred_element_type=F32)


def joined(items, axis):
    return items[0] if len(items) == 1 else jnp.concatenate(items, axis=axis)


def dealt(refs, counts):
    lists, at = [], 0
    for count in counts:
        lists.append(refs[at : at + count])
        at += count
    return lists, refs[at:]


def loads(lists, buf, sems):
    copies, at = [], 0
    for i, refs in enumerate(lists):
        mine, row = [], 0
        for ref in refs:
            rows = ref.shape[0]
            mine.append(
                pltpu.make_async_copy(ref, buf.at[i, pl.ds(row, rows)], sems.at[at])
            )
            row += rows
            at += 1
        copies.append(mine)
    return copies


def start(copies):
    for copy in copies:
        copy.start()


def wait(copies):
    for copy in copies:
        copy.wait()


def added(terms, cols):
    total = None
    for refs in terms:
        term = joined([ref[:, cols].astype(F32) for ref in refs], 0)
        total = term if total is None else total + term
    return total


def diagonal(pair):
    zero = jnp.zeros((pair.shape[0], HD), pair.dtype)
    top = jnp.concatenate([pair[:, :HD], zero], axis=1)
    low = jnp.concatenate([zero, pair[:, HD:]], axis=1)
    return jnp.concatenate([top, low], axis=0)


def gate_kernel(me_ref, sel_ref, mine_ref, other_ref, q_ref, aux_ref, mark_ref):
    chips, block_count, width = mine_ref.shape
    block_total = 2 * chips * block_count
    rows = q_ref.shape[0]
    me = me_ref[0]
    for j in range(chips):
        mark_ref[me ^ (2 * j)] = mine_ref[j]
        mark_ref[me ^ (2 * j + 1)] = other_ref[j]
    heads = width // HD
    scale = HD ** (-0.5)
    ids = lax.broadcasted_iota(jnp.int32, (block_total, rows), 0)
    picks = [sel_ref[t : t + 1, :] == ids for t in range(TOPK)]
    chosen = picks[0]
    for t in range(1, TOPK):
        chosen = chosen | picks[t]
    bias = jnp.where(chosen, 0.0, -1e30)
    gates = [[None] * heads for _ in range(TOPK)]
    for h in range(heads):
        cols = slice(h * HD, (h + 1) * HD)
        marks = mark_ref[:, :, cols].reshape(block_total, HD)
        logits = scale * mm(marks, q_ref[:, cols], NT) + bias
        weight = jnp.exp(logits - jnp.max(logits, axis=0, keepdims=True))
        inverse = 1.0 / jnp.sum(weight, axis=0, keepdims=True)
        for t in range(TOPK):
            gates[t][h] = inverse * jnp.sum(
                jnp.where(picks[t], weight, 0.0), axis=0, keepdims=True
            )
    high = (sel_ref[...] >> 4).astype(F32)
    low = (sel_ref[...] & 15).astype(F32)
    lines = [gates[t][h] for t in range(TOPK) for h in range(heads)] + [high, low]
    lines.append(jnp.zeros((HD - TOPK * heads - 2 * TOPK, rows), F32))
    aux_ref[...] = jnp.concatenate(lines, axis=0).astype(BF16)


def block_ids(aux, heads):
    at = TOPK * heads
    return 16.0 * aux[at : at + TOPK] + aux[at + TOPK : at + 2 * TOPK]


def forward_kernel(counts, span, cap, me_ref, mine_ref, other_ref, k_any, v_any, *refs):
    chunks = len(counts)
    q_refs, refs = dealt(refs, counts)
    part_refs, refs = refs[:chunks], refs[chunks:]
    qg_any, p_any, gate_ref, hot_any = refs[:4]
    q_buf, k_ref, v_ref, qg_ref, p_ref, hot_ref, auxg_ref, out_ref, in_sems, kv_sems, out_sems = refs[4:]
    q_copies = loads(q_refs, q_buf, in_sems)
    kv_copies = [
        pltpu.make_async_copy(k_any, k_ref, kv_sems.at[0]),
        pltpu.make_async_copy(v_any, v_ref, kv_sems.at[1]),
    ]
    out_copies = [
        pltpu.make_async_copy(qg_ref, qg_any, out_sems.at[chunks]),
        pltpu.make_async_copy(hot_ref, hot_any, out_sems.at[chunks + 1]),
        pltpu.make_async_copy(p_ref, p_any, out_sems.at[chunks + 2]),
    ]
    for copies in q_copies:
        start(copies)
    start(kv_copies)
    aux_refs = [(other_ref if m % 2 else mine_ref).at[m // 2] for m in range(chunks)]
    block_count, _, width = k_ref.shape
    heads = width // HD
    rows = part_refs[0].shape[0]
    group_rows = rows * span
    groups = chunks // span
    me = me_ref[0]
    rate = HD ** (-0.5) * 1.4426950408889634
    base = me * block_count

    before = lax.broadcasted_iota(jnp.int32, (group_rows, group_rows), 0)
    after = lax.broadcasted_iota(jnp.int32, (group_rows, group_rows), 1)
    earlier = (before < after).astype(BF16)
    own_ids = (base + lax.broadcasted_iota(jnp.int32, (block_count, group_rows), 0)).astype(F32)
    place = lax.broadcasted_iota(jnp.int32, (cap, group_rows), 0).astype(F32)
    for g in range(groups):
        aux = joined([aux_refs[g * span + i][...] for i in range(span)], 1)
        picked = block_ids(aux.astype(F32), heads)
        own = picked[0:1, :] == own_ids
        for t in range(1, TOPK):
            own = own | (picked[t : t + 1, :] == own_ids)
        own = jnp.where(own, 1.0, 0.0)
        rank = jnp.where(own > 0.5, mm(own.astype(BF16), earlier), -1.0)
        hot = jnp.concatenate(
            [jnp.where(rank[b : b + 1, :] == place, 1.0, 0.0) for b in range(block_count)], axis=0
        ).astype(BF16)
        hot_ref[g] = hot
        auxg_ref[:, g * cap : (g + 1) * cap, :] = mm(hot, aux, NT).reshape(block_count, cap, HD)
        for i in range(span):
            wait(q_copies[g * span + i])
        q_group = joined([q_buf[g * span + i] for i in range(span)], 0)
        qg_ref[:, g * cap : (g + 1) * cap, :] = (
            mm(hot, q_group).astype(BF16).reshape(block_count, cap, width)
        )

    start(out_copies[:2])
    wait(kv_copies)

    def one_block(b, carry):
        pairs = [slice(p * 2 * HD, (p + 1) * 2 * HD) for p in range(heads // 2)]
        logits = [mm(diagonal(k_ref[b, :, cols]), qg_ref[b, :, cols], NT) for cols in pairs]
        wide = [diagonal(v_ref[b, :, cols]) for cols in pairs]
        aux = auxg_ref[b].T
        ids = block_ids(aux, heads)
        mine = (base + b).astype(F32)
        gates = jnp.where(ids[0:1] == mine, aux[:heads], 0.0)
        for t in range(1, TOPK):
            gates = gates + jnp.where(
                ids[t : t + 1] == mine, aux[t * heads : (t + 1) * heads], 0.0
            )
        probs, gated = [], []
        for p in range(heads // 2):
            for i in range(2):
                part = logits[p][i * BLOCK : (i + 1) * BLOCK]
                weight = jnp.exp2(rate * (part - jnp.max(part, axis=0, keepdims=True)))
                inverse = 1.0 / jnp.sum(weight, axis=0, keepdims=True)
                gate = gates[2 * p + i : 2 * p + i + 1, :]
                probs.append((weight * inverse).astype(BF16))
                gated.append((weight * (inverse * gate)).astype(BF16))
        outs = [
            mm(jnp.concatenate(gated[2 * p : 2 * p + 2], axis=0), wide[p], TN).astype(BF16)
            for p in range(heads // 2)
        ]
        gate_ref[b] = gates
        for p in range(heads // 2):
            p_ref[b, p] = jnp.concatenate(probs[2 * p : 2 * p + 2], axis=0)
            out_ref[b, :, pairs[p]] = outs[p]
        return carry

    lax.fori_loop(0, block_count, one_block, 0)
    start(out_copies[2:])

    for g in range(groups):
        slots = out_ref[:, g * cap : (g + 1) * cap, :].reshape(block_count * cap, width)
        part = mm(hot_ref[g], slots, TN).astype(BF16)
        for i in range(span):
            m = g * span + i
            q_buf[m] = part[i * rows : (i + 1) * rows]
            copy = pltpu.make_async_copy(q_buf.at[m], part_refs[m], out_sems.at[m])
            copy.start()
            out_copies.append(copy)
    wait(out_copies)


def grad_kernel(lines, chips, at_ref, w_ref, *refs):
    own_ref, up_refs, down_refs = refs[0], refs[1:lines], refs[lines : 2 * lines - 1]
    ga_ref, slab_refs = refs[2 * lines - 1], refs[2 * lines : 2 * lines + chips]
    full_ref, w_buf, sems, piece_sems = refs[2 * lines + chips :]
    width = own_ref.shape[1]
    share = slab_refs[0].shape[1]
    line, chip = at_ref[0], at_ref[1]

    def placed(ref, i):
        return pltpu.make_async_copy(ref, full_ref.at[i], piece_sems.at[i])

    placed(own_ref, line).start()
    for d in range(1, lines):

        @pl.when(line >= d)
        def _():
            placed(up_refs[d - 1], line - d).start()

        @pl.when(line + d < lines)
        def _():
            placed(down_refs[d - 1], line + d).start()

    copies = [
        pltpu.make_async_copy(w_ref.at[pl.ds(i * width, width)], w_buf.at[i], sems.at[i])
        for i in range(lines)
    ]
    start(copies)
    for i in range(lines):
        placed(own_ref, i).wait()
    for j in range(chips):
        first = (chip ^ j) * share
        cols = pl.ds(pl.multiple_of(first % width, HD), share)
        slab_refs[j][...] = full_ref[first // width, :, cols]
    total = None
    for i in range(lines):
        copies[i].wait()
        term = mm(full_ref[i], w_buf[i])
        total = term if total is None else total + term
    ga_ref[...] = total.astype(BF16)


def finish_kernel(counts, *refs):
    terms, (ga_ref, attn_ref, ext_ref) = dealt(refs, counts)
    rows, width = ga_ref.shape
    heads = width // HD
    lane = lax.broadcasted_iota(jnp.int32, (rows, HD), 1)
    high = jnp.zeros((rows, HD), F32)
    low = jnp.zeros((rows, HD), F32)
    ext_ref[:, :width] = ga_ref[...]
    for h in range(heads):
        cols = slice(h * HD, (h + 1) * HD)
        total = added(terms, cols)
        attn_ref[:, cols] = total.astype(BF16)
        dots = jnp.sum(total * ga_ref[:, cols].astype(F32), axis=1, keepdims=True)
        upper = dots.astype(BF16).astype(F32)
        high = jnp.where(lane == h, upper, high)
        low = jnp.where(lane == heads + h, dots - upper, low)
    ext_ref[:, width:] = (high + low).astype(BF16)


def total_kernel(counts, *refs):
    terms, (out_ref,) = dealt(refs, counts)
    for h in range(out_ref.shape[1] // HD):
        cols = slice(h * HD, (h + 1) * HD)
        out_ref[:, cols] = added(terms, cols)


def backward_kernel(counts, span, cap, gate_ref, hot_any, qg_any, p_any, k_any, v_any, *refs):
    chunks = len(counts)
    ga_refs, refs = dealt(refs, counts)
    part_refs, refs = refs[:chunks], refs[chunks:]
    dk_any, dv_any = refs[:2]
    ga_buf, hot_ref, qg_ref, p_ref, k_ref, v_ref, gag_ref, dq_ref, dk_ref, dv_ref = refs[2:12]
    in_sems, hot_sem, block_sems, out_sems, part_sems = refs[12:]
    ga_copies = loads(ga_refs, ga_buf, in_sems)
    hot_copy = pltpu.make_async_copy(hot_any, hot_ref, hot_sem.at[0])
    hot_copy.start()
    for copies in ga_copies:
        start(copies)

    def block_loads(b):
        pairs = ((qg_any, qg_ref), (p_any, p_ref), (k_any, k_ref), (v_any, v_ref))
        return [
            pltpu.make_async_copy(far.at[b], near.at[b], block_sems.at[i, b])
            for i, (far, near) in enumerate(pairs)
        ]

    def block_stores(b):
        return [
            pltpu.make_async_copy(dk_ref.at[b], dk_any.at[b], out_sems.at[0, b]),
            pltpu.make_async_copy(dv_ref.at[b], dv_any.at[b], out_sems.at[1, b]),
        ]

    block_count, _, width = k_ref.shape
    heads = width // HD
    rows = part_refs[0].shape[0]
    groups = chunks // span
    scale = HD ** (-0.5)

    for b in range(block_count):
        start(block_loads(b))
    hot_copy.wait()
    for g in range(groups):
        for i in range(span):
            wait(ga_copies[g * span + i])
        ga_group = joined([ga_buf[g * span + i] for i in range(span)], 0)
        gag_ref[:, g * cap : (g + 1) * cap, :] = (
            mm(hot_ref[g], ga_group).astype(BF16).reshape(block_count, cap, width + HD)
        )
    last = lax.broadcasted_iota(jnp.int32, (BLOCK, groups * cap), 0) == BLOCK - 1

    def one_block(b, carry):
        wait(block_loads(b))
        pairs = [slice(p * 2 * HD, (p + 1) * 2 * HD) for p in range(heads // 2)]
        q = [qg_ref[b, :, cols] for cols in pairs]
        ga = [gag_ref[b, :, cols] for cols in pairs]
        grads = [mm(diagonal(v_ref[b, :, cols]), ga[p], NT) for p, cols in enumerate(pairs)]
        wide = [diagonal(k_ref[b, :, cols]) for cols in pairs]
        probs = [p_ref[b, p].astype(F32) for p in range(heads // 2)]
        gates = gate_ref[b]
        dots = gag_ref[b, :, width:].astype(F32).T
        dots = dots[:heads] + dots[heads : 2 * heads]
        gated, score = [], []
        for p in range(heads // 2):
            for i in range(2):
                at = slice(i * BLOCK, (i + 1) * BLOCK)
                h = 2 * p + i
                gate = gates[h : h + 1, :]
                grad = grads[p][at]
                delta = jnp.sum(probs[p][at] * grad, axis=0, keepdims=True)
                weight = probs[p][at] * gate
                extra = jnp.where(last, scale * gate * (delta - dots[h : h + 1, :]), 0.0)
                score.append((weight * (scale * (grad - delta)) + extra).astype(BF16))
                gated.append(weight.astype(BF16))
        for p, cols in enumerate(pairs):
            both = jnp.concatenate(gated[2 * p : 2 * p + 2], axis=0)
            scores = jnp.concatenate(score[2 * p : 2 * p + 2], axis=0)
            dv = mm(both, ga[p])
            dk = mm(scores, q[p])
            dq = mm(scores, wide[p], TN).astype(BF16)
            dv_ref[b, :, cols] = jnp.concatenate([dv[:BLOCK, :HD], dv[BLOCK:, HD:]], axis=1)
            dk_ref[b, :, cols] = jnp.concatenate([dk[:BLOCK, :HD], dk[BLOCK:, HD:]], axis=1)
            dq_ref[b, :, cols] = dq
        start(block_stores(b))
        return carry

    lax.fori_loop(0, block_count, one_block, 0)

    part_copies = []

    for g in range(groups):
        slots = dq_ref[:, g * cap : (g + 1) * cap, :].reshape(block_count * cap, width)
        part = mm(hot_ref[g], slots, TN).astype(BF16)
        for i in range(span):
            m = g * span + i
            ga_buf[m, :, :width] = part[i * rows : (i + 1) * rows]
            copy = pltpu.make_async_copy(
                ga_buf.at[m, :, pl.ds(0, width)], part_refs[m], part_sems.at[m]
            )
            copy.start()
            part_copies.append(copy)
    for b in range(block_count):
        wait(block_stores(b))
    wait(part_copies)


def weight_kernel(counts, me_ref, *refs):
    chips = len(counts)
    slabs = refs[:chips]
    attns, (own_ref, other_ref) = dealt(refs[chips:], counts)
    half = own_ref.shape[0]
    core = me_ref[0] % 2
    attn = joined([ref[...] for pieces in attns for ref in pieces], 0)

    def side(which):
        cols = pl.ds(pl.multiple_of(which * half, half), half)
        return mm(joined([ref[:, cols] for ref in slabs], 0), attn, TN)

    own_ref[...] = side(core)
    other_ref[...] = side(1 - core).astype(BF16)


def swap(x, bits):
    count = lax.axis_size("ctx")
    return lax.ppermute(x, "ctx", [(i, i ^ bits) for i in range(count)])


def after(x, *others):
    return lax.optimization_barrier((x, *others))[0]


def flat(lists):
    return [x for pieces in lists for x in pieces]


def spread_chips(x):
    chips = lax.axis_size("ctx") // 2
    if chips != 4:
        return [[x]] + [[swap(x, 2 * j)] for j in range(1, chips)]
    half = x.shape[0] // 2
    top, low = x[:half], x[half:]
    x_top, y_low = swap(top, 2), swap(low, 4)
    x_low, y_top = swap(low, 2), swap(top, 4)
    return [[x], [x_top, x_low], [y_top, y_low], [swap(x_top, 4), swap(y_low, 2)]]


def collect_chips(parts, *before):
    chips = len(parts) // 2
    received = [None] * chips
    for j in reversed(range(chips)):
        received[j] = after(swap(parts[2 * j + 1], 1), *before)

    def both(j, rows, extra=None):
        total = parts[2 * j][rows].astype(F32) + received[j][rows].astype(F32)
        if extra is not None:
            total = total + extra.astype(F32)
        return total.astype(BF16)

    terms = [[parts[0]], [received[0]]]
    if chips != 4:
        terms += [[swap(both(j, slice(None)), 2 * j)] for j in range(1, chips)]
        return terms, terms[2][0]
    half = parts[0].shape[0] // 2
    top, low = slice(0, half), slice(half, None)
    x_far, y_far = swap(both(3, top), 2), swap(both(3, low), 4)
    x_top, y_low = swap(both(1, top), 2), swap(both(2, low), 4)
    x_low, y_top = swap(both(1, low, y_far), 2), swap(both(2, top, x_far), 4)
    return terms + [[x_top, x_low], [y_top, y_low]], y_far


def spread_line(x):
    lines = lax.axis_size("head")
    ups, downs = [x], [x]
    for d in range(1, lines):
        ups.append(lax.ppermute(ups[-1], "head", [(i, i + 1) for i in range(d - 1, lines - 1)]))
        downs.append(lax.ppermute(downs[-1], "head", [(i, i - 1) for i in range(1, lines - d + 1)]))
    return ups[1:], downs[1:]


def body(queries, key_rows, value_rows, selected, out_grad, out_weight):
    chunks = lax.axis_size("ctx")
    chips = chunks // 2
    lines = lax.axis_size("head")
    rows, width = queries.shape
    features = out_weight.shape[0]
    share = features // chips
    heads = width // HD
    block_count = key_rows.shape[0] // BLOCK
    block_total = block_count * chunks
    capacity = 2 * rows * TOPK // block_total
    span = max(1, 16 // capacity)
    cap = capacity * span
    groups = chunks // span
    slots = groups * cap
    index = lax.axis_index("ctx").astype(jnp.int32)
    me = index.reshape(1)
    at = jnp.stack([lax.axis_index("head").astype(jnp.int32), index // 2])
    keys = key_rows.reshape(block_count, BLOCK, width)
    values = value_rows.reshape(block_count, BLOCK, width)
    vmem = pl.BlockSpec(memory_space=pltpu.VMEM)
    smem = pl.BlockSpec(memory_space=pltpu.SMEM)
    anywhere = pl.BlockSpec(memory_space=pl.ANY)

    def limit(mib):
        return pltpu.CompilerParams(vmem_limit_bytes=mib * MIB)

    def shaped(shape, kind=BF16):
        return jax.ShapeDtypeStruct(shape, kind)

    marks = keys[:, BLOCK - 1]
    marks = jnp.stack([marks] + [swap(marks, 2 * j) for j in range(1, chips)])
    ups, downs = spread_line(out_grad)
    query_chips = spread_chips(queries)
    first = [query_chips[1][0], query_chips[-1][0] if chips != 4 else query_chips[2][1]]
    aux = pl.pallas_call(
        gate_kernel,
        out_shape=shaped((HD, rows)),
        in_specs=[smem] + [vmem] * 4,
        out_specs=vmem,
        scratch_shapes=[pltpu.VMEM((chunks, block_count, width), BF16)],
        compiler_params=limit(24),
        name="gates",
    )(me, selected.T, after(marks, *first), swap(marks, 1), queries)
    aux = jnp.stack([aux] + [swap(aux, 2 * j) for j in range(1, chips)])
    query_all = [[queries], [swap(after(queries, ups[0], downs[0]), 1)]]
    for pieces in query_chips[1:]:
        query_all += [pieces, [swap(piece, 1) for piece in pieces]]

    outs = pl.pallas_call(
        functools.partial(forward_kernel, [len(pieces) for pieces in query_all], span, cap),
        out_shape=[shaped((rows, width))] * chunks
        + [
            shaped((block_count, slots, width)),
            shaped((block_count, heads // 2, 2 * BLOCK, slots)),
            shaped((block_count, heads, slots), F32),
            shaped((groups, block_count * cap, rows * span)),
        ],
        in_specs=[smem] + [vmem] * 2 + [anywhere] * (2 + len(flat(query_all))),
        out_specs=[anywhere] * (chunks + 2) + [vmem, anywhere],
        scratch_shapes=[
            pltpu.VMEM((chunks, rows, width), BF16),
            pltpu.VMEM((block_count, BLOCK, width), BF16),
            pltpu.VMEM((block_count, BLOCK, width), BF16),
            pltpu.VMEM((block_count, slots, width), BF16),
            pltpu.VMEM((block_count, heads // 2, 2 * BLOCK, slots), BF16),
            pltpu.VMEM((groups, block_count * cap, rows * span), BF16),
            pltpu.VMEM((block_count, slots, HD), F32),
            pltpu.VMEM((block_count, slots, width), BF16),
            pltpu.SemaphoreType.DMA((len(flat(query_all)),)),
            pltpu.SemaphoreType.DMA((2,)),
            pltpu.SemaphoreType.DMA((chunks + 3,)),
        ],
        compiler_params=limit(36),
        name="forward",
    )(after(me, *ups[:2], *downs[:2]), aux, swap(aux, 1), keys, values, *flat(query_all))
    q_slots, probs, gates, hot = outs[chunks:]

    grad_attn, *slabs = pl.pallas_call(
        functools.partial(grad_kernel, lines, chips),
        out_shape=[shaped((rows, width))] + [shaped((rows, share))] * chips,
        in_specs=[smem] + [anywhere] * (2 * lines),
        out_specs=[vmem] * (1 + chips),
        scratch_shapes=[
            pltpu.VMEM((lines, rows, width), BF16),
            pltpu.VMEM((lines, width, width), BF16),
            pltpu.SemaphoreType.DMA((lines,)),
            pltpu.SemaphoreType.DMA((lines,)),
        ],
        compiler_params=limit(24),
        name="grad",
    )(at, out_weight, out_grad, *ups, *downs)
    terms, _ = collect_chips(outs[:chunks], grad_attn)
    attn_out, extended = pl.pallas_call(
        functools.partial(finish_kernel, [len(pieces) for pieces in terms]),
        out_shape=[shaped((rows, width)), shaped((rows, width + HD))],
        in_specs=[vmem] * (len(flat(terms)) + 1),
        out_specs=[vmem] * 2,
        compiler_params=limit(24),
        name="finish",
    )(*flat(terms), grad_attn)
    grad_chips = spread_chips(extended)
    grad_all = []
    for pieces in grad_chips:
        grad_all += [pieces, [swap(piece, 1) for piece in pieces]]

    arrived = flat(grad_chips[1:3])
    attns = [[attn_out]] + [[swap(after(attn_out, *arrived), 2 * j)] for j in range(1, chips)]
    slabs = [slabs[0]] + [swap(after(slabs[j], *arrived), 2 * j) for j in range(1, chips)]

    outs = pl.pallas_call(
        functools.partial(backward_kernel, [len(pieces) for pieces in grad_all], span, cap),
        out_shape=[shaped((rows, width))] * chunks
        + [shaped((block_count, BLOCK, width), F32)] * 2,
        in_specs=[vmem] + [anywhere] * (5 + len(flat(grad_all))),
        out_specs=[anywhere] * (chunks + 2),
        scratch_shapes=[
            pltpu.VMEM((chunks, rows, width + HD), BF16),
            pltpu.VMEM((groups, block_count * cap, rows * span), BF16),
            pltpu.VMEM((block_count, slots, width), BF16),
            pltpu.VMEM((block_count, heads // 2, 2 * BLOCK, slots), BF16),
            pltpu.VMEM((block_count, BLOCK, width), BF16),
            pltpu.VMEM((block_count, BLOCK, width), BF16),
            pltpu.VMEM((block_count, slots, width + HD), BF16),
            pltpu.VMEM((block_count, slots, width), BF16),
            pltpu.VMEM((block_count, BLOCK, width), F32),
            pltpu.VMEM((block_count, BLOCK, width), F32),
            pltpu.SemaphoreType.DMA((len(flat(grad_all)),)),
            pltpu.SemaphoreType.DMA((1,)),
            pltpu.SemaphoreType.DMA((4, block_count)),
            pltpu.SemaphoreType.DMA((2, block_count)),
            pltpu.SemaphoreType.DMA((chunks,)),
        ],
        compiler_params=limit(44),
        name="backward",
    )(gates, hot, q_slots, probs, keys, values, *flat(grad_all))
    key_grad, value_grad = outs[chunks:]
    terms, far = collect_chips(outs[:chunks])
    query_grad = pl.pallas_call(
        functools.partial(total_kernel, [len(pieces) for pieces in terms]),
        out_shape=shaped((rows, width), F32),
        in_specs=[vmem] * len(flat(terms)),
        out_specs=vmem,
        compiler_params=limit(24),
        name="total",
    )(*flat(terms))

    weight_own, weight_other = pl.pallas_call(
        functools.partial(weight_kernel, [len(pieces) for pieces in attns]),
        out_shape=[shaped((share // 2, width), F32), shaped((share // 2, width))],
        in_specs=[smem] + [vmem] * (chips + len(flat(attns))),
        out_specs=[vmem] * 2,
        compiler_params=limit(24),
        name="weight",
    )(after(me, far), *slabs, *flat(attns))
    weight_grad = weight_own + swap(weight_other, 1).astype(F32)
    return (
        query_grad,
        key_grad.reshape(-1, width),
        value_grad.reshape(-1, width),
        weight_grad,
    )


def solution(mesh):
    return jax.shard_map(
        body,
        mesh=mesh,
        in_specs=(
            P("ctx", "head"),
            P("ctx", "head"),
            P("ctx", "head"),
            P("ctx", None),
            P("ctx", "head"),
            P(None, "head"),
        ),
        out_specs=(P("ctx", "head"), P("ctx", "head"), P("ctx", "head"), P("ctx", "head")),
        check_vma=False,
    )
```

```python
import functools

import jax
import jax.numpy as jnp
from jax import lax
from jax.experimental import pallas as pl
from jax.experimental.pallas import tpu as pltpu
from jax.sharding import PartitionSpec as P

HD = 128
BLOCK = 64
TOPK = 4
F32 = jnp.float32
BF16 = jnp.bfloat16
MIB = 1024 * 1024
PAD = 16
LOW = -(2.0**99)
NN = (((1,), (0,)), ((), ()))
NT = (((1,), (1,)), ((), ()))
TN = (((0,), (0,)), ((), ()))


def mm(a, b, dims=NN):
    return lax.dot_general(a, b, dims, preferred_element_type=F32)


def joined(items, axis):
    return items[0] if len(items) == 1 else jnp.concatenate(items, axis=axis)


def dealt(refs, counts):
    lists, at = [], 0
    for count in counts:
        lists.append(refs[at : at + count])
        at += count
    return lists, refs[at:]


def start(copies):
    for copy in copies:
        copy.start()


def whole(refs):
    return joined([ref[...] for ref in refs], 0)


def added(terms, cols):
    total = None
    for refs in terms:
        term = joined([ref[:, cols].astype(F32) for ref in refs], 0)
        total = term if total is None else total + term
    return total


def diagonal(pair):
    zero = jnp.zeros((pair.shape[0], HD), pair.dtype)
    top = jnp.concatenate([pair[:, :HD], zero], axis=1)
    low = jnp.concatenate([zero, pair[:, HD:]], axis=1)
    return jnp.concatenate([top, low], axis=0)


def pack_kernel(sel_ref, q_ref, out_ref):
    rows, width = q_ref.shape
    out_ref[:rows] = q_ref[...]
    digits = [(sel_ref[...] >> 4).astype(F32), (sel_ref[...] & 15).astype(F32)]
    if width > 2 * rows:
        digits.append(jnp.zeros((TOPK, width - 2 * rows), F32))
    lines = [jnp.concatenate(digits, axis=1), jnp.zeros((PAD - TOPK, width), F32)]
    out_ref[rows:] = jnp.concatenate(lines, axis=0).astype(BF16)


def forward_kernel(counts, span, cap, me_ref, mark_ref, k_ref, v_ref, *refs):
    chunks = len(counts)
    q_refs, refs = dealt(refs, counts)
    part_refs, refs = refs[:chunks], refs[chunks:]
    qg_ref, p_ref, logit_ref, hot_ref, topg_ref, out_ref = refs
    block_count, _, width = k_ref.shape
    heads = width // HD
    rows = part_refs[0].shape[0]
    group_rows = rows * span
    groups = chunks // span
    scale = HD ** (-0.5)
    rate = scale * 1.4426950408889634
    base = me_ref[0] * block_count

    before = lax.broadcasted_iota(jnp.int32, (group_rows, group_rows), 0)
    later = lax.broadcasted_iota(jnp.int32, (group_rows, group_rows), 1)
    earlier = (before < later).astype(BF16)
    own_ids = (base + lax.broadcasted_iota(jnp.int32, (block_count, group_rows), 0)).astype(F32)
    place = lax.broadcasted_iota(jnp.int32, (cap, group_rows), 0).astype(F32)
    for g in range(groups):
        packs = [whole(q_refs[g * span + i]) for i in range(span)]
        digits = [pack[rows : rows + PAD].astype(F32)[:TOPK] for pack in packs]
        picked = joined([16.0 * d[:, :rows] + d[:, rows : 2 * rows] for d in digits], 1)
        own = picked[0:1, :] == own_ids
        for t in range(1, TOPK):
            own = own | (picked[t : t + 1, :] == own_ids)
        own = jnp.where(own, 1.0, 0.0)
        rank = jnp.where(own > 0.5, mm(own.astype(BF16), earlier), -1.0)
        hot = jnp.concatenate(
            [jnp.where(rank[b : b + 1, :] == place, 1.0, 0.0) for b in range(block_count)], axis=0
        ).astype(BF16)
        hot_ref[g] = hot
        q_group = joined([pack[:rows] for pack in packs], 0)
        tops, sums = [], []
        for h in range(heads):
            cols = slice(h * HD, (h + 1) * HD)
            marks = scale * mm(mark_ref[:, cols], q_group[:, cols], NT)
            marks = jnp.where(own > 0.5, marks, LOW)
            top = jnp.max(marks, axis=0, keepdims=True).astype(BF16).astype(F32)
            tops.append(top)
            sums.append(jnp.sum(own * jnp.exp(marks - top), axis=0, keepdims=True))
        tops, sums = jnp.concatenate(tops, axis=0), jnp.concatenate(sums, axis=0)
        upper = sums.astype(BF16).astype(F32)
        spare = jnp.zeros((HD - 3 * heads, group_rows), F32)
        tail = jnp.concatenate([tops, upper, sums - upper, spare], axis=0)
        topg_ref[:, g * cap : (g + 1) * cap, :] = mm(hot, tail.astype(BF16), NT).reshape(
            block_count, cap, HD
        )
        for i in range(span):
            part_refs[g * span + i][:, width:] = tail[:, i * rows : (i + 1) * rows].T.astype(BF16)
        qg_ref[:, g * cap : (g + 1) * cap, :] = (
            mm(hot, q_group).astype(BF16).reshape(block_count, cap, width)
        )

    def one_block(b, carry):
        pairs = [slice(p * 2 * HD, (p + 1) * 2 * HD) for p in range(heads // 2)]
        logits = [mm(diagonal(k_ref[b, :, cols]), qg_ref[b, :, cols], NT) for cols in pairs]
        wide = [diagonal(v_ref[b, :, cols]) for cols in pairs]
        tops = topg_ref[b].T[:heads]
        marks = scale * jnp.concatenate(
            [logits[h // 2][(h % 2 + 1) * BLOCK - 1 : (h % 2 + 1) * BLOCK] for h in range(heads)],
            axis=0,
        )
        gates = jnp.exp(marks - tops)
        probs, gated = [], []
        for p in range(heads // 2):
            for i in range(2):
                part = logits[p][i * BLOCK : (i + 1) * BLOCK]
                weight = jnp.exp2(rate * (part - jnp.max(part, axis=0, keepdims=True)))
                inverse = 1.0 / jnp.sum(weight, axis=0, keepdims=True)
                gate = gates[2 * p + i : 2 * p + i + 1, :]
                probs.append((weight * inverse).astype(BF16))
                gated.append((weight * (inverse * gate)).astype(BF16))
        outs = [
            mm(jnp.concatenate(gated[2 * p : 2 * p + 2], axis=0), wide[p], TN).astype(BF16)
            for p in range(heads // 2)
        ]
        logit_ref[b] = marks
        for p in range(heads // 2):
            p_ref[b, p] = jnp.concatenate(probs[2 * p : 2 * p + 2], axis=0)
            out_ref[b, :, pairs[p]] = outs[p]
        return carry

    lax.fori_loop(0, block_count, one_block, 0)

    for g in range(groups):
        slots = out_ref[:, g * cap : (g + 1) * cap, :].reshape(block_count * cap, width)
        part = mm(hot_ref[g], slots, TN).astype(BF16)
        for i in range(span):
            part_refs[g * span + i][:, :width] = part[i * rows : (i + 1) * rows]


def blend(terms, heads):
    width = heads * HD
    tails = [joined([ref[rows, width:] for ref, rows in term], 0).astype(F32) for term in terms]
    top = tails[0]
    for tail in tails[1:]:
        top = jnp.maximum(top, tail)
    tops, sums, columns = [], [], []
    for h in range(heads):
        cols = slice(h * HD, (h + 1) * HD)
        peak = top[:, h : h + 1]
        total, column = None, None
        for term, tail in zip(terms, tails):
            factor = jnp.exp(tail[:, h : h + 1] - peak)
            low = 2 * heads + h
            share = factor * (tail[:, heads + h : heads + h + 1] + tail[:, low : low + 1])
            part = factor * joined([ref[rows, cols] for ref, rows in term], 0).astype(F32)
            total = share if total is None else total + share
            column = part if column is None else column + part
        tops.append(peak)
        sums.append(total)
        columns.append(column)
    return tops, sums, columns


def tailed(groups, rows):
    lane = lax.broadcasted_iota(jnp.int32, (rows, HD), 1)
    tail = jnp.zeros((rows, HD), F32)
    at = 0
    for group in groups:
        for column in group:
            tail = jnp.where(lane == at, column, tail)
            at += 1
    return tail.astype(BF16)


def digits_of(columns, count):
    groups = []
    for _ in range(count):
        upper = [column.astype(BF16).astype(F32) for column in columns]
        groups.append(upper)
        columns = [column - part for column, part in zip(columns, upper)]
    return groups


def merge_kernel(plan, heads, *refs):
    ins, outs = refs[: len(refs) - len(plan)], refs[len(refs) - len(plan) :]
    for terms, out_ref in zip(plan, outs):
        tops, sums, columns = blend(
            [[(ins[i], pl.ds(first, count))] for i, first, count in terms], heads
        )
        for h in range(heads):
            out_ref[:, h * HD : (h + 1) * HD] = columns[h].astype(BF16)
        out_ref[:, heads * HD :] = tailed([tops] + digits_of(sums, 2), out_ref.shape[0])


def grad_kernel(lines, chips, at_ref, w_ref, *refs):
    own_ref, up_refs, down_refs = refs[0], refs[1:lines], refs[lines : 2 * lines - 1]
    ga_ref, slab_refs = refs[2 * lines - 1], refs[2 * lines : 2 * lines + chips]
    full_ref, w_buf, sems, piece_sems = refs[2 * lines + chips :]
    width = own_ref.shape[1]
    share = slab_refs[0].shape[1]
    line, chip = at_ref[0], at_ref[1]

    def placed(ref, i):
        return pltpu.make_async_copy(ref, full_ref.at[i], piece_sems.at[i])

    placed(own_ref, line).start()
    for d in range(1, lines):

        @pl.when(line >= d)
        def _():
            placed(up_refs[d - 1], line - d).start()

        @pl.when(line + d < lines)
        def _():
            placed(down_refs[d - 1], line + d).start()

    copies = [
        pltpu.make_async_copy(w_ref.at[pl.ds(i * width, width)], w_buf.at[i], sems.at[i])
        for i in range(lines)
    ]
    start(copies)
    for i in range(lines):
        placed(own_ref, i).wait()
    for j in range(chips):
        first = (chip ^ j) * share
        cols = pl.ds(pl.multiple_of(first % width, HD), share)
        slab_refs[j][...] = full_ref[first // width, :, cols]
    total = None
    for i in range(lines):
        copies[i].wait()
        term = mm(full_ref[i], w_buf[i])
        total = term if total is None else total + term
    ga_ref[...] = total.astype(BF16)


def finish_kernel(counts, *refs):
    terms, (ga_ref, attn_ref, ext_ref) = dealt(refs, counts)
    rows, width = ga_ref.shape
    heads = width // HD
    tops, sums, columns = blend(
        [[(ref, slice(None)) for ref in pieces] for pieces in terms], heads
    )
    ext_ref[:, :width] = ga_ref[...]
    dots, levels = [], []
    for h in range(heads):
        cols = slice(h * HD, (h + 1) * HD)
        total = columns[h] * (1.0 / sums[h])
        attn_ref[:, cols] = total.astype(BF16)
        dots.append(jnp.sum(total * ga_ref[:, cols].astype(F32), axis=1, keepdims=True))
        levels.append(tops[h] + jnp.log(sums[h]))
    ext_ref[:, width:] = tailed(digits_of(dots, 2) + digits_of(levels, 3), rows)


def total_kernel(counts, *refs):
    terms, (out_ref,) = dealt(refs, counts)
    for h in range(out_ref.shape[1] // HD):
        cols = slice(h * HD, (h + 1) * HD)
        out_ref[:, cols] = added(terms, cols)


def backward_kernel(counts, span, cap, hot_ref, qg_ref, p_ref, logit_ref, k_ref, v_ref, *refs):
    chunks = len(counts)
    ga_refs, refs = dealt(refs, counts)
    part_refs, refs = refs[:chunks], refs[chunks:]
    dk_ref, dv_ref, gag_ref, dq_ref = refs
    block_count, _, width = k_ref.shape
    heads = width // HD
    rows = part_refs[0].shape[0]
    groups = chunks // span
    scale = HD ** (-0.5)

    for g in range(groups):
        ga_group = joined([whole(ga_refs[g * span + i]) for i in range(span)], 0)
        gag_ref[:, g * cap : (g + 1) * cap, :] = (
            mm(hot_ref[g], ga_group).astype(BF16).reshape(block_count, cap, width + HD)
        )
    last = lax.broadcasted_iota(jnp.int32, (BLOCK, groups * cap), 0) == BLOCK - 1

    def one_block(b, carry):
        pairs = [slice(p * 2 * HD, (p + 1) * 2 * HD) for p in range(heads // 2)]
        q = [qg_ref[b, :, cols] for cols in pairs]
        ga = [gag_ref[b, :, cols] for cols in pairs]
        grads = [mm(diagonal(v_ref[b, :, cols]), ga[p], NT) for p, cols in enumerate(pairs)]
        wide = [diagonal(k_ref[b, :, cols]) for cols in pairs]
        probs = [p_ref[b, p].astype(F32) for p in range(heads // 2)]
        tail = gag_ref[b, :, width:].astype(F32).T
        tail = [tail[i * heads : (i + 1) * heads] for i in range(5)]
        dots = tail[0] + tail[1]
        gates = jnp.exp(jnp.minimum(logit_ref[b] - (tail[2] + tail[3] + tail[4]), 0.0))
        gated, score = [], []
        for p in range(heads // 2):
            for i in range(2):
                at = slice(i * BLOCK, (i + 1) * BLOCK)
                h = 2 * p + i
                gate = gates[h : h + 1, :]
                grad = grads[p][at]
                delta = jnp.sum(probs[p][at] * grad, axis=0, keepdims=True)
                weight = probs[p][at] * gate
                extra = jnp.where(last, scale * gate * (delta - dots[h : h + 1, :]), 0.0)
                score.append((weight * (scale * (grad - delta)) + extra).astype(BF16))
                gated.append(weight.astype(BF16))
        for p, cols in enumerate(pairs):
            both = jnp.concatenate(gated[2 * p : 2 * p + 2], axis=0)
            scores = jnp.concatenate(score[2 * p : 2 * p + 2], axis=0)
            dv = mm(both, ga[p])
            dk = mm(scores, q[p])
            dq = mm(scores, wide[p], TN).astype(BF16)
            dv_ref[b, :, cols] = jnp.concatenate([dv[:BLOCK, :HD], dv[BLOCK:, HD:]], axis=1)
            dk_ref[b, :, cols] = jnp.concatenate([dk[:BLOCK, :HD], dk[BLOCK:, HD:]], axis=1)
            dq_ref[b, :, cols] = dq
        return carry

    lax.fori_loop(0, block_count, one_block, 0)

    for g in range(groups):
        slots = dq_ref[:, g * cap : (g + 1) * cap, :].reshape(block_count * cap, width)
        part = mm(hot_ref[g], slots, TN).astype(BF16)
        for i in range(span):
            part_refs[g * span + i][...] = part[i * rows : (i + 1) * rows]


def weight_kernel(counts, me_ref, *refs):
    chips = len(counts)
    slabs = refs[:chips]
    attns, (own_ref, other_ref) = dealt(refs[chips:], counts)
    half = own_ref.shape[0]
    core = me_ref[0] % 2
    attn = joined([whole(pieces) for pieces in attns], 0)

    def side(which):
        cols = pl.ds(pl.multiple_of(which * half, half), half)
        return mm(joined([ref[:, cols] for ref in slabs], 0), attn, TN)

    own_ref[...] = side(core)
    other_ref[...] = side(1 - core).astype(BF16)


def swap(x, bits):
    count = lax.axis_size("ctx")
    return lax.ppermute(x, "ctx", [(i, i ^ bits) for i in range(count)])


def after(x, *others):
    return lax.optimization_barrier((x, *others))[0]


def flat(lists):
    return [x for pieces in lists for x in pieces]


def spread_chips(x, half):
    chips = lax.axis_size("ctx") // 2
    near = [swap(x, 2 * j) for j in range(1, chips)] if chips != 4 else [swap(x, 2), swap(x, 4)]
    if chips != 4:
        return [[x]] + [[piece] for piece in near]
    far = [swap(near[0][:half], 4), swap(near[1][half:], 2)]
    return [[x], [near[0]], [near[1]], far]


def with_cores(lists, own):
    both = [lists[0], [swap(own, 1)]]
    for pieces in lists[1:]:
        both += [pieces, [swap(piece, 1) for piece in pieces]]
    return both


def from_core(parts, *before):
    received = [None] * (len(parts) // 2)
    for j in reversed(range(len(received))):
        received[j] = after(swap(parts[2 * j + 1], 1), *before)
    return received


def collect_chips(parts, received):
    chips = len(received)

    def both(j, rows, extra=None):
        total = parts[2 * j][rows].astype(F32) + received[j][rows].astype(F32)
        if extra is not None:
            total = total + extra.astype(F32)
        return total.astype(BF16)

    terms = [[parts[0]], [received[0]]]
    if chips != 4:
        return terms + [[swap(both(j, slice(None)), 2 * j)] for j in range(1, chips)]
    half = parts[0].shape[0] // 2
    top, low = slice(0, half), slice(half, None)
    x_far, y_far = swap(both(3, top), 2), swap(both(3, low), 4)
    x_top, y_low = swap(both(1, top), 2), swap(both(2, low), 4)
    x_low, y_top = swap(both(1, low, y_far), 2), swap(both(2, top, x_far), 4)
    return terms + [[x_top, x_low], [y_top, y_low]]


def merge_chips(parts, received, heads):
    chips = len(received)
    rows = parts[0].shape[0]
    half = rows // 2

    def merged(ins, plan):
        return pl.pallas_call(
            functools.partial(merge_kernel, plan, heads),
            out_shape=[
                jax.ShapeDtypeStruct((terms[0][2], ins[0].shape[1]), BF16) for terms in plan
            ],
            in_specs=[pl.BlockSpec(memory_space=pltpu.VMEM)] * len(ins),
            out_specs=[pl.BlockSpec(memory_space=pltpu.VMEM)] * len(plan),
            compiler_params=pltpu.CompilerParams(vmem_limit_bytes=24 * MIB),
            name="merge",
        )(*ins)

    terms = [[parts[0]], [received[0]]]
    if chips != 4:
        for j in range(1, chips):
            (both,) = merged([parts[2 * j], received[j]], [[(0, 0, rows), (1, 0, rows)]])
            terms.append([swap(both, 2 * j)])
        return terms
    top, low = (0, half), (half, half)
    x_far, y_far = merged(
        [parts[6], received[3]], [[(0, *top), (1, *top)], [(0, *low), (1, *low)]]
    )
    x_far, y_far = swap(x_far, 2), swap(y_far, 4)
    ins = [parts[2], received[1], parts[4], received[2]]
    x_top, y_low = merged(ins, [[(0, *top), (1, *top)], [(2, *low), (3, *low)]])
    x_top, y_low = swap(x_top, 2), swap(y_low, 4)
    x_low, y_top = merged(
        ins + [y_far, x_far],
        [[(0, *low), (1, *low), (4, *top)], [(2, *top), (3, *top), (5, *top)]],
    )
    x_low, y_top = swap(x_low, 2), swap(y_top, 4)
    return terms + [[x_top, x_low], [y_top, y_low]]


def spread_line(x):
    lines = lax.axis_size("head")
    ups, downs = [x], [x]
    for d in range(1, lines):
        ups.append(lax.ppermute(ups[-1], "head", [(i, i + 1) for i in range(d - 1, lines - 1)]))
        downs.append(lax.ppermute(downs[-1], "head", [(i, i - 1) for i in range(1, lines - d + 1)]))
    return ups[1:], downs[1:]


def body(queries, key_rows, value_rows, selected, out_grad, out_weight):
    chunks = lax.axis_size("ctx")
    chips = chunks // 2
    lines = lax.axis_size("head")
    rows, width = queries.shape
    features = out_weight.shape[0]
    share = features // chips
    heads = width // HD
    block_count = key_rows.shape[0] // BLOCK
    block_total = block_count * chunks
    capacity = 2 * rows * TOPK // block_total
    span = max(1, 16 // capacity)
    cap = capacity * span
    groups = chunks // span
    slots = groups * cap
    index = lax.axis_index("ctx").astype(jnp.int32)
    me = index.reshape(1)
    at = jnp.stack([lax.axis_index("head").astype(jnp.int32), index // 2])
    keys = key_rows.reshape(block_count, BLOCK, width)
    values = value_rows.reshape(block_count, BLOCK, width)
    vmem = pl.BlockSpec(memory_space=pltpu.VMEM)
    smem = pl.BlockSpec(memory_space=pltpu.SMEM)
    anywhere = pl.BlockSpec(memory_space=pl.ANY)

    def limit(mib):
        return pltpu.CompilerParams(vmem_limit_bytes=mib * MIB)

    def shaped(shape, kind=BF16):
        return jax.ShapeDtypeStruct(shape, kind)

    ups, downs = spread_line(out_grad)
    packed = pl.pallas_call(
        pack_kernel,
        out_shape=shaped((rows + PAD, width)),
        in_specs=[vmem] * 2,
        out_specs=vmem,
        compiler_params=limit(8),
        name="pack",
    )(selected.T, queries)
    query_chips = spread_chips(packed, rows // 2)
    query_all = with_cores(query_chips, after(packed, ups[0], downs[0]))

    outs = pl.pallas_call(
        functools.partial(forward_kernel, [len(pieces) for pieces in query_all], span, cap),
        out_shape=[shaped((rows, width + HD))] * chunks
        + [
            shaped((block_count, slots, width)),
            shaped((block_count, heads // 2, 2 * BLOCK, slots)),
            shaped((block_count, heads, slots), F32),
            shaped((groups, block_count * cap, rows * span)),
        ],
        in_specs=[smem] + [vmem] * (3 + len(flat(query_all))),
        out_specs=[vmem] * (chunks + 4),
        scratch_shapes=[
            pltpu.VMEM((block_count, slots, HD), F32),
            pltpu.VMEM((block_count, slots, width), BF16),
        ],
        compiler_params=limit(40),
        name="forward",
    )(after(me, *ups[:2], *downs[:2]), keys[:, BLOCK - 1], keys, values, *flat(query_all))
    q_slots, probs, logits, hot = outs[chunks:]

    grad_attn, *slabs = pl.pallas_call(
        functools.partial(grad_kernel, lines, chips),
        out_shape=[shaped((rows, width))] + [shaped((rows, share))] * chips,
        in_specs=[smem] + [anywhere] * (2 * lines),
        out_specs=[vmem] * (1 + chips),
        scratch_shapes=[
            pltpu.VMEM((lines, rows, width), BF16),
            pltpu.VMEM((lines, width, width), BF16),
            pltpu.SemaphoreType.DMA((lines,)),
            pltpu.SemaphoreType.DMA((lines,)),
        ],
        compiler_params=limit(24),
        name="grad",
    )(at, out_weight, out_grad, *ups, *downs)
    terms = merge_chips(outs[:chunks], from_core(outs[:chunks], grad_attn), heads)
    attn_out, extended = pl.pallas_call(
        functools.partial(finish_kernel, [len(pieces) for pieces in terms]),
        out_shape=[shaped((rows, width)), shaped((rows, width + HD))],
        in_specs=[vmem] * (len(flat(terms)) + 1),
        out_specs=[vmem] * 2,
        compiler_params=limit(24),
        name="finish",
    )(*flat(terms), grad_attn)
    grad_chips = spread_chips(extended, rows // 2)
    grad_all = with_cores(grad_chips, extended)

    arrived = flat(grad_chips[1:3])
    attns = [[attn_out]] + [[swap(after(attn_out, *arrived), 2 * j)] for j in range(1, chips)]
    slabs = [slabs[0]] + [swap(after(slabs[j], *arrived), 2 * j) for j in range(1, chips)]

    outs = pl.pallas_call(
        functools.partial(backward_kernel, [len(pieces) for pieces in grad_all], span, cap),
        out_shape=[shaped((rows, width))] * chunks
        + [shaped((block_count, BLOCK, width), F32)] * 2,
        in_specs=[vmem] * (6 + len(flat(grad_all))),
        out_specs=[vmem] * (chunks + 2),
        scratch_shapes=[
            pltpu.VMEM((block_count, slots, width + HD), BF16),
            pltpu.VMEM((block_count, slots, width), BF16),
        ],
        compiler_params=limit(44),
        name="backward",
    )(hot, q_slots, probs, logits, keys, values, *flat(grad_all))
    key_grad, value_grad = outs[chunks:]
    terms = collect_chips(outs[:chunks], from_core(outs[:chunks], *flat(attns[1:])))
    query_grad = pl.pallas_call(
        functools.partial(total_kernel, [len(pieces) for pieces in terms]),
        out_shape=shaped((rows, width), F32),
        in_specs=[vmem] * len(flat(terms)),
        out_specs=vmem,
        compiler_params=limit(24),
        name="total",
    )(*flat(terms))

    weight_own, weight_other = pl.pallas_call(
        functools.partial(weight_kernel, [len(pieces) for pieces in attns]),
        out_shape=[shaped((share // 2, width), F32), shaped((share // 2, width))],
        in_specs=[smem] + [vmem] * (chips + len(flat(attns))),
        out_specs=[vmem] * 2,
        compiler_params=limit(24),
        name="weight",
    )(after(me, terms[2][0], terms[-1][-1]), *slabs, *flat(attns))
    weight_grad = weight_own + swap(weight_other, 1).astype(F32)
    return (
        query_grad,
        key_grad.reshape(-1, width),
        value_grad.reshape(-1, width),
        weight_grad,
    )


def solution(mesh):
    return jax.shard_map(
        body,
        mesh=mesh,
        in_specs=(
            P("ctx", "head"),
            P("ctx", "head"),
            P("ctx", "head"),
            P("ctx", None),
            P("ctx", "head"),
            P(None, "head"),
        ),
        out_specs=(P("ctx", "head"), P("ctx", "head"), P("ctx", "head"), P("ctx", "head")),
        check_vma=False,
    )
```

```python
import functools

import jax
import jax.numpy as jnp
from jax import lax
from jax.experimental import pallas as pl
from jax.experimental.pallas import tpu as pltpu
from jax.sharding import PartitionSpec as P

HD = 128
BLOCK = 64
TOPK = 4
F32 = jnp.float32
BF16 = jnp.bfloat16
MIB = 1024 * 1024
PAD = 16
LOW = -(2.0**99)
NN = (((1,), (0,)), ((), ()))
NT = (((1,), (1,)), ((), ()))
TN = (((0,), (0,)), ((), ()))


def mm(a, b, dims=NN):
    return lax.dot_general(a, b, dims, preferred_element_type=F32)


def joined(items, axis):
    return items[0] if len(items) == 1 else jnp.concatenate(items, axis=axis)


def dealt(refs, counts):
    lists, at = [], 0
    for count in counts:
        lists.append(refs[at : at + count])
        at += count
    return lists, refs[at:]


def start(copies):
    for copy in copies:
        copy.start()


def whole(refs):
    return joined([ref[...] for ref in refs], 0)


def added(terms, cols):
    total = None
    for refs in terms:
        term = joined([ref[:, cols].astype(F32) for ref in refs], 0)
        total = term if total is None else total + term
    return total


def diagonal(pair):
    zero = jnp.zeros((pair.shape[0], HD), pair.dtype)
    top = jnp.concatenate([pair[:, :HD], zero], axis=1)
    low = jnp.concatenate([zero, pair[:, HD:]], axis=1)
    return jnp.concatenate([top, low], axis=0)


def pack_kernel(sel_ref, q_ref, out_ref):
    rows, width = q_ref.shape
    out_ref[:rows] = q_ref[...]
    digits = [(sel_ref[...] >> 4).astype(F32), (sel_ref[...] & 15).astype(F32)]
    if width > 2 * rows:
        digits.append(jnp.zeros((TOPK, width - 2 * rows), F32))
    lines = [jnp.concatenate(digits, axis=1), jnp.zeros((PAD - TOPK, width), F32)]
    out_ref[rows:] = jnp.concatenate(lines, axis=0).astype(BF16)


def forward_kernel(counts, span, cap, me_ref, mark_ref, k_ref, v_ref, *refs):
    chunks = len(counts)
    q_refs, refs = dealt(refs, counts)
    part_refs, refs = refs[:chunks], refs[chunks:]
    qg_ref, p_ref, logit_ref, hot_ref, topg_ref, out_ref = refs
    block_count, _, width = k_ref.shape
    heads = width // HD
    rows = part_refs[0].shape[0]
    group_rows = rows * span
    groups = chunks // span
    scale = HD ** (-0.5)
    rate = scale * 1.4426950408889634
    base = me_ref[0] * block_count

    before = lax.broadcasted_iota(jnp.int32, (group_rows, group_rows), 0)
    later = lax.broadcasted_iota(jnp.int32, (group_rows, group_rows), 1)
    earlier = (before < later).astype(BF16)
    own_ids = (base + lax.broadcasted_iota(jnp.int32, (block_count, group_rows), 0)).astype(F32)
    place = lax.broadcasted_iota(jnp.int32, (cap, group_rows), 0).astype(F32)
    zero = jnp.zeros((block_count, HD), BF16)
    wide_marks = jnp.concatenate(
        [
            jnp.concatenate(
                [mark_ref[:, i * HD : (i + 1) * HD] if i == h else zero for i in range(heads)], axis=1
            )
            for h in range(heads)
        ],
        axis=0,
    )
    for g in range(groups):
        packs = [whole(q_refs[g * span + i]) for i in range(span)]
        digits = [pack[rows : rows + PAD].astype(F32)[:TOPK] for pack in packs]
        picked = joined([16.0 * d[:, :rows] + d[:, rows : 2 * rows] for d in digits], 1)
        own = picked[0:1, :] == own_ids
        for t in range(1, TOPK):
            own = own | (picked[t : t + 1, :] == own_ids)
        own = jnp.where(own, 1.0, 0.0)
        rank = jnp.where(own > 0.5, mm(own.astype(BF16), earlier), -1.0)
        hot = jnp.concatenate(
            [jnp.where(rank[b : b + 1, :] == place, 1.0, 0.0) for b in range(block_count)], axis=0
        ).astype(BF16)
        hot_ref[g] = hot
        q_group = joined([pack[:rows] for pack in packs], 0)
        tops, sums = [], []
        marks = scale * mm(wide_marks, q_group, NT)
        for h in range(heads):
            mark = jnp.where(own > 0.5, marks[h * block_count : (h + 1) * block_count], LOW)
            top = jnp.max(mark, axis=0, keepdims=True).astype(BF16).astype(F32)
            tops.append(top)
            sums.append(jnp.sum(own * jnp.exp(mark - top), axis=0, keepdims=True))
        tops, sums = jnp.concatenate(tops, axis=0), jnp.concatenate(sums, axis=0)
        upper = sums.astype(BF16).astype(F32)
        spare = jnp.zeros((HD - 3 * heads, group_rows), F32)
        tail = jnp.concatenate([tops, upper, sums - upper, spare], axis=0)
        topg_ref[:, g * cap : (g + 1) * cap, :] = mm(hot, tail.astype(BF16), NT).reshape(
            block_count, cap, HD
        )
        for i in range(span):
            part_refs[g * span + i][:, width:] = tail[:, i * rows : (i + 1) * rows].T.astype(BF16)
        qg_ref[:, g * cap : (g + 1) * cap, :] = (
            mm(hot, q_group).astype(BF16).reshape(block_count, cap, width)
        )

    def one_block(b, carry):
        pairs = [slice(p * 2 * HD, (p + 1) * 2 * HD) for p in range(heads // 2)]
        logits = [mm(diagonal(k_ref[b, :, cols]), qg_ref[b, :, cols], NT) for cols in pairs]
        wide = [diagonal(v_ref[b, :, cols]) for cols in pairs]
        tops = topg_ref[b].T[:heads]
        marks = scale * jnp.concatenate(
            [logits[h // 2][(h % 2 + 1) * BLOCK - 1 : (h % 2 + 1) * BLOCK] for h in range(heads)],
            axis=0,
        )
        gates = jnp.exp(marks - tops)
        probs, gated = [], []
        for p in range(heads // 2):
            for i in range(2):
                part = logits[p][i * BLOCK : (i + 1) * BLOCK]
                weight = jnp.exp2(rate * (part - jnp.max(part, axis=0, keepdims=True)))
                inverse = 1.0 / jnp.sum(weight, axis=0, keepdims=True)
                gate = gates[2 * p + i : 2 * p + i + 1, :]
                probs.append((weight * inverse).astype(BF16))
                gated.append((weight * (inverse * gate)).astype(BF16))
        outs = [
            mm(jnp.concatenate(gated[2 * p : 2 * p + 2], axis=0), wide[p], TN).astype(BF16)
            for p in range(heads // 2)
        ]
        logit_ref[b] = marks
        for p in range(heads // 2):
            p_ref[b, p] = jnp.concatenate(probs[2 * p : 2 * p + 2], axis=0)
            out_ref[b, :, pairs[p]] = outs[p]
        return carry

    lax.fori_loop(0, block_count, one_block, 0)

    for g in range(groups):
        slots = out_ref[:, g * cap : (g + 1) * cap, :].reshape(block_count * cap, width)
        part = mm(hot_ref[g], slots, TN).astype(BF16)
        for i in range(span):
            part_refs[g * span + i][:, :width] = part[i * rows : (i + 1) * rows]


def blend(terms, heads):
    width = heads * HD
    tails = [joined([ref[rows, width:] for ref, rows in term], 0).astype(F32) for term in terms]
    top = tails[0]
    for tail in tails[1:]:
        top = jnp.maximum(top, tail)
    tops, sums, columns = [], [], []
    for h in range(heads):
        cols = slice(h * HD, (h + 1) * HD)
        peak = top[:, h : h + 1]
        total, column = None, None
        for term, tail in zip(terms, tails):
            factor = jnp.exp(tail[:, h : h + 1] - peak)
            low = 2 * heads + h
            share = factor * (tail[:, heads + h : heads + h + 1] + tail[:, low : low + 1])
            part = factor * joined([ref[rows, cols] for ref, rows in term], 0).astype(F32)
            total = share if total is None else total + share
            column = part if column is None else column + part
        tops.append(peak)
        sums.append(total)
        columns.append(column)
    return tops, sums, columns


def tailed(groups, rows):
    lane = lax.broadcasted_iota(jnp.int32, (rows, HD), 1)
    tail = jnp.zeros((rows, HD), F32)
    at = 0
    for group in groups:
        for column in group:
            tail = jnp.where(lane == at, column, tail)
            at += 1
    return tail.astype(BF16)


def digits_of(columns, count):
    groups = []
    for _ in range(count):
        upper = [column.astype(BF16).astype(F32) for column in columns]
        groups.append(upper)
        columns = [column - part for column, part in zip(columns, upper)]
    return groups


def merge_kernel(plan, heads, *refs):
    ins, outs = refs[: len(refs) - len(plan)], refs[len(refs) - len(plan) :]
    for terms, out_ref in zip(plan, outs):
        tops, sums, columns = blend(
            [[(ins[i], pl.ds(first, count))] for i, first, count in terms], heads
        )
        for h in range(heads):
            out_ref[:, h * HD : (h + 1) * HD] = columns[h].astype(BF16)
        out_ref[:, heads * HD :] = tailed([tops] + digits_of(sums, 2), out_ref.shape[0])


def grad_kernel(w_ref, full_ref, ga_ref, w_buf, sems):
    parts, step = w_buf.shape[0], w_buf.shape[1]
    copies = [
        pltpu.make_async_copy(w_ref.at[pl.ds(i * step, step)], w_buf.at[i], sems.at[i])
        for i in range(parts)
    ]
    start(copies)
    total = None
    for i in range(parts):
        copies[i].wait()
        term = mm(full_ref[i * step : (i + 1) * step], w_buf[i], TN)
        total = term if total is None else total + term
    ga_ref[...] = total.astype(BF16)


def finish_kernel(counts, *refs):
    terms, (ga_ref, attn_ref, ext_ref) = dealt(refs, counts)
    rows, width = ga_ref.shape
    heads = width // HD
    tops, sums, columns = blend(
        [[(ref, slice(None)) for ref in pieces] for pieces in terms], heads
    )
    ext_ref[:, :width] = ga_ref[...]
    dots, levels = [], []
    for h in range(heads):
        cols = slice(h * HD, (h + 1) * HD)
        total = columns[h] * (1.0 / sums[h])
        attn_ref[:, cols] = total.astype(BF16)
        dots.append(jnp.sum(total * ga_ref[:, cols].astype(F32), axis=1, keepdims=True))
        levels.append(tops[h] + jnp.log(sums[h]))
    ext_ref[:, width:] = tailed(digits_of(dots, 2) + digits_of(levels, 3), rows)


def total_kernel(counts, *refs):
    terms, (out_ref,) = dealt(refs, counts)
    for h in range(out_ref.shape[1] // HD):
        cols = slice(h * HD, (h + 1) * HD)
        out_ref[:, cols] = added(terms, cols)


def backward_kernel(counts, span, cap, hot_ref, qg_ref, p_ref, logit_ref, k_ref, v_ref, *refs):
    chunks = len(counts)
    ga_refs, refs = dealt(refs, counts)
    part_refs, refs = refs[:chunks], refs[chunks:]
    dk_ref, dv_ref, gag_ref, dq_ref = refs
    block_count, _, width = k_ref.shape
    heads = width // HD
    rows = part_refs[0].shape[0]
    groups = chunks // span
    scale = HD ** (-0.5)

    for g in range(groups):
        ga_group = joined([whole(ga_refs[g * span + i]) for i in range(span)], 0)
        gag_ref[:, g * cap : (g + 1) * cap, :] = (
            mm(hot_ref[g], ga_group).astype(BF16).reshape(block_count, cap, width + HD)
        )
    last = lax.broadcasted_iota(jnp.int32, (BLOCK, groups * cap), 0) == BLOCK - 1

    def one_block(b, carry):
        pairs = [slice(p * 2 * HD, (p + 1) * 2 * HD) for p in range(heads // 2)]
        q = [qg_ref[b, :, cols] for cols in pairs]
        ga = [gag_ref[b, :, cols] for cols in pairs]
        grads = [mm(diagonal(v_ref[b, :, cols]), ga[p], NT) for p, cols in enumerate(pairs)]
        wide = [diagonal(k_ref[b, :, cols]) for cols in pairs]
        probs = [p_ref[b, p].astype(F32) for p in range(heads // 2)]
        tail = gag_ref[b, :, width:].astype(F32).T
        tail = [tail[i * heads : (i + 1) * heads] for i in range(5)]
        dots = tail[0] + tail[1]
        gates = jnp.exp(jnp.minimum(logit_ref[b] - (tail[2] + tail[3] + tail[4]), 0.0))
        gated, score = [], []
        for p in range(heads // 2):
            for i in range(2):
                at = slice(i * BLOCK, (i + 1) * BLOCK)
                h = 2 * p + i
                gate = gates[h : h + 1, :]
                grad = grads[p][at]
                delta = jnp.sum(probs[p][at] * grad, axis=0, keepdims=True)
                weight = probs[p][at] * gate
                extra = jnp.where(last, scale * gate * (delta - dots[h : h + 1, :]), 0.0)
                score.append((weight * (scale * (grad - delta)) + extra).astype(BF16))
                gated.append(weight.astype(BF16))
        for p, cols in enumerate(pairs):
            both = jnp.concatenate(gated[2 * p : 2 * p + 2], axis=0)
            scores = jnp.concatenate(score[2 * p : 2 * p + 2], axis=0)
            dv = mm(both, ga[p])
            dk = mm(scores, q[p])
            dq = mm(scores, wide[p], TN).astype(BF16)
            dv_ref[b, :, cols] = jnp.concatenate([dv[:BLOCK, :HD], dv[BLOCK:, HD:]], axis=1)
            dk_ref[b, :, cols] = jnp.concatenate([dk[:BLOCK, :HD], dk[BLOCK:, HD:]], axis=1)
            dq_ref[b, :, cols] = dq
        return carry

    lax.fori_loop(0, block_count, one_block, 0)

    for g in range(groups):
        slots = dq_ref[:, g * cap : (g + 1) * cap, :].reshape(block_count * cap, width)
        part = mm(hot_ref[g], slots, TN).astype(BF16)
        for i in range(span):
            part_refs[g * span + i][...] = part[i * rows : (i + 1) * rows]


def weight_kernel(counts, me_ref, cols_ref, *refs):
    attns, (out_ref,) = dealt(refs, counts)
    me = me_ref[0]
    columns = joined([cols_ref[me ^ m] for m in range(len(counts))], 1)
    out_ref[...] = mm(columns, joined([whole(pieces) for pieces in attns], 0))


def swap(x, bits):
    count = lax.axis_size("ctx")
    return lax.ppermute(x, "ctx", [(i, i ^ bits) for i in range(count)])


def after(x, *others):
    return lax.optimization_barrier((x, *others))[0]


def flat(lists):
    return [x for pieces in lists for x in pieces]


def spread_chips(x, half, *before):
    chips = lax.axis_size("ctx") // 2
    near = [swap(x, 2 * j) for j in range(1, chips)] if chips != 4 else [swap(x, 2), swap(x, 4)]
    if chips != 4:
        return [[x]] + [[piece] for piece in near]
    far = [swap(after(near[0][:half], *before), 4), swap(after(near[1][half:], *before), 2)]
    return [[x], [near[0]], [near[1]], far]


def with_cores(lists, own):
    both = [lists[0], [swap(own, 1)]]
    for pieces in lists[1:]:
        both += [pieces, [swap(piece, 1) for piece in pieces]]
    return both


def from_core(parts, *before):
    received = [None] * (len(parts) // 2)
    for j in reversed(range(len(received))):
        received[j] = after(swap(parts[2 * j + 1], 1), *before)
    return received


def collect_chips(parts, received):
    chips = len(received)

    def both(j, rows, extra=None):
        total = parts[2 * j][rows].astype(F32) + received[j][rows].astype(F32)
        if extra is not None:
            total = total + extra.astype(F32)
        return total.astype(BF16)

    terms = [[parts[0]], [received[0]]]
    if chips != 4:
        return terms + [[swap(both(j, slice(None)), 2 * j)] for j in range(1, chips)]
    half = parts[0].shape[0] // 2
    top, low = slice(0, half), slice(half, None)
    x_far, y_far = swap(both(3, top), 2), swap(both(3, low), 4)
    x_top, y_low = swap(both(1, top), 2), swap(both(2, low), 4)
    x_low, y_top = swap(both(1, low, y_far), 2), swap(both(2, top, x_far), 4)
    return terms + [[x_top, x_low], [y_top, y_low]]


def merge_chips(parts, received, heads, *before):
    chips = len(received)
    rows = parts[0].shape[0]
    half = rows // 2

    def merged(ins, plan):
        return pl.pallas_call(
            functools.partial(merge_kernel, plan, heads),
            out_shape=[
                jax.ShapeDtypeStruct((terms[0][2], ins[0].shape[1]), BF16) for terms in plan
            ],
            in_specs=[pl.BlockSpec(memory_space=pltpu.VMEM)] * len(ins),
            out_specs=[pl.BlockSpec(memory_space=pltpu.VMEM)] * len(plan),
            compiler_params=pltpu.CompilerParams(vmem_limit_bytes=24 * MIB),
            name="merge",
        )(*ins)

    terms = [[parts[0]], [received[0]]]
    if chips != 4:
        for j in range(1, chips):
            (both,) = merged([parts[2 * j], received[j]], [[(0, 0, rows), (1, 0, rows)]])
            terms.append([swap(both, 2 * j)])
        return terms
    top, low = (0, half), (half, half)
    x_far, y_far = merged(
        [parts[6], received[3]], [[(0, *top), (1, *top)], [(0, *low), (1, *low)]]
    )
    x_far, y_far = swap(x_far, 2), swap(y_far, 4)
    ins = [parts[2], received[1], parts[4], received[2]]
    x_top, y_low = merged(ins, [[(0, *top), (1, *top)], [(2, *low), (3, *low)]])
    x_top, y_low = swap(x_top, 2), swap(y_low, 4)
    x_low, y_top = merged(
        ins + [after(y_far, *before), x_far],
        [[(0, *low), (1, *low), (4, *top)], [(2, *top), (3, *top), (5, *top)]],
    )
    x_low, y_top = swap(x_low, 2), swap(y_top, 4)
    return terms + [[x_top, x_low], [y_top, y_low]]


def body(queries, key_rows, value_rows, selected, out_grad, out_weight):
    chunks = lax.axis_size("ctx")
    chips = chunks // 2
    rows, width = queries.shape
    features = out_weight.shape[0]
    heads = width // HD
    block_count = key_rows.shape[0] // BLOCK
    block_total = block_count * chunks
    capacity = 2 * rows * TOPK // block_total
    span = max(1, 16 // capacity)
    cap = capacity * span
    groups = chunks // span
    slots = groups * cap
    index = lax.axis_index("ctx").astype(jnp.int32)
    me = index.reshape(1)
    keys = key_rows.reshape(block_count, BLOCK, width)
    values = value_rows.reshape(block_count, BLOCK, width)
    vmem = pl.BlockSpec(memory_space=pltpu.VMEM)
    smem = pl.BlockSpec(memory_space=pltpu.SMEM)
    anywhere = pl.BlockSpec(memory_space=pl.ANY)

    def limit(mib):
        return pltpu.CompilerParams(vmem_limit_bytes=mib * MIB)

    def shaped(shape, kind=BF16):
        return jax.ShapeDtypeStruct(shape, kind)

    grad_full = lax.all_gather(out_grad.T, "head", axis=0, tiled=True)
    columns = lax.all_to_all(grad_full, "ctx", split_axis=0, concat_axis=0, tiled=True)
    packed = pl.pallas_call(
        pack_kernel,
        out_shape=shaped((rows + PAD, width)),
        in_specs=[vmem] * 2,
        out_specs=vmem,
        compiler_params=limit(8),
        name="pack",
    )(selected.T, queries)
    query_chips = spread_chips(packed, rows // 2)
    query_all = with_cores(query_chips, packed)

    outs = pl.pallas_call(
        functools.partial(forward_kernel, [len(pieces) for pieces in query_all], span, cap),
        out_shape=[shaped((rows, width + HD))] * chunks
        + [
            shaped((block_count, slots, width)),
            shaped((block_count, heads // 2, 2 * BLOCK, slots)),
            shaped((block_count, heads, slots), F32),
            shaped((groups, block_count * cap, rows * span)),
        ],
        in_specs=[smem] + [vmem] * (3 + len(flat(query_all))),
        out_specs=[vmem] * (chunks + 4),
        scratch_shapes=[
            pltpu.VMEM((block_count, slots, HD), F32),
            pltpu.VMEM((block_count, slots, width), BF16),
        ],
        compiler_params=limit(40),
        name="forward",
    )(me, keys[:, BLOCK - 1], keys, values, *flat(query_all))
    q_slots, probs, logits, hot = outs[chunks:]

    grad_attn = pl.pallas_call(
        grad_kernel,
        out_shape=shaped((rows, width)),
        in_specs=[anywhere, vmem],
        out_specs=vmem,
        scratch_shapes=[
            pltpu.VMEM((features // width, width, width), BF16),
            pltpu.SemaphoreType.DMA((features // width,)),
        ],
        compiler_params=limit(24),
        name="grad",
    )(out_weight, grad_full)
    terms = merge_chips(outs[:chunks], from_core(outs[:chunks]), heads, grad_attn)
    attn_out, extended = pl.pallas_call(
        functools.partial(finish_kernel, [len(pieces) for pieces in terms]),
        out_shape=[shaped((rows, width)), shaped((rows, width + HD))],
        in_specs=[vmem] * (len(flat(terms)) + 1),
        out_specs=[vmem] * 2,
        compiler_params=limit(24),
        name="finish",
    )(*flat(terms), grad_attn)
    grad_chips = spread_chips(extended, rows // 2, columns)
    grad_all = with_cores(grad_chips, extended)
    arrived = flat(grad_chips[1:3])
    attns = [[attn_out]] + [[swap(after(attn_out, *arrived), 2 * j)] for j in range(1, chips)]

    outs = pl.pallas_call(
        functools.partial(backward_kernel, [len(pieces) for pieces in grad_all], span, cap),
        out_shape=[shaped((rows, width))] * chunks
        + [shaped((block_count, BLOCK, width), F32)] * 2,
        in_specs=[vmem] * (6 + len(flat(grad_all))),
        out_specs=[vmem] * (chunks + 2),
        scratch_shapes=[
            pltpu.VMEM((block_count, slots, width + HD), BF16),
            pltpu.VMEM((block_count, slots, width), BF16),
        ],
        compiler_params=limit(44),
        name="backward",
    )(hot, q_slots, probs, logits, keys, values, *flat(grad_all))
    key_grad, value_grad = outs[chunks:]
    terms = collect_chips(outs[:chunks], from_core(outs[:chunks], *flat(attns[1:])))
    query_grad = pl.pallas_call(
        functools.partial(total_kernel, [len(pieces) for pieces in terms]),
        out_shape=shaped((rows, width), F32),
        in_specs=[vmem] * len(flat(terms)),
        out_specs=vmem,
        compiler_params=limit(24),
        name="total",
    )(*flat(terms))

    attns = with_cores(attns, attn_out)
    weight_grad = pl.pallas_call(
        functools.partial(weight_kernel, [len(pieces) for pieces in attns]),
        out_shape=shaped((features // chunks, width), F32),
        in_specs=[smem] + [vmem] * (1 + len(flat(attns))),
        out_specs=vmem,
        compiler_params=limit(24),
        name="weight",
    )(after(me, *flat(terms)), columns.reshape(chunks, features // chunks, rows), *flat(attns))
    return (
        query_grad,
        key_grad.reshape(-1, width),
        value_grad.reshape(-1, width),
        weight_grad,
    )


def solution(mesh):
    return jax.shard_map(
        body,
        mesh=mesh,
        in_specs=(
            P("ctx", "head"),
            P("ctx", "head"),
            P("ctx", "head"),
            P("ctx", None),
            P("ctx", "head"),
            P(None, "head"),
        ),
        out_specs=(P("ctx", "head"), P("ctx", "head"), P("ctx", "head"), P("ctx", "head")),
        check_vma=False,
    )
```

```python
import functools

import jax
import jax.numpy as jnp
from jax import lax
from jax.experimental import pallas as pl
from jax.experimental.pallas import tpu as pltpu
from jax.sharding import PartitionSpec as P

HD = 128
BLOCK = 64
TOPK = 4
F32 = jnp.float32
BF16 = jnp.bfloat16
MIB = 1024 * 1024
PAD = 16
LOW = -(2.0**99)
NN = (((1,), (0,)), ((), ()))
NT = (((1,), (1,)), ((), ()))
TN = (((0,), (0,)), ((), ()))


def mm(a, b, dims=NN):
    return lax.dot_general(a, b, dims, preferred_element_type=F32)


def joined(items, axis):
    return items[0] if len(items) == 1 else jnp.concatenate(items, axis=axis)


def dealt(refs, counts):
    lists, at = [], 0
    for count in counts:
        lists.append(refs[at : at + count])
        at += count
    return lists, refs[at:]


def start(copies):
    for copy in copies:
        copy.start()


def whole(refs):
    return joined([ref[...] for ref in refs], 0)


def added(terms, cols):
    total = None
    for refs in terms:
        term = joined([ref[:, cols].astype(F32) for ref in refs], 0)
        total = term if total is None else total + term
    return total


def diagonal(pair):
    zero = jnp.zeros((pair.shape[0], HD), pair.dtype)
    top = jnp.concatenate([pair[:, :HD], zero], axis=1)
    low = jnp.concatenate([zero, pair[:, HD:]], axis=1)
    return jnp.concatenate([top, low], axis=0)


def pack_kernel(sel_ref, q_ref, out_ref):
    rows, width = q_ref.shape
    out_ref[:rows] = q_ref[...]
    digits = [(sel_ref[...] >> 4).astype(F32), (sel_ref[...] & 15).astype(F32)]
    if width > 2 * rows:
        digits.append(jnp.zeros((TOPK, width - 2 * rows), F32))
    lines = [jnp.concatenate(digits, axis=1), jnp.zeros((PAD - TOPK, width), F32)]
    out_ref[rows:] = jnp.concatenate(lines, axis=0).astype(BF16)


def forward_kernel(counts, span, cap, me_ref, mark_ref, k_ref, v_ref, *refs):
    chunks = len(counts)
    q_refs, refs = dealt(refs, counts)
    part_refs, refs = refs[:chunks], refs[chunks:]
    qg_ref, p_ref, logit_ref, hot_ref, topg_ref, out_ref = refs
    block_count, _, width = k_ref.shape
    heads = width // HD
    rows = part_refs[0].shape[0]
    group_rows = rows * span
    groups = chunks // span
    scale = HD ** (-0.5)
    rate = scale * 1.4426950408889634
    base = me_ref[0] * block_count

    before = lax.broadcasted_iota(jnp.int32, (group_rows, group_rows), 0)
    later = lax.broadcasted_iota(jnp.int32, (group_rows, group_rows), 1)
    earlier = (before < later).astype(BF16)
    own_ids = (base + lax.broadcasted_iota(jnp.int32, (block_count, group_rows), 0)).astype(F32)
    place = lax.broadcasted_iota(jnp.int32, (cap, group_rows), 0).astype(F32)
    zero = jnp.zeros((block_count, HD), BF16)
    wide_marks = jnp.concatenate(
        [
            jnp.concatenate(
                [mark_ref[:, i * HD : (i + 1) * HD] if i == h else zero for i in range(heads)], axis=1
            )
            for h in range(heads)
        ],
        axis=0,
    )
    q_groups, owns = [], []
    for g in range(groups):
        packs = [whole(q_refs[g * span + i]) for i in range(span)]
        digits = [pack[rows : rows + PAD].astype(F32)[:TOPK] for pack in packs]
        picked = joined([16.0 * d[:, :rows] + d[:, rows : 2 * rows] for d in digits], 1)
        own = picked[0:1, :] == own_ids
        for t in range(1, TOPK):
            own = own | (picked[t : t + 1, :] == own_ids)
        owns.append(jnp.where(own, 1.0, 0.0))
        q_groups.append(joined([pack[:rows] for pack in packs], 0))
    own_all = jnp.concatenate(owns, axis=0)
    rank_all = jnp.where(own_all > 0.5, mm(own_all.astype(BF16), earlier), -1.0)
    hots = []
    for g in range(groups):
        rank = rank_all[g * block_count : (g + 1) * block_count]
        hots.append(
            jnp.concatenate(
                [
                    jnp.where(rank[b : b + 1, :] == place, 1.0, 0.0).astype(BF16)
                    for b in range(block_count)
                ],
                axis=0,
            )
        )
        hot_ref[g] = hots[g]
    all_marks = [mm(wide_marks, q_groups[g], NT) for g in range(groups)]
    for g in range(groups):
        qg_ref[:, g * cap : (g + 1) * cap, :] = (
            mm(hots[g], q_groups[g]).astype(BF16).reshape(block_count, cap, width)
        )
    tails = []
    for g in range(groups):
        tops, sums = [], []
        for h in range(heads):
            mark = scale * all_marks[g][h * block_count : (h + 1) * block_count]
            mark = jnp.where(owns[g] > 0.5, mark, LOW)
            top = jnp.max(mark, axis=0, keepdims=True).astype(BF16).astype(F32)
            tops.append(top)
            sums.append(jnp.sum(owns[g] * jnp.exp(mark - top), axis=0, keepdims=True))
        tops, sums = jnp.concatenate(tops, axis=0), jnp.concatenate(sums, axis=0)
        upper = sums.astype(BF16).astype(F32)
        spare = jnp.zeros((HD - 3 * heads, group_rows), F32)
        tails.append(jnp.concatenate([tops, upper, sums - upper, spare], axis=0))
    for g in range(groups):
        topg_ref[:, g * cap : (g + 1) * cap, :] = mm(hots[g], tails[g].astype(BF16), NT).reshape(
            block_count, cap, HD
        )
    for g in range(groups):
        for i in range(span):
            part_refs[g * span + i][:, width:] = (
                tails[g][:, i * rows : (i + 1) * rows].T.astype(BF16)
            )

    def one_block(b, carry):
        pairs = [slice(p * 2 * HD, (p + 1) * 2 * HD) for p in range(heads // 2)]
        logits = [mm(diagonal(k_ref[b, :, cols]), qg_ref[b, :, cols], NT) for cols in pairs]
        wide = [diagonal(v_ref[b, :, cols]) for cols in pairs]
        tops = topg_ref[b].T[:heads]
        marks = scale * jnp.concatenate(
            [logits[h // 2][(h % 2 + 1) * BLOCK - 1 : (h % 2 + 1) * BLOCK] for h in range(heads)],
            axis=0,
        )
        gates = jnp.exp(marks - tops)
        probs, gated = [], []
        for p in range(heads // 2):
            for i in range(2):
                part = logits[p][i * BLOCK : (i + 1) * BLOCK]
                weight = jnp.exp2(rate * (part - jnp.max(part, axis=0, keepdims=True)))
                inverse = 1.0 / jnp.sum(weight, axis=0, keepdims=True)
                gate = gates[2 * p + i : 2 * p + i + 1, :]
                probs.append((weight * inverse).astype(BF16))
                gated.append((weight * (inverse * gate)).astype(BF16))
        outs = [
            mm(jnp.concatenate(gated[2 * p : 2 * p + 2], axis=0), wide[p], TN).astype(BF16)
            for p in range(heads // 2)
        ]
        logit_ref[b] = marks
        for p in range(heads // 2):
            p_ref[b, p] = jnp.concatenate(probs[2 * p : 2 * p + 2], axis=0)
            out_ref[b, :, pairs[p]] = outs[p]
        return carry

    lax.fori_loop(0, block_count, one_block, 0)

    for g in range(groups):
        slots = out_ref[:, g * cap : (g + 1) * cap, :].reshape(block_count * cap, width)
        part = mm(hot_ref[g], slots, TN).astype(BF16)
        for i in range(span):
            part_refs[g * span + i][:, :width] = part[i * rows : (i + 1) * rows]


def blend(terms, heads):
    width = heads * HD
    tails = [joined([ref[rows, width:] for ref, rows in term], 0).astype(F32) for term in terms]
    top = tails[0]
    for tail in tails[1:]:
        top = jnp.maximum(top, tail)
    tops, sums, columns = [], [], []
    for h in range(heads):
        cols = slice(h * HD, (h + 1) * HD)
        peak = top[:, h : h + 1]
        total, column = None, None
        for term, tail in zip(terms, tails):
            factor = jnp.exp(tail[:, h : h + 1] - peak)
            low = 2 * heads + h
            share = factor * (tail[:, heads + h : heads + h + 1] + tail[:, low : low + 1])
            part = factor * joined([ref[rows, cols] for ref, rows in term], 0).astype(F32)
            total = share if total is None else total + share
            column = part if column is None else column + part
        tops.append(peak)
        sums.append(total)
        columns.append(column)
    return tops, sums, columns


def tailed(groups, rows):
    lane = lax.broadcasted_iota(jnp.int32, (rows, HD), 1)
    tail = jnp.zeros((rows, HD), F32)
    at = 0
    for group in groups:
        for column in group:
            tail = jnp.where(lane == at, column, tail)
            at += 1
    return tail.astype(BF16)


def digits_of(columns, count):
    groups = []
    for _ in range(count):
        upper = [column.astype(BF16).astype(F32) for column in columns]
        groups.append(upper)
        columns = [column - part for column, part in zip(columns, upper)]
    return groups


def merge_kernel(plan, heads, *refs):
    ins, outs = refs[: len(refs) - len(plan)], refs[len(refs) - len(plan) :]
    for terms, out_ref in zip(plan, outs):
        tops, sums, columns = blend(
            [[(ins[i], pl.ds(first, count))] for i, first, count in terms], heads
        )
        for h in range(heads):
            out_ref[:, h * HD : (h + 1) * HD] = columns[h].astype(BF16)
        out_ref[:, heads * HD :] = tailed([tops] + digits_of(sums, 2), out_ref.shape[0])


def grad_kernel(lines, line_ref, w_ref, *refs):
    own_ref, up_refs, down_refs = refs[0], refs[1:lines], refs[lines : 2 * lines - 1]
    ga_ref, blocks_ref, full_ref, w_buf, sems = refs[2 * lines - 1 :]
    width = own_ref.shape[1]
    chunks, _, share = blocks_ref.shape
    line = line_ref[0]
    copies = [
        pltpu.make_async_copy(w_ref.at[pl.ds(i * width, width)], w_buf.at[i], sems.at[i])
        for i in range(lines)
    ]
    start(copies)
    full_ref[line] = own_ref[...]
    for d in range(1, lines):

        @pl.when(line >= d)
        def _():
            full_ref[line - d] = up_refs[d - 1][...]

        @pl.when(line + d < lines)
        def _():
            full_ref[line + d] = down_refs[d - 1][...]

    for j in range(chunks):
        first = j * share
        blocks_ref[j] = full_ref[first // width, :, first % width : first % width + share]
    total = None
    for i in range(lines):
        copies[i].wait()
        term = mm(full_ref[i], w_buf[i])
        total = term if total is None else total + term
    ga_ref[...] = total.astype(BF16)


def finish_kernel(counts, *refs):
    terms, (ga_ref, attn_ref, ext_ref) = dealt(refs, counts)
    rows, width = ga_ref.shape
    heads = width // HD
    tops, sums, columns = blend(
        [[(ref, slice(None)) for ref in pieces] for pieces in terms], heads
    )
    ext_ref[:, :width] = ga_ref[...]
    dots, levels = [], []
    for h in range(heads):
        cols = slice(h * HD, (h + 1) * HD)
        total = columns[h] * (1.0 / sums[h])
        attn_ref[:, cols] = total.astype(BF16)
        dots.append(jnp.sum(total * ga_ref[:, cols].astype(F32), axis=1, keepdims=True))
        levels.append(tops[h] + jnp.log(sums[h]))
    ext_ref[:, width:] = tailed(digits_of(dots, 2) + digits_of(levels, 3), rows)


def total_kernel(counts, *refs):
    terms, (out_ref,) = dealt(refs, counts)
    for h in range(out_ref.shape[1] // HD):
        cols = slice(h * HD, (h + 1) * HD)
        out_ref[:, cols] = added(terms, cols)


def backward_kernel(counts, span, cap, hot_ref, qg_ref, p_ref, logit_ref, k_ref, v_ref, *refs):
    chunks = len(counts)
    ga_refs, refs = dealt(refs, counts)
    part_refs, refs = refs[:chunks], refs[chunks:]
    dk_ref, dv_ref, gag_ref, dq_ref = refs
    block_count, _, width = k_ref.shape
    heads = width // HD
    rows = part_refs[0].shape[0]
    groups = chunks // span
    scale = HD ** (-0.5)

    for g in range(groups):
        ga_group = joined([whole(ga_refs[g * span + i]) for i in range(span)], 0)
        gag_ref[:, g * cap : (g + 1) * cap, :] = (
            mm(hot_ref[g], ga_group).astype(BF16).reshape(block_count, cap, width + HD)
        )
    last = lax.broadcasted_iota(jnp.int32, (BLOCK, groups * cap), 0) == BLOCK - 1

    def one_block(b, carry):
        pairs = [slice(p * 2 * HD, (p + 1) * 2 * HD) for p in range(heads // 2)]
        q = [qg_ref[b, :, cols] for cols in pairs]
        ga = [gag_ref[b, :, cols] for cols in pairs]
        grads = [mm(diagonal(v_ref[b, :, cols]), ga[p], NT) for p, cols in enumerate(pairs)]
        wide = [diagonal(k_ref[b, :, cols]) for cols in pairs]
        probs = [p_ref[b, p].astype(F32) for p in range(heads // 2)]
        tail = gag_ref[b, :, width:].astype(F32).T
        tail = [tail[i * heads : (i + 1) * heads] for i in range(5)]
        dots = tail[0] + tail[1]
        gates = jnp.exp(jnp.minimum(logit_ref[b] - (tail[2] + tail[3] + tail[4]), 0.0))
        gated, score = [], []
        for p in range(heads // 2):
            for i in range(2):
                at = slice(i * BLOCK, (i + 1) * BLOCK)
                h = 2 * p + i
                gate = gates[h : h + 1, :]
                grad = grads[p][at]
                delta = jnp.sum(probs[p][at] * grad, axis=0, keepdims=True)
                weight = probs[p][at] * gate
                extra = jnp.where(last, scale * gate * (delta - dots[h : h + 1, :]), 0.0)
                score.append((weight * (scale * (grad - delta)) + extra).astype(BF16))
                gated.append(weight.astype(BF16))
        for p, cols in enumerate(pairs):
            both = jnp.concatenate(gated[2 * p : 2 * p + 2], axis=0)
            scores = jnp.concatenate(score[2 * p : 2 * p + 2], axis=0)
            dv = mm(both, ga[p])
            dk = mm(scores, q[p])
            dq = mm(scores, wide[p], TN).astype(BF16)
            dv_ref[b, :, cols] = jnp.concatenate([dv[:BLOCK, :HD], dv[BLOCK:, HD:]], axis=1)
            dk_ref[b, :, cols] = jnp.concatenate([dk[:BLOCK, :HD], dk[BLOCK:, HD:]], axis=1)
            dq_ref[b, :, cols] = dq
        return carry

    lax.fori_loop(0, block_count, one_block, 0)

    for g in range(groups):
        slots = dq_ref[:, g * cap : (g + 1) * cap, :].reshape(block_count * cap, width)
        part = mm(hot_ref[g], slots, TN).astype(BF16)
        for i in range(span):
            part_refs[g * span + i][...] = part[i * rows : (i + 1) * rows]


def weight_kernel(counts, me_ref, cols_ref, *refs):
    attns, (out_ref,) = dealt(refs, counts)
    me = me_ref[0]
    columns = joined([cols_ref[me ^ m] for m in range(len(counts))], 0)
    out_ref[...] = mm(columns, joined([whole(pieces) for pieces in attns], 0), TN)


def swap(x, bits):
    count = lax.axis_size("ctx")
    return lax.ppermute(x, "ctx", [(i, i ^ bits) for i in range(count)])


def after(x, *others):
    return lax.optimization_barrier((x, *others))[0]


def flat(lists):
    return [x for pieces in lists for x in pieces]


def spread_chips(x, half, *before):
    chips = lax.axis_size("ctx") // 2
    near = [swap(x, 2 * j) for j in range(1, chips)] if chips != 4 else [swap(x, 2), swap(x, 4)]
    if chips != 4:
        return [[x]] + [[piece] for piece in near]
    far = [swap(after(near[0][:half], *before), 4), swap(after(near[1][half:], *before), 2)]
    return [[x], [near[0]], [near[1]], far]


def with_cores(lists, *before):
    both = []
    for pieces in lists:
        if before and pieces is lists[-1]:
            pieces = [after(piece, *before) for piece in pieces]
        both += [pieces, [swap(piece, 1) for piece in pieces]]
    return both


def from_core(parts, *before):
    received = [None] * (len(parts) // 2)
    for j in reversed(range(len(received))):
        received[j] = swap(after(parts[2 * j + 1], *before), 1)
    return received


def collect_chips(parts, received):
    chips = len(received)

    def both(j, rows, extra=None):
        total = parts[2 * j][rows].astype(F32) + received[j][rows].astype(F32)
        if extra is not None:
            total = total + extra.astype(F32)
        return total.astype(BF16)

    terms = [[parts[0]], [received[0]]]
    if chips != 4:
        return terms + [[swap(both(j, slice(None)), 2 * j)] for j in range(1, chips)]
    half = parts[0].shape[0] // 2
    top, low = slice(0, half), slice(half, None)
    x_far, y_far = swap(both(3, top), 2), swap(both(3, low), 4)
    x_top, y_low = swap(both(1, top), 2), swap(both(2, low), 4)
    x_low, y_top = swap(both(1, low, y_far), 2), swap(both(2, top, x_far), 4)
    return terms + [[x_top, x_low], [y_top, y_low]]


def merge_chips(parts, received, heads, *before):
    chips = len(received)
    rows = parts[0].shape[0]
    half = rows // 2

    def merged(ins, plan):
        return pl.pallas_call(
            functools.partial(merge_kernel, plan, heads),
            out_shape=[
                jax.ShapeDtypeStruct((terms[0][2], ins[0].shape[1]), BF16) for terms in plan
            ],
            in_specs=[pl.BlockSpec(memory_space=pltpu.VMEM)] * len(ins),
            out_specs=[pl.BlockSpec(memory_space=pltpu.VMEM)] * len(plan),
            compiler_params=pltpu.CompilerParams(vmem_limit_bytes=24 * MIB),
            name="merge",
        )(*ins)

    terms = [[parts[0]], [received[0]]]
    if chips != 4:
        for j in range(1, chips):
            (both,) = merged([parts[2 * j], received[j]], [[(0, 0, rows), (1, 0, rows)]])
            terms.append([swap(both, 2 * j)])
        return terms
    top, low = (0, half), (half, half)
    x_far, y_far = merged(
        [parts[6], received[3]], [[(0, *top), (1, *top)], [(0, *low), (1, *low)]]
    )
    x_far, y_far = swap(x_far, 2), swap(y_far, 4)
    ins = [parts[2], received[1], parts[4], received[2]]
    x_top, y_low = merged(ins, [[(0, *top), (1, *top)], [(2, *low), (3, *low)]])
    x_top, y_low = swap(x_top, 2), swap(y_low, 4)
    x_low, y_top = merged(
        ins + [after(y_far, *before), x_far],
        [[(0, *low), (1, *low), (4, *top)], [(2, *top), (3, *top), (5, *top)]],
    )
    x_low, y_top = swap(x_low, 2), swap(y_top, 4)
    return terms + [[x_top, x_low], [y_top, y_low]]


def spread_line(x):
    lines = lax.axis_size("head")
    ups, downs = [x], [x]
    for d in range(1, lines):
        ups.append(lax.ppermute(ups[-1], "head", [(i, i + 1) for i in range(d - 1, lines - 1)]))
        downs.append(lax.ppermute(downs[-1], "head", [(i, i - 1) for i in range(1, lines - d + 1)]))
    return ups[1:], downs[1:]


def body(queries, key_rows, value_rows, selected, out_grad, out_weight):
    chunks = lax.axis_size("ctx")
    chips = chunks // 2
    lines = lax.axis_size("head")
    rows, width = queries.shape
    features = out_weight.shape[0]
    heads = width // HD
    block_count = key_rows.shape[0] // BLOCK
    block_total = block_count * chunks
    capacity = 2 * rows * TOPK // block_total
    span = max(1, 16 // capacity)
    cap = capacity * span
    groups = chunks // span
    slots = groups * cap
    index = lax.axis_index("ctx").astype(jnp.int32)
    me = index.reshape(1)
    keys = key_rows.reshape(block_count, BLOCK, width)
    values = value_rows.reshape(block_count, BLOCK, width)
    vmem = pl.BlockSpec(memory_space=pltpu.VMEM)
    smem = pl.BlockSpec(memory_space=pltpu.SMEM)

    def limit(mib):
        return pltpu.CompilerParams(vmem_limit_bytes=mib * MIB)

    def shaped(shape, kind=BF16):
        return jax.ShapeDtypeStruct(shape, kind)

    ups, downs = spread_line(out_grad)
    packed = pl.pallas_call(
        pack_kernel,
        out_shape=shaped((rows + PAD, width)),
        in_specs=[vmem] * 2,
        out_specs=vmem,
        compiler_params=limit(8),
        name="pack",
    )(selected.T, queries)
    query_chips = spread_chips(packed, rows // 2, ups[0], downs[0])
    query_all = with_cores(query_chips, ups[1], downs[1])

    outs = pl.pallas_call(
        functools.partial(forward_kernel, [len(pieces) for pieces in query_all], span, cap),
        out_shape=[shaped((rows, width + HD))] * chunks
        + [
            shaped((block_count, slots, width)),
            shaped((block_count, heads // 2, 2 * BLOCK, slots)),
            shaped((block_count, heads, slots), F32),
            shaped((groups, block_count * cap, rows * span)),
        ],
        in_specs=[smem] + [vmem] * (3 + len(flat(query_all))),
        out_specs=[vmem] * (chunks + 4),
        scratch_shapes=[
            pltpu.VMEM((block_count, slots, HD), F32),
            pltpu.VMEM((block_count, slots, width), BF16),
        ],
        compiler_params=limit(30),
        name="forward",
    )(me, keys[:, BLOCK - 1], keys, values, *flat(query_all))
    q_slots, probs, logits, hot = outs[chunks:]

    line = lax.axis_index("head").astype(jnp.int32).reshape(1)
    grad_attn, blocks = pl.pallas_call(
        functools.partial(grad_kernel, lines),
        out_shape=[shaped((rows, width)), shaped((chunks, rows, features // chunks))],
        in_specs=[smem, pl.BlockSpec(memory_space=pltpu.HBM)] + [vmem] * (2 * lines - 1),
        out_specs=[vmem] * 2,
        scratch_shapes=[
            pltpu.VMEM((lines, rows, width), BF16),
            pltpu.VMEM((lines, width, width), BF16),
            pltpu.SemaphoreType.DMA((lines,)),
        ],
        compiler_params=limit(28),
        name="grad",
    )(line, out_weight, out_grad, *ups, *downs)
    columns = lax.all_to_all(blocks, "ctx", split_axis=0, concat_axis=0, tiled=True)
    received = from_core(outs[:chunks], *ups[2:], *downs[2:])
    terms = merge_chips(outs[:chunks], received, heads, grad_attn)
    attn_out, extended = pl.pallas_call(
        functools.partial(finish_kernel, [len(pieces) for pieces in terms]),
        out_shape=[shaped((rows, width)), shaped((rows, width + HD))],
        in_specs=[vmem] * (len(flat(terms)) + 1),
        out_specs=[vmem] * 2,
        compiler_params=limit(24),
        name="finish",
    )(*flat(terms), grad_attn)
    grad_chips = spread_chips(extended, rows // 2)
    grad_all = with_cores(grad_chips)
    arrived = flat(grad_chips[1:3])
    attns = [[attn_out]] + [[swap(after(attn_out, *arrived), 2 * j)] for j in range(1, chips)]

    outs = pl.pallas_call(
        functools.partial(backward_kernel, [len(pieces) for pieces in grad_all], span, cap),
        out_shape=[shaped((rows, width))] * chunks
        + [shaped((block_count, BLOCK, width), F32)] * 2,
        in_specs=[vmem] * (6 + len(flat(grad_all))),
        out_specs=[vmem] * (chunks + 2),
        scratch_shapes=[
            pltpu.VMEM((block_count, slots, width + HD), BF16),
            pltpu.VMEM((block_count, slots, width), BF16),
        ],
        compiler_params=limit(40),
        name="backward",
    )(hot, q_slots, probs, after(logits, columns), keys, values, *flat(grad_all))
    key_grad, value_grad = outs[chunks:]
    terms = collect_chips(outs[:chunks], from_core(outs[:chunks], *flat(attns[1:])))
    query_grad = pl.pallas_call(
        functools.partial(total_kernel, [len(pieces) for pieces in terms]),
        out_shape=shaped((rows, width), F32),
        in_specs=[vmem] * len(flat(terms)),
        out_specs=vmem,
        compiler_params=limit(24),
        name="total",
    )(*flat(terms))

    attns = with_cores(attns)
    weight_grad = pl.pallas_call(
        functools.partial(weight_kernel, [len(pieces) for pieces in attns]),
        out_shape=shaped((features // chunks, width), F32),
        in_specs=[smem] + [vmem] * (1 + len(flat(attns))),
        out_specs=vmem,
        compiler_params=limit(24),
        name="weight",
    )(after(me, *flat(terms)), columns, *flat(attns))
    return (
        query_grad,
        key_grad.reshape(-1, width),
        value_grad.reshape(-1, width),
        weight_grad,
    )


def solution(mesh):
    return jax.shard_map(
        body,
        mesh=mesh,
        in_specs=(
            P("ctx", "head"),
            P("ctx", "head"),
            P("ctx", "head"),
            P("ctx", None),
            P("ctx", "head"),
            P(None, "head"),
        ),
        out_specs=(P("ctx", "head"), P("ctx", "head"), P("ctx", "head"), P("ctx", "head")),
        check_vma=False,
    )
```

```python
import functools

import jax
import jax.numpy as jnp
from jax import lax
from jax.experimental import pallas as pl
from jax.experimental.pallas import tpu as pltpu
from jax.sharding import PartitionSpec as P

HD = 128
BLOCK = 64
TOPK = 4
F32 = jnp.float32
BF16 = jnp.bfloat16
MIB = 1024 * 1024
PAD = 16
LOW = -(2.0**99)
NN = (((1,), (0,)), ((), ()))
NT = (((1,), (1,)), ((), ()))
TN = (((0,), (0,)), ((), ()))


def mm(a, b, dims=NN):
    return lax.dot_general(a, b, dims, preferred_element_type=F32)


def joined(items, axis):
    return items[0] if len(items) == 1 else jnp.concatenate(items, axis=axis)


def dealt(refs, counts):
    lists, at = [], 0
    for count in counts:
        lists.append(refs[at : at + count])
        at += count
    return lists, refs[at:]


def start(copies):
    for copy in copies:
        copy.start()


def whole(refs):
    return joined([ref[...] for ref in refs], 0)


def added(terms, cols):
    total = None
    for refs in terms:
        term = joined([ref[:, cols].astype(F32) for ref in refs], 0)
        total = term if total is None else total + term
    return total


def diagonal(pair):
    zero = jnp.zeros((pair.shape[0], HD), pair.dtype)
    top = jnp.concatenate([pair[:, :HD], zero], axis=1)
    low = jnp.concatenate([zero, pair[:, HD:]], axis=1)
    return jnp.concatenate([top, low], axis=0)


def pack_kernel(sel_ref, q_ref, out_ref):
    rows, width = q_ref.shape
    out_ref[:rows] = q_ref[...]
    digits = [(sel_ref[...] >> 4).astype(F32), (sel_ref[...] & 15).astype(F32)]
    if width > 2 * rows:
        digits.append(jnp.zeros((TOPK, width - 2 * rows), F32))
    lines = [jnp.concatenate(digits, axis=1), jnp.zeros((PAD - TOPK, width), F32)]
    out_ref[rows:] = jnp.concatenate(lines, axis=0).astype(BF16)


def forward_kernel(counts, span, cap, me_ref, mark_ref, k_ref, v_ref, *refs):
    chunks = len(counts)
    q_refs, refs = dealt(refs, counts)
    part_refs, refs = refs[:chunks], refs[chunks:]
    qg_ref, p_ref, logit_ref, hot_ref, topg_ref, out_ref = refs
    block_count, _, width = k_ref.shape
    heads = width // HD
    rows = part_refs[0].shape[0]
    group_rows = rows * span
    groups = chunks // span
    scale = HD ** (-0.5)
    rate = scale * 1.4426950408889634
    base = me_ref[0] * block_count

    before = lax.broadcasted_iota(jnp.int32, (group_rows, group_rows), 0)
    later = lax.broadcasted_iota(jnp.int32, (group_rows, group_rows), 1)
    earlier = (before < later).astype(BF16)
    own_ids = (base + lax.broadcasted_iota(jnp.int32, (block_count, group_rows), 0)).astype(F32)
    place = lax.broadcasted_iota(jnp.int32, (cap, group_rows), 0).astype(F32)
    zero = jnp.zeros((block_count, HD), BF16)
    wide_marks = jnp.concatenate(
        [
            jnp.concatenate(
                [mark_ref[:, i * HD : (i + 1) * HD] if i == h else zero for i in range(heads)], axis=1
            )
            for h in range(heads)
        ],
        axis=0,
    )
    q_groups, owns = [], []
    for g in range(groups):
        packs = [whole(q_refs[g * span + i]) for i in range(span)]
        digits = [pack[rows : rows + PAD].astype(F32)[:TOPK] for pack in packs]
        picked = joined([16.0 * d[:, :rows] + d[:, rows : 2 * rows] for d in digits], 1)
        own = picked[0:1, :] == own_ids
        for t in range(1, TOPK):
            own = own | (picked[t : t + 1, :] == own_ids)
        owns.append(jnp.where(own, 1.0, 0.0))
        q_groups.append(joined([pack[:rows] for pack in packs], 0))
    own_all = jnp.concatenate(owns, axis=0)
    rank_all = jnp.where(own_all > 0.5, mm(own_all.astype(BF16), earlier), -1.0)
    hots = []
    for g in range(groups):
        rank = rank_all[g * block_count : (g + 1) * block_count]
        hots.append(
            jnp.concatenate(
                [
                    jnp.where(rank[b : b + 1, :] == place, 1.0, 0.0).astype(BF16)
                    for b in range(block_count)
                ],
                axis=0,
            )
        )
        hot_ref[g] = hots[g]
    all_marks = [mm(wide_marks, q_groups[g], NT) for g in range(groups)]
    for g in range(groups):
        qg_ref[:, g * cap : (g + 1) * cap, :] = (
            mm(hots[g], q_groups[g]).astype(BF16).reshape(block_count, cap, width)
        )
    tails = []
    for g in range(groups):
        tops, sums = [], []
        for h in range(heads):
            mark = scale * all_marks[g][h * block_count : (h + 1) * block_count]
            mark = jnp.where(owns[g] > 0.5, mark, LOW)
            top = jnp.max(mark, axis=0, keepdims=True).astype(BF16).astype(F32)
            tops.append(top)
            sums.append(jnp.sum(owns[g] * jnp.exp(mark - top), axis=0, keepdims=True))
        tops, sums = jnp.concatenate(tops, axis=0), jnp.concatenate(sums, axis=0)
        upper = sums.astype(BF16).astype(F32)
        spare = jnp.zeros((HD - 3 * heads, group_rows), F32)
        tails.append(jnp.concatenate([tops, upper, sums - upper, spare], axis=0))
    for g in range(groups):
        topg_ref[:, g * cap : (g + 1) * cap, :] = mm(hots[g], tails[g].astype(BF16), NT).reshape(
            block_count, cap, HD
        )
    for g in range(groups):
        for i in range(span):
            part_refs[g * span + i][:, width:] = (
                tails[g][:, i * rows : (i + 1) * rows].T.astype(BF16)
            )

    def one_block(b, carry):
        pairs = [slice(p * 2 * HD, (p + 1) * 2 * HD) for p in range(heads // 2)]
        logits = [mm(diagonal(k_ref[b, :, cols]), qg_ref[b, :, cols], NT) for cols in pairs]
        wide = [diagonal(v_ref[b, :, cols]) for cols in pairs]
        tops = topg_ref[b].T[:heads]
        marks = scale * jnp.concatenate(
            [logits[h // 2][(h % 2 + 1) * BLOCK - 1 : (h % 2 + 1) * BLOCK] for h in range(heads)],
            axis=0,
        )
        gates = jnp.exp(marks - tops)
        probs, gated = [], []
        for p in range(heads // 2):
            for i in range(2):
                part = logits[p][i * BLOCK : (i + 1) * BLOCK]
                weight = jnp.exp2(rate * (part - jnp.max(part, axis=0, keepdims=True)))
                inverse = 1.0 / jnp.sum(weight, axis=0, keepdims=True)
                gate = gates[2 * p + i : 2 * p + i + 1, :]
                probs.append((weight * inverse).astype(BF16))
                gated.append((weight * (inverse * gate)).astype(BF16))
        outs = [
            mm(jnp.concatenate(gated[2 * p : 2 * p + 2], axis=0), wide[p], TN).astype(BF16)
            for p in range(heads // 2)
        ]
        logit_ref[b] = marks
        for p in range(heads // 2):
            p_ref[b, p] = jnp.concatenate(probs[2 * p : 2 * p + 2], axis=0)
            out_ref[b, :, pairs[p]] = outs[p]
        return carry

    lax.fori_loop(0, block_count, one_block, 0)

    for g in range(groups):
        slots = out_ref[:, g * cap : (g + 1) * cap, :].reshape(block_count * cap, width)
        part = mm(hot_ref[g], slots, TN).astype(BF16)
        for i in range(span):
            part_refs[g * span + i][:, :width] = part[i * rows : (i + 1) * rows]


def blend(terms, heads):
    width = heads * HD
    tails = [joined([ref[rows, width:] for ref, rows in term], 0).astype(F32) for term in terms]
    top = tails[0]
    for tail in tails[1:]:
        top = jnp.maximum(top, tail)
    tops, sums, columns = [], [], []
    for h in range(heads):
        cols = slice(h * HD, (h + 1) * HD)
        peak = top[:, h : h + 1]
        total, column = None, None
        for term, tail in zip(terms, tails):
            factor = jnp.exp(tail[:, h : h + 1] - peak)
            low = 2 * heads + h
            share = factor * (tail[:, heads + h : heads + h + 1] + tail[:, low : low + 1])
            part = factor * joined([ref[rows, cols] for ref, rows in term], 0).astype(F32)
            total = share if total is None else total + share
            column = part if column is None else column + part
        tops.append(peak)
        sums.append(total)
        columns.append(column)
    return tops, sums, columns


def tailed(groups, rows):
    lane = lax.broadcasted_iota(jnp.int32, (rows, HD), 1)
    tail = jnp.zeros((rows, HD), F32)
    at = 0
    for group in groups:
        for column in group:
            tail = jnp.where(lane == at, column, tail)
            at += 1
    return tail.astype(BF16)


def digits_of(columns, count):
    groups = []
    for _ in range(count):
        upper = [column.astype(BF16).astype(F32) for column in columns]
        groups.append(upper)
        columns = [column - part for column, part in zip(columns, upper)]
    return groups


def merge_kernel(plan, heads, *refs):
    ins, outs = refs[: len(refs) - len(plan)], refs[len(refs) - len(plan) :]
    for terms, out_ref in zip(plan, outs):
        tops, sums, columns = blend(
            [[(ins[i], pl.ds(first, count))] for i, first, count in terms], heads
        )
        for h in range(heads):
            out_ref[:, h * HD : (h + 1) * HD] = columns[h].astype(BF16)
        out_ref[:, heads * HD :] = tailed([tops] + digits_of(sums, 2), out_ref.shape[0])


def grad_kernel(lines, line_ref, w_ref, *refs):
    own_ref, up_refs, down_refs = refs[0], refs[1:lines], refs[lines : 2 * lines - 1]
    ga_ref, blocks_ref, full_ref, w_buf, sems, piece_sems = refs[2 * lines - 1 :]
    width = own_ref.shape[1]
    chunks, _, share = blocks_ref.shape
    line = line_ref[0]
    copies = [
        pltpu.make_async_copy(w_ref.at[pl.ds(i * width, width)], w_buf.at[i], sems.at[i])
        for i in range(lines)
    ]
    start(copies)

    def placed(ref, i):
        return pltpu.make_async_copy(ref, full_ref.at[i], piece_sems.at[i])

    placed(own_ref, line).start()
    for d in range(1, lines):

        @pl.when(line >= d)
        def _():
            placed(up_refs[d - 1], line - d).start()

        @pl.when(line + d < lines)
        def _():
            placed(down_refs[d - 1], line + d).start()

    for i in range(lines):
        placed(own_ref, i).wait()
    for j in range(chunks):
        first = j * share
        blocks_ref[j] = full_ref[first // width, :, first % width : first % width + share]
    total = None
    for i in range(lines):
        copies[i].wait()
        term = mm(full_ref[i], w_buf[i])
        total = term if total is None else total + term
    ga_ref[...] = total.astype(BF16)


def finish_kernel(counts, *refs):
    terms, (ga_ref, attn_ref, ext_ref) = dealt(refs, counts)
    rows, width = ga_ref.shape
    heads = width // HD
    tops, sums, columns = blend(
        [[(ref, slice(None)) for ref in pieces] for pieces in terms], heads
    )
    ext_ref[:, :width] = ga_ref[...]
    dots, levels = [], []
    for h in range(heads):
        cols = slice(h * HD, (h + 1) * HD)
        total = columns[h] * (1.0 / sums[h])
        attn_ref[:, cols] = total.astype(BF16)
        dots.append(jnp.sum(total * ga_ref[:, cols].astype(F32), axis=1, keepdims=True))
        levels.append(tops[h] + jnp.log(sums[h]))
    ext_ref[:, width:] = tailed(digits_of(dots, 2) + digits_of(levels, 3), rows)


def total_kernel(counts, *refs):
    terms, (out_ref,) = dealt(refs, counts)
    for h in range(out_ref.shape[1] // HD):
        cols = slice(h * HD, (h + 1) * HD)
        out_ref[:, cols] = added(terms, cols)


def backward_kernel(counts, span, cap, hot_ref, qg_ref, p_ref, logit_ref, k_ref, v_ref, *refs):
    chunks = len(counts)
    ga_refs, refs = dealt(refs, counts)
    part_refs, refs = refs[:chunks], refs[chunks:]
    dk_ref, dv_ref, gag_ref, dq_ref = refs
    block_count, _, width = k_ref.shape
    heads = width // HD
    rows = part_refs[0].shape[0]
    groups = chunks // span
    scale = HD ** (-0.5)

    for g in range(groups):
        ga_group = joined([whole(ga_refs[g * span + i]) for i in range(span)], 0)
        gag_ref[:, g * cap : (g + 1) * cap, :] = (
            mm(hot_ref[g], ga_group).astype(BF16).reshape(block_count, cap, width + HD)
        )
    last = lax.broadcasted_iota(jnp.int32, (BLOCK, groups * cap), 0) == BLOCK - 1

    def one_block(b, carry):
        pairs = [slice(p * 2 * HD, (p + 1) * 2 * HD) for p in range(heads // 2)]
        q = [qg_ref[b, :, cols] for cols in pairs]
        ga = [gag_ref[b, :, cols] for cols in pairs]
        grads = [mm(diagonal(v_ref[b, :, cols]), ga[p], NT) for p, cols in enumerate(pairs)]
        wide = [diagonal(k_ref[b, :, cols]) for cols in pairs]
        probs = [p_ref[b, p].astype(F32) for p in range(heads // 2)]
        tail = gag_ref[b, :, width:].astype(F32).T
        tail = [tail[i * heads : (i + 1) * heads] for i in range(5)]
        dots = tail[0] + tail[1]
        gates = jnp.exp(jnp.minimum(logit_ref[b] - (tail[2] + tail[3] + tail[4]), 0.0))
        gated, score = [], []
        for p in range(heads // 2):
            for i in range(2):
                at = slice(i * BLOCK, (i + 1) * BLOCK)
                h = 2 * p + i
                gate = gates[h : h + 1, :]
                grad = grads[p][at]
                delta = jnp.sum(probs[p][at] * grad, axis=0, keepdims=True)
                weight = probs[p][at] * gate
                extra = jnp.where(last, scale * gate * (delta - dots[h : h + 1, :]), 0.0)
                score.append((weight * (scale * (grad - delta)) + extra).astype(BF16))
                gated.append(weight.astype(BF16))
        for p, cols in enumerate(pairs):
            both = jnp.concatenate(gated[2 * p : 2 * p + 2], axis=0)
            scores = jnp.concatenate(score[2 * p : 2 * p + 2], axis=0)
            dv = mm(both, ga[p])
            dk = mm(scores, q[p])
            dq = mm(scores, wide[p], TN).astype(BF16)
            dv_ref[b, :, cols] = jnp.concatenate([dv[:BLOCK, :HD], dv[BLOCK:, HD:]], axis=1)
            dk_ref[b, :, cols] = jnp.concatenate([dk[:BLOCK, :HD], dk[BLOCK:, HD:]], axis=1)
            dq_ref[b, :, cols] = dq
        return carry

    lax.fori_loop(0, block_count, one_block, 0)

    for g in range(groups):
        slots = dq_ref[:, g * cap : (g + 1) * cap, :].reshape(block_count * cap, width)
        part = mm(hot_ref[g], slots, TN).astype(BF16)
        for i in range(span):
            part_refs[g * span + i][...] = part[i * rows : (i + 1) * rows]


def weight_kernel(counts, me_ref, cols_ref, *refs):
    attns, (out_ref,) = dealt(refs, counts)
    me = me_ref[0]
    columns = joined([cols_ref[me ^ m] for m in range(len(counts))], 0)
    out_ref[...] = mm(columns, joined([whole(pieces) for pieces in attns], 0), TN)


def swap(x, bits):
    count = lax.axis_size("ctx")
    return lax.ppermute(x, "ctx", [(i, i ^ bits) for i in range(count)])


def after(x, *others):
    return lax.optimization_barrier((x, *others))[0]


def flat(lists):
    return [x for pieces in lists for x in pieces]


def spread_chips(x, half, *before):
    chips = lax.axis_size("ctx") // 2
    near = [swap(x, 2 * j) for j in range(1, chips)] if chips != 4 else [swap(x, 2), swap(x, 4)]
    if chips != 4:
        return [[x]] + [[piece] for piece in near]
    far = [swap(after(near[0][:half], *before), 4), swap(after(near[1][half:], *before), 2)]
    return [[x], [near[0]], [near[1]], far]


def with_cores(lists, *before):
    both = []
    for pieces in lists:
        if before and pieces is lists[-1]:
            pieces = [after(piece, *before) for piece in pieces]
        both += [pieces, [swap(piece, 1) for piece in pieces]]
    return both


def from_core(parts, *before):
    received = [None] * (len(parts) // 2)
    for j in reversed(range(len(received))):
        received[j] = swap(after(parts[2 * j + 1], *before), 1)
    return received


def collect_chips(parts, received):
    chips = len(received)

    def both(j, rows, extra=None):
        total = parts[2 * j][rows].astype(F32) + received[j][rows].astype(F32)
        if extra is not None:
            total = total + extra.astype(F32)
        return total.astype(BF16)

    terms = [[parts[0]], [received[0]]]
    if chips != 4:
        return terms + [[swap(both(j, slice(None)), 2 * j)] for j in range(1, chips)]
    half = parts[0].shape[0] // 2
    top, low = slice(0, half), slice(half, None)
    x_far, y_far = swap(both(3, top), 2), swap(both(3, low), 4)
    x_top, y_low = swap(both(1, top), 2), swap(both(2, low), 4)
    x_low, y_top = swap(both(1, low, y_far), 2), swap(both(2, top, x_far), 4)
    return terms + [[x_top, x_low], [y_top, y_low]]


def merge_chips(parts, received, heads, between):
    chips = len(received)
    rows = parts[0].shape[0]
    half = rows // 2

    def merged(ins, plan):
        return pl.pallas_call(
            functools.partial(merge_kernel, plan, heads),
            out_shape=[
                jax.ShapeDtypeStruct((terms[0][2], ins[0].shape[1]), BF16) for terms in plan
            ],
            in_specs=[pl.BlockSpec(memory_space=pltpu.VMEM)] * len(ins),
            out_specs=[pl.BlockSpec(memory_space=pltpu.VMEM)] * len(plan),
            compiler_params=pltpu.CompilerParams(vmem_limit_bytes=24 * MIB),
            name="merge",
        )(*ins)

    terms = [[parts[0]], [received[0]]]
    if chips != 4:
        for j in range(1, chips):
            (both,) = merged([parts[2 * j], received[j]], [[(0, 0, rows), (1, 0, rows)]])
            terms.append([swap(both, 2 * j)])
        return terms, between(received[0])
    top, low = (0, half), (half, half)
    x_far, y_far = merged(
        [parts[6], received[3]], [[(0, *top), (1, *top)], [(0, *low), (1, *low)]]
    )
    x_far, y_far = swap(x_far, 2), swap(y_far, 4)
    ins = [parts[2], received[1], parts[4], received[2]]
    x_top, y_low = merged(ins, [[(0, *top), (1, *top)], [(2, *low), (3, *low)]])
    done = between(x_top, y_low)
    x_top, y_low = swap(x_top, 2), swap(y_low, 4)
    x_low, y_top = merged(
        ins + [after(y_far, done[0]), x_far],
        [[(0, *low), (1, *low), (4, *top)], [(2, *top), (3, *top), (5, *top)]],
    )
    x_low, y_top = swap(x_low, 2), swap(y_top, 4)
    return terms + [[x_top, x_low], [y_top, y_low]], done


def spread_line(x):
    lines = lax.axis_size("head")
    ups, downs = [x], [x]
    for d in range(1, lines):
        ups.append(lax.ppermute(ups[-1], "head", [(i, i + 1) for i in range(d - 1, lines - 1)]))
        downs.append(lax.ppermute(downs[-1], "head", [(i, i - 1) for i in range(1, lines - d + 1)]))
    return ups[1:], downs[1:]


def body(queries, key_rows, value_rows, selected, out_grad, out_weight):
    chunks = lax.axis_size("ctx")
    chips = chunks // 2
    lines = lax.axis_size("head")
    rows, width = queries.shape
    features = out_weight.shape[0]
    heads = width // HD
    block_count = key_rows.shape[0] // BLOCK
    block_total = block_count * chunks
    capacity = 2 * rows * TOPK // block_total
    span = max(1, 16 // capacity)
    cap = capacity * span
    groups = chunks // span
    slots = groups * cap
    index = lax.axis_index("ctx").astype(jnp.int32)
    me = index.reshape(1)
    keys = key_rows.reshape(block_count, BLOCK, width)
    values = value_rows.reshape(block_count, BLOCK, width)
    vmem = pl.BlockSpec(memory_space=pltpu.VMEM)
    smem = pl.BlockSpec(memory_space=pltpu.SMEM)

    def limit(mib):
        return pltpu.CompilerParams(vmem_limit_bytes=mib * MIB)

    def shaped(shape, kind=BF16):
        return jax.ShapeDtypeStruct(shape, kind)

    ups, downs = spread_line(out_grad)
    packed = pl.pallas_call(
        pack_kernel,
        out_shape=shaped((rows + PAD, width)),
        in_specs=[vmem] * 2,
        out_specs=vmem,
        compiler_params=limit(8),
        name="pack",
    )(selected.T, queries)
    query_chips = spread_chips(packed, rows // 2, ups[0], downs[0])
    query_all = with_cores(query_chips)

    outs = pl.pallas_call(
        functools.partial(forward_kernel, [len(pieces) for pieces in query_all], span, cap),
        out_shape=[shaped((rows, width + HD))] * chunks
        + [
            shaped((block_count, slots, width)),
            shaped((block_count, heads // 2, 2 * BLOCK, slots)),
            shaped((block_count, heads, slots), F32),
            shaped((groups, block_count * cap, rows * span)),
        ],
        in_specs=[smem] + [vmem] * (3 + len(flat(query_all))),
        out_specs=[vmem] * (chunks + 4),
        scratch_shapes=[
            pltpu.VMEM((block_count, slots, HD), F32),
            pltpu.VMEM((block_count, slots, width), BF16),
        ],
        compiler_params=limit(40),
        name="forward",
    )(me, keys[:, BLOCK - 1], keys, values, *flat(query_all))
    q_slots, probs, logits, hot = outs[chunks:]

    line = lax.axis_index("head").astype(jnp.int32).reshape(1)
    make_grad = pl.pallas_call(
        functools.partial(grad_kernel, lines),
        out_shape=[shaped((rows, width)), shaped((chunks, rows, features // chunks))],
        in_specs=[smem] + [pl.BlockSpec(memory_space=pltpu.HBM)] * (2 * lines),
        out_specs=[vmem] * 2,
        scratch_shapes=[
            pltpu.VMEM((lines, rows, width), BF16),
            pltpu.VMEM((lines, width, width), BF16),
            pltpu.SemaphoreType.DMA((lines,)),
            pltpu.SemaphoreType.DMA((lines,)),
        ],
        compiler_params=limit(28),
        name="grad",
    )
    received = from_core(outs[:chunks], ups[1], downs[1])
    terms, (grad_attn, blocks) = merge_chips(
        outs[:chunks],
        received,
        heads,
        lambda *before: make_grad(after(line, *before), out_weight, out_grad, *ups, *downs),
    )
    attn_out, extended = pl.pallas_call(
        functools.partial(finish_kernel, [len(pieces) for pieces in terms]),
        out_shape=[shaped((rows, width)), shaped((rows, width + HD))],
        in_specs=[vmem] * (len(flat(terms)) + 1),
        out_specs=[vmem] * 2,
        compiler_params=limit(24),
        name="finish",
    )(*flat(terms), grad_attn)
    grad_chips = spread_chips(extended, rows // 2)
    grad_all = with_cores(grad_chips)
    arrived = flat(grad_chips[1:3])
    attns = spread_chips(after(attn_out, *arrived), rows // 2)
    columns = lax.all_to_all(
        after(blocks, *arrived), "ctx", split_axis=0, concat_axis=0, tiled=True
    )

    outs = pl.pallas_call(
        functools.partial(backward_kernel, [len(pieces) for pieces in grad_all], span, cap),
        out_shape=[shaped((rows, width))] * chunks
        + [shaped((block_count, BLOCK, width), F32)] * 2,
        in_specs=[vmem] * (6 + len(flat(grad_all))),
        out_specs=[vmem] * (chunks + 2),
        scratch_shapes=[
            pltpu.VMEM((block_count, slots, width + HD), BF16),
            pltpu.VMEM((block_count, slots, width), BF16),
        ],
        compiler_params=limit(44),
        name="backward",
    )(hot, q_slots, probs, logits, keys, values, *flat(grad_all))
    key_grad, value_grad = outs[chunks:]
    terms = collect_chips(outs[:chunks], from_core(outs[:chunks], *flat(attns[1:3])))
    query_grad = pl.pallas_call(
        functools.partial(total_kernel, [len(pieces) for pieces in terms]),
        out_shape=shaped((rows, width), F32),
        in_specs=[vmem] * len(flat(terms)),
        out_specs=vmem,
        compiler_params=limit(24),
        name="total",
    )(*flat(terms))

    attns = with_cores(attns)
    weight_grad = pl.pallas_call(
        functools.partial(weight_kernel, [len(pieces) for pieces in attns]),
        out_shape=shaped((features // chunks, width), F32),
        in_specs=[smem] + [vmem] * (1 + len(flat(attns))),
        out_specs=vmem,
        compiler_params=limit(24),
        name="weight",
    )(after(me, *flat(terms)), columns, *flat(attns))
    return (
        query_grad,
        key_grad.reshape(-1, width),
        value_grad.reshape(-1, width),
        weight_grad,
    )


def solution(mesh):
    return jax.shard_map(
        body,
        mesh=mesh,
        in_specs=(
            P("ctx", "head"),
            P("ctx", "head"),
            P("ctx", "head"),
            P("ctx", None),
            P("ctx", "head"),
            P(None, "head"),
        ),
        out_specs=(P("ctx", "head"), P("ctx", "head"), P("ctx", "head"), P("ctx", "head")),
        check_vma=False,
    )
```

```python
import functools

import jax
import jax.numpy as jnp
from jax import lax
from jax.experimental import pallas as pl
from jax.experimental.pallas import tpu as pltpu
from jax.sharding import PartitionSpec as P

HD = 128
BLOCK = 64
TOPK = 4
F32 = jnp.float32
BF16 = jnp.bfloat16
MOST = 58 * 1024 * 1024
SOME = 20 * 1024 * 1024
PAD = 16
LOW = -(2.0**99)
NN = (((1,), (0,)), ((), ()))
NT = (((1,), (1,)), ((), ()))
TN = (((0,), (0,)), ((), ()))


def mm(a, b, dims=NN):
    return lax.dot_general(a, b, dims, preferred_element_type=F32)


def joined(items, axis):
    return items[0] if len(items) == 1 else jnp.concatenate(items, axis=axis)


def dealt(refs, counts):
    lists, at = [], 0
    for count in counts:
        lists.append(refs[at : at + count])
        at += count
    return lists, refs[at:]


def loads(lists, buf, sems):
    copies, at = [], 0
    for i, refs in enumerate(lists):
        mine, row = [], 0
        for ref in refs:
            rows = ref.shape[0]
            mine.append(
                pltpu.make_async_copy(ref, buf.at[i, pl.ds(row, rows)], sems.at[at])
            )
            row += rows
            at += 1
        copies.append(mine)
    return copies


def start(copies):
    for copy in copies:
        copy.start()


def wait(copies):
    for copy in copies:
        copy.wait()


def whole(refs):
    return joined([ref[...] for ref in refs], 0)


def added(terms, cols):
    total = None
    for refs in terms:
        term = joined([ref[:, cols].astype(F32) for ref in refs], 0)
        total = term if total is None else total + term
    return total


def diagonal(pair):
    zero = jnp.zeros((pair.shape[0], HD), pair.dtype)
    top = jnp.concatenate([pair[:, :HD], zero], axis=1)
    low = jnp.concatenate([zero, pair[:, HD:]], axis=1)
    return jnp.concatenate([top, low], axis=0)


def pack_kernel(sel_ref, q_ref, out_ref):
    rows, width = q_ref.shape
    out_ref[:rows] = q_ref[...]
    digits = [(sel_ref[...] >> 4).astype(F32), (sel_ref[...] & 15).astype(F32)]
    if width > 2 * rows:
        digits.append(jnp.zeros((TOPK, width - 2 * rows), F32))
    lines = [jnp.concatenate(digits, axis=1), jnp.zeros((PAD - TOPK, width), F32)]
    out_ref[rows:] = jnp.concatenate(lines, axis=0).astype(BF16)


def forward_kernel(counts, span, cap, me_ref, mark_ref, k_any, v_any, *refs):
    chunks = len(counts)
    q_refs, refs = dealt(refs, counts)
    part_any, refs = refs[:chunks], refs[chunks:]
    qg_any, p_any, logit_ref, hot_any = refs[:4]
    q_buf, part_refs, k_ref, v_ref, qg_ref, p_ref, hot_ref, topg_ref, out_ref = refs[4:13]
    in_sems, kv_sems, out_sems = refs[13:]
    q_copies = loads(q_refs, q_buf, in_sems)
    kv_copies = [
        pltpu.make_async_copy(k_any, k_ref, kv_sems.at[0]),
        pltpu.make_async_copy(v_any, v_ref, kv_sems.at[1]),
    ]
    out_copies = [
        pltpu.make_async_copy(qg_ref, qg_any, out_sems.at[chunks]),
        pltpu.make_async_copy(hot_ref, hot_any, out_sems.at[chunks + 1]),
        pltpu.make_async_copy(p_ref, p_any, out_sems.at[chunks + 2]),
    ]
    for copies in q_copies:
        start(copies)
    start(kv_copies)
    block_count, _, width = k_ref.shape
    heads = width // HD
    rows = part_any[0].shape[0]
    group_rows = rows * span
    groups = chunks // span
    scale = HD ** (-0.5)
    rate = scale * 1.4426950408889634
    base = me_ref[0] * block_count

    before = lax.broadcasted_iota(jnp.int32, (group_rows, group_rows), 0)
    later = lax.broadcasted_iota(jnp.int32, (group_rows, group_rows), 1)
    earlier = (before < later).astype(BF16)
    own_ids = (base + lax.broadcasted_iota(jnp.int32, (block_count, group_rows), 0)).astype(F32)
    place = lax.broadcasted_iota(jnp.int32, (cap, group_rows), 0).astype(F32)
    zero = jnp.zeros((block_count, HD), BF16)
    wide_marks = jnp.concatenate(
        [
            jnp.concatenate(
                [mark_ref[:, i * HD : (i + 1) * HD] if i == h else zero for i in range(heads)], axis=1
            )
            for h in range(heads)
        ],
        axis=0,
    )
    q_groups, owns = [], []
    for g in range(groups):
        for i in range(span):
            wait(q_copies[g * span + i])
        packs = [q_buf[g * span + i] for i in range(span)]
        digits = [pack[rows : rows + PAD].astype(F32)[:TOPK] for pack in packs]
        picked = joined([16.0 * d[:, :rows] + d[:, rows : 2 * rows] for d in digits], 1)
        own = picked[0:1, :] == own_ids
        for t in range(1, TOPK):
            own = own | (picked[t : t + 1, :] == own_ids)
        owns.append(jnp.where(own, 1.0, 0.0))
        q_groups.append(joined([pack[:rows] for pack in packs], 0))
    own_all = jnp.concatenate(owns, axis=0)
    rank_all = jnp.where(own_all > 0.5, mm(own_all.astype(BF16), earlier), -1.0)
    hots = []
    for g in range(groups):
        rank = rank_all[g * block_count : (g + 1) * block_count]
        hots.append(
            jnp.concatenate(
                [
                    jnp.where(rank[b : b + 1, :] == place, 1.0, 0.0).astype(BF16)
                    for b in range(block_count)
                ],
                axis=0,
            )
        )
        hot_ref[g] = hots[g]
    all_marks = [mm(wide_marks, q_groups[g], NT) for g in range(groups)]
    for g in range(groups):
        qg_ref[:, g * cap : (g + 1) * cap, :] = (
            mm(hots[g], q_groups[g]).astype(BF16).reshape(block_count, cap, width)
        )
    tails = []
    for g in range(groups):
        tops, sums = [], []
        for h in range(heads):
            mark = scale * all_marks[g][h * block_count : (h + 1) * block_count]
            mark = jnp.where(owns[g] > 0.5, mark, LOW)
            top = jnp.max(mark, axis=0, keepdims=True).astype(BF16).astype(F32)
            tops.append(top)
            sums.append(jnp.sum(owns[g] * jnp.exp(mark - top), axis=0, keepdims=True))
        tops, sums = jnp.concatenate(tops, axis=0), jnp.concatenate(sums, axis=0)
        upper = sums.astype(BF16).astype(F32)
        spare = jnp.zeros((HD - 3 * heads, group_rows), F32)
        tails.append(jnp.concatenate([tops, upper, sums - upper, spare], axis=0))
    for g in range(groups):
        topg_ref[:, g * cap : (g + 1) * cap, :] = mm(hots[g], tails[g].astype(BF16), NT).reshape(
            block_count, cap, HD
        )
    for g in range(groups):
        for i in range(span):
            part_refs[g * span + i, :, width:] = (
                tails[g][:, i * rows : (i + 1) * rows].T.astype(BF16)
            )
    start(out_copies[:2])
    wait(kv_copies)

    def one_block(b, carry):
        pairs = [slice(p * 2 * HD, (p + 1) * 2 * HD) for p in range(heads // 2)]
        logits = [mm(diagonal(k_ref[b, :, cols]), qg_ref[b, :, cols], NT) for cols in pairs]
        wide = [diagonal(v_ref[b, :, cols]) for cols in pairs]
        tops = topg_ref[b].T[:heads]
        marks = scale * jnp.concatenate(
            [logits[h // 2][(h % 2 + 1) * BLOCK - 1 : (h % 2 + 1) * BLOCK] for h in range(heads)],
            axis=0,
        )
        gates = jnp.exp(marks - tops)
        probs, gated = [], []
        for p in range(heads // 2):
            for i in range(2):
                part = logits[p][i * BLOCK : (i + 1) * BLOCK]
                weight = jnp.exp2(rate * (part - jnp.max(part, axis=0, keepdims=True)))
                inverse = 1.0 / jnp.sum(weight, axis=0, keepdims=True)
                gate = gates[2 * p + i : 2 * p + i + 1, :]
                probs.append((weight * inverse).astype(BF16))
                gated.append((weight * (inverse * gate)).astype(BF16))
        outs = [
            mm(jnp.concatenate(gated[2 * p : 2 * p + 2], axis=0), wide[p], TN).astype(BF16)
            for p in range(heads // 2)
        ]
        logit_ref[b] = marks
        for p in range(heads // 2):
            p_ref[b, p] = jnp.concatenate(probs[2 * p : 2 * p + 2], axis=0)
            out_ref[b, :, pairs[p]] = outs[p]
        return carry

    lax.fori_loop(0, block_count, one_block, 0)
    start(out_copies[2:])

    for g in range(groups):
        slots = out_ref[:, g * cap : (g + 1) * cap, :].reshape(block_count * cap, width)
        part = mm(hot_ref[g], slots, TN).astype(BF16)
        for i in range(span):
            m = g * span + i
            part_refs[m, :, :width] = part[i * rows : (i + 1) * rows]
            copy = pltpu.make_async_copy(part_refs.at[m], part_any[m], out_sems.at[m])
            copy.start()
            out_copies.append(copy)
    wait(out_copies)


def shift(heads, *moves):
    row = lax.broadcasted_iota(jnp.int32, (HD, HD), 0)
    col = lax.broadcasted_iota(jnp.int32, (HD, HD), 1)
    total = jnp.zeros((HD, HD), F32)
    for source, target in moves:
        inside = (row >= source * heads) & (row < (source + 1) * heads)
        hit = inside & (col - target * heads == row - source * heads)
        total = jnp.where(hit, 1.0, total)
    return total.astype(BF16)


def blend(terms, heads):
    width = heads * HD
    tails = [joined([ref[rows, width:] for ref, rows in term], 0) for term in terms]
    wide = [tail.astype(F32) for tail in tails]
    top = wide[0]
    for tail in wide[1:]:
        top = jnp.maximum(top, tail)
    gather = shift(heads, (1, 0), (2, 0))
    factors = [jnp.exp(tail - top) for tail in wide]
    total = None
    for tail, factor in zip(tails, factors):
        share = factor * mm(tail, gather)
        total = share if total is None else total + share
    columns = []
    for h in range(heads):
        cols = slice(h * HD, (h + 1) * HD)
        column = None
        for term, factor in zip(terms, factors):
            values = joined([ref[rows, cols] for ref, rows in term], 0).astype(F32)
            part = factor[:, h : h + 1] * values
            column = part if column is None else column + part
        columns.append(column)
    return top, total, columns


def digits_of(tile, count):
    digits = []
    for _ in range(count):
        upper = tile.astype(BF16)
        digits.append(upper)
        tile = tile - upper.astype(F32)
    return digits


def packed_tail(digits, heads):
    total = None
    for i, digit in enumerate(digits):
        part = mm(digit, shift(heads, (0, i)))
        total = part if total is None else total + part
    return total.astype(BF16)


def merge_kernel(plan, heads, *refs):
    ins, outs = refs[: len(refs) - len(plan)], refs[len(refs) - len(plan) :]
    for terms, out_ref in zip(plan, outs):
        top, total, columns = blend(
            [[(ins[i], pl.ds(first, count))] for i, first, count in terms], heads
        )
        for h in range(heads):
            out_ref[:, h * HD : (h + 1) * HD] = columns[h].astype(BF16)
        out_ref[:, heads * HD :] = packed_tail([top.astype(BF16)] + digits_of(total, 2), heads)


def grad_kernel(lines, line_ref, w_ref, *refs):
    own_ref, up_refs, down_refs = refs[0], refs[1:lines], refs[lines : 2 * lines - 1]
    ga_ref, blocks_ref, full_ref, w_buf, sems, piece_sems = refs[2 * lines - 1 :]
    width = own_ref.shape[1]
    chunks, _, share = blocks_ref.shape
    line = line_ref[0]
    copies = [
        pltpu.make_async_copy(w_ref.at[pl.ds(i * width, width)], w_buf.at[i], sems.at[i])
        for i in range(lines)
    ]
    start(copies)

    def placed(ref, i):
        return pltpu.make_async_copy(ref, full_ref.at[i], piece_sems.at[i])

    placed(own_ref, line).start()
    for d in range(1, lines):

        @pl.when(line >= d)
        def _():
            placed(up_refs[d - 1], line - d).start()

        @pl.when(line + d < lines)
        def _():
            placed(down_refs[d - 1], line + d).start()

    for i in range(lines):
        placed(own_ref, i).wait()
    for j in range(chunks):
        first = j * share
        blocks_ref[j] = full_ref[first // width, :, first % width : first % width + share]
    total = None
    for i in range(lines):
        copies[i].wait()
        term = mm(full_ref[i], w_buf[i])
        total = term if total is None else total + term
    ga_ref[...] = total.astype(BF16)


def finish_kernel(counts, *refs):
    terms, (ga_ref, attn_ref, ext_ref) = dealt(refs, counts)
    rows, width = ga_ref.shape
    heads = width // HD
    top, total, columns = blend(
        [[(ref, slice(None)) for ref in pieces] for pieces in terms], heads
    )
    lane = lax.broadcasted_iota(jnp.int32, (rows, HD), 1)
    total = jnp.where(lane < heads, total, 1.0)
    inverse = 1.0 / total
    dots = jnp.zeros((rows, HD), F32)
    ext_ref[:, :width] = ga_ref[...]
    for h in range(heads):
        cols = slice(h * HD, (h + 1) * HD)
        attn = columns[h] * inverse[:, h : h + 1]
        attn_ref[:, cols] = attn.astype(BF16)
        dot = jnp.sum(attn * ga_ref[:, cols].astype(F32), axis=1, keepdims=True)
        dots = jnp.where(lane == h, dot, dots)
    level = jnp.where(lane < heads, top + jnp.log(total), 0.0)
    ext_ref[:, width:] = packed_tail(digits_of(dots, 2) + digits_of(level, 3), heads)


def total_kernel(counts, *refs):
    terms, (out_ref,) = dealt(refs, counts)
    for h in range(out_ref.shape[1] // HD):
        cols = slice(h * HD, (h + 1) * HD)
        out_ref[:, cols] = added(terms, cols)


def backward_kernel(counts, span, cap, logit_ref, hot_any, qg_any, p_any, k_any, v_any, *refs):
    chunks = len(counts)
    ga_refs, refs = dealt(refs, counts)
    part_refs, refs = refs[:chunks], refs[chunks:]
    dk_any, dv_any = refs[:2]
    ga_buf, hot_ref, qg_ref, p_ref, k_ref, v_ref, gag_ref, dq_ref, dk_ref, dv_ref = refs[2:12]
    in_sems, hot_sem, block_sems, out_sems, part_sems = refs[12:]
    ga_copies = loads(ga_refs, ga_buf, in_sems)
    hot_copy = pltpu.make_async_copy(hot_any, hot_ref, hot_sem.at[0])
    hot_copy.start()
    for copies in ga_copies:
        start(copies)

    def block_loads(b):
        pairs = ((qg_any, qg_ref), (p_any, p_ref), (k_any, k_ref), (v_any, v_ref))
        return [
            pltpu.make_async_copy(far.at[b], near.at[b], block_sems.at[i, b])
            for i, (far, near) in enumerate(pairs)
        ]

    def block_stores(b):
        return [
            pltpu.make_async_copy(dk_ref.at[b], dk_any.at[b], out_sems.at[0, b]),
            pltpu.make_async_copy(dv_ref.at[b], dv_any.at[b], out_sems.at[1, b]),
        ]

    block_count, _, width = k_ref.shape
    heads = width // HD
    rows = part_refs[0].shape[0]
    groups = chunks // span
    scale = HD ** (-0.5)

    for b in range(block_count):
        start(block_loads(b))
    hot_copy.wait()
    for g in range(groups):
        for i in range(span):
            wait(ga_copies[g * span + i])
        ga_group = joined([ga_buf[g * span + i] for i in range(span)], 0)
        gag_ref[:, g * cap : (g + 1) * cap, :] = (
            mm(hot_ref[g], ga_group).astype(BF16).reshape(block_count, cap, width + HD)
        )
    last = lax.broadcasted_iota(jnp.int32, (BLOCK, groups * cap), 0) == BLOCK - 1

    def one_block(b, carry):
        wait(block_loads(b))
        pairs = [slice(p * 2 * HD, (p + 1) * 2 * HD) for p in range(heads // 2)]
        q = [qg_ref[b, :, cols] for cols in pairs]
        ga = [gag_ref[b, :, cols] for cols in pairs]
        grads = [mm(diagonal(v_ref[b, :, cols]), ga[p], NT) for p, cols in enumerate(pairs)]
        wide = [diagonal(k_ref[b, :, cols]) for cols in pairs]
        probs = [p_ref[b, p].astype(F32) for p in range(heads // 2)]
        tail = gag_ref[b, :, width:].astype(F32).T
        tail = [tail[i * heads : (i + 1) * heads] for i in range(5)]
        dots = tail[0] + tail[1]
        gates = jnp.exp(jnp.minimum(logit_ref[b] - (tail[2] + tail[3] + tail[4]), 0.0))
        gated, score = [], []
        for p in range(heads // 2):
            for i in range(2):
                at = slice(i * BLOCK, (i + 1) * BLOCK)
                h = 2 * p + i
                gate = gates[h : h + 1, :]
                grad = grads[p][at]
                delta = jnp.sum(probs[p][at] * grad, axis=0, keepdims=True)
                weight = probs[p][at] * gate
                extra = jnp.where(last, scale * gate * (delta - dots[h : h + 1, :]), 0.0)
                score.append((weight * (scale * (grad - delta)) + extra).astype(BF16))
                gated.append(weight.astype(BF16))
        for p, cols in enumerate(pairs):
            both = jnp.concatenate(gated[2 * p : 2 * p + 2], axis=0)
            scores = jnp.concatenate(score[2 * p : 2 * p + 2], axis=0)
            dv = mm(both, ga[p])
            dk = mm(scores, q[p])
            dq = mm(scores, wide[p], TN).astype(BF16)
            dv_ref[b, :, cols] = jnp.concatenate([dv[:BLOCK, :HD], dv[BLOCK:, HD:]], axis=1)
            dk_ref[b, :, cols] = jnp.concatenate([dk[:BLOCK, :HD], dk[BLOCK:, HD:]], axis=1)
            dq_ref[b, :, cols] = dq
        start(block_stores(b))
        return carry

    lax.fori_loop(0, block_count, one_block, 0)

    part_copies = []

    for g in range(groups):
        slots = dq_ref[:, g * cap : (g + 1) * cap, :].reshape(block_count * cap, width)
        part = mm(hot_ref[g], slots, TN).astype(BF16)
        for i in range(span):
            m = g * span + i
            ga_buf[m, :, :width] = part[i * rows : (i + 1) * rows]
            copy = pltpu.make_async_copy(
                ga_buf.at[m, :, pl.ds(0, width)], part_refs[m], part_sems.at[m]
            )
            copy.start()
            part_copies.append(copy)
    for b in range(block_count):
        wait(block_stores(b))
    wait(part_copies)


def weight_kernel(counts, me_ref, cols_ref, *refs):
    attns, (out_ref,) = dealt(refs, counts)
    me = me_ref[0]
    columns = joined([cols_ref[me ^ m] for m in range(len(counts))], 0)
    out_ref[...] = mm(columns, joined([whole(pieces) for pieces in attns], 0), TN)


def swap(x, bits):
    count = lax.axis_size("ctx")
    return lax.ppermute(x, "ctx", [(i, i ^ bits) for i in range(count)])


def after(x, *others):
    return lax.optimization_barrier((x, *others))[0]


def flat(lists):
    return [x for pieces in lists for x in pieces]


def spread_chips(x, half, *before):
    chips = lax.axis_size("ctx") // 2
    near = [swap(x, 2 * j) for j in range(1, chips)] if chips != 4 else [swap(x, 2), swap(x, 4)]
    if chips != 4:
        return [[x]] + [[piece] for piece in near]
    far = [swap(after(near[0][:half], *before), 4), swap(after(near[1][half:], *before), 2)]
    return [[x], [near[0]], [near[1]], far]


def with_cores(lists, *before):
    both = []
    for pieces in lists:
        if before and pieces is lists[-1]:
            pieces = [after(piece, *before) for piece in pieces]
        both += [pieces, [swap(piece, 1) for piece in pieces]]
    return both


def from_core(parts, *before):
    received = [None] * (len(parts) // 2)
    for j in reversed(range(len(received))):
        received[j] = swap(after(parts[2 * j + 1], *before), 1)
    return received


def collect_chips(parts, received):
    chips = len(received)

    def both(j, rows, extra=None):
        total = parts[2 * j][rows].astype(F32) + received[j][rows].astype(F32)
        if extra is not None:
            total = total + extra.astype(F32)
        return total.astype(BF16)

    terms = [[parts[0]], [received[0]]]
    if chips != 4:
        return terms + [[swap(both(j, slice(None)), 2 * j)] for j in range(1, chips)]
    half = parts[0].shape[0] // 2
    top, low = slice(0, half), slice(half, None)
    x_far, y_far = swap(both(3, top), 2), swap(both(3, low), 4)
    x_top, y_low = swap(both(1, top), 2), swap(both(2, low), 4)
    x_low, y_top = swap(both(1, low, y_far), 2), swap(both(2, top, x_far), 4)
    return terms + [[x_top, x_low], [y_top, y_low]]


def merge_chips(parts, received, heads, between):
    chips = len(received)
    rows = parts[0].shape[0]
    half = rows // 2

    def merged(ins, plan):
        return pl.pallas_call(
            functools.partial(merge_kernel, plan, heads),
            out_shape=[
                jax.ShapeDtypeStruct((terms[0][2], ins[0].shape[1]), BF16) for terms in plan
            ],
            in_specs=[pl.BlockSpec(memory_space=pltpu.VMEM)] * len(ins),
            out_specs=[pl.BlockSpec(memory_space=pltpu.VMEM)] * len(plan),
            compiler_params=pltpu.CompilerParams(vmem_limit_bytes=SOME),
            name="merge",
        )(*ins)

    terms = [[parts[0]], [received[0]]]
    if chips != 4:
        for j in range(1, chips):
            (both,) = merged([parts[2 * j], received[j]], [[(0, 0, rows), (1, 0, rows)]])
            terms.append([swap(both, 2 * j)])
        return terms, between(received[0])
    top, low = (0, half), (half, half)
    x_far, y_far = merged(
        [parts[6], received[3]], [[(0, *top), (1, *top)], [(0, *low), (1, *low)]]
    )
    x_far, y_far = swap(x_far, 2), swap(y_far, 4)
    ins = [parts[2], received[1], parts[4], received[2]]
    x_top, y_low = merged(ins, [[(0, *top), (1, *top)], [(2, *low), (3, *low)]])
    done = between(x_top, y_low)
    x_top, y_low = swap(x_top, 2), swap(y_low, 4)
    x_low, y_top = merged(
        ins + [after(y_far, done[0]), x_far],
        [[(0, *low), (1, *low), (4, *top)], [(2, *top), (3, *top), (5, *top)]],
    )
    x_low, y_top = swap(x_low, 2), swap(y_top, 4)
    return terms + [[x_top, x_low], [y_top, y_low]], done


def spread_line(x):
    lines = lax.axis_size("head")
    ups, downs = [x], [x]
    for d in range(1, lines):
        ups.append(lax.ppermute(ups[-1], "head", [(i, i + 1) for i in range(d - 1, lines - 1)]))
        downs.append(lax.ppermute(downs[-1], "head", [(i, i - 1) for i in range(1, lines - d + 1)]))
    return ups[1:], downs[1:]


def body(queries, key_rows, value_rows, selected, out_grad, out_weight):
    chunks = lax.axis_size("ctx")
    chips = chunks // 2
    lines = lax.axis_size("head")
    rows, width = queries.shape
    features = out_weight.shape[0]
    heads = width // HD
    block_count = key_rows.shape[0] // BLOCK
    block_total = block_count * chunks
    capacity = 2 * rows * TOPK // block_total
    span = max(1, 16 // capacity)
    cap = capacity * span
    groups = chunks // span
    slots = groups * cap
    index = lax.axis_index("ctx").astype(jnp.int32)
    me = index.reshape(1)
    keys = key_rows.reshape(block_count, BLOCK, width)
    values = value_rows.reshape(block_count, BLOCK, width)
    vmem = pl.BlockSpec(memory_space=pltpu.VMEM)
    smem = pl.BlockSpec(memory_space=pltpu.SMEM)
    anywhere = pl.BlockSpec(memory_space=pl.ANY)
    params = pltpu.CompilerParams(vmem_limit_bytes=MOST)
    small = pltpu.CompilerParams(vmem_limit_bytes=SOME)

    def shaped(shape, kind=BF16):
        return jax.ShapeDtypeStruct(shape, kind)

    ups, downs = spread_line(out_grad)
    packed = pl.pallas_call(
        pack_kernel,
        out_shape=shaped((rows + PAD, width)),
        in_specs=[vmem] * 2,
        out_specs=vmem,
        compiler_params=small,
        name="pack",
    )(selected.T, queries)
    query_chips = spread_chips(packed, rows // 2, ups[0], downs[0])
    query_all = with_cores(query_chips, ups[1], downs[1])

    outs = pl.pallas_call(
        functools.partial(forward_kernel, [len(pieces) for pieces in query_all], span, cap),
        out_shape=[shaped((rows, width + HD))] * chunks
        + [
            shaped((block_count, slots, width)),
            shaped((block_count, heads // 2, 2 * BLOCK, slots)),
            shaped((block_count, heads, slots), F32),
            shaped((groups, block_count * cap, rows * span)),
        ],
        in_specs=[smem, vmem] + [anywhere] * (2 + len(flat(query_all))),
        out_specs=[anywhere] * (chunks + 2) + [vmem, anywhere],
        scratch_shapes=[
            pltpu.VMEM((chunks, rows + PAD, width), BF16),
            pltpu.VMEM((chunks, rows, width + HD), BF16),
            pltpu.VMEM((block_count, BLOCK, width), BF16),
            pltpu.VMEM((block_count, BLOCK, width), BF16),
            pltpu.VMEM((block_count, slots, width), BF16),
            pltpu.VMEM((block_count, heads // 2, 2 * BLOCK, slots), BF16),
            pltpu.VMEM((groups, block_count * cap, rows * span), BF16),
            pltpu.VMEM((block_count, slots, HD), F32),
            pltpu.VMEM((block_count, slots, width), BF16),
            pltpu.SemaphoreType.DMA((len(flat(query_all)),)),
            pltpu.SemaphoreType.DMA((2,)),
            pltpu.SemaphoreType.DMA((chunks + 3,)),
        ],
        compiler_params=params,
        name="forward",
    )(me, keys[:, BLOCK - 1], keys, values, *flat(query_all))
    q_slots, probs, logits, hot = outs[chunks:]

    line = lax.axis_index("head").astype(jnp.int32).reshape(1)
    make_grad = pl.pallas_call(
        functools.partial(grad_kernel, lines),
        out_shape=[shaped((rows, width)), shaped((chunks, rows, features // chunks))],
        in_specs=[smem] + [anywhere] * (2 * lines),
        out_specs=[vmem] * 2,
        scratch_shapes=[
            pltpu.VMEM((lines, rows, width), BF16),
            pltpu.VMEM((lines, width, width), BF16),
            pltpu.SemaphoreType.DMA((lines,)),
            pltpu.SemaphoreType.DMA((lines,)),
        ],
        compiler_params=small,
        name="grad",
    )
    received = from_core(outs[:chunks], *ups[2:], *downs[2:])
    terms, (grad_attn, blocks) = merge_chips(
        outs[:chunks],
        received,
        heads,
        lambda *before: make_grad(after(line, *before), out_weight, out_grad, *ups, *downs),
    )
    attn_out, extended = pl.pallas_call(
        functools.partial(finish_kernel, [len(pieces) for pieces in terms]),
        out_shape=[shaped((rows, width)), shaped((rows, width + HD))],
        in_specs=[vmem] * (len(flat(terms)) + 1),
        out_specs=[vmem] * 2,
        compiler_params=small,
        name="finish",
    )(*flat(terms), grad_attn)
    grad_chips = spread_chips(extended, rows // 2)
    grad_all = with_cores(grad_chips)
    arrived = flat(grad_chips[1:3])
    attns = spread_chips(after(attn_out, *arrived), rows // 2)
    columns = lax.all_to_all(
        after(blocks, *arrived), "ctx", split_axis=0, concat_axis=0, tiled=True
    )

    outs = pl.pallas_call(
        functools.partial(backward_kernel, [len(pieces) for pieces in grad_all], span, cap),
        out_shape=[shaped((rows, width))] * chunks
        + [shaped((block_count, BLOCK, width), F32)] * 2,
        in_specs=[vmem] + [anywhere] * (5 + len(flat(grad_all))),
        out_specs=[anywhere] * (chunks + 2),
        scratch_shapes=[
            pltpu.VMEM((chunks, rows, width + HD), BF16),
            pltpu.VMEM((groups, block_count * cap, rows * span), BF16),
            pltpu.VMEM((block_count, slots, width), BF16),
            pltpu.VMEM((block_count, heads // 2, 2 * BLOCK, slots), BF16),
            pltpu.VMEM((block_count, BLOCK, width), BF16),
            pltpu.VMEM((block_count, BLOCK, width), BF16),
            pltpu.VMEM((block_count, slots, width + HD), BF16),
            pltpu.VMEM((block_count, slots, width), BF16),
            pltpu.VMEM((block_count, BLOCK, width), F32),
            pltpu.VMEM((block_count, BLOCK, width), F32),
            pltpu.SemaphoreType.DMA((len(flat(grad_all)),)),
            pltpu.SemaphoreType.DMA((1,)),
            pltpu.SemaphoreType.DMA((4, block_count)),
            pltpu.SemaphoreType.DMA((2, block_count)),
            pltpu.SemaphoreType.DMA((chunks,)),
        ],
        compiler_params=params,
        name="backward",
    )(logits, hot, q_slots, probs, keys, values, *flat(grad_all))
    key_grad, value_grad = outs[chunks:]
    terms = collect_chips(outs[:chunks], from_core(outs[:chunks], columns, *flat(attns[1:3])))
    query_grad = pl.pallas_call(
        functools.partial(total_kernel, [len(pieces) for pieces in terms]),
        out_shape=shaped((rows, width), F32),
        in_specs=[vmem] * len(flat(terms)),
        out_specs=vmem,
        compiler_params=small,
        name="total",
    )(*flat(terms))

    attns = with_cores(attns)
    weight_grad = pl.pallas_call(
        functools.partial(weight_kernel, [len(pieces) for pieces in attns]),
        out_shape=shaped((features // chunks, width), F32),
        in_specs=[smem] + [vmem] * (1 + len(flat(attns))),
        out_specs=vmem,
        compiler_params=small,
        name="weight",
    )(after(me, *flat(terms)), columns, *flat(attns))
    return (
        query_grad,
        key_grad.reshape(-1, width),
        value_grad.reshape(-1, width),
        weight_grad,
    )


def solution(mesh):
    return jax.shard_map(
        body,
        mesh=mesh,
        in_specs=(
            P("ctx", "head"),
            P("ctx", "head"),
            P("ctx", "head"),
            P("ctx", None),
            P("ctx", "head"),
            P(None, "head"),
        ),
        out_specs=(P("ctx", "head"), P("ctx", "head"), P("ctx", "head"), P("ctx", "head")),
        check_vma=False,
    )
```

```python
import functools

import jax
import jax.numpy as jnp
from jax import lax
from jax.experimental import pallas as pl
from jax.experimental.pallas import tpu as pltpu
from jax.sharding import PartitionSpec as P

HD = 128
BLOCK = 64
TOPK = 4
F32 = jnp.float32
BF16 = jnp.bfloat16
MOST = 58 * 1024 * 1024
SOME = 20 * 1024 * 1024
PAD = 16
TOGETHER = 2
LOW = -(2.0**99)
NN = (((1,), (0,)), ((), ()))
NT = (((1,), (1,)), ((), ()))
TN = (((0,), (0,)), ((), ()))


def mm(a, b, dims=NN):
    return lax.dot_general(a, b, dims, preferred_element_type=F32)


def joined(items, axis):
    return items[0] if len(items) == 1 else jnp.concatenate(items, axis=axis)


def dealt(refs, counts):
    lists, at = [], 0
    for count in counts:
        lists.append(refs[at : at + count])
        at += count
    return lists, refs[at:]


def loads(lists, buf, sems):
    copies, at = [], 0
    for i, refs in enumerate(lists):
        mine, row = [], 0
        for ref in refs:
            rows = ref.shape[0]
            mine.append(
                pltpu.make_async_copy(ref, buf.at[i, pl.ds(row, rows)], sems.at[at])
            )
            row += rows
            at += 1
        copies.append(mine)
    return copies


def start(copies):
    for copy in copies:
        copy.start()


def wait(copies):
    for copy in copies:
        copy.wait()


def whole(refs):
    return joined([ref[...] for ref in refs], 0)


def added(terms, cols):
    total = None
    for refs in terms:
        term = joined([ref[:, cols].astype(F32) for ref in refs], 0)
        total = term if total is None else total + term
    return total


def diagonal(pair):
    zero = jnp.zeros((pair.shape[0], HD), pair.dtype)
    top = jnp.concatenate([pair[:, :HD], zero], axis=1)
    low = jnp.concatenate([zero, pair[:, HD:]], axis=1)
    return jnp.concatenate([top, low], axis=0)


def pack_kernel(sel_ref, q_ref, out_ref):
    rows, width = q_ref.shape
    out_ref[:rows] = q_ref[...]
    digits = [(sel_ref[...] >> 4).astype(F32), (sel_ref[...] & 15).astype(F32)]
    if width > 2 * rows:
        digits.append(jnp.zeros((TOPK, width - 2 * rows), F32))
    lines = [jnp.concatenate(digits, axis=1), jnp.zeros((PAD - TOPK, width), F32)]
    out_ref[rows:] = jnp.concatenate(lines, axis=0).astype(BF16)


def forward_kernel(counts, span, cap, me_ref, mark_ref, k_any, v_any, *refs):
    chunks = len(counts)
    q_refs, refs = dealt(refs, counts)
    part_any, refs = refs[:chunks], refs[chunks:]
    qg_any, p_any, logit_ref, hot_any = refs[:4]
    q_buf, part_refs, k_ref, v_ref, qg_ref, p_ref, hot_ref, topg_ref, out_ref = refs[4:13]
    in_sems, kv_sems, out_sems = refs[13:]
    q_copies = loads(q_refs, q_buf, in_sems)
    kv_copies = [
        pltpu.make_async_copy(k_any, k_ref, kv_sems.at[0]),
        pltpu.make_async_copy(v_any, v_ref, kv_sems.at[1]),
    ]
    out_copies = [
        pltpu.make_async_copy(qg_ref, qg_any, out_sems.at[chunks]),
        pltpu.make_async_copy(hot_ref, hot_any, out_sems.at[chunks + 1]),
        pltpu.make_async_copy(p_ref, p_any, out_sems.at[chunks + 2]),
    ]
    for copies in q_copies:
        start(copies)
    start(kv_copies)
    block_count, _, width = k_ref.shape
    heads = width // HD
    rows = part_any[0].shape[0]
    group_rows = rows * span
    groups = chunks // span
    scale = HD ** (-0.5)
    rate = scale * 1.4426950408889634
    base = me_ref[0] * block_count

    before = lax.broadcasted_iota(jnp.int32, (group_rows, group_rows), 0)
    later = lax.broadcasted_iota(jnp.int32, (group_rows, group_rows), 1)
    earlier = (before < later).astype(BF16)
    own_ids = (base + lax.broadcasted_iota(jnp.int32, (block_count, group_rows), 0)).astype(F32)
    place = lax.broadcasted_iota(jnp.int32, (cap, group_rows), 0).astype(F32)
    zero = jnp.zeros((block_count, HD), BF16)
    wide_marks = jnp.concatenate(
        [
            jnp.concatenate(
                [mark_ref[:, i * HD : (i + 1) * HD] if i == h else zero for i in range(heads)], axis=1
            )
            for h in range(heads)
        ],
        axis=0,
    )
    q_groups, owns = [], []
    for g in range(groups):
        for i in range(span):
            wait(q_copies[g * span + i])
        packs = [q_buf[g * span + i] for i in range(span)]
        digits = [pack[rows : rows + PAD].astype(F32)[:TOPK] for pack in packs]
        picked = joined([16.0 * d[:, :rows] + d[:, rows : 2 * rows] for d in digits], 1)
        own = picked[0:1, :] == own_ids
        for t in range(1, TOPK):
            own = own | (picked[t : t + 1, :] == own_ids)
        owns.append(jnp.where(own, 1.0, 0.0))
        q_groups.append(joined([pack[:rows] for pack in packs], 0))
    own_all = jnp.concatenate(owns, axis=0)
    rank_all = jnp.where(own_all > 0.5, mm(own_all.astype(BF16), earlier), -1.0)
    hots = []
    for g in range(groups):
        rank = rank_all[g * block_count : (g + 1) * block_count]
        hots.append(
            jnp.concatenate(
                [
                    jnp.where(rank[b : b + 1, :] == place, 1.0, 0.0).astype(BF16)
                    for b in range(block_count)
                ],
                axis=0,
            )
        )
        hot_ref[g] = hots[g]
    all_marks = [mm(wide_marks, q_groups[g], NT) for g in range(groups)]
    for g in range(groups):
        qg_ref[:, g * cap : (g + 1) * cap, :] = (
            mm(hots[g], q_groups[g]).astype(BF16).reshape(block_count, cap, width)
        )
    tails = []
    for g in range(groups):
        tops, sums = [], []
        for h in range(heads):
            mark = scale * all_marks[g][h * block_count : (h + 1) * block_count]
            mark = jnp.where(owns[g] > 0.5, mark, LOW)
            top = jnp.max(mark, axis=0, keepdims=True).astype(BF16).astype(F32)
            tops.append(top)
            sums.append(jnp.sum(owns[g] * jnp.exp(mark - top), axis=0, keepdims=True))
        tops, sums = jnp.concatenate(tops, axis=0), jnp.concatenate(sums, axis=0)
        upper = sums.astype(BF16).astype(F32)
        spare = jnp.zeros((HD - 3 * heads, group_rows), F32)
        tails.append(jnp.concatenate([tops, upper, sums - upper, spare], axis=0))
    for g in range(groups):
        topg_ref[:, g * cap : (g + 1) * cap, :] = mm(hots[g], tails[g].astype(BF16), NT).reshape(
            block_count, cap, HD
        )
    for g in range(groups):
        for i in range(span):
            part_refs[g * span + i, :, width:] = (
                tails[g][:, i * rows : (i + 1) * rows].T.astype(BF16)
            )
    start(out_copies[:2])
    wait(kv_copies)

    pairs = [slice(p * 2 * HD, (p + 1) * 2 * HD) for p in range(heads // 2)]

    def some_blocks(step, carry):
        blocks = [step * TOGETHER + u for u in range(TOGETHER)]
        logits = [
            [mm(diagonal(k_ref[b, :, cols]), qg_ref[b, :, cols], NT) for cols in pairs]
            for b in blocks
        ]
        probs, gated, kept = [], [], []
        for b, scores in zip(blocks, logits):
            tops = topg_ref[b].T[:heads]
            marks = scale * jnp.concatenate(
                [scores[h // 2][(h % 2 + 1) * BLOCK - 1 : (h % 2 + 1) * BLOCK] for h in range(heads)],
                axis=0,
            )
            gates = jnp.exp(marks - tops)
            kept.append(marks)
            for p in range(heads // 2):
                low, high = [], []
                for i in range(2):
                    part = scores[p][i * BLOCK : (i + 1) * BLOCK]
                    weight = jnp.exp2(rate * (part - jnp.max(part, axis=0, keepdims=True)))
                    inverse = 1.0 / jnp.sum(weight, axis=0, keepdims=True)
                    gate = gates[2 * p + i : 2 * p + i + 1, :]
                    low.append((weight * inverse).astype(BF16))
                    high.append((weight * (inverse * gate)).astype(BF16))
                probs.append(jnp.concatenate(low, axis=0))
                gated.append(jnp.concatenate(high, axis=0))
        outs = []
        for u, b in enumerate(blocks):
            for p, cols in enumerate(pairs):
                both = gated[u * len(pairs) + p]
                outs.append(mm(both, diagonal(v_ref[b, :, cols]), TN).astype(BF16))
        for u, b in enumerate(blocks):
            logit_ref[b] = kept[u]
            for p, cols in enumerate(pairs):
                p_ref[b, p] = probs[u * len(pairs) + p]
                out_ref[b, :, cols] = outs[u * len(pairs) + p]
        return carry

    lax.fori_loop(0, block_count // TOGETHER, some_blocks, 0)
    start(out_copies[2:])

    for g in range(groups):
        slots = out_ref[:, g * cap : (g + 1) * cap, :].reshape(block_count * cap, width)
        part = mm(hot_ref[g], slots, TN).astype(BF16)
        for i in range(span):
            m = g * span + i
            part_refs[m, :, :width] = part[i * rows : (i + 1) * rows]
            copy = pltpu.make_async_copy(part_refs.at[m], part_any[m], out_sems.at[m])
            copy.start()
            out_copies.append(copy)
    wait(out_copies)


def shift(heads, *moves):
    row = lax.broadcasted_iota(jnp.int32, (HD, HD), 0)
    col = lax.broadcasted_iota(jnp.int32, (HD, HD), 1)
    total = jnp.zeros((HD, HD), F32)
    for source, target in moves:
        inside = (row >= source * heads) & (row < (source + 1) * heads)
        hit = inside & (col - target * heads == row - source * heads)
        total = jnp.where(hit, 1.0, total)
    return total.astype(BF16)


def blend(terms, heads):
    width = heads * HD
    tails = [joined([ref[rows, width:] for ref, rows in term], 0) for term in terms]
    wide = [tail.astype(F32) for tail in tails]
    top = wide[0]
    for tail in wide[1:]:
        top = jnp.maximum(top, tail)
    gather = shift(heads, (1, 0), (2, 0))
    factors = [jnp.exp(tail - top) for tail in wide]
    total = None
    for tail, factor in zip(tails, factors):
        share = factor * mm(tail, gather)
        total = share if total is None else total + share
    columns = []
    for h in range(heads):
        cols = slice(h * HD, (h + 1) * HD)
        column = None
        for term, factor in zip(terms, factors):
            values = joined([ref[rows, cols] for ref, rows in term], 0).astype(F32)
            part = factor[:, h : h + 1] * values
            column = part if column is None else column + part
        columns.append(column)
    return top, total, columns


def digits_of(tile, count):
    digits = []
    for _ in range(count):
        upper = tile.astype(BF16)
        digits.append(upper)
        tile = tile - upper.astype(F32)
    return digits


def packed_tail(digits, heads):
    total = None
    for i, digit in enumerate(digits):
        part = mm(digit, shift(heads, (0, i)))
        total = part if total is None else total + part
    return total.astype(BF16)


def merge_kernel(plan, heads, *refs):
    ins, outs = refs[: len(refs) - len(plan)], refs[len(refs) - len(plan) :]
    for terms, out_ref in zip(plan, outs):
        top, total, columns = blend(
            [[(ins[i], pl.ds(first, count))] for i, first, count in terms], heads
        )
        for h in range(heads):
            out_ref[:, h * HD : (h + 1) * HD] = columns[h].astype(BF16)
        out_ref[:, heads * HD :] = packed_tail([top.astype(BF16)] + digits_of(total, 2), heads)


def grad_kernel(lines, line_ref, w_ref, *refs):
    own_ref, up_refs, down_refs = refs[0], refs[1:lines], refs[lines : 2 * lines - 1]
    ga_ref, blocks_ref, full_ref, w_buf, sems, piece_sems = refs[2 * lines - 1 :]
    width = own_ref.shape[1]
    chunks, _, share = blocks_ref.shape
    line = line_ref[0]
    copies = [
        pltpu.make_async_copy(w_ref.at[pl.ds(i * width, width)], w_buf.at[i], sems.at[i])
        for i in range(lines)
    ]
    start(copies)

    def placed(ref, i):
        return pltpu.make_async_copy(ref, full_ref.at[i], piece_sems.at[i])

    placed(own_ref, line).start()
    for d in range(1, lines):

        @pl.when(line >= d)
        def _():
            placed(up_refs[d - 1], line - d).start()

        @pl.when(line + d < lines)
        def _():
            placed(down_refs[d - 1], line + d).start()

    for i in range(lines):
        placed(own_ref, i).wait()
    for j in range(chunks):
        first = j * share
        blocks_ref[j] = full_ref[first // width, :, first % width : first % width + share]
    total = None
    for i in range(lines):
        copies[i].wait()
        term = mm(full_ref[i], w_buf[i])
        total = term if total is None else total + term
    ga_ref[...] = total.astype(BF16)


def finish_kernel(counts, *refs):
    terms, (ga_ref, attn_ref, ext_ref) = dealt(refs, counts)
    rows, width = ga_ref.shape
    heads = width // HD
    top, total, columns = blend(
        [[(ref, slice(None)) for ref in pieces] for pieces in terms], heads
    )
    lane = lax.broadcasted_iota(jnp.int32, (rows, HD), 1)
    total = jnp.where(lane < heads, total, 1.0)
    inverse = 1.0 / total
    dots = jnp.zeros((rows, HD), F32)
    ext_ref[:, :width] = ga_ref[...]
    for h in range(heads):
        cols = slice(h * HD, (h + 1) * HD)
        attn = columns[h] * inverse[:, h : h + 1]
        attn_ref[:, cols] = attn.astype(BF16)
        dot = jnp.sum(attn * ga_ref[:, cols].astype(F32), axis=1, keepdims=True)
        dots = jnp.where(lane == h, dot, dots)
    level = jnp.where(lane < heads, top + jnp.log(total), 0.0)
    ext_ref[:, width:] = packed_tail(digits_of(dots, 2) + digits_of(level, 3), heads)


def total_kernel(counts, *refs):
    terms, (out_ref,) = dealt(refs, counts)
    for h in range(out_ref.shape[1] // HD):
        cols = slice(h * HD, (h + 1) * HD)
        out_ref[:, cols] = added(terms, cols)


def backward_kernel(counts, span, cap, logit_ref, hot_any, qg_any, p_any, k_any, v_any, *refs):
    chunks = len(counts)
    ga_refs, refs = dealt(refs, counts)
    part_refs, refs = refs[:chunks], refs[chunks:]
    dk_any, dv_any = refs[:2]
    ga_buf, hot_ref, qg_ref, p_ref, k_ref, v_ref, gag_ref, dq_ref, dk_ref, dv_ref = refs[2:12]
    in_sems, hot_sem, block_sems, out_sems, part_sems = refs[12:]
    ga_copies = loads(ga_refs, ga_buf, in_sems)
    hot_copy = pltpu.make_async_copy(hot_any, hot_ref, hot_sem.at[0])
    hot_copy.start()
    for copies in ga_copies:
        start(copies)

    def block_loads(b):
        pairs = ((qg_any, qg_ref), (p_any, p_ref), (k_any, k_ref), (v_any, v_ref))
        return [
            pltpu.make_async_copy(far.at[b], near.at[b], block_sems.at[i, b])
            for i, (far, near) in enumerate(pairs)
        ]

    def block_stores(b):
        return [
            pltpu.make_async_copy(dk_ref.at[b], dk_any.at[b], out_sems.at[0, b]),
            pltpu.make_async_copy(dv_ref.at[b], dv_any.at[b], out_sems.at[1, b]),
        ]

    block_count, _, width = k_ref.shape
    heads = width // HD
    rows = part_refs[0].shape[0]
    groups = chunks // span
    scale = HD ** (-0.5)

    for b in range(block_count):
        start(block_loads(b))
    hot_copy.wait()
    for g in range(groups):
        for i in range(span):
            wait(ga_copies[g * span + i])
        ga_group = joined([ga_buf[g * span + i] for i in range(span)], 0)
        gag_ref[:, g * cap : (g + 1) * cap, :] = (
            mm(hot_ref[g], ga_group).astype(BF16).reshape(block_count, cap, width + HD)
        )
    last = lax.broadcasted_iota(jnp.int32, (BLOCK, groups * cap), 0) == BLOCK - 1

    pairs = [slice(p * 2 * HD, (p + 1) * 2 * HD) for p in range(heads // 2)]

    def some_blocks(step, carry):
        blocks = [step * TOGETHER + u for u in range(TOGETHER)]
        for b in blocks:
            wait(block_loads(b))
        grads = [
            [mm(diagonal(v_ref[b, :, cols]), gag_ref[b, :, cols], NT) for cols in pairs]
            for b in blocks
        ]
        gated, scores = [], []
        for b, grad_pairs in zip(blocks, grads):
            tail = gag_ref[b, :, width:].astype(F32).T
            tail = [tail[i * heads : (i + 1) * heads] for i in range(5)]
            dots = tail[0] + tail[1]
            gates = jnp.exp(jnp.minimum(logit_ref[b] - (tail[2] + tail[3] + tail[4]), 0.0))
            for p in range(heads // 2):
                both = p_ref[b, p].astype(F32)
                low, high = [], []
                for i in range(2):
                    at = slice(i * BLOCK, (i + 1) * BLOCK)
                    h = 2 * p + i
                    gate = gates[h : h + 1, :]
                    grad, probs = grad_pairs[p][at], both[at]
                    delta = jnp.sum(probs * grad, axis=0, keepdims=True)
                    weight = probs * gate
                    extra = jnp.where(last, scale * gate * (delta - dots[h : h + 1, :]), 0.0)
                    low.append((weight * (scale * (grad - delta)) + extra).astype(BF16))
                    high.append(weight.astype(BF16))
                scores.append(jnp.concatenate(low, axis=0))
                gated.append(jnp.concatenate(high, axis=0))
        for u, b in enumerate(blocks):
            for p, cols in enumerate(pairs):
                score, weight = scores[u * len(pairs) + p], gated[u * len(pairs) + p]
                dv = mm(weight, gag_ref[b, :, cols])
                dk = mm(score, qg_ref[b, :, cols])
                dq = mm(score, diagonal(k_ref[b, :, cols]), TN).astype(BF16)
                dv_ref[b, :, cols] = jnp.concatenate([dv[:BLOCK, :HD], dv[BLOCK:, HD:]], axis=1)
                dk_ref[b, :, cols] = jnp.concatenate([dk[:BLOCK, :HD], dk[BLOCK:, HD:]], axis=1)
                dq_ref[b, :, cols] = dq
        for b in blocks:
            start(block_stores(b))
        return carry

    lax.fori_loop(0, block_count // TOGETHER, some_blocks, 0)

    part_copies = []

    for g in range(groups):
        slots = dq_ref[:, g * cap : (g + 1) * cap, :].reshape(block_count * cap, width)
        part = mm(hot_ref[g], slots, TN).astype(BF16)
        for i in range(span):
            m = g * span + i
            ga_buf[m, :, :width] = part[i * rows : (i + 1) * rows]
            copy = pltpu.make_async_copy(
                ga_buf.at[m, :, pl.ds(0, width)], part_refs[m], part_sems.at[m]
            )
            copy.start()
            part_copies.append(copy)
    for b in range(block_count):
        wait(block_stores(b))
    wait(part_copies)


def weight_kernel(counts, me_ref, cols_ref, *refs):
    attns, (out_ref,) = dealt(refs, counts)
    me = me_ref[0]
    columns = joined([cols_ref[me ^ m] for m in range(len(counts))], 0)
    out_ref[...] = mm(columns, joined([whole(pieces) for pieces in attns], 0), TN)


def swap(x, bits):
    count = lax.axis_size("ctx")
    return lax.ppermute(x, "ctx", [(i, i ^ bits) for i in range(count)])


def after(x, *others):
    return lax.optimization_barrier((x, *others))[0]


def flat(lists):
    return [x for pieces in lists for x in pieces]


def spread_near(x):
    chips = lax.axis_size("ctx") // 2
    return [[x]] + [[swap(x, 2 * j)] for j in range(1, chips if chips != 4 else 3)]


def spread_far(near, half, *before):
    if len(near) != 3:
        return near
    (x_way,), (y_way,) = near[1:]
    far = [swap(after(x_way[:half], *before), 4), swap(after(y_way[half:], *before), 2)]
    return near + [far]


def spread_chips(x, half, *before):
    return spread_far(spread_near(x), half, *before)


def with_cores(lists, *before):
    both = []
    for pieces in lists:
        if before and pieces is lists[-1]:
            pieces = [after(piece, *before) for piece in pieces]
        both += [pieces, [swap(piece, 1) for piece in pieces]]
    return both


def from_core(parts, *before):
    received = [None] * (len(parts) // 2)
    for j in reversed(range(len(received))):
        received[j] = swap(after(parts[2 * j + 1], *before), 1)
    return received


def collect_chips(parts, received):
    chips = len(received)

    def both(j, rows, extra=None, earlier=None):
        mine = parts[2 * j] if earlier is None else after(parts[2 * j], earlier)
        total = mine[rows].astype(F32) + received[j][rows].astype(F32)
        if extra is not None:
            total = total + extra.astype(F32)
        return total.astype(BF16)

    terms = [[parts[0]], [received[0]]]
    if chips != 4:
        return terms + [[swap(both(j, slice(None)), 2 * j)] for j in range(1, chips)]
    half = parts[0].shape[0] // 2
    top, low = slice(0, half), slice(half, None)
    x_far, y_far = swap(both(3, top), 2), swap(both(3, low), 4)
    x_sum, y_sum = both(1, top), both(2, low)
    x_top, y_low = swap(x_sum, 2), swap(y_sum, 4)
    x_low, y_top = swap(both(1, low, y_far, x_sum), 2), swap(both(2, top, x_far, y_sum), 4)
    return terms + [[x_top, x_low], [y_top, y_low]]


def merge_chips(parts, received, heads, between):
    chips = len(received)
    rows = parts[0].shape[0]
    half = rows // 2

    def merged(ins, plan):
        return pl.pallas_call(
            functools.partial(merge_kernel, plan, heads),
            out_shape=[
                jax.ShapeDtypeStruct((terms[0][2], ins[0].shape[1]), BF16) for terms in plan
            ],
            in_specs=[pl.BlockSpec(memory_space=pltpu.VMEM)] * len(ins),
            out_specs=[pl.BlockSpec(memory_space=pltpu.VMEM)] * len(plan),
            compiler_params=pltpu.CompilerParams(vmem_limit_bytes=SOME),
            name="merge",
        )(*ins)

    terms = [[parts[0]], [received[0]]]
    if chips != 4:
        for j in range(1, chips):
            (both,) = merged([parts[2 * j], received[j]], [[(0, 0, rows), (1, 0, rows)]])
            terms.append([swap(both, 2 * j)])
        return terms, between(received[0])
    top, low = (0, half), (half, half)
    x_far, y_far = merged(
        [parts[6], received[3]], [[(0, *top), (1, *top)], [(0, *low), (1, *low)]]
    )
    x_far, y_far = swap(x_far, 2), swap(y_far, 4)
    ins = [parts[2], received[1], parts[4], received[2]]
    x_top, y_low = merged(ins, [[(0, *top), (1, *top)], [(2, *low), (3, *low)]])
    done = between(x_top, y_low)
    x_top, y_low = swap(x_top, 2), swap(y_low, 4)
    x_low, y_top = merged(
        ins + [after(y_far, done[0]), x_far],
        [[(0, *low), (1, *low), (4, *top)], [(2, *top), (3, *top), (5, *top)]],
    )
    x_low, y_top = swap(x_low, 2), swap(y_top, 4)
    return terms + [[x_top, x_low], [y_top, y_low]], done


def spread_line(x):
    lines = lax.axis_size("head")
    ups, downs = [x], [x]
    for d in range(1, lines):
        ups.append(lax.ppermute(ups[-1], "head", [(i, i + 1) for i in range(d - 1, lines - 1)]))
        downs.append(lax.ppermute(downs[-1], "head", [(i, i - 1) for i in range(1, lines - d + 1)]))
    return ups[1:], downs[1:]


def body(queries, key_rows, value_rows, selected, out_grad, out_weight):
    chunks = lax.axis_size("ctx")
    chips = chunks // 2
    lines = lax.axis_size("head")
    rows, width = queries.shape
    features = out_weight.shape[0]
    heads = width // HD
    block_count = key_rows.shape[0] // BLOCK
    block_total = block_count * chunks
    capacity = 2 * rows * TOPK // block_total
    span = max(1, 16 // capacity)
    cap = capacity * span
    groups = chunks // span
    slots = groups * cap
    index = lax.axis_index("ctx").astype(jnp.int32)
    me = index.reshape(1)
    keys = key_rows.reshape(block_count, BLOCK, width)
    values = value_rows.reshape(block_count, BLOCK, width)
    vmem = pl.BlockSpec(memory_space=pltpu.VMEM)
    smem = pl.BlockSpec(memory_space=pltpu.SMEM)
    anywhere = pl.BlockSpec(memory_space=pl.ANY)
    params = pltpu.CompilerParams(vmem_limit_bytes=MOST)
    small = pltpu.CompilerParams(vmem_limit_bytes=SOME)

    def shaped(shape, kind=BF16):
        return jax.ShapeDtypeStruct(shape, kind)

    ups, downs = spread_line(out_grad)
    packed = pl.pallas_call(
        pack_kernel,
        out_shape=shaped((rows + PAD, width)),
        in_specs=[vmem] * 2,
        out_specs=vmem,
        compiler_params=small,
        name="pack",
    )(selected.T, queries)
    query_chips = spread_chips(packed, rows // 2, ups[0], downs[0])
    query_all = with_cores(query_chips, ups[1], downs[1])

    outs = pl.pallas_call(
        functools.partial(forward_kernel, [len(pieces) for pieces in query_all], span, cap),
        out_shape=[shaped((rows, width + HD))] * chunks
        + [
            shaped((block_count, slots, width)),
            shaped((block_count, heads // 2, 2 * BLOCK, slots)),
            shaped((block_count, heads, slots), F32),
            shaped((groups, block_count * cap, rows * span)),
        ],
        in_specs=[smem, vmem] + [anywhere] * (2 + len(flat(query_all))),
        out_specs=[anywhere] * (chunks + 2) + [vmem, anywhere],
        scratch_shapes=[
            pltpu.VMEM((chunks, rows + PAD, width), BF16),
            pltpu.VMEM((chunks, rows, width + HD), BF16),
            pltpu.VMEM((block_count, BLOCK, width), BF16),
            pltpu.VMEM((block_count, BLOCK, width), BF16),
            pltpu.VMEM((block_count, slots, width), BF16),
            pltpu.VMEM((block_count, heads // 2, 2 * BLOCK, slots), BF16),
            pltpu.VMEM((groups, block_count * cap, rows * span), BF16),
            pltpu.VMEM((block_count, slots, HD), F32),
            pltpu.VMEM((block_count, slots, width), BF16),
            pltpu.SemaphoreType.DMA((len(flat(query_all)),)),
            pltpu.SemaphoreType.DMA((2,)),
            pltpu.SemaphoreType.DMA((chunks + 3,)),
        ],
        compiler_params=params,
        name="forward",
    )(me, keys[:, BLOCK - 1], keys, values, *flat(query_all))
    q_slots, probs, logits, hot = outs[chunks:]

    line = lax.axis_index("head").astype(jnp.int32).reshape(1)
    make_grad = pl.pallas_call(
        functools.partial(grad_kernel, lines),
        out_shape=[shaped((rows, width)), shaped((chunks, rows, features // chunks))],
        in_specs=[smem] + [anywhere] * (2 * lines),
        out_specs=[vmem] * 2,
        scratch_shapes=[
            pltpu.VMEM((lines, rows, width), BF16),
            pltpu.VMEM((lines, width, width), BF16),
            pltpu.SemaphoreType.DMA((lines,)),
            pltpu.SemaphoreType.DMA((lines,)),
        ],
        compiler_params=params,
        name="grad",
    )
    received = from_core(outs[:chunks], *ups[2:], *downs[2:])
    terms, (grad_attn, blocks) = merge_chips(
        outs[:chunks],
        received,
        heads,
        lambda *before: make_grad(after(line, *before), out_weight, out_grad, *ups, *downs),
    )
    attn_out, extended = pl.pallas_call(
        functools.partial(finish_kernel, [len(pieces) for pieces in terms]),
        out_shape=[shaped((rows, width)), shaped((rows, width + HD))],
        in_specs=[vmem] * (len(flat(terms)) + 1),
        out_specs=[vmem] * 2,
        compiler_params=small,
        name="finish",
    )(*flat(terms), grad_attn)
    grad_chips = spread_chips(extended, rows // 2)
    grad_all = with_cores(grad_chips)
    arrived = flat(grad_chips[1:3])
    attns = spread_near(after(attn_out, *arrived))
    columns = lax.all_to_all(
        after(blocks, *flat(grad_chips)), "ctx", split_axis=0, concat_axis=0, tiled=True
    )

    outs = pl.pallas_call(
        functools.partial(backward_kernel, [len(pieces) for pieces in grad_all], span, cap),
        out_shape=[shaped((rows, width))] * chunks
        + [shaped((block_count, BLOCK, width), F32)] * 2,
        in_specs=[vmem] + [anywhere] * (5 + len(flat(grad_all))),
        out_specs=[anywhere] * (chunks + 2),
        scratch_shapes=[
            pltpu.VMEM((chunks, rows, width + HD), BF16),
            pltpu.VMEM((groups, block_count * cap, rows * span), BF16),
            pltpu.VMEM((block_count, slots, width), BF16),
            pltpu.VMEM((block_count, heads // 2, 2 * BLOCK, slots), BF16),
            pltpu.VMEM((block_count, BLOCK, width), BF16),
            pltpu.VMEM((block_count, BLOCK, width), BF16),
            pltpu.VMEM((block_count, slots, width + HD), BF16),
            pltpu.VMEM((block_count, slots, width), BF16),
            pltpu.VMEM((block_count, BLOCK, width), F32),
            pltpu.VMEM((block_count, BLOCK, width), F32),
            pltpu.SemaphoreType.DMA((len(flat(grad_all)),)),
            pltpu.SemaphoreType.DMA((1,)),
            pltpu.SemaphoreType.DMA((4, block_count)),
            pltpu.SemaphoreType.DMA((2, block_count)),
            pltpu.SemaphoreType.DMA((chunks,)),
        ],
        compiler_params=params,
        name="backward",
    )(logits, hot, q_slots, probs, keys, values, *flat(grad_all))
    key_grad, value_grad = outs[chunks:]
    terms = collect_chips(outs[:chunks], from_core(outs[:chunks], columns, *flat(attns[1:3])))
    query_grad = pl.pallas_call(
        functools.partial(total_kernel, [len(pieces) for pieces in terms]),
        out_shape=shaped((rows, width), F32),
        in_specs=[vmem] * len(flat(terms)),
        out_specs=vmem,
        compiler_params=small,
        name="total",
    )(*flat(terms))

    attns = with_cores(spread_far(attns, rows // 2, terms[2][0], terms[-1][-1]))
    weight_grad = pl.pallas_call(
        functools.partial(weight_kernel, [len(pieces) for pieces in attns]),
        out_shape=shaped((features // chunks, width), F32),
        in_specs=[smem] + [vmem] * (1 + len(flat(attns))),
        out_specs=vmem,
        compiler_params=small,
        name="weight",
    )(after(me, *flat(terms)), columns, *flat(attns))
    return (
        query_grad,
        key_grad.reshape(-1, width),
        value_grad.reshape(-1, width),
        weight_grad,
    )


def solution(mesh):
    return jax.shard_map(
        body,
        mesh=mesh,
        in_specs=(
            P("ctx", "head"),
            P("ctx", "head"),
            P("ctx", "head"),
            P("ctx", None),
            P("ctx", "head"),
            P(None, "head"),
        ),
        out_specs=(P("ctx", "head"), P("ctx", "head"), P("ctx", "head"), P("ctx", "head")),
        check_vma=False,
    )
```

```python
import functools

import jax
import jax.numpy as jnp
from jax import lax
from jax.experimental import pallas as pl
from jax.experimental.pallas import tpu as pltpu
from jax.sharding import PartitionSpec as P

HD = 128
BLOCK = 64
TOPK = 4
F32 = jnp.float32
BF16 = jnp.bfloat16
MOST = 58 * 1024 * 1024
SOME = 20 * 1024 * 1024
PAD = 16
TOGETHER = 4
LOW = -(2.0**99)
NN = (((1,), (0,)), ((), ()))
NT = (((1,), (1,)), ((), ()))
TN = (((0,), (0,)), ((), ()))


def mm(a, b, dims=NN):
    return lax.dot_general(a, b, dims, preferred_element_type=F32)


def joined(items, axis):
    return items[0] if len(items) == 1 else jnp.concatenate(items, axis=axis)


def dealt(refs, counts):
    lists, at = [], 0
    for count in counts:
        lists.append(refs[at : at + count])
        at += count
    return lists, refs[at:]


def loads(lists, buf, sems):
    copies, at = [], 0
    for i, refs in enumerate(lists):
        mine, row = [], 0
        for ref in refs:
            rows = ref.shape[0]
            mine.append(
                pltpu.make_async_copy(ref, buf.at[i, pl.ds(row, rows)], sems.at[at])
            )
            row += rows
            at += 1
        copies.append(mine)
    return copies


def start(copies):
    for copy in copies:
        copy.start()


def wait(copies):
    for copy in copies:
        copy.wait()


def whole(refs):
    return joined([ref[...] for ref in refs], 0)


def added(terms, cols):
    total = None
    for refs in terms:
        term = joined([ref[:, cols].astype(F32) for ref in refs], 0)
        total = term if total is None else total + term
    return total


def diagonal(pair):
    zero = jnp.zeros((pair.shape[0], HD), pair.dtype)
    top = jnp.concatenate([pair[:, :HD], zero], axis=1)
    low = jnp.concatenate([zero, pair[:, HD:]], axis=1)
    return jnp.concatenate([top, low], axis=0)


def pack_kernel(sel_ref, q_ref, out_ref):
    rows, width = q_ref.shape
    out_ref[:rows] = q_ref[...]
    digits = [(sel_ref[...] >> 4).astype(F32), (sel_ref[...] & 15).astype(F32)]
    if width > 2 * rows:
        digits.append(jnp.zeros((TOPK, width - 2 * rows), F32))
    lines = [jnp.concatenate(digits, axis=1), jnp.zeros((PAD - TOPK, width), F32)]
    out_ref[rows:] = jnp.concatenate(lines, axis=0).astype(BF16)


def forward_kernel(counts, span, cap, me_ref, mark_ref, k_any, v_any, *refs):
    chunks = len(counts)
    q_refs, refs = dealt(refs, counts)
    part_any, refs = refs[:chunks], refs[chunks:]
    qg_any, p_any, logit_ref, hot_any = refs[:4]
    q_buf, part_refs, k_ref, v_ref, qg_ref, p_ref, hot_ref, topg_ref, out_ref = refs[4:13]
    in_sems, kv_sems, out_sems = refs[13:]
    q_copies = loads(q_refs, q_buf, in_sems)
    kv_copies = [
        pltpu.make_async_copy(k_any, k_ref, kv_sems.at[0]),
        pltpu.make_async_copy(v_any, v_ref, kv_sems.at[1]),
    ]
    out_copies = [
        pltpu.make_async_copy(qg_ref, qg_any, out_sems.at[chunks]),
        pltpu.make_async_copy(hot_ref, hot_any, out_sems.at[chunks + 1]),
        pltpu.make_async_copy(p_ref, p_any, out_sems.at[chunks + 2]),
    ]
    for copies in q_copies:
        start(copies)
    start(kv_copies)
    block_count, _, width = k_ref.shape
    heads = width // HD
    rows = part_any[0].shape[0]
    group_rows = rows * span
    groups = chunks // span
    scale = HD ** (-0.5)
    rate = scale * 1.4426950408889634
    base = me_ref[0] * block_count

    before = lax.broadcasted_iota(jnp.int32, (group_rows, group_rows), 0)
    later = lax.broadcasted_iota(jnp.int32, (group_rows, group_rows), 1)
    earlier = (before < later).astype(BF16)
    own_ids = (base + lax.broadcasted_iota(jnp.int32, (block_count, group_rows), 0)).astype(F32)
    place = lax.broadcasted_iota(jnp.int32, (cap, group_rows), 0).astype(F32)
    zero = jnp.zeros((block_count, HD), BF16)
    wide_marks = jnp.concatenate(
        [
            jnp.concatenate(
                [mark_ref[:, i * HD : (i + 1) * HD] if i == h else zero for i in range(heads)], axis=1
            )
            for h in range(heads)
        ],
        axis=0,
    )
    q_groups, owns = [], []
    for g in range(groups):
        for i in range(span):
            wait(q_copies[g * span + i])
        packs = [q_buf[g * span + i] for i in range(span)]
        digits = [pack[rows : rows + PAD].astype(F32)[:TOPK] for pack in packs]
        picked = joined([16.0 * d[:, :rows] + d[:, rows : 2 * rows] for d in digits], 1)
        own = picked[0:1, :] == own_ids
        for t in range(1, TOPK):
            own = own | (picked[t : t + 1, :] == own_ids)
        owns.append(jnp.where(own, 1.0, 0.0))
        q_groups.append(joined([pack[:rows] for pack in packs], 0))
    own_all = jnp.concatenate(owns, axis=0)
    rank_all = jnp.where(own_all > 0.5, mm(own_all.astype(BF16), earlier), -1.0)
    hots = []
    for g in range(groups):
        rank = rank_all[g * block_count : (g + 1) * block_count]
        hots.append(
            jnp.concatenate(
                [
                    jnp.where(rank[b : b + 1, :] == place, 1.0, 0.0).astype(BF16)
                    for b in range(block_count)
                ],
                axis=0,
            )
        )
        hot_ref[g] = hots[g]
    all_marks = [mm(wide_marks, q_groups[g], NT) for g in range(groups)]
    for g in range(groups):
        qg_ref[:, g * cap : (g + 1) * cap, :] = (
            mm(hots[g], q_groups[g]).astype(BF16).reshape(block_count, cap, width)
        )
    tails = []
    for g in range(groups):
        tops, sums = [], []
        for h in range(heads):
            mark = scale * all_marks[g][h * block_count : (h + 1) * block_count]
            mark = jnp.where(owns[g] > 0.5, mark, LOW)
            top = jnp.max(mark, axis=0, keepdims=True).astype(BF16).astype(F32)
            tops.append(top)
            sums.append(jnp.sum(owns[g] * jnp.exp(mark - top), axis=0, keepdims=True))
        tops, sums = jnp.concatenate(tops, axis=0), jnp.concatenate(sums, axis=0)
        upper = sums.astype(BF16).astype(F32)
        spare = jnp.zeros((HD - 3 * heads, group_rows), F32)
        tails.append(jnp.concatenate([tops, upper, sums - upper, spare], axis=0))
    for g in range(groups):
        topg_ref[:, g * cap : (g + 1) * cap, :] = mm(hots[g], tails[g].astype(BF16), NT).reshape(
            block_count, cap, HD
        )
    for g in range(groups):
        for i in range(span):
            part_refs[g * span + i, :, width:] = (
                tails[g][:, i * rows : (i + 1) * rows].T.astype(BF16)
            )
    start(out_copies[:2])
    wait(kv_copies)

    pairs = [slice(p * 2 * HD, (p + 1) * 2 * HD) for p in range(heads // 2)]

    def some_blocks(step, carry):
        blocks = [step * TOGETHER + u for u in range(TOGETHER)]
        logits = [
            [mm(diagonal(k_ref[b, :, cols]), qg_ref[b, :, cols], NT) for cols in pairs]
            for b in blocks
        ]
        probs, gated, kept = [], [], []
        for b, scores in zip(blocks, logits):
            tops = topg_ref[b].T[:heads]
            marks = scale * jnp.concatenate(
                [scores[h // 2][(h % 2 + 1) * BLOCK - 1 : (h % 2 + 1) * BLOCK] for h in range(heads)],
                axis=0,
            )
            gates = jnp.exp(marks - tops)
            kept.append(marks)
            for p in range(heads // 2):
                low, high = [], []
                for i in range(2):
                    part = scores[p][i * BLOCK : (i + 1) * BLOCK]
                    weight = jnp.exp2(rate * (part - jnp.max(part, axis=0, keepdims=True)))
                    inverse = 1.0 / jnp.sum(weight, axis=0, keepdims=True)
                    gate = gates[2 * p + i : 2 * p + i + 1, :]
                    low.append((weight * inverse).astype(BF16))
                    high.append((weight * (inverse * gate)).astype(BF16))
                probs.append(jnp.concatenate(low, axis=0))
                gated.append(jnp.concatenate(high, axis=0))
        outs = []
        for u, b in enumerate(blocks):
            for p, cols in enumerate(pairs):
                both = gated[u * len(pairs) + p]
                outs.append(mm(both, diagonal(v_ref[b, :, cols]), TN).astype(BF16))
        for u, b in enumerate(blocks):
            logit_ref[b] = kept[u]
            for p, cols in enumerate(pairs):
                p_ref[b, p] = probs[u * len(pairs) + p]
                out_ref[b, :, cols] = outs[u * len(pairs) + p]
        return carry

    lax.fori_loop(0, block_count // TOGETHER, some_blocks, 0)
    start(out_copies[2:])

    for g in range(groups):
        slots = out_ref[:, g * cap : (g + 1) * cap, :].reshape(block_count * cap, width)
        part = mm(hot_ref[g], slots, TN).astype(BF16)
        for i in range(span):
            m = g * span + i
            part_refs[m, :, :width] = part[i * rows : (i + 1) * rows]
            copy = pltpu.make_async_copy(part_refs.at[m], part_any[m], out_sems.at[m])
            copy.start()
            out_copies.append(copy)
    wait(out_copies)


def shift(heads, *moves):
    row = lax.broadcasted_iota(jnp.int32, (HD, HD), 0)
    col = lax.broadcasted_iota(jnp.int32, (HD, HD), 1)
    total = jnp.zeros((HD, HD), F32)
    for source, target in moves:
        inside = (row >= source * heads) & (row < (source + 1) * heads)
        hit = inside & (col - target * heads == row - source * heads)
        total = jnp.where(hit, 1.0, total)
    return total.astype(BF16)


def blend(terms, heads):
    width = heads * HD
    tails = [joined([ref[rows, width:] for ref, rows in term], 0) for term in terms]
    wide = [tail.astype(F32) for tail in tails]
    top = wide[0]
    for tail in wide[1:]:
        top = jnp.maximum(top, tail)
    gather = shift(heads, (1, 0), (2, 0))
    factors = [jnp.exp(tail - top) for tail in wide]
    total = None
    for tail, factor in zip(tails, factors):
        share = factor * mm(tail, gather)
        total = share if total is None else total + share
    columns = []
    for h in range(heads):
        cols = slice(h * HD, (h + 1) * HD)
        column = None
        for term, factor in zip(terms, factors):
            values = joined([ref[rows, cols] for ref, rows in term], 0).astype(F32)
            part = factor[:, h : h + 1] * values
            column = part if column is None else column + part
        columns.append(column)
    return top, total, columns


def digits_of(tile, count):
    digits = []
    for _ in range(count):
        upper = tile.astype(BF16)
        digits.append(upper)
        tile = tile - upper.astype(F32)
    return digits


def packed_tail(digits, heads):
    total = None
    for i, digit in enumerate(digits):
        part = mm(digit, shift(heads, (0, i)))
        total = part if total is None else total + part
    return total.astype(BF16)


def merge_kernel(plan, heads, *refs):
    ins, outs = refs[: len(refs) - len(plan)], refs[len(refs) - len(plan) :]
    for terms, out_ref in zip(plan, outs):
        top, total, columns = blend(
            [[(ins[i], pl.ds(first, count))] for i, first, count in terms], heads
        )
        for h in range(heads):
            out_ref[:, h * HD : (h + 1) * HD] = columns[h].astype(BF16)
        out_ref[:, heads * HD :] = packed_tail([top.astype(BF16)] + digits_of(total, 2), heads)


def grad_kernel(lines, line_ref, w_ref, *refs):
    own_ref, up_refs, down_refs = refs[0], refs[1:lines], refs[lines : 2 * lines - 1]
    ga_ref, blocks_ref, full_ref, w_buf, sems, piece_sems = refs[2 * lines - 1 :]
    width = own_ref.shape[1]
    chunks, _, share = blocks_ref.shape
    line = line_ref[0]
    copies = [
        pltpu.make_async_copy(w_ref.at[pl.ds(i * width, width)], w_buf.at[i], sems.at[i])
        for i in range(lines)
    ]
    start(copies)

    def placed(ref, i):
        return pltpu.make_async_copy(ref, full_ref.at[i], piece_sems.at[i])

    placed(own_ref, line).start()
    for d in range(1, lines):

        @pl.when(line >= d)
        def _():
            placed(up_refs[d - 1], line - d).start()

        @pl.when(line + d < lines)
        def _():
            placed(down_refs[d - 1], line + d).start()

    for i in range(lines):
        placed(own_ref, i).wait()
    for j in range(chunks):
        first = j * share
        blocks_ref[j] = full_ref[first // width, :, first % width : first % width + share]
    total = None
    for i in range(lines):
        copies[i].wait()
        term = mm(full_ref[i], w_buf[i])
        total = term if total is None else total + term
    ga_ref[...] = total.astype(BF16)


def finish_kernel(counts, *refs):
    terms, (ga_ref, attn_ref, *ext_refs) = dealt(refs, counts)
    rows, width = ga_ref.shape
    half = rows // len(ext_refs)
    heads = width // HD
    top, total, columns = blend(
        [[(ref, slice(None)) for ref in pieces] for pieces in terms], heads
    )
    lane = lax.broadcasted_iota(jnp.int32, (rows, HD), 1)
    total = jnp.where(lane < heads, total, 1.0)
    inverse = 1.0 / total
    dots = jnp.zeros((rows, HD), F32)
    for i, ext_ref in enumerate(ext_refs):
        ext_ref[:, :width] = ga_ref[i * half : (i + 1) * half]
    for h in range(heads):
        cols = slice(h * HD, (h + 1) * HD)
        attn = columns[h] * inverse[:, h : h + 1]
        attn_ref[:, cols] = attn.astype(BF16)
        dot = jnp.sum(attn * ga_ref[:, cols].astype(F32), axis=1, keepdims=True)
        dots = jnp.where(lane == h, dot, dots)
    level = jnp.where(lane < heads, top + jnp.log(total), 0.0)
    tail = packed_tail(digits_of(dots, 2) + digits_of(level, 3), heads)
    for i, ext_ref in enumerate(ext_refs):
        ext_ref[:, width:] = tail[i * half : (i + 1) * half]


def total_kernel(counts, *refs):
    terms, (out_ref,) = dealt(refs, counts)
    for h in range(out_ref.shape[1] // HD):
        cols = slice(h * HD, (h + 1) * HD)
        out_ref[:, cols] = added(terms, cols)


def backward_kernel(counts, span, cap, logit_ref, hot_any, qg_any, p_any, k_any, v_any, *refs):
    chunks = len(counts)
    ga_refs, refs = dealt(refs, counts)
    part_refs, refs = refs[:chunks], refs[chunks:]
    dk_any, dv_any = refs[:2]
    ga_buf, hot_ref, qg_ref, p_ref, k_ref, v_ref, gag_ref, dq_ref, dk_ref, dv_ref = refs[2:12]
    in_sems, hot_sem, block_sems, out_sems, part_sems = refs[12:]
    ga_copies = loads(ga_refs, ga_buf, in_sems)
    hot_copy = pltpu.make_async_copy(hot_any, hot_ref, hot_sem.at[0])
    hot_copy.start()
    for copies in ga_copies:
        start(copies)

    def block_loads(b):
        pairs = ((qg_any, qg_ref), (p_any, p_ref), (k_any, k_ref), (v_any, v_ref))
        return [
            pltpu.make_async_copy(far.at[b], near.at[b], block_sems.at[i, b])
            for i, (far, near) in enumerate(pairs)
        ]

    def block_stores(b):
        return [
            pltpu.make_async_copy(dk_ref.at[b], dk_any.at[b], out_sems.at[0, b]),
            pltpu.make_async_copy(dv_ref.at[b], dv_any.at[b], out_sems.at[1, b]),
        ]

    block_count, _, width = k_ref.shape
    heads = width // HD
    rows = part_refs[0].shape[0]
    groups = chunks // span
    scale = HD ** (-0.5)

    for b in range(block_count):
        start(block_loads(b))
    hot_copy.wait()
    for g in range(groups):
        for i in range(span):
            wait(ga_copies[g * span + i])
        ga_group = joined([ga_buf[g * span + i] for i in range(span)], 0)
        gag_ref[:, g * cap : (g + 1) * cap, :] = (
            mm(hot_ref[g], ga_group).astype(BF16).reshape(block_count, cap, width + HD)
        )
    last = lax.broadcasted_iota(jnp.int32, (BLOCK, groups * cap), 0) == BLOCK - 1

    pairs = [slice(p * 2 * HD, (p + 1) * 2 * HD) for p in range(heads // 2)]

    def some_blocks(step, carry):
        blocks = [step * TOGETHER + u for u in range(TOGETHER)]
        for b in blocks:
            wait(block_loads(b))
        grads = [
            [mm(diagonal(v_ref[b, :, cols]), gag_ref[b, :, cols], NT) for cols in pairs]
            for b in blocks
        ]
        gated, scores = [], []
        for b, grad_pairs in zip(blocks, grads):
            tail = gag_ref[b, :, width:].astype(F32).T
            tail = [tail[i * heads : (i + 1) * heads] for i in range(5)]
            dots = tail[0] + tail[1]
            gates = jnp.exp(jnp.minimum(logit_ref[b] - (tail[2] + tail[3] + tail[4]), 0.0))
            for p in range(heads // 2):
                both = p_ref[b, p].astype(F32)
                low, high = [], []
                for i in range(2):
                    at = slice(i * BLOCK, (i + 1) * BLOCK)
                    h = 2 * p + i
                    gate = gates[h : h + 1, :]
                    grad, probs = grad_pairs[p][at], both[at]
                    delta = jnp.sum(probs * grad, axis=0, keepdims=True)
                    weight = probs * gate
                    extra = jnp.where(last, scale * gate * (delta - dots[h : h + 1, :]), 0.0)
                    low.append((weight * (scale * (grad - delta)) + extra).astype(BF16))
                    high.append(weight.astype(BF16))
                scores.append(jnp.concatenate(low, axis=0))
                gated.append(jnp.concatenate(high, axis=0))
        for u, b in enumerate(blocks):
            for p, cols in enumerate(pairs):
                score, weight = scores[u * len(pairs) + p], gated[u * len(pairs) + p]
                dv = mm(weight, gag_ref[b, :, cols])
                dk = mm(score, qg_ref[b, :, cols])
                dq = mm(score, diagonal(k_ref[b, :, cols]), TN).astype(BF16)
                dv_ref[b, :, cols] = jnp.concatenate([dv[:BLOCK, :HD], dv[BLOCK:, HD:]], axis=1)
                dk_ref[b, :, cols] = jnp.concatenate([dk[:BLOCK, :HD], dk[BLOCK:, HD:]], axis=1)
                dq_ref[b, :, cols] = dq
        for b in blocks:
            start(block_stores(b))
        return carry

    lax.fori_loop(0, block_count // TOGETHER, some_blocks, 0)

    part_copies = []

    for g in range(groups):
        slots = dq_ref[:, g * cap : (g + 1) * cap, :].reshape(block_count * cap, width)
        part = mm(hot_ref[g], slots, TN).astype(BF16)
        for i in range(span):
            m = g * span + i
            ga_buf[m, :, :width] = part[i * rows : (i + 1) * rows]
            copy = pltpu.make_async_copy(
                ga_buf.at[m, :, pl.ds(0, width)], part_refs[m], part_sems.at[m]
            )
            copy.start()
            part_copies.append(copy)
    for b in range(block_count):
        wait(block_stores(b))
    wait(part_copies)


def weight_kernel(counts, me_ref, cols_ref, *refs):
    attns, (out_ref,) = dealt(refs, counts)
    me = me_ref[0]
    columns = joined([cols_ref[me ^ m] for m in range(len(counts))], 0)
    out_ref[...] = mm(columns, joined([whole(pieces) for pieces in attns], 0), TN)


def swap(x, bits):
    count = lax.axis_size("ctx")
    return lax.ppermute(x, "ctx", [(i, i ^ bits) for i in range(count)])


def after(x, *others):
    return lax.optimization_barrier((x, *others))[0]


def flat(lists):
    return [x for pieces in lists for x in pieces]


def spread_near(x):
    chips = lax.axis_size("ctx") // 2
    return [[x]] + [[swap(x, 2 * j)] for j in range(1, chips if chips != 4 else 3)]


def spread_far(near, half, *before):
    if len(near) != 3:
        return near
    (x_way,), (y_way,) = near[1:]
    far = [swap(after(x_way[:half], *before), 4), swap(after(y_way[half:], *before), 2)]
    return near + [far]


def spread_chips(x, half, *before):
    return spread_far(spread_near(x), half, *before)


def spread_halves(top, low):
    chips = lax.axis_size("ctx") // 2
    if chips != 4:
        return [[swap(x, 2 * j) if j else x for x in (top, low)] for j in range(chips)]
    x_top, y_low = swap(top, 2), swap(low, 4)
    x_low, y_top = swap(low, 2), swap(top, 4)
    return [[top, low], [x_top, x_low], [y_top, y_low], [swap(x_top, 4), swap(y_low, 2)]]


def with_cores(lists, *before):
    both = []
    for pieces in lists:
        if before and pieces is lists[-1]:
            pieces = [after(piece, *before) for piece in pieces]
        both += [pieces, [swap(piece, 1) for piece in pieces]]
    return both


def from_core(parts, *before):
    received = [None] * (len(parts) // 2)
    for j in reversed(range(len(received))):
        received[j] = swap(after(parts[2 * j + 1], *before), 1)
    return received


def collect_chips(parts, received):
    chips = len(received)

    def both(j, rows, extra=None, earlier=None):
        mine = parts[2 * j] if earlier is None else after(parts[2 * j], earlier)
        total = mine[rows].astype(F32) + received[j][rows].astype(F32)
        if extra is not None:
            total = total + extra.astype(F32)
        return total.astype(BF16)

    terms = [[parts[0]], [received[0]]]
    if chips != 4:
        return terms + [[swap(both(j, slice(None)), 2 * j)] for j in range(1, chips)]
    half = parts[0].shape[0] // 2
    top, low = slice(0, half), slice(half, None)
    x_far, y_far = swap(both(3, top), 2), swap(both(3, low), 4)
    x_sum, y_sum = both(1, top), both(2, low)
    x_top, y_low = swap(x_sum, 2), swap(y_sum, 4)
    x_low, y_top = swap(both(1, low, y_far, x_sum), 2), swap(both(2, top, x_far, y_sum), 4)
    return terms + [[x_top, x_low], [y_top, y_low]]


def merge_chips(parts, received, heads, between):
    chips = len(received)
    rows = parts[0].shape[0]
    half = rows // 2

    def merged(ins, plan):
        return pl.pallas_call(
            functools.partial(merge_kernel, plan, heads),
            out_shape=[
                jax.ShapeDtypeStruct((terms[0][2], ins[0].shape[1]), BF16) for terms in plan
            ],
            in_specs=[pl.BlockSpec(memory_space=pltpu.VMEM)] * len(ins),
            out_specs=[pl.BlockSpec(memory_space=pltpu.VMEM)] * len(plan),
            compiler_params=pltpu.CompilerParams(vmem_limit_bytes=SOME),
            name="merge",
        )(*ins)

    terms = [[parts[0]], [received[0]]]
    if chips != 4:
        for j in range(1, chips):
            (both,) = merged([parts[2 * j], received[j]], [[(0, 0, rows), (1, 0, rows)]])
            terms.append([swap(both, 2 * j)])
        return terms, between(received[0])
    top, low = (0, half), (half, half)
    x_far, y_far = merged(
        [parts[6], received[3]], [[(0, *top), (1, *top)], [(0, *low), (1, *low)]]
    )
    x_far, y_far = swap(x_far, 2), swap(y_far, 4)
    ins = [parts[2], received[1], parts[4], received[2]]
    x_top, y_low = merged(ins, [[(0, *top), (1, *top)], [(2, *low), (3, *low)]])
    x_top, y_low = swap(x_top, 2), swap(y_low, 4)
    x_low, y_top = merged(
        ins + [y_far, x_far],
        [[(0, *low), (1, *low), (4, *top)], [(2, *top), (3, *top), (5, *top)]],
    )
    done = between(x_low, y_top)
    x_low, y_top = swap(x_low, 2), swap(y_top, 4)
    return terms + [[x_top, x_low], [y_top, y_low]], done


def spread_line(x):
    lines = lax.axis_size("head")
    ups, downs = [x], [x]
    for d in range(1, lines):
        ups.append(lax.ppermute(ups[-1], "head", [(i, i + 1) for i in range(d - 1, lines - 1)]))
        downs.append(lax.ppermute(downs[-1], "head", [(i, i - 1) for i in range(1, lines - d + 1)]))
    return ups[1:], downs[1:]


def body(queries, key_rows, value_rows, selected, out_grad, out_weight):
    chunks = lax.axis_size("ctx")
    chips = chunks // 2
    lines = lax.axis_size("head")
    rows, width = queries.shape
    features = out_weight.shape[0]
    heads = width // HD
    block_count = key_rows.shape[0] // BLOCK
    block_total = block_count * chunks
    capacity = 2 * rows * TOPK // block_total
    span = max(1, 16 // capacity)
    cap = capacity * span
    groups = chunks // span
    slots = groups * cap
    index = lax.axis_index("ctx").astype(jnp.int32)
    me = index.reshape(1)
    keys = key_rows.reshape(block_count, BLOCK, width)
    values = value_rows.reshape(block_count, BLOCK, width)
    vmem = pl.BlockSpec(memory_space=pltpu.VMEM)
    smem = pl.BlockSpec(memory_space=pltpu.SMEM)
    anywhere = pl.BlockSpec(memory_space=pl.ANY)
    params = pltpu.CompilerParams(vmem_limit_bytes=MOST)
    small = pltpu.CompilerParams(vmem_limit_bytes=SOME)

    def shaped(shape, kind=BF16):
        return jax.ShapeDtypeStruct(shape, kind)

    ups, downs = spread_line(out_grad)
    packed = pl.pallas_call(
        pack_kernel,
        out_shape=shaped((rows + PAD, width)),
        in_specs=[vmem] * 2,
        out_specs=vmem,
        compiler_params=small,
        name="pack",
    )(selected.T, queries)
    query_chips = spread_chips(packed, rows // 2)
    query_all = with_cores(query_chips, ups[0], downs[0])

    outs = pl.pallas_call(
        functools.partial(forward_kernel, [len(pieces) for pieces in query_all], span, cap),
        out_shape=[shaped((rows, width + HD))] * chunks
        + [
            shaped((block_count, slots, width)),
            shaped((block_count, heads // 2, 2 * BLOCK, slots)),
            shaped((block_count, heads, slots), F32),
            shaped((groups, block_count * cap, rows * span)),
        ],
        in_specs=[smem, vmem] + [anywhere] * (2 + len(flat(query_all))),
        out_specs=[anywhere] * (chunks + 2) + [vmem, anywhere],
        scratch_shapes=[
            pltpu.VMEM((chunks, rows + PAD, width), BF16),
            pltpu.VMEM((chunks, rows, width + HD), BF16),
            pltpu.VMEM((block_count, BLOCK, width), BF16),
            pltpu.VMEM((block_count, BLOCK, width), BF16),
            pltpu.VMEM((block_count, slots, width), BF16),
            pltpu.VMEM((block_count, heads // 2, 2 * BLOCK, slots), BF16),
            pltpu.VMEM((groups, block_count * cap, rows * span), BF16),
            pltpu.VMEM((block_count, slots, HD), F32),
            pltpu.VMEM((block_count, slots, width), BF16),
            pltpu.SemaphoreType.DMA((len(flat(query_all)),)),
            pltpu.SemaphoreType.DMA((2,)),
            pltpu.SemaphoreType.DMA((chunks + 3,)),
        ],
        compiler_params=params,
        name="forward",
    )(me, keys[:, BLOCK - 1], keys, values, *flat(query_all))
    q_slots, probs, logits, hot = outs[chunks:]

    line = lax.axis_index("head").astype(jnp.int32).reshape(1)
    make_grad = pl.pallas_call(
        functools.partial(grad_kernel, lines),
        out_shape=[shaped((rows, width)), shaped((chunks, rows, features // chunks))],
        in_specs=[smem] + [anywhere] * (2 * lines),
        out_specs=[vmem] * 2,
        scratch_shapes=[
            pltpu.VMEM((lines, rows, width), BF16),
            pltpu.VMEM((lines, width, width), BF16),
            pltpu.SemaphoreType.DMA((lines,)),
            pltpu.SemaphoreType.DMA((lines,)),
        ],
        compiler_params=params,
        name="grad",
    )
    received = from_core(outs[:chunks], ups[1], downs[1])
    terms, (grad_attn, blocks) = merge_chips(
        outs[:chunks],
        received,
        heads,
        lambda *before: make_grad(after(line, *before), out_weight, out_grad, *ups, *downs),
    )
    attn_out, *extended = pl.pallas_call(
        functools.partial(finish_kernel, [len(pieces) for pieces in terms]),
        out_shape=[shaped((rows, width))] + [shaped((rows // 2, width + HD))] * 2,
        in_specs=[vmem] * (len(flat(terms)) + 1),
        out_specs=[vmem] * 3,
        compiler_params=small,
        name="finish",
    )(*flat(terms), grad_attn)
    grad_chips = spread_halves(*extended)
    grad_all = with_cores(grad_chips)
    arrived = [grad_chips[1][-1], grad_chips[2][0]]
    attns = spread_near(after(attn_out, *arrived))
    columns = lax.all_to_all(
        after(blocks, *arrived), "ctx", split_axis=0, concat_axis=0, tiled=True
    )

    outs = pl.pallas_call(
        functools.partial(backward_kernel, [len(pieces) for pieces in grad_all], span, cap),
        out_shape=[shaped((rows, width))] * chunks
        + [shaped((block_count, BLOCK, width), F32)] * 2,
        in_specs=[vmem] + [anywhere] * (5 + len(flat(grad_all))),
        out_specs=[anywhere] * (chunks + 2),
        scratch_shapes=[
            pltpu.VMEM((chunks, rows, width + HD), BF16),
            pltpu.VMEM((groups, block_count * cap, rows * span), BF16),
            pltpu.VMEM((block_count, slots, width), BF16),
            pltpu.VMEM((block_count, heads // 2, 2 * BLOCK, slots), BF16),
            pltpu.VMEM((block_count, BLOCK, width), BF16),
            pltpu.VMEM((block_count, BLOCK, width), BF16),
            pltpu.VMEM((block_count, slots, width + HD), BF16),
            pltpu.VMEM((block_count, slots, width), BF16),
            pltpu.VMEM((block_count, BLOCK, width), F32),
            pltpu.VMEM((block_count, BLOCK, width), F32),
            pltpu.SemaphoreType.DMA((len(flat(grad_all)),)),
            pltpu.SemaphoreType.DMA((1,)),
            pltpu.SemaphoreType.DMA((4, block_count)),
            pltpu.SemaphoreType.DMA((2, block_count)),
            pltpu.SemaphoreType.DMA((chunks,)),
        ],
        compiler_params=params,
        name="backward",
    )(logits, hot, q_slots, probs, keys, values, *flat(grad_all))
    key_grad, value_grad = outs[chunks:]
    received = from_core(outs[:chunks], columns, *flat(attns[1:3]))
    terms = collect_chips(outs[:chunks], received)
    query_grad = pl.pallas_call(
        functools.partial(total_kernel, [len(pieces) for pieces in terms]),
        out_shape=shaped((rows, width), F32),
        in_specs=[vmem] * len(flat(terms)),
        out_specs=vmem,
        compiler_params=small,
        name="total",
    )(*flat(terms))

    attns = with_cores(spread_far(attns, rows // 2, terms[2][0], terms[-1][-1]))
    weight_grad = pl.pallas_call(
        functools.partial(weight_kernel, [len(pieces) for pieces in attns]),
        out_shape=shaped((features // chunks, width), F32),
        in_specs=[smem] + [vmem] * (1 + len(flat(attns))),
        out_specs=vmem,
        compiler_params=small,
        name="weight",
    )(after(me, *flat(terms)), columns, *flat(attns))
    return (
        query_grad,
        key_grad.reshape(-1, width),
        value_grad.reshape(-1, width),
        weight_grad,
    )


def solution(mesh):
    return jax.shard_map(
        body,
        mesh=mesh,
        in_specs=(
            P("ctx", "head"),
            P("ctx", "head"),
            P("ctx", "head"),
            P("ctx", None),
            P("ctx", "head"),
            P(None, "head"),
        ),
        out_specs=(P("ctx", "head"), P("ctx", "head"), P("ctx", "head"), P("ctx", "head")),
        check_vma=False,
    )
```

```python
import functools

import jax
import jax.numpy as jnp
from jax import lax
from jax.experimental import pallas as pl
from jax.experimental.pallas import tpu as pltpu
from jax.sharding import PartitionSpec as P

HD = 128
BLOCK = 64
TOPK = 4
F32 = jnp.float32
BF16 = jnp.bfloat16
MOST = 58 * 1024 * 1024
SOME = 20 * 1024 * 1024
PAD = 16
TOGETHER = 4
LOW = -(2.0**99)
NN = (((1,), (0,)), ((), ()))
NT = (((1,), (1,)), ((), ()))
TN = (((0,), (0,)), ((), ()))


def mm(a, b, dims=NN):
    return lax.dot_general(a, b, dims, preferred_element_type=F32)


def joined(items, axis):
    return items[0] if len(items) == 1 else jnp.concatenate(items, axis=axis)


def dealt(refs, counts):
    lists, at = [], 0
    for count in counts:
        lists.append(refs[at : at + count])
        at += count
    return lists, refs[at:]


def loads(lists, buf, sems):
    copies, at = [], 0
    for i, refs in enumerate(lists):
        mine, row = [], 0
        for ref in refs:
            rows = ref.shape[0]
            mine.append(
                pltpu.make_async_copy(ref, buf.at[i, pl.ds(row, rows)], sems.at[at])
            )
            row += rows
            at += 1
        copies.append(mine)
    return copies


def start(copies):
    for copy in copies:
        copy.start()


def wait(copies):
    for copy in copies:
        copy.wait()


def whole(refs):
    return joined([ref[...] for ref in refs], 0)


def added(terms, cols):
    total = None
    for refs in terms:
        term = joined([ref[:, cols].astype(F32) for ref in refs], 0)
        total = term if total is None else total + term
    return total


def diagonal(pair):
    zero = jnp.zeros((pair.shape[0], HD), pair.dtype)
    top = jnp.concatenate([pair[:, :HD], zero], axis=1)
    low = jnp.concatenate([zero, pair[:, HD:]], axis=1)
    return jnp.concatenate([top, low], axis=0)


def pack_kernel(sel_ref, q_ref, out_ref):
    rows, width = q_ref.shape
    out_ref[:rows] = q_ref[...]
    digits = [(sel_ref[...] >> 4).astype(F32), (sel_ref[...] & 15).astype(F32)]
    if width > 2 * rows:
        digits.append(jnp.zeros((TOPK, width - 2 * rows), F32))
    lines = [jnp.concatenate(digits, axis=1), jnp.zeros((PAD - TOPK, width), F32)]
    out_ref[rows:] = jnp.concatenate(lines, axis=0).astype(BF16)


def forward_kernel(counts, span, cap, me_ref, mark_ref, k_any, v_any, *refs):
    chunks = len(counts)
    q_refs, refs = dealt(refs, counts)
    part_any, refs = refs[:chunks], refs[chunks:]
    qg_any, p_any, logit_ref, hot_any = refs[:4]
    q_buf, part_refs, k_ref, v_ref, qg_ref, p_ref, hot_ref, topg_ref, out_ref = refs[4:13]
    in_sems, kv_sems, out_sems = refs[13:]
    q_copies = loads(q_refs, q_buf, in_sems)
    kv_copies = [
        pltpu.make_async_copy(k_any, k_ref, kv_sems.at[0]),
        pltpu.make_async_copy(v_any, v_ref, kv_sems.at[1]),
    ]
    out_copies = [
        pltpu.make_async_copy(qg_ref, qg_any, out_sems.at[chunks]),
        pltpu.make_async_copy(hot_ref, hot_any, out_sems.at[chunks + 1]),
        pltpu.make_async_copy(p_ref, p_any, out_sems.at[chunks + 2]),
    ]
    for copies in q_copies:
        start(copies)
    start(kv_copies)
    block_count, _, width = k_ref.shape
    heads = width // HD
    rows = part_any[0].shape[0]
    group_rows = rows * span
    groups = chunks // span
    scale = HD ** (-0.5)
    rate = scale * 1.4426950408889634
    base = me_ref[0] * block_count

    before = lax.broadcasted_iota(jnp.int32, (group_rows, group_rows), 0)
    later = lax.broadcasted_iota(jnp.int32, (group_rows, group_rows), 1)
    earlier = (before < later).astype(BF16)
    own_ids = (base + lax.broadcasted_iota(jnp.int32, (block_count, group_rows), 0)).astype(F32)
    place = lax.broadcasted_iota(jnp.int32, (cap, group_rows), 0).astype(F32)
    zero = jnp.zeros((block_count, HD), BF16)
    wide_marks = jnp.concatenate(
        [
            jnp.concatenate(
                [mark_ref[:, i * HD : (i + 1) * HD] if i == h else zero for i in range(heads)], axis=1
            )
            for h in range(heads)
        ],
        axis=0,
    )
    q_groups, owns = [], []
    for g in range(groups):
        for i in range(span):
            wait(q_copies[g * span + i])
        packs = [q_buf[g * span + i] for i in range(span)]
        digits = [pack[rows : rows + PAD].astype(F32)[:TOPK] for pack in packs]
        picked = joined([16.0 * d[:, :rows] + d[:, rows : 2 * rows] for d in digits], 1)
        own = picked[0:1, :] == own_ids
        for t in range(1, TOPK):
            own = own | (picked[t : t + 1, :] == own_ids)
        owns.append(jnp.where(own, 1.0, 0.0))
        q_groups.append(joined([pack[:rows] for pack in packs], 0))
    own_all = jnp.concatenate(owns, axis=0)
    rank_all = jnp.where(own_all > 0.5, mm(own_all.astype(BF16), earlier), -1.0)
    hots = []
    for g in range(groups):
        rank = rank_all[g * block_count : (g + 1) * block_count]
        hots.append(
            jnp.concatenate(
                [
                    jnp.where(rank[b : b + 1, :] == place, 1.0, 0.0).astype(BF16)
                    for b in range(block_count)
                ],
                axis=0,
            )
        )
        hot_ref[g] = hots[g]
    all_marks = [mm(wide_marks, q_groups[g], NT) for g in range(groups)]
    for g in range(groups):
        qg_ref[:, g * cap : (g + 1) * cap, :] = (
            mm(hots[g], q_groups[g]).astype(BF16).reshape(block_count, cap, width)
        )
    tails = []
    for g in range(groups):
        tops, sums = [], []
        for h in range(heads):
            mark = scale * all_marks[g][h * block_count : (h + 1) * block_count]
            mark = jnp.where(owns[g] > 0.5, mark, LOW)
            top = jnp.max(mark, axis=0, keepdims=True).astype(BF16).astype(F32)
            tops.append(top)
            sums.append(jnp.sum(owns[g] * jnp.exp(mark - top), axis=0, keepdims=True))
        tops, sums = jnp.concatenate(tops, axis=0), jnp.concatenate(sums, axis=0)
        upper = sums.astype(BF16).astype(F32)
        spare = jnp.zeros((HD - 3 * heads, group_rows), F32)
        tails.append(jnp.concatenate([tops, upper, sums - upper, spare], axis=0))
    for g in range(groups):
        topg_ref[:, g * cap : (g + 1) * cap, :] = mm(hots[g], tails[g].astype(BF16), NT).reshape(
            block_count, cap, HD
        )
    for g in range(groups):
        for i in range(span):
            part_refs[g * span + i, :, width:] = (
                tails[g][:, i * rows : (i + 1) * rows].T.astype(BF16)
            )
    start(out_copies[:2])
    wait(kv_copies)

    pairs = [slice(p * 2 * HD, (p + 1) * 2 * HD) for p in range(heads // 2)]

    def some_blocks(step, carry):
        blocks = [step * TOGETHER + u for u in range(TOGETHER)]
        logits = [
            [mm(diagonal(k_ref[b, :, cols]), qg_ref[b, :, cols], NT) for cols in pairs]
            for b in blocks
        ]
        probs, gated, kept = [], [], []
        for b, scores in zip(blocks, logits):
            tops = topg_ref[b].T[:heads]
            marks = scale * jnp.concatenate(
                [scores[h // 2][(h % 2 + 1) * BLOCK - 1 : (h % 2 + 1) * BLOCK] for h in range(heads)],
                axis=0,
            )
            gates = jnp.exp(marks - tops)
            kept.append(marks)
            for p in range(heads // 2):
                low, high = [], []
                for i in range(2):
                    part = scores[p][i * BLOCK : (i + 1) * BLOCK]
                    weight = jnp.exp2(rate * (part - jnp.max(part, axis=0, keepdims=True)))
                    inverse = 1.0 / jnp.sum(weight, axis=0, keepdims=True)
                    gate = gates[2 * p + i : 2 * p + i + 1, :]
                    low.append((weight * inverse).astype(BF16))
                    high.append((weight * (inverse * gate)).astype(BF16))
                probs.append(jnp.concatenate(low, axis=0))
                gated.append(jnp.concatenate(high, axis=0))
        outs = []
        for u, b in enumerate(blocks):
            for p, cols in enumerate(pairs):
                both = gated[u * len(pairs) + p]
                outs.append(mm(both, diagonal(v_ref[b, :, cols]), TN).astype(BF16))
        for u, b in enumerate(blocks):
            logit_ref[b] = kept[u]
            for p, cols in enumerate(pairs):
                p_ref[b, p] = probs[u * len(pairs) + p]
                out_ref[b, :, cols] = outs[u * len(pairs) + p]
        return carry

    lax.fori_loop(0, block_count // TOGETHER, some_blocks, 0)
    start(out_copies[2:])

    for g in range(groups):
        slots = out_ref[:, g * cap : (g + 1) * cap, :].reshape(block_count * cap, width)
        part = mm(hot_ref[g], slots, TN).astype(BF16)
        for i in range(span):
            m = g * span + i
            part_refs[m, :, :width] = part[i * rows : (i + 1) * rows]
            copy = pltpu.make_async_copy(part_refs.at[m], part_any[m], out_sems.at[m])
            copy.start()
            out_copies.append(copy)
    wait(out_copies)


def shift(heads, *moves):
    row = lax.broadcasted_iota(jnp.int32, (HD, HD), 0)
    col = lax.broadcasted_iota(jnp.int32, (HD, HD), 1)
    total = jnp.zeros((HD, HD), F32)
    for source, target in moves:
        inside = (row >= source * heads) & (row < (source + 1) * heads)
        hit = inside & (col - target * heads == row - source * heads)
        total = jnp.where(hit, 1.0, total)
    return total.astype(BF16)


def blend(terms, heads):
    width = heads * HD
    tails = [joined([ref[rows, width:] for ref, rows in term], 0) for term in terms]
    wide = [tail.astype(F32) for tail in tails]
    top = wide[0]
    for tail in wide[1:]:
        top = jnp.maximum(top, tail)
    gather = shift(heads, (1, 0), (2, 0))
    factors = [jnp.exp(tail - top) for tail in wide]
    total = None
    for tail, factor in zip(tails, factors):
        share = factor * mm(tail, gather)
        total = share if total is None else total + share
    columns = []
    for h in range(heads):
        cols = slice(h * HD, (h + 1) * HD)
        column = None
        for term, factor in zip(terms, factors):
            values = joined([ref[rows, cols] for ref, rows in term], 0).astype(F32)
            part = factor[:, h : h + 1] * values
            column = part if column is None else column + part
        columns.append(column)
    return top, total, columns


def digits_of(tile, count):
    digits = []
    for _ in range(count):
        upper = tile.astype(BF16)
        digits.append(upper)
        tile = tile - upper.astype(F32)
    return digits


def packed_tail(digits, heads):
    total = None
    for i, digit in enumerate(digits):
        part = mm(digit, shift(heads, (0, i)))
        total = part if total is None else total + part
    return total.astype(BF16)


def merge_kernel(plan, heads, *refs):
    ins, outs = refs[: len(refs) - len(plan)], refs[len(refs) - len(plan) :]
    for terms, out_ref in zip(plan, outs):
        top, total, columns = blend(
            [[(ins[i], pl.ds(first, count))] for i, first, count in terms], heads
        )
        for h in range(heads):
            out_ref[:, h * HD : (h + 1) * HD] = columns[h].astype(BF16)
        out_ref[:, heads * HD :] = packed_tail([top.astype(BF16)] + digits_of(total, 2), heads)


def grad_kernel(lines, line_ref, w_ref, *refs):
    own_ref, up_refs, down_refs = refs[0], refs[1:lines], refs[lines : 2 * lines - 1]
    ga_ref, blocks_ref, full_ref, w_buf, sems, piece_sems = refs[2 * lines - 1 :]
    width = own_ref.shape[1]
    chunks, _, share = blocks_ref.shape
    line = line_ref[0]
    copies = [
        pltpu.make_async_copy(w_ref.at[pl.ds(i * width, width)], w_buf.at[i], sems.at[i])
        for i in range(lines)
    ]
    start(copies)

    def placed(ref, i):
        return pltpu.make_async_copy(ref, full_ref.at[i], piece_sems.at[i])

    placed(own_ref, line).start()
    for d in range(1, lines):

        @pl.when(line >= d)
        def _():
            placed(up_refs[d - 1], line - d).start()

        @pl.when(line + d < lines)
        def _():
            placed(down_refs[d - 1], line + d).start()

    for i in range(lines):
        placed(own_ref, i).wait()
    for j in range(chunks):
        first = j * share
        blocks_ref[j] = full_ref[first // width, :, first % width : first % width + share]
    total = None
    for i in range(lines):
        copies[i].wait()
        term = mm(full_ref[i], w_buf[i])
        total = term if total is None else total + term
    ga_ref[...] = total.astype(BF16)


def finish_kernel(counts, *refs):
    terms, (ga_ref, attn_ref, *ext_refs) = dealt(refs, counts)
    rows, width = ga_ref.shape
    half = rows // len(ext_refs)
    heads = width // HD
    top, total, columns = blend(
        [[(ref, slice(None)) for ref in pieces] for pieces in terms], heads
    )
    lane = lax.broadcasted_iota(jnp.int32, (rows, HD), 1)
    total = jnp.where(lane < heads, total, 1.0)
    inverse = 1.0 / total
    dots = jnp.zeros((rows, HD), F32)
    for i, ext_ref in enumerate(ext_refs):
        ext_ref[:, :width] = ga_ref[i * half : (i + 1) * half]
    for h in range(heads):
        cols = slice(h * HD, (h + 1) * HD)
        attn = columns[h] * inverse[:, h : h + 1]
        attn_ref[:, cols] = attn.astype(BF16)
        dot = jnp.sum(attn * ga_ref[:, cols].astype(F32), axis=1, keepdims=True)
        dots = jnp.where(lane == h, dot, dots)
    level = jnp.where(lane < heads, top + jnp.log(total), 0.0)
    tail = packed_tail(digits_of(dots, 2) + digits_of(level, 3), heads)
    for i, ext_ref in enumerate(ext_refs):
        ext_ref[:, width:] = tail[i * half : (i + 1) * half]


def total_kernel(counts, *refs):
    terms, (out_ref,) = dealt(refs, counts)
    for h in range(out_ref.shape[1] // HD):
        cols = slice(h * HD, (h + 1) * HD)
        out_ref[:, cols] = added(terms, cols)


def backward_kernel(counts, span, cap, logit_ref, hot_any, qg_any, p_any, k_any, v_any, *refs):
    chunks = len(counts)
    ga_refs, refs = dealt(refs, counts)
    part_refs, refs = refs[:chunks], refs[chunks:]
    dk_any, dv_any = refs[:2]
    ga_buf, hot_ref, qg_ref, p_ref, k_ref, v_ref, gag_ref, dq_ref, dk_ref, dv_ref = refs[2:12]
    in_sems, hot_sem, block_sems, out_sems, part_sems = refs[12:]
    ga_copies = loads(ga_refs, ga_buf, in_sems)
    hot_copy = pltpu.make_async_copy(hot_any, hot_ref, hot_sem.at[0])
    hot_copy.start()
    for copies in ga_copies:
        start(copies)

    def block_loads(b):
        pairs = ((qg_any, qg_ref), (p_any, p_ref), (k_any, k_ref), (v_any, v_ref))
        return [
            pltpu.make_async_copy(far.at[b], near.at[b], block_sems.at[i, b])
            for i, (far, near) in enumerate(pairs)
        ]

    def block_stores(b):
        return [
            pltpu.make_async_copy(dk_ref.at[b], dk_any.at[b], out_sems.at[0, b]),
            pltpu.make_async_copy(dv_ref.at[b], dv_any.at[b], out_sems.at[1, b]),
        ]

    block_count, _, width = k_ref.shape
    heads = width // HD
    rows = part_refs[0].shape[0]
    groups = chunks // span
    scale = HD ** (-0.5)

    for b in range(block_count):
        start(block_loads(b))
    hot_copy.wait()
    for g in range(groups):
        for i in range(span):
            wait(ga_copies[g * span + i])
        ga_group = joined([ga_buf[g * span + i] for i in range(span)], 0)
        gag_ref[:, g * cap : (g + 1) * cap, :] = (
            mm(hot_ref[g], ga_group).astype(BF16).reshape(block_count, cap, width + HD)
        )
    last = lax.broadcasted_iota(jnp.int32, (BLOCK, groups * cap), 0) == BLOCK - 1

    pairs = [slice(p * 2 * HD, (p + 1) * 2 * HD) for p in range(heads // 2)]

    def some_blocks(step, carry):
        blocks = [step * TOGETHER + u for u in range(TOGETHER)]
        for b in blocks:
            wait(block_loads(b))
        grads = [
            [mm(diagonal(v_ref[b, :, cols]), gag_ref[b, :, cols], NT) for cols in pairs]
            for b in blocks
        ]
        gated, scores = [], []
        for b, grad_pairs in zip(blocks, grads):
            tail = gag_ref[b, :, width:].astype(F32).T
            tail = [tail[i * heads : (i + 1) * heads] for i in range(5)]
            dots = tail[0] + tail[1]
            gates = jnp.exp(jnp.minimum(logit_ref[b] - (tail[2] + tail[3] + tail[4]), 0.0))
            for p in range(heads // 2):
                both = p_ref[b, p].astype(F32)
                low, high = [], []
                for i in range(2):
                    at = slice(i * BLOCK, (i + 1) * BLOCK)
                    h = 2 * p + i
                    gate = gates[h : h + 1, :]
                    grad, probs = grad_pairs[p][at], both[at]
                    delta = jnp.sum(probs * grad, axis=0, keepdims=True)
                    weight = probs * gate
                    extra = jnp.where(last, scale * gate * (delta - dots[h : h + 1, :]), 0.0)
                    low.append((weight * (scale * (grad - delta)) + extra).astype(BF16))
                    high.append(weight.astype(BF16))
                scores.append(low)
                gated.append(high)
        for u, b in enumerate(blocks):
            for p, cols in enumerate(pairs):
                score, weight = scores[u * len(pairs) + p], gated[u * len(pairs) + p]
                for i in range(2):
                    head = slice((2 * p + i) * HD, (2 * p + i + 1) * HD)
                    dv_ref[b, :, head] = mm(weight[i], gag_ref[b, :, head])
                    dk_ref[b, :, head] = mm(score[i], qg_ref[b, :, head])
                both = jnp.concatenate(score, axis=0)
                dq_ref[b, :, cols] = mm(both, diagonal(k_ref[b, :, cols]), TN).astype(BF16)
        for b in blocks:
            start(block_stores(b))
        return carry

    lax.fori_loop(0, block_count // TOGETHER, some_blocks, 0)

    part_copies = []

    for g in range(groups):
        slots = dq_ref[:, g * cap : (g + 1) * cap, :].reshape(block_count * cap, width)
        part = mm(hot_ref[g], slots, TN).astype(BF16)
        for i in range(span):
            m = g * span + i
            ga_buf[m, :, :width] = part[i * rows : (i + 1) * rows]
            copy = pltpu.make_async_copy(
                ga_buf.at[m, :, pl.ds(0, width)], part_refs[m], part_sems.at[m]
            )
            copy.start()
            part_copies.append(copy)
    for b in range(block_count):
        wait(block_stores(b))
    wait(part_copies)


def weight_kernel(counts, first, me_ref, cols_ref, *refs):
    attns, (*before, out_ref) = dealt(refs, counts)
    me = me_ref[0]
    columns = joined([cols_ref[me ^ (first + m)] for m in range(len(counts))], 0)
    total = mm(columns, joined([whole(pieces) for pieces in attns], 0), TN)
    for ref in before:
        total = total + ref[...]
    out_ref[...] = total


def swap(x, bits):
    count = lax.axis_size("ctx")
    return lax.ppermute(x, "ctx", [(i, i ^ bits) for i in range(count)])


def after(x, *others):
    return lax.optimization_barrier((x, *others))[0]


def flat(lists):
    return [x for pieces in lists for x in pieces]


def spread_near(x):
    chips = lax.axis_size("ctx") // 2
    return [[x]] + [[swap(x, 2 * j)] for j in range(1, chips if chips != 4 else 3)]


def spread_far(near, half, *before):
    if len(near) != 3:
        return near
    (x_way,), (y_way,) = near[1:]
    far = [swap(after(x_way[:half], *before), 4), swap(after(y_way[half:], *before), 2)]
    return near + [far]


def spread_chips(x, half, *before):
    return spread_far(spread_near(x), half, *before)


def spread_halves(top, low):
    chips = lax.axis_size("ctx") // 2
    if chips != 4:
        return [[swap(x, 2 * j) if j else x for x in (top, low)] for j in range(chips)]
    x_top, y_low = swap(top, 2), swap(low, 4)
    x_low, y_top = swap(low, 2), swap(top, 4)
    return [[top, low], [x_top, x_low], [y_top, y_low], [swap(x_top, 4), swap(y_low, 2)]]


def with_cores(lists, *before):
    both = []
    for pieces in lists:
        if before and pieces is lists[-1]:
            pieces = [after(piece, *before) for piece in pieces]
        both += [pieces, [swap(piece, 1) for piece in pieces]]
    return both


def from_core(parts, *before):
    received = [None] * (len(parts) // 2)
    for j in reversed(range(len(received))):
        received[j] = swap(after(parts[2 * j + 1], *before), 1)
    return received


def collect_chips(parts, received):
    chips = len(received)

    def both(j, rows, extra=None, earlier=None):
        mine = parts[2 * j] if earlier is None else after(parts[2 * j], earlier)
        total = mine[rows].astype(F32) + received[j][rows].astype(F32)
        if extra is not None:
            total = total + extra.astype(F32)
        return total.astype(BF16)

    terms = [[parts[0]], [received[0]]]
    if chips != 4:
        return terms + [[swap(both(j, slice(None)), 2 * j)] for j in range(1, chips)], []
    half = parts[0].shape[0] // 2
    top, low = slice(0, half), slice(half, None)
    x_sum, y_sum = both(3, top), both(3, low)
    x_far, y_far = swap(x_sum, 2), swap(y_sum, 4)
    x_sum, y_sum = both(1, top, None, x_sum), both(2, low, None, y_sum)
    x_top, y_low = swap(x_sum, 2), swap(y_sum, 4)
    x_sum, y_sum = both(1, low, y_far, x_sum), both(2, top, x_far, y_sum)
    x_low, y_top = swap(x_sum, 2), swap(y_sum, 4)
    return terms + [[x_top, x_low], [y_top, y_low]], [x_sum, y_sum]


def merge_chips(parts, received, heads, between):
    chips = len(received)
    rows = parts[0].shape[0]
    half = rows // 2

    def merged(ins, plan):
        return pl.pallas_call(
            functools.partial(merge_kernel, plan, heads),
            out_shape=[
                jax.ShapeDtypeStruct((terms[0][2], ins[0].shape[1]), BF16) for terms in plan
            ],
            in_specs=[pl.BlockSpec(memory_space=pltpu.VMEM)] * len(ins),
            out_specs=[pl.BlockSpec(memory_space=pltpu.VMEM)] * len(plan),
            compiler_params=pltpu.CompilerParams(vmem_limit_bytes=SOME),
            name="merge",
        )(*ins)

    terms = [[parts[0]], [received[0]]]
    if chips != 4:
        for j in range(1, chips):
            (both,) = merged([parts[2 * j], received[j]], [[(0, 0, rows), (1, 0, rows)]])
            terms.append([swap(both, 2 * j)])
        return terms, between(received[0])
    top, low = (0, half), (half, half)
    x_far, y_far = merged(
        [parts[6], received[3]], [[(0, *top), (1, *top)], [(0, *low), (1, *low)]]
    )
    x_far, y_far = swap(x_far, 2), swap(y_far, 4)
    ins = [parts[2], received[1], parts[4], received[2]]
    x_top, y_low = merged(ins, [[(0, *top), (1, *top)], [(2, *low), (3, *low)]])
    x_top, y_low = swap(x_top, 2), swap(y_low, 4)
    x_low, y_top = merged(
        ins + [y_far, x_far],
        [[(0, *low), (1, *low), (4, *top)], [(2, *top), (3, *top), (5, *top)]],
    )
    done = between(x_low, y_top)
    x_low, y_top = swap(x_low, 2), swap(y_top, 4)
    return terms + [[x_top, x_low], [y_top, y_low]], done


def spread_line(x):
    lines = lax.axis_size("head")
    ups, downs = [x], [x]
    for d in range(1, lines):
        ups.append(lax.ppermute(ups[-1], "head", [(i, i + 1) for i in range(d - 1, lines - 1)]))
        downs.append(lax.ppermute(downs[-1], "head", [(i, i - 1) for i in range(1, lines - d + 1)]))
    return ups[1:], downs[1:]


def body(queries, key_rows, value_rows, selected, out_grad, out_weight):
    chunks = lax.axis_size("ctx")
    chips = chunks // 2
    lines = lax.axis_size("head")
    rows, width = queries.shape
    features = out_weight.shape[0]
    heads = width // HD
    block_count = key_rows.shape[0] // BLOCK
    block_total = block_count * chunks
    capacity = 2 * rows * TOPK // block_total
    span = max(1, 16 // capacity)
    cap = capacity * span
    groups = chunks // span
    slots = groups * cap
    index = lax.axis_index("ctx").astype(jnp.int32)
    me = index.reshape(1)
    keys = key_rows.reshape(block_count, BLOCK, width)
    values = value_rows.reshape(block_count, BLOCK, width)
    vmem = pl.BlockSpec(memory_space=pltpu.VMEM)
    smem = pl.BlockSpec(memory_space=pltpu.SMEM)
    anywhere = pl.BlockSpec(memory_space=pl.ANY)
    params = pltpu.CompilerParams(vmem_limit_bytes=MOST)
    small = pltpu.CompilerParams(vmem_limit_bytes=SOME)

    def shaped(shape, kind=BF16):
        return jax.ShapeDtypeStruct(shape, kind)

    ups, downs = spread_line(out_grad)
    packed = pl.pallas_call(
        pack_kernel,
        out_shape=shaped((rows + PAD, width)),
        in_specs=[vmem] * 2,
        out_specs=vmem,
        compiler_params=small,
        name="pack",
    )(selected.T, queries)
    query_chips = spread_chips(packed, rows // 2)
    query_all = with_cores(query_chips, ups[0], downs[0])

    outs = pl.pallas_call(
        functools.partial(forward_kernel, [len(pieces) for pieces in query_all], span, cap),
        out_shape=[shaped((rows, width + HD))] * chunks
        + [
            shaped((block_count, slots, width)),
            shaped((block_count, heads // 2, 2 * BLOCK, slots)),
            shaped((block_count, heads, slots), F32),
            shaped((groups, block_count * cap, rows * span)),
        ],
        in_specs=[smem, vmem] + [anywhere] * (2 + len(flat(query_all))),
        out_specs=[anywhere] * (chunks + 2) + [vmem, anywhere],
        scratch_shapes=[
            pltpu.VMEM((chunks, rows + PAD, width), BF16),
            pltpu.VMEM((chunks, rows, width + HD), BF16),
            pltpu.VMEM((block_count, BLOCK, width), BF16),
            pltpu.VMEM((block_count, BLOCK, width), BF16),
            pltpu.VMEM((block_count, slots, width), BF16),
            pltpu.VMEM((block_count, heads // 2, 2 * BLOCK, slots), BF16),
            pltpu.VMEM((groups, block_count * cap, rows * span), BF16),
            pltpu.VMEM((block_count, slots, HD), F32),
            pltpu.VMEM((block_count, slots, width), BF16),
            pltpu.SemaphoreType.DMA((len(flat(query_all)),)),
            pltpu.SemaphoreType.DMA((2,)),
            pltpu.SemaphoreType.DMA((chunks + 3,)),
        ],
        compiler_params=params,
        name="forward",
    )(me, keys[:, BLOCK - 1], keys, values, *flat(query_all))
    q_slots, probs, logits, hot = outs[chunks:]

    line = lax.axis_index("head").astype(jnp.int32).reshape(1)
    make_grad = pl.pallas_call(
        functools.partial(grad_kernel, lines),
        out_shape=[shaped((rows, width)), shaped((chunks, rows, features // chunks))],
        in_specs=[smem] + [anywhere] * (2 * lines),
        out_specs=[vmem] * 2,
        scratch_shapes=[
            pltpu.VMEM((lines, rows, width), BF16),
            pltpu.VMEM((lines, width, width), BF16),
            pltpu.SemaphoreType.DMA((lines,)),
            pltpu.SemaphoreType.DMA((lines,)),
        ],
        compiler_params=params,
        name="grad",
    )
    received = from_core(outs[:chunks], ups[1], downs[1])
    terms, (grad_attn, blocks) = merge_chips(
        outs[:chunks],
        received,
        heads,
        lambda *before: make_grad(after(line, *before), out_weight, out_grad, *ups, *downs),
    )
    attn_out, *extended = pl.pallas_call(
        functools.partial(finish_kernel, [len(pieces) for pieces in terms]),
        out_shape=[shaped((rows, width))] + [shaped((rows // 2, width + HD))] * 2,
        in_specs=[vmem] * (len(flat(terms)) + 1),
        out_specs=[vmem] * 3,
        compiler_params=small,
        name="finish",
    )(*flat(terms), grad_attn)
    grad_chips = spread_halves(*extended)
    grad_all = with_cores(grad_chips)
    arrived = flat(grad_chips[1:])
    attns = spread_near(after(attn_out, *arrived))
    columns = lax.all_to_all(
        after(blocks, *arrived), "ctx", split_axis=0, concat_axis=0, tiled=True
    )

    outs = pl.pallas_call(
        functools.partial(backward_kernel, [len(pieces) for pieces in grad_all], span, cap),
        out_shape=[shaped((rows, width))] * chunks
        + [shaped((block_count, BLOCK, width), F32)] * 2,
        in_specs=[vmem] + [anywhere] * (5 + len(flat(grad_all))),
        out_specs=[anywhere] * (chunks + 2),
        scratch_shapes=[
            pltpu.VMEM((chunks, rows, width + HD), BF16),
            pltpu.VMEM((groups, block_count * cap, rows * span), BF16),
            pltpu.VMEM((block_count, slots, width), BF16),
            pltpu.VMEM((block_count, heads // 2, 2 * BLOCK, slots), BF16),
            pltpu.VMEM((block_count, BLOCK, width), BF16),
            pltpu.VMEM((block_count, BLOCK, width), BF16),
            pltpu.VMEM((block_count, slots, width + HD), BF16),
            pltpu.VMEM((block_count, slots, width), BF16),
            pltpu.VMEM((block_count, BLOCK, width), F32),
            pltpu.VMEM((block_count, BLOCK, width), F32),
            pltpu.SemaphoreType.DMA((len(flat(grad_all)),)),
            pltpu.SemaphoreType.DMA((1,)),
            pltpu.SemaphoreType.DMA((4, block_count)),
            pltpu.SemaphoreType.DMA((2, block_count)),
            pltpu.SemaphoreType.DMA((chunks,)),
        ],
        compiler_params=params,
        name="backward",
    )(logits, hot, q_slots, probs, keys, values, *flat(grad_all))
    key_grad, value_grad = outs[chunks:]
    received = from_core(outs[:chunks], columns, *flat(attns[1:3]))
    terms, last_sums = collect_chips(outs[:chunks], received)
    attns = with_cores(spread_far(attns, rows // 2, *last_sums))

    def weight_part(chosen, first, when, *before):
        return pl.pallas_call(
            functools.partial(weight_kernel, [len(pieces) for pieces in chosen], first),
            out_shape=shaped((features // chunks, width), F32),
            in_specs=[smem] + [vmem] * (1 + len(flat(chosen)) + len(before)),
            out_specs=vmem,
            compiler_params=small,
            name="weight",
        )(when, columns, *flat(chosen), *before)

    weight_near = weight_part(attns[:-2], 0, after(me, terms[2][0]))
    query_grad = pl.pallas_call(
        functools.partial(total_kernel, [len(pieces) for pieces in terms]),
        out_shape=shaped((rows, width), F32),
        in_specs=[vmem] * len(flat(terms)),
        out_specs=vmem,
        compiler_params=small,
        name="total",
    )(after(terms[0][0], weight_near), *flat(terms[1:]))
    weight_grad = weight_part(attns[-2:], chunks - 2, after(me, query_grad), weight_near)
    return (
        query_grad,
        key_grad.reshape(-1, width),
        value_grad.reshape(-1, width),
        weight_grad,
    )


def solution(mesh):
    return jax.shard_map(
        body,
        mesh=mesh,
        in_specs=(
            P("ctx", "head"),
            P("ctx", "head"),
            P("ctx", "head"),
            P("ctx", None),
            P("ctx", "head"),
            P(None, "head"),
        ),
        out_specs=(P("ctx", "head"), P("ctx", "head"), P("ctx", "head"), P("ctx", "head")),
        check_vma=False,
    )
```

```python
import functools

import jax
import jax.numpy as jnp
from jax import lax
from jax.experimental import pallas as pl
from jax.experimental.pallas import tpu as pltpu
from jax.sharding import PartitionSpec as P

HD = 128
BLOCK = 64
TOPK = 4
F32 = jnp.float32
BF16 = jnp.bfloat16
MOST = 58 * 1024 * 1024
SOME = 20 * 1024 * 1024
PAD = 16
TOGETHER = 4
LOW = -(2.0**99)
NN = (((1,), (0,)), ((), ()))
NT = (((1,), (1,)), ((), ()))
TN = (((0,), (0,)), ((), ()))


def mm(a, b, dims=NN):
    return lax.dot_general(a, b, dims, preferred_element_type=F32)


def joined(items, axis):
    return items[0] if len(items) == 1 else jnp.concatenate(items, axis=axis)


def dealt(refs, counts):
    lists, at = [], 0
    for count in counts:
        lists.append(refs[at : at + count])
        at += count
    return lists, refs[at:]


def loads(lists, buf, sems):
    copies, at = [], 0
    for i, refs in enumerate(lists):
        mine, row = [], 0
        for ref in refs:
            rows = ref.shape[0]
            mine.append(
                pltpu.make_async_copy(ref, buf.at[i, pl.ds(row, rows)], sems.at[at])
            )
            row += rows
            at += 1
        copies.append(mine)
    return copies


def start(copies):
    for copy in copies:
        copy.start()


def wait(copies):
    for copy in copies:
        copy.wait()


def whole(refs):
    return joined([ref[...] for ref in refs], 0)


def added(terms, cols):
    total = None
    for refs in terms:
        term = joined([ref[:, cols].astype(F32) for ref in refs], 0)
        total = term if total is None else total + term
    return total


def diagonal(pair):
    zero = jnp.zeros((pair.shape[0], HD), pair.dtype)
    top = jnp.concatenate([pair[:, :HD], zero], axis=1)
    low = jnp.concatenate([zero, pair[:, HD:]], axis=1)
    return jnp.concatenate([top, low], axis=0)


def pack_kernel(sel_ref, q_ref, out_ref):
    rows, width = q_ref.shape
    out_ref[:rows] = q_ref[...]
    digits = [(sel_ref[...] >> 4).astype(F32), (sel_ref[...] & 15).astype(F32)]
    if width > 2 * rows:
        digits.append(jnp.zeros((TOPK, width - 2 * rows), F32))
    lines = [jnp.concatenate(digits, axis=1), jnp.zeros((PAD - TOPK, width), F32)]
    out_ref[rows:] = jnp.concatenate(lines, axis=0).astype(BF16)


def forward_kernel(counts, span, cap, me_ref, mark_ref, k_any, v_any, *refs):
    chunks = len(counts)
    q_refs, refs = dealt(refs, counts)
    part_any, refs = refs[:chunks], refs[chunks:]
    qg_any, p_any, logit_ref, hot_any = refs[:4]
    q_buf, part_refs, k_ref, v_ref, qg_ref, p_ref, hot_ref, topg_ref, out_ref = refs[4:13]
    in_sems, kv_sems, out_sems = refs[13:]
    q_copies = loads(q_refs, q_buf, in_sems)
    kv_copies = [
        pltpu.make_async_copy(k_any, k_ref, kv_sems.at[0]),
        pltpu.make_async_copy(v_any, v_ref, kv_sems.at[1]),
    ]
    out_copies = [
        pltpu.make_async_copy(qg_ref, qg_any, out_sems.at[chunks]),
        pltpu.make_async_copy(hot_ref, hot_any, out_sems.at[chunks + 1]),
        pltpu.make_async_copy(p_ref, p_any, out_sems.at[chunks + 2]),
    ]
    for copies in q_copies:
        start(copies)
    start(kv_copies)
    block_count, _, width = k_ref.shape
    heads = width // HD
    rows = part_any[0].shape[0]
    group_rows = rows * span
    groups = chunks // span
    scale = HD ** (-0.5)
    rate = scale * 1.4426950408889634
    base = me_ref[0] * block_count

    before = lax.broadcasted_iota(jnp.int32, (group_rows, group_rows), 0)
    later = lax.broadcasted_iota(jnp.int32, (group_rows, group_rows), 1)
    earlier = (before < later).astype(BF16)
    own_ids = (base + lax.broadcasted_iota(jnp.int32, (block_count, group_rows), 0)).astype(F32)
    place = lax.broadcasted_iota(jnp.int32, (cap, group_rows), 0).astype(F32)
    zero = jnp.zeros((block_count, HD), BF16)
    wide_marks = jnp.concatenate(
        [
            jnp.concatenate(
                [mark_ref[:, i * HD : (i + 1) * HD] if i == h else zero for i in range(heads)], axis=1
            )
            for h in range(heads)
        ],
        axis=0,
    )
    q_groups, owns = [], []
    for g in range(groups):
        for i in range(span):
            wait(q_copies[g * span + i])
        packs = [q_buf[g * span + i] for i in range(span)]
        digits = [pack[rows : rows + PAD].astype(F32)[:TOPK] for pack in packs]
        picked = joined([16.0 * d[:, :rows] + d[:, rows : 2 * rows] for d in digits], 1)
        own = picked[0:1, :] == own_ids
        for t in range(1, TOPK):
            own = own | (picked[t : t + 1, :] == own_ids)
        owns.append(jnp.where(own, 1.0, 0.0))
        q_groups.append(joined([pack[:rows] for pack in packs], 0))
    own_all = jnp.concatenate(owns, axis=0)
    rank_all = jnp.where(own_all > 0.5, mm(own_all.astype(BF16), earlier), -1.0)
    hots = []
    for g in range(groups):
        rank = rank_all[g * block_count : (g + 1) * block_count]
        hots.append(
            jnp.concatenate(
                [
                    jnp.where(rank[b : b + 1, :] == place, 1.0, 0.0).astype(BF16)
                    for b in range(block_count)
                ],
                axis=0,
            )
        )
        hot_ref[g] = hots[g]
    all_marks = [mm(wide_marks, q_groups[g], NT) for g in range(groups)]
    for g in range(groups):
        qg_ref[:, g * cap : (g + 1) * cap, :] = (
            mm(hots[g], q_groups[g]).astype(BF16).reshape(block_count, cap, width)
        )
    tails = []
    for g in range(groups):
        tops, sums = [], []
        for h in range(heads):
            mark = scale * all_marks[g][h * block_count : (h + 1) * block_count]
            mark = jnp.where(owns[g] > 0.5, mark, LOW)
            top = jnp.max(mark, axis=0, keepdims=True).astype(BF16).astype(F32)
            tops.append(top)
            sums.append(jnp.sum(owns[g] * jnp.exp(mark - top), axis=0, keepdims=True))
        tops, sums = jnp.concatenate(tops, axis=0), jnp.concatenate(sums, axis=0)
        upper = sums.astype(BF16).astype(F32)
        spare = jnp.zeros((HD - 3 * heads, group_rows), F32)
        tails.append(jnp.concatenate([tops, upper, sums - upper, spare], axis=0))
    for g in range(groups):
        topg_ref[:, g * cap : (g + 1) * cap, :] = mm(hots[g], tails[g].astype(BF16), NT).reshape(
            block_count, cap, HD
        )
    for g in range(groups):
        for i in range(span):
            part_refs[g * span + i, :, width:] = (
                tails[g][:, i * rows : (i + 1) * rows].T.astype(BF16)
            )
    start(out_copies[:2])
    wait(kv_copies)

    pairs = [slice(p * 2 * HD, (p + 1) * 2 * HD) for p in range(heads // 2)]

    def some_blocks(step, carry):
        blocks = [step * TOGETHER + u for u in range(TOGETHER)]
        logits = [
            [mm(diagonal(k_ref[b, :, cols]), qg_ref[b, :, cols], NT) for cols in pairs]
            for b in blocks
        ]
        probs, gated, kept = [], [], []
        for b, scores in zip(blocks, logits):
            tops = topg_ref[b].T[:heads]
            marks = scale * jnp.concatenate(
                [scores[h // 2][(h % 2 + 1) * BLOCK - 1 : (h % 2 + 1) * BLOCK] for h in range(heads)],
                axis=0,
            )
            gates = jnp.exp(marks - tops)
            kept.append(marks)
            for p in range(heads // 2):
                low, high = [], []
                for i in range(2):
                    part = scores[p][i * BLOCK : (i + 1) * BLOCK]
                    weight = jnp.exp2(rate * (part - jnp.max(part, axis=0, keepdims=True)))
                    inverse = 1.0 / jnp.sum(weight, axis=0, keepdims=True)
                    gate = gates[2 * p + i : 2 * p + i + 1, :]
                    low.append((weight * inverse).astype(BF16))
                    high.append((weight * (inverse * gate)).astype(BF16))
                probs.append(jnp.concatenate(low, axis=0))
                gated.append(jnp.concatenate(high, axis=0))
        outs = []
        for u, b in enumerate(blocks):
            for p, cols in enumerate(pairs):
                both = gated[u * len(pairs) + p]
                outs.append(mm(both, diagonal(v_ref[b, :, cols]), TN).astype(BF16))
        for u, b in enumerate(blocks):
            logit_ref[b] = kept[u]
            for p, cols in enumerate(pairs):
                p_ref[b, p] = probs[u * len(pairs) + p]
                out_ref[b, :, cols] = outs[u * len(pairs) + p]
        return carry

    lax.fori_loop(0, block_count // TOGETHER, some_blocks, 0)
    start(out_copies[2:])

    for g in range(groups):
        slots = out_ref[:, g * cap : (g + 1) * cap, :].reshape(block_count * cap, width)
        part = mm(hot_ref[g], slots, TN).astype(BF16)
        for i in range(span):
            m = g * span + i
            part_refs[m, :, :width] = part[i * rows : (i + 1) * rows]
            copy = pltpu.make_async_copy(part_refs.at[m], part_any[m], out_sems.at[m])
            copy.start()
            out_copies.append(copy)
    wait(out_copies)


def shift(heads, *moves):
    row = lax.broadcasted_iota(jnp.int32, (HD, HD), 0)
    col = lax.broadcasted_iota(jnp.int32, (HD, HD), 1)
    total = jnp.zeros((HD, HD), F32)
    for source, target in moves:
        inside = (row >= source * heads) & (row < (source + 1) * heads)
        hit = inside & (col - target * heads == row - source * heads)
        total = jnp.where(hit, 1.0, total)
    return total.astype(BF16)


def blend(terms, heads):
    width = heads * HD
    tails = [joined([ref[rows, width:] for ref, rows in term], 0) for term in terms]
    wide = [tail.astype(F32) for tail in tails]
    top = wide[0]
    for tail in wide[1:]:
        top = jnp.maximum(top, tail)
    gather = shift(heads, (1, 0), (2, 0))
    factors = [jnp.exp(tail - top) for tail in wide]
    total = None
    for tail, factor in zip(tails, factors):
        share = factor * mm(tail, gather)
        total = share if total is None else total + share
    columns = []
    for h in range(heads):
        cols = slice(h * HD, (h + 1) * HD)
        column = None
        for term, factor in zip(terms, factors):
            values = joined([ref[rows, cols] for ref, rows in term], 0).astype(F32)
            part = factor[:, h : h + 1] * values
            column = part if column is None else column + part
        columns.append(column)
    return top, total, columns


def digits_of(tile, count):
    digits = []
    for _ in range(count):
        upper = tile.astype(BF16)
        digits.append(upper)
        tile = tile - upper.astype(F32)
    return digits


def packed_tail(digits, heads):
    total = None
    for i, digit in enumerate(digits):
        part = mm(digit, shift(heads, (0, i)))
        total = part if total is None else total + part
    return total.astype(BF16)


def merge_kernel(plan, heads, *refs):
    ins, outs = refs[: len(refs) - len(plan)], refs[len(refs) - len(plan) :]
    for terms, out_ref in zip(plan, outs):
        top, total, columns = blend(
            [[(ins[i], pl.ds(first, count))] for i, first, count in terms], heads
        )
        for h in range(heads):
            out_ref[:, h * HD : (h + 1) * HD] = columns[h].astype(BF16)
        out_ref[:, heads * HD :] = packed_tail([top.astype(BF16)] + digits_of(total, 2), heads)


def grad_kernel(lines, line_ref, w_ref, *refs):
    own_ref, up_refs, down_refs = refs[0], refs[1:lines], refs[lines : 2 * lines - 1]
    ga_ref, blocks_ref, full_ref, w_buf, sems, piece_sems = refs[2 * lines - 1 :]
    width = own_ref.shape[1]
    chunks, _, share = blocks_ref.shape
    line = line_ref[0]
    copies = [
        pltpu.make_async_copy(w_ref.at[pl.ds(i * width, width)], w_buf.at[i], sems.at[i])
        for i in range(lines)
    ]
    start(copies)

    def placed(ref, i):
        return pltpu.make_async_copy(ref, full_ref.at[i], piece_sems.at[i])

    placed(own_ref, line).start()
    for d in range(1, lines):

        @pl.when(line >= d)
        def _():
            placed(up_refs[d - 1], line - d).start()

        @pl.when(line + d < lines)
        def _():
            placed(down_refs[d - 1], line + d).start()

    for i in range(lines):
        placed(own_ref, i).wait()
    for j in range(chunks):
        first = j * share
        blocks_ref[j] = full_ref[first // width, :, first % width : first % width + share]
    total = None
    for i in range(lines):
        copies[i].wait()
        term = mm(full_ref[i], w_buf[i])
        total = term if total is None else total + term
    ga_ref[...] = total.astype(BF16)


def finish_kernel(counts, *refs):
    terms, (ga_ref, attn_ref, *ext_refs) = dealt(refs, counts)
    rows, width = ga_ref.shape
    half = rows // len(ext_refs)
    heads = width // HD
    top, total, columns = blend(
        [[(ref, slice(None)) for ref in pieces] for pieces in terms], heads
    )
    lane = lax.broadcasted_iota(jnp.int32, (rows, HD), 1)
    total = jnp.where(lane < heads, total, 1.0)
    inverse = 1.0 / total
    dots = jnp.zeros((rows, HD), F32)
    for i, ext_ref in enumerate(ext_refs):
        ext_ref[:, :width] = ga_ref[i * half : (i + 1) * half]
    for h in range(heads):
        cols = slice(h * HD, (h + 1) * HD)
        attn = columns[h] * inverse[:, h : h + 1]
        attn_ref[:, cols] = attn.astype(BF16)
        dot = jnp.sum(attn * ga_ref[:, cols].astype(F32), axis=1, keepdims=True)
        dots = jnp.where(lane == h, dot, dots)
    level = jnp.where(lane < heads, top + jnp.log(total), 0.0)
    tail = packed_tail(digits_of(dots, 2) + digits_of(level, 3), heads)
    for i, ext_ref in enumerate(ext_refs):
        ext_ref[:, width:] = tail[i * half : (i + 1) * half]


def total_kernel(counts, *refs):
    terms, (out_ref,) = dealt(refs, counts)
    for h in range(out_ref.shape[1] // HD):
        cols = slice(h * HD, (h + 1) * HD)
        out_ref[:, cols] = added(terms, cols)


def backward_kernel(counts, span, cap, logit_ref, hot_any, qg_any, p_any, k_any, v_any, *refs):
    chunks = len(counts)
    ga_refs, refs = dealt(refs, counts)
    part_refs, refs = refs[:chunks], refs[chunks:]
    dk_any, dv_any = refs[:2]
    ga_buf, hot_ref, qg_ref, p_ref, k_ref, v_ref, gag_ref, dq_ref, dk_ref, dv_ref = refs[2:12]
    in_sems, hot_sem, block_sems, out_sems, part_sems = refs[12:]
    ga_copies = loads(ga_refs, ga_buf, in_sems)
    hot_copy = pltpu.make_async_copy(hot_any, hot_ref, hot_sem.at[0])
    hot_copy.start()
    for copies in ga_copies:
        start(copies)

    def block_loads(b):
        pairs = ((qg_any, qg_ref), (p_any, p_ref), (k_any, k_ref), (v_any, v_ref))
        return [
            pltpu.make_async_copy(far.at[b], near.at[b], block_sems.at[i, b])
            for i, (far, near) in enumerate(pairs)
        ]

    def block_stores(b):
        return [
            pltpu.make_async_copy(dk_ref.at[b], dk_any.at[b], out_sems.at[0, b]),
            pltpu.make_async_copy(dv_ref.at[b], dv_any.at[b], out_sems.at[1, b]),
        ]

    block_count, _, width = k_ref.shape
    heads = width // HD
    rows = part_refs[0].shape[0]
    groups = chunks // span
    scale = HD ** (-0.5)

    for b in range(block_count):
        start(block_loads(b))
    hot_copy.wait()
    for g in range(groups):
        for i in range(span):
            wait(ga_copies[g * span + i])
        ga_group = joined([ga_buf[g * span + i] for i in range(span)], 0)
        gag_ref[:, g * cap : (g + 1) * cap, :] = (
            mm(hot_ref[g], ga_group).astype(BF16).reshape(block_count, cap, width + HD)
        )
    last = lax.broadcasted_iota(jnp.int32, (BLOCK, groups * cap), 0) == BLOCK - 1

    pairs = [slice(p * 2 * HD, (p + 1) * 2 * HD) for p in range(heads // 2)]

    def some_blocks(step, carry):
        blocks = [step * TOGETHER + u for u in range(TOGETHER)]
        for b in blocks:
            wait(block_loads(b))
        grads = [
            [mm(diagonal(v_ref[b, :, cols]), gag_ref[b, :, cols], NT) for cols in pairs]
            for b in blocks
        ]
        gated, scores = [], []
        for b, grad_pairs in zip(blocks, grads):
            tail = gag_ref[b, :, width:].astype(F32).T
            tail = [tail[i * heads : (i + 1) * heads] for i in range(5)]
            dots = tail[0] + tail[1]
            gates = jnp.exp(jnp.minimum(logit_ref[b] - (tail[2] + tail[3] + tail[4]), 0.0))
            for p in range(heads // 2):
                both = p_ref[b, p].astype(F32)
                low, high = [], []
                for i in range(2):
                    at = slice(i * BLOCK, (i + 1) * BLOCK)
                    h = 2 * p + i
                    gate = gates[h : h + 1, :]
                    grad, probs = grad_pairs[p][at], both[at]
                    delta = jnp.sum(probs * grad, axis=0, keepdims=True)
                    weight = probs * gate
                    extra = jnp.where(last, scale * gate * (delta - dots[h : h + 1, :]), 0.0)
                    low.append((weight * (scale * (grad - delta)) + extra).astype(BF16))
                    high.append(weight.astype(BF16))
                scores.append(low)
                gated.append(high)
        for u, b in enumerate(blocks):
            for p, cols in enumerate(pairs):
                score, weight = scores[u * len(pairs) + p], gated[u * len(pairs) + p]
                for i in range(2):
                    head = slice((2 * p + i) * HD, (2 * p + i + 1) * HD)
                    dv_ref[b, :, head] = mm(weight[i], gag_ref[b, :, head])
                    dk_ref[b, :, head] = mm(score[i], qg_ref[b, :, head])
                both = jnp.concatenate(score, axis=0)
                dq_ref[b, :, cols] = mm(both, diagonal(k_ref[b, :, cols]), TN).astype(BF16)
        for b in blocks:
            start(block_stores(b))
        return carry

    lax.fori_loop(0, block_count // TOGETHER, some_blocks, 0)

    part_copies = []

    for g in range(groups):
        slots = dq_ref[:, g * cap : (g + 1) * cap, :].reshape(block_count * cap, width)
        part = mm(hot_ref[g], slots, TN).astype(BF16)
        for i in range(span):
            m = g * span + i
            ga_buf[m, :, :width] = part[i * rows : (i + 1) * rows]
            copy = pltpu.make_async_copy(
                ga_buf.at[m, :, pl.ds(0, width)], part_refs[m], part_sems.at[m]
            )
            copy.start()
            part_copies.append(copy)
    for b in range(block_count):
        wait(block_stores(b))
    wait(part_copies)


def weight_kernel(counts, first, me_ref, cols_ref, *refs):
    attns, (*before, out_ref) = dealt(refs, counts)
    me = me_ref[0]
    columns = joined([cols_ref[me ^ (first + m)] for m in range(len(counts))], 0)
    total = mm(columns, joined([whole(pieces) for pieces in attns], 0), TN)
    for ref in before:
        total = total + ref[...]
    out_ref[...] = total


def swap(x, bits):
    count = lax.axis_size("ctx")
    return lax.ppermute(x, "ctx", [(i, i ^ bits) for i in range(count)])


def after(x, *others):
    return lax.optimization_barrier((x, *others))[0]


def flat(lists):
    return [x for pieces in lists for x in pieces]


def spread_near(x):
    chips = lax.axis_size("ctx") // 2
    return [[x]] + [[swap(x, 2 * j)] for j in range(1, chips if chips != 4 else 3)]


def spread_far(near, half, *before):
    if len(near) != 3:
        return near
    (x_way,), (y_way,) = near[1:]
    far = [swap(after(x_way[:half], *before), 4), swap(after(y_way[half:], *before), 2)]
    return near + [far]


def spread_chips(x, half, *before):
    return spread_far(spread_near(x), half, *before)


def spread_halves(top, low):
    chips = lax.axis_size("ctx") // 2
    if chips != 4:
        return [[swap(x, 2 * j) if j else x for x in (top, low)] for j in range(chips)]
    x_top, y_low = swap(top, 2), swap(low, 4)
    x_low, y_top = swap(low, 2), swap(top, 4)
    return [[top, low], [x_top, x_low], [y_top, y_low], [swap(x_top, 4), swap(y_low, 2)]]


def with_cores(lists, *before):
    both = []
    for pieces in lists:
        if before and pieces is lists[-1]:
            pieces = [after(piece, *before) for piece in pieces]
        both += [pieces, [swap(piece, 1) for piece in pieces]]
    return both


def from_core(parts, *before):
    received = [None] * (len(parts) // 2)
    for j in reversed(range(len(received))):
        received[j] = swap(after(parts[2 * j + 1], *before), 1)
    return received


def collect_chips(parts, received):
    chips = len(received)

    def both(j, rows, extra=None, earlier=None):
        mine = parts[2 * j] if earlier is None else after(parts[2 * j], earlier)
        total = mine[rows].astype(F32) + received[j][rows].astype(F32)
        if extra is not None:
            total = total + extra.astype(F32)
        return total.astype(BF16)

    terms = [[parts[0]], [received[0]]]
    if chips != 4:
        return terms + [[swap(both(j, slice(None)), 2 * j)] for j in range(1, chips)], []
    half = parts[0].shape[0] // 2
    top, low = slice(0, half), slice(half, None)
    x_sum, y_sum = both(3, top), both(3, low)
    x_far, y_far = swap(x_sum, 2), swap(y_sum, 4)
    x_sum, y_sum = both(1, top, None, x_sum), both(2, low, None, y_sum)
    x_top, y_low = swap(x_sum, 2), swap(y_sum, 4)
    x_sum, y_sum = both(1, low, y_far, x_sum), both(2, top, x_far, y_sum)
    x_low, y_top = swap(x_sum, 2), swap(y_sum, 4)
    return terms + [[x_top, x_low], [y_top, y_low]], [x_sum, y_sum]


def merge_chips(parts, received, heads, between):
    chips = len(received)
    rows = parts[0].shape[0]
    half = rows // 2

    def merged(ins, plan):
        return pl.pallas_call(
            functools.partial(merge_kernel, plan, heads),
            out_shape=[
                jax.ShapeDtypeStruct((terms[0][2], ins[0].shape[1]), BF16) for terms in plan
            ],
            in_specs=[pl.BlockSpec(memory_space=pltpu.VMEM)] * len(ins),
            out_specs=[pl.BlockSpec(memory_space=pltpu.VMEM)] * len(plan),
            compiler_params=pltpu.CompilerParams(vmem_limit_bytes=SOME),
            name="merge",
        )(*ins)

    terms = [[parts[0]], [received[0]]]
    if chips != 4:
        for j in range(1, chips):
            (both,) = merged([parts[2 * j], received[j]], [[(0, 0, rows), (1, 0, rows)]])
            terms.append([swap(both, 2 * j)])
        return terms, between(received[0])
    top, low = (0, half), (half, half)
    x_far, y_far = merged(
        [parts[6], received[3]], [[(0, *top), (1, *top)], [(0, *low), (1, *low)]]
    )
    x_far, y_far = swap(x_far, 2), swap(y_far, 4)
    ins = [parts[2], received[1], parts[4], received[2]]
    x_top, y_low = merged(ins, [[(0, *top), (1, *top)], [(2, *low), (3, *low)]])
    x_top, y_low = swap(x_top, 2), swap(y_low, 4)
    x_low, y_top = merged(
        ins + [y_far, x_far],
        [[(0, *low), (1, *low), (4, *top)], [(2, *top), (3, *top), (5, *top)]],
    )
    done = between(x_low, y_top)
    x_low, y_top = swap(x_low, 2), swap(y_top, 4)
    return terms + [[x_top, x_low], [y_top, y_low]], done


def spread_line(x):
    lines = lax.axis_size("head")
    ups, downs = [x], [x]
    for d in range(1, lines):
        up = [(i, i + 1) for i in range(d - 1, lines - 1)]
        down = [(i, i - 1) for i in range(1, lines - d + 1)]
        if d == lines - 1 and lines > 2:
            last = jnp.where(lax.axis_index("head") == lines - 2, ups[-1], downs[-1])
            last = lax.ppermute(last, "head", up + down)
            ups.append(last)
            downs.append(last)
        else:
            ups.append(lax.ppermute(ups[-1], "head", up))
            downs.append(lax.ppermute(downs[-1], "head", down))
    return ups[1:], downs[1:]


def body(queries, key_rows, value_rows, selected, out_grad, out_weight):
    chunks = lax.axis_size("ctx")
    chips = chunks // 2
    lines = lax.axis_size("head")
    rows, width = queries.shape
    features = out_weight.shape[0]
    heads = width // HD
    block_count = key_rows.shape[0] // BLOCK
    block_total = block_count * chunks
    capacity = 2 * rows * TOPK // block_total
    span = max(1, 16 // capacity)
    cap = capacity * span
    groups = chunks // span
    slots = groups * cap
    index = lax.axis_index("ctx").astype(jnp.int32)
    me = index.reshape(1)
    keys = key_rows.reshape(block_count, BLOCK, width)
    values = value_rows.reshape(block_count, BLOCK, width)
    vmem = pl.BlockSpec(memory_space=pltpu.VMEM)
    smem = pl.BlockSpec(memory_space=pltpu.SMEM)
    anywhere = pl.BlockSpec(memory_space=pl.ANY)
    params = pltpu.CompilerParams(vmem_limit_bytes=MOST)
    small = pltpu.CompilerParams(vmem_limit_bytes=SOME)

    def shaped(shape, kind=BF16):
        return jax.ShapeDtypeStruct(shape, kind)

    ups, downs = spread_line(out_grad)
    packed = pl.pallas_call(
        pack_kernel,
        out_shape=shaped((rows + PAD, width)),
        in_specs=[vmem] * 2,
        out_specs=vmem,
        compiler_params=small,
        name="pack",
    )(selected.T, queries)
    query_chips = spread_chips(packed, rows // 2)
    query_all = with_cores(query_chips, ups[0], downs[0])

    outs = pl.pallas_call(
        functools.partial(forward_kernel, [len(pieces) for pieces in query_all], span, cap),
        out_shape=[shaped((rows, width + HD))] * chunks
        + [
            shaped((block_count, slots, width)),
            shaped((block_count, heads // 2, 2 * BLOCK, slots)),
            shaped((block_count, heads, slots), F32),
            shaped((groups, block_count * cap, rows * span)),
        ],
        in_specs=[smem, vmem] + [anywhere] * (2 + len(flat(query_all))),
        out_specs=[anywhere] * (chunks + 2) + [vmem, anywhere],
        scratch_shapes=[
            pltpu.VMEM((chunks, rows + PAD, width), BF16),
            pltpu.VMEM((chunks, rows, width + HD), BF16),
            pltpu.VMEM((block_count, BLOCK, width), BF16),
            pltpu.VMEM((block_count, BLOCK, width), BF16),
            pltpu.VMEM((block_count, slots, width), BF16),
            pltpu.VMEM((block_count, heads // 2, 2 * BLOCK, slots), BF16),
            pltpu.VMEM((groups, block_count * cap, rows * span), BF16),
            pltpu.VMEM((block_count, slots, HD), F32),
            pltpu.VMEM((block_count, slots, width), BF16),
            pltpu.SemaphoreType.DMA((len(flat(query_all)),)),
            pltpu.SemaphoreType.DMA((2,)),
            pltpu.SemaphoreType.DMA((chunks + 3,)),
        ],
        compiler_params=params,
        name="forward",
    )(me, keys[:, BLOCK - 1], keys, values, *flat(query_all))
    q_slots, probs, logits, hot = outs[chunks:]

    line = lax.axis_index("head").astype(jnp.int32).reshape(1)
    make_grad = pl.pallas_call(
        functools.partial(grad_kernel, lines),
        out_shape=[shaped((rows, width)), shaped((chunks, rows, features // chunks))],
        in_specs=[smem] + [anywhere] * (2 * lines),
        out_specs=[vmem] * 2,
        scratch_shapes=[
            pltpu.VMEM((lines, rows, width), BF16),
            pltpu.VMEM((lines, width, width), BF16),
            pltpu.SemaphoreType.DMA((lines,)),
            pltpu.SemaphoreType.DMA((lines,)),
        ],
        compiler_params=params,
        name="grad",
    )
    received = from_core(outs[:chunks], ups[1], downs[1])
    terms, (grad_attn, blocks) = merge_chips(
        outs[:chunks],
        received,
        heads,
        lambda *before: make_grad(after(line, *before), out_weight, out_grad, *ups, *downs),
    )
    attn_out, *extended = pl.pallas_call(
        functools.partial(finish_kernel, [len(pieces) for pieces in terms]),
        out_shape=[shaped((rows, width))] + [shaped((rows // 2, width + HD))] * 2,
        in_specs=[vmem] * (len(flat(terms)) + 1),
        out_specs=[vmem] * 3,
        compiler_params=small,
        name="finish",
    )(*flat(terms), grad_attn)
    grad_chips = spread_halves(*extended)
    grad_all = with_cores(grad_chips)
    arrived = flat(grad_chips[1:])
    attns = spread_near(after(attn_out, *flat(grad_chips[1:3])))
    columns = lax.all_to_all(
        after(blocks, *arrived), "ctx", split_axis=0, concat_axis=0, tiled=True
    )

    outs = pl.pallas_call(
        functools.partial(backward_kernel, [len(pieces) for pieces in grad_all], span, cap),
        out_shape=[shaped((rows, width))] * chunks
        + [shaped((block_count, BLOCK, width), F32)] * 2,
        in_specs=[vmem] + [anywhere] * (5 + len(flat(grad_all))),
        out_specs=[anywhere] * (chunks + 2),
        scratch_shapes=[
            pltpu.VMEM((chunks, rows, width + HD), BF16),
            pltpu.VMEM((groups, block_count * cap, rows * span), BF16),
            pltpu.VMEM((block_count, slots, width), BF16),
            pltpu.VMEM((block_count, heads // 2, 2 * BLOCK, slots), BF16),
            pltpu.VMEM((block_count, BLOCK, width), BF16),
            pltpu.VMEM((block_count, BLOCK, width), BF16),
            pltpu.VMEM((block_count, slots, width + HD), BF16),
            pltpu.VMEM((block_count, slots, width), BF16),
            pltpu.VMEM((block_count, BLOCK, width), F32),
            pltpu.VMEM((block_count, BLOCK, width), F32),
            pltpu.SemaphoreType.DMA((len(flat(grad_all)),)),
            pltpu.SemaphoreType.DMA((1,)),
            pltpu.SemaphoreType.DMA((4, block_count)),
            pltpu.SemaphoreType.DMA((2, block_count)),
            pltpu.SemaphoreType.DMA((chunks,)),
        ],
        compiler_params=params,
        name="backward",
    )(logits, hot, q_slots, probs, keys, values, *flat(grad_all))
    key_grad, value_grad = outs[chunks:]
    received = from_core(outs[:chunks], columns, *flat(attns[1:3]))
    terms, last_sums = collect_chips(outs[:chunks], received)
    near = [[after(x, *last_sums) for x in pieces] for pieces in attns]
    attns = with_cores(spread_far(near, rows // 2, terms[2][0], terms[-1][-1]))

    def weight_part(chosen, first, when, *before):
        return pl.pallas_call(
            functools.partial(weight_kernel, [len(pieces) for pieces in chosen], first),
            out_shape=shaped((features // chunks, width), F32),
            in_specs=[smem] + [vmem] * (1 + len(flat(chosen)) + len(before)),
            out_specs=vmem,
            compiler_params=small,
            name="weight",
        )(when, columns, *flat(chosen), *before)

    weight_near = weight_part(attns[:-2], 0, after(me, terms[2][0]))
    query_grad = pl.pallas_call(
        functools.partial(total_kernel, [len(pieces) for pieces in terms]),
        out_shape=shaped((rows, width), F32),
        in_specs=[vmem] * len(flat(terms)),
        out_specs=vmem,
        compiler_params=small,
        name="total",
    )(after(terms[0][0], weight_near), *flat(terms[1:]))
    weight_grad = weight_part(attns[-2:], chunks - 2, after(me, query_grad), weight_near)
    return (
        query_grad,
        key_grad.reshape(-1, width),
        value_grad.reshape(-1, width),
        weight_grad,
    )


def solution(mesh):
    return jax.shard_map(
        body,
        mesh=mesh,
        in_specs=(
            P("ctx", "head"),
            P("ctx", "head"),
            P("ctx", "head"),
            P("ctx", None),
            P("ctx", "head"),
            P(None, "head"),
        ),
        out_specs=(P("ctx", "head"), P("ctx", "head"), P("ctx", "head"), P("ctx", "head")),
        check_vma=False,
    )
```

```python
import functools

import jax
import jax.numpy as jnp
from jax import lax
from jax.experimental import pallas as pl
from jax.experimental.pallas import tpu as pltpu
from jax.sharding import PartitionSpec as P

HD = 128
BLOCK = 64
TOPK = 4
F32 = jnp.float32
BF16 = jnp.bfloat16
MOST = 58 * 1024 * 1024
SOME = 20 * 1024 * 1024
PAD = 16
TOGETHER = 4
LOW = -(2.0**99)
NN = (((1,), (0,)), ((), ()))
NT = (((1,), (1,)), ((), ()))
TN = (((0,), (0,)), ((), ()))


def mm(a, b, dims=NN):
    return lax.dot_general(a, b, dims, preferred_element_type=F32)


def joined(items, axis):
    return items[0] if len(items) == 1 else jnp.concatenate(items, axis=axis)


def dealt(refs, counts):
    lists, at = [], 0
    for count in counts:
        lists.append(refs[at : at + count])
        at += count
    return lists, refs[at:]


def loads(lists, buf, sems):
    copies, at = [], 0
    for i, refs in enumerate(lists):
        mine, row = [], 0
        for ref in refs:
            rows = ref.shape[0]
            mine.append(
                pltpu.make_async_copy(ref, buf.at[i, pl.ds(row, rows)], sems.at[at])
            )
            row += rows
            at += 1
        copies.append(mine)
    return copies


def start(copies):
    for copy in copies:
        copy.start()


def wait(copies):
    for copy in copies:
        copy.wait()


def whole(refs):
    return joined([ref[...] for ref in refs], 0)


def added(terms, cols):
    total = None
    for refs in terms:
        term = joined([ref[:, cols].astype(F32) for ref in refs], 0)
        total = term if total is None else total + term
    return total


def diagonal(pair):
    zero = jnp.zeros((pair.shape[0], HD), pair.dtype)
    top = jnp.concatenate([pair[:, :HD], zero], axis=1)
    low = jnp.concatenate([zero, pair[:, HD:]], axis=1)
    return jnp.concatenate([top, low], axis=0)


def pack_kernel(sel_ref, q_ref, out_ref):
    rows, width = q_ref.shape
    out_ref[:rows] = q_ref[...]
    digits = [(sel_ref[...] >> 4).astype(F32), (sel_ref[...] & 15).astype(F32)]
    if width > 2 * rows:
        digits.append(jnp.zeros((TOPK, width - 2 * rows), F32))
    lines = [jnp.concatenate(digits, axis=1), jnp.zeros((PAD - TOPK, width), F32)]
    out_ref[rows:] = jnp.concatenate(lines, axis=0).astype(BF16)


def forward_kernel(counts, span, cap, me_ref, mark_ref, k_any, v_any, *refs):
    chunks = len(counts)
    q_refs, refs = dealt(refs, counts)
    part_any, refs = refs[:chunks], refs[chunks:]
    qg_any, p_any, logit_ref, hot_any = refs[:4]
    q_buf, part_refs, k_ref, v_ref, qg_ref, p_ref, hot_ref, topg_ref, out_ref = refs[4:13]
    in_sems, kv_sems, out_sems = refs[13:]
    q_copies = loads(q_refs, q_buf, in_sems)
    kv_copies = [
        pltpu.make_async_copy(k_any, k_ref, kv_sems.at[0]),
        pltpu.make_async_copy(v_any, v_ref, kv_sems.at[1]),
    ]
    out_copies = [
        pltpu.make_async_copy(qg_ref, qg_any, out_sems.at[chunks]),
        pltpu.make_async_copy(hot_ref, hot_any, out_sems.at[chunks + 1]),
        pltpu.make_async_copy(p_ref, p_any, out_sems.at[chunks + 2]),
    ]
    for copies in q_copies:
        start(copies)
    start(kv_copies)
    block_count, _, width = k_ref.shape
    heads = width // HD
    rows = part_any[0].shape[0]
    group_rows = rows * span
    groups = chunks // span
    scale = HD ** (-0.5)
    rate = scale * 1.4426950408889634
    base = me_ref[0] * block_count

    before = lax.broadcasted_iota(jnp.int32, (group_rows, group_rows), 0)
    later = lax.broadcasted_iota(jnp.int32, (group_rows, group_rows), 1)
    earlier = (before < later).astype(BF16)
    own_ids = (base + lax.broadcasted_iota(jnp.int32, (block_count, group_rows), 0)).astype(F32)
    place = lax.broadcasted_iota(jnp.int32, (cap, group_rows), 0).astype(F32)
    zero = jnp.zeros((block_count, HD), BF16)
    wide_marks = jnp.concatenate(
        [
            jnp.concatenate(
                [mark_ref[:, i * HD : (i + 1) * HD] if i == h else zero for i in range(heads)], axis=1
            )
            for h in range(heads)
        ],
        axis=0,
    )
    q_groups, owns = [], []
    for g in range(groups):
        for i in range(span):
            wait(q_copies[g * span + i])
        packs = [q_buf[g * span + i] for i in range(span)]
        digits = [pack[rows : rows + PAD].astype(F32)[:TOPK] for pack in packs]
        picked = joined([16.0 * d[:, :rows] + d[:, rows : 2 * rows] for d in digits], 1)
        own = picked[0:1, :] == own_ids
        for t in range(1, TOPK):
            own = own | (picked[t : t + 1, :] == own_ids)
        owns.append(jnp.where(own, 1.0, 0.0))
        q_groups.append(joined([pack[:rows] for pack in packs], 0))
    own_all = jnp.concatenate(owns, axis=0)
    rank_all = jnp.where(own_all > 0.5, mm(own_all.astype(BF16), earlier), -1.0)
    hots = []
    for g in range(groups):
        rank = rank_all[g * block_count : (g + 1) * block_count]
        hots.append(
            jnp.concatenate(
                [
                    jnp.where(rank[b : b + 1, :] == place, 1.0, 0.0).astype(BF16)
                    for b in range(block_count)
                ],
                axis=0,
            )
        )
        hot_ref[g] = hots[g]
    all_marks = [mm(wide_marks, q_groups[g], NT) for g in range(groups)]
    for g in range(groups):
        qg_ref[:, g * cap : (g + 1) * cap, :] = (
            mm(hots[g], q_groups[g]).astype(BF16).reshape(block_count, cap, width)
        )
    tails = []
    for g in range(groups):
        tops, sums = [], []
        for h in range(heads):
            mark = scale * all_marks[g][h * block_count : (h + 1) * block_count]
            mark = jnp.where(owns[g] > 0.5, mark, LOW)
            top = jnp.max(mark, axis=0, keepdims=True).astype(BF16).astype(F32)
            tops.append(top)
            sums.append(jnp.sum(owns[g] * jnp.exp(mark - top), axis=0, keepdims=True))
        tops, sums = jnp.concatenate(tops, axis=0), jnp.concatenate(sums, axis=0)
        upper = sums.astype(BF16).astype(F32)
        spare = jnp.zeros((HD - 3 * heads, group_rows), F32)
        tails.append(jnp.concatenate([tops, upper, sums - upper, spare], axis=0))
    for g in range(groups):
        topg_ref[:, g * cap : (g + 1) * cap, :] = mm(hots[g], tails[g].astype(BF16), NT).reshape(
            block_count, cap, HD
        )
    for g in range(groups):
        for i in range(span):
            part_refs[g * span + i, :, width:] = (
                tails[g][:, i * rows : (i + 1) * rows].T.astype(BF16)
            )
    start(out_copies[:2])
    wait(kv_copies)

    pairs = [slice(p * 2 * HD, (p + 1) * 2 * HD) for p in range(heads // 2)]

    def some_blocks(step, carry):
        blocks = [step * TOGETHER + u for u in range(TOGETHER)]
        logits = [
            [mm(diagonal(k_ref[b, :, cols]), qg_ref[b, :, cols], NT) for cols in pairs]
            for b in blocks
        ]
        probs, gated, kept = [], [], []
        for b, scores in zip(blocks, logits):
            tops = topg_ref[b].T[:heads]
            marks = scale * jnp.concatenate(
                [scores[h // 2][(h % 2 + 1) * BLOCK - 1 : (h % 2 + 1) * BLOCK] for h in range(heads)],
                axis=0,
            )
            gates = jnp.exp(marks - tops)
            kept.append(marks)
            for p in range(heads // 2):
                low, high = [], []
                for i in range(2):
                    part = scores[p][i * BLOCK : (i + 1) * BLOCK]
                    weight = jnp.exp2(rate * (part - jnp.max(part, axis=0, keepdims=True)))
                    inverse = 1.0 / jnp.sum(weight, axis=0, keepdims=True)
                    gate = gates[2 * p + i : 2 * p + i + 1, :]
                    low.append((weight * inverse).astype(BF16))
                    high.append((weight * (inverse * gate)).astype(BF16))
                probs.append(jnp.concatenate(low, axis=0))
                gated.append(jnp.concatenate(high, axis=0))
        outs = []
        for u, b in enumerate(blocks):
            for p, cols in enumerate(pairs):
                both = gated[u * len(pairs) + p]
                outs.append(mm(both, diagonal(v_ref[b, :, cols]), TN).astype(BF16))
        for u, b in enumerate(blocks):
            logit_ref[b] = kept[u]
            for p, cols in enumerate(pairs):
                p_ref[b, p] = probs[u * len(pairs) + p]
                out_ref[b, :, cols] = outs[u * len(pairs) + p]
        return carry

    lax.fori_loop(0, block_count // TOGETHER, some_blocks, 0)
    start(out_copies[2:])

    for g in range(groups):
        slots = out_ref[:, g * cap : (g + 1) * cap, :].reshape(block_count * cap, width)
        part = mm(hot_ref[g], slots, TN).astype(BF16)
        for i in range(span):
            m = g * span + i
            part_refs[m, :, :width] = part[i * rows : (i + 1) * rows]
            copy = pltpu.make_async_copy(part_refs.at[m], part_any[m], out_sems.at[m])
            copy.start()
            out_copies.append(copy)
    wait(out_copies)


def shift(heads, *moves):
    row = lax.broadcasted_iota(jnp.int32, (HD, HD), 0)
    col = lax.broadcasted_iota(jnp.int32, (HD, HD), 1)
    total = jnp.zeros((HD, HD), F32)
    for source, target in moves:
        inside = (row >= source * heads) & (row < (source + 1) * heads)
        hit = inside & (col - target * heads == row - source * heads)
        total = jnp.where(hit, 1.0, total)
    return total.astype(BF16)


def blend(terms, heads):
    width = heads * HD
    tails = [joined([ref[rows, width:] for ref, rows in term], 0) for term in terms]
    wide = [tail.astype(F32) for tail in tails]
    top = wide[0]
    for tail in wide[1:]:
        top = jnp.maximum(top, tail)
    gather = shift(heads, (1, 0), (2, 0))
    factors = [jnp.exp(tail - top) for tail in wide]
    total = None
    for tail, factor in zip(tails, factors):
        share = factor * mm(tail, gather)
        total = share if total is None else total + share
    columns = []
    for h in range(heads):
        cols = slice(h * HD, (h + 1) * HD)
        column = None
        for term, factor in zip(terms, factors):
            values = joined([ref[rows, cols] for ref, rows in term], 0).astype(F32)
            part = factor[:, h : h + 1] * values
            column = part if column is None else column + part
        columns.append(column)
    return top, total, columns


def digits_of(tile, count):
    digits = []
    for _ in range(count):
        upper = tile.astype(BF16)
        digits.append(upper)
        tile = tile - upper.astype(F32)
    return digits


def packed_tail(digits, heads):
    total = None
    for i, digit in enumerate(digits):
        part = mm(digit, shift(heads, (0, i)))
        total = part if total is None else total + part
    return total.astype(BF16)


def merge_kernel(plan, heads, *refs):
    ins, outs = refs[: len(refs) - len(plan)], refs[len(refs) - len(plan) :]
    for terms, out_ref in zip(plan, outs):
        top, total, columns = blend(
            [[(ins[i], pl.ds(first, count))] for i, first, count in terms], heads
        )
        for h in range(heads):
            out_ref[:, h * HD : (h + 1) * HD] = columns[h].astype(BF16)
        out_ref[:, heads * HD :] = packed_tail([top.astype(BF16)] + digits_of(total, 2), heads)


def grad_kernel(lines, line_ref, w_ref, *refs):
    own_ref, up_refs, down_refs = refs[0], refs[1:lines], refs[lines : 2 * lines - 1]
    ga_ref, blocks_ref, full_ref, w_buf, sems, piece_sems = refs[2 * lines - 1 :]
    width = own_ref.shape[1]
    chunks, _, share = blocks_ref.shape
    line = line_ref[0]
    copies = [
        pltpu.make_async_copy(w_ref.at[pl.ds(i * width, width)], w_buf.at[i], sems.at[i])
        for i in range(lines)
    ]
    start(copies)

    def placed(ref, i):
        return pltpu.make_async_copy(ref, full_ref.at[i], piece_sems.at[i])

    placed(own_ref, line).start()
    for d in range(1, lines):

        @pl.when(line >= d)
        def _():
            placed(up_refs[d - 1], line - d).start()

        @pl.when(line + d < lines)
        def _():
            placed(down_refs[d - 1], line + d).start()

    for i in range(lines):
        placed(own_ref, i).wait()
    for j in range(chunks):
        first = j * share
        blocks_ref[j] = full_ref[first // width, :, first % width : first % width + share]
    total = None
    for i in range(lines):
        copies[i].wait()
        term = mm(full_ref[i], w_buf[i])
        total = term if total is None else total + term
    ga_ref[...] = total.astype(BF16)


def finish_kernel(counts, *refs):
    terms, (ga_ref, attn_ref, *ext_refs) = dealt(refs, counts)
    rows, width = ga_ref.shape
    half = rows // len(ext_refs)
    heads = width // HD
    top, total, columns = blend(
        [[(ref, slice(None)) for ref in pieces] for pieces in terms], heads
    )
    lane = lax.broadcasted_iota(jnp.int32, (rows, HD), 1)
    total = jnp.where(lane < heads, total, 1.0)
    inverse = 1.0 / total
    dots = jnp.zeros((rows, HD), F32)
    for i, ext_ref in enumerate(ext_refs):
        ext_ref[:, :width] = ga_ref[i * half : (i + 1) * half]
    for h in range(heads):
        cols = slice(h * HD, (h + 1) * HD)
        attn = columns[h] * inverse[:, h : h + 1]
        attn_ref[:, cols] = attn.astype(BF16)
        dot = jnp.sum(attn * ga_ref[:, cols].astype(F32), axis=1, keepdims=True)
        dots = jnp.where(lane == h, dot, dots)
    level = jnp.where(lane < heads, top + jnp.log(total), 0.0)
    tail = packed_tail(digits_of(dots, 2) + digits_of(level, 3), heads)
    for i, ext_ref in enumerate(ext_refs):
        ext_ref[:, width:] = tail[i * half : (i + 1) * half]


def total_kernel(counts, *refs):
    terms, (out_ref,) = dealt(refs, counts)
    for h in range(out_ref.shape[1] // HD):
        cols = slice(h * HD, (h + 1) * HD)
        out_ref[:, cols] = added(terms, cols)


def backward_kernel(counts, span, cap, logit_ref, hot_any, qg_any, p_any, k_any, v_any, *refs):
    chunks = len(counts)
    ga_refs, refs = dealt(refs, counts)
    part_refs, refs = refs[:chunks], refs[chunks:]
    dk_any, dv_any = refs[:2]
    ga_buf, hot_ref, qg_ref, p_ref, k_ref, v_ref, gag_ref, dq_ref, dk_ref, dv_ref = refs[2:12]
    in_sems, hot_sem, block_sems, out_sems, part_sems = refs[12:]
    ga_copies = loads(ga_refs, ga_buf, in_sems)
    hot_copy = pltpu.make_async_copy(hot_any, hot_ref, hot_sem.at[0])
    hot_copy.start()
    for copies in ga_copies:
        start(copies)

    def block_loads(b):
        pairs = ((qg_any, qg_ref), (p_any, p_ref), (k_any, k_ref), (v_any, v_ref))
        return [
            pltpu.make_async_copy(far.at[b], near.at[b], block_sems.at[i, b])
            for i, (far, near) in enumerate(pairs)
        ]

    def block_stores(b):
        return [
            pltpu.make_async_copy(dk_ref.at[b], dk_any.at[b], out_sems.at[0, b]),
            pltpu.make_async_copy(dv_ref.at[b], dv_any.at[b], out_sems.at[1, b]),
        ]

    block_count, _, width = k_ref.shape
    heads = width // HD
    rows = part_refs[0].shape[0]
    groups = chunks // span
    scale = HD ** (-0.5)

    for b in range(block_count):
        start(block_loads(b))
    hot_copy.wait()
    for g in range(groups):
        for i in range(span):
            wait(ga_copies[g * span + i])
        ga_group = joined([ga_buf[g * span + i] for i in range(span)], 0)
        gag_ref[:, g * cap : (g + 1) * cap, :] = (
            mm(hot_ref[g], ga_group).astype(BF16).reshape(block_count, cap, width + HD)
        )
    last = lax.broadcasted_iota(jnp.int32, (BLOCK, groups * cap), 0) == BLOCK - 1

    pairs = [slice(p * 2 * HD, (p + 1) * 2 * HD) for p in range(heads // 2)]

    def some_blocks(step, carry):
        blocks = [step * TOGETHER + u for u in range(TOGETHER)]
        for b in blocks:
            wait(block_loads(b))
        grads = [
            [mm(diagonal(v_ref[b, :, cols]), gag_ref[b, :, cols], NT) for cols in pairs]
            for b in blocks
        ]
        gated, scores = [], []
        for b, grad_pairs in zip(blocks, grads):
            tail = gag_ref[b, :, width:].astype(F32).T
            tail = [tail[i * heads : (i + 1) * heads] for i in range(5)]
            dots = tail[0] + tail[1]
            gates = jnp.exp(jnp.minimum(logit_ref[b] - (tail[2] + tail[3] + tail[4]), 0.0))
            for p in range(heads // 2):
                both = p_ref[b, p].astype(F32)
                low, high = [], []
                for i in range(2):
                    at = slice(i * BLOCK, (i + 1) * BLOCK)
                    h = 2 * p + i
                    gate = gates[h : h + 1, :]
                    grad, probs = grad_pairs[p][at], both[at]
                    delta = jnp.sum(probs * grad, axis=0, keepdims=True)
                    weight = probs * gate
                    extra = jnp.where(last, scale * gate * (delta - dots[h : h + 1, :]), 0.0)
                    low.append((weight * (scale * (grad - delta)) + extra).astype(BF16))
                    high.append(weight.astype(BF16))
                scores.append(low)
                gated.append(high)
        for u, b in enumerate(blocks):
            for p, cols in enumerate(pairs):
                score, weight = scores[u * len(pairs) + p], gated[u * len(pairs) + p]
                for i in range(2):
                    head = slice((2 * p + i) * HD, (2 * p + i + 1) * HD)
                    dv_ref[b, :, head] = mm(weight[i], gag_ref[b, :, head])
                    dk_ref[b, :, head] = mm(score[i], qg_ref[b, :, head])
                both = jnp.concatenate(score, axis=0)
                dq_ref[b, :, cols] = mm(both, diagonal(k_ref[b, :, cols]), TN).astype(BF16)
        for b in blocks:
            start(block_stores(b))
        return carry

    lax.fori_loop(0, block_count // TOGETHER, some_blocks, 0)

    part_copies = []

    for g in range(groups):
        slots = dq_ref[:, g * cap : (g + 1) * cap, :].reshape(block_count * cap, width)
        part = mm(hot_ref[g], slots, TN).astype(BF16)
        for i in range(span):
            m = g * span + i
            ga_buf[m, :, :width] = part[i * rows : (i + 1) * rows]
            copy = pltpu.make_async_copy(
                ga_buf.at[m, :, pl.ds(0, width)], part_refs[m], part_sems.at[m]
            )
            copy.start()
            part_copies.append(copy)
    for b in range(block_count):
        wait(block_stores(b))
    wait(part_copies)


def weight_kernel(counts, first, me_ref, cols_ref, *refs):
    attns, (*before, out_ref) = dealt(refs, counts)
    me = me_ref[0]
    columns = joined([cols_ref[me ^ (first + m)] for m in range(len(counts))], 0)
    total = mm(columns, joined([whole(pieces) for pieces in attns], 0), TN)
    for ref in before:
        total = total + ref[...]
    out_ref[...] = total


def swap(x, bits):
    count = lax.axis_size("ctx")
    return lax.ppermute(x, "ctx", [(i, i ^ bits) for i in range(count)])


def after(x, *others):
    return lax.optimization_barrier((x, *others))[0]


def flat(lists):
    return [x for pieces in lists for x in pieces]


def spread_near(x):
    chips = lax.axis_size("ctx") // 2
    return [[x]] + [[swap(x, 2 * j)] for j in range(1, chips if chips != 4 else 3)]


def spread_far(near, half, *before):
    if len(near) != 3:
        return near
    (x_way,), (y_way,) = near[1:]
    far = [swap(after(x_way[:half], *before), 4), swap(after(y_way[half:], *before), 2)]
    return near + [far]


def spread_chips(x, half, *before):
    return spread_far(spread_near(x), half, *before)


def spread_halves(top, low):
    chips = lax.axis_size("ctx") // 2
    if chips != 4:
        return [[swap(x, 2 * j) if j else x for x in (top, low)] for j in range(chips)]
    x_top, y_low = swap(top, 2), swap(low, 4)
    x_low, y_top = swap(low, 2), swap(top, 4)
    return [[top, low], [x_top, x_low], [y_top, y_low], [swap(x_top, 4), swap(y_low, 2)]]


def with_cores(lists, *before):
    both = []
    for pieces in lists:
        if before and pieces is lists[-1]:
            pieces = [after(piece, *before) for piece in pieces]
        both += [pieces, [swap(piece, 1) for piece in pieces]]
    return both


def from_core(parts, *before):
    received = [None] * (len(parts) // 2)
    for j in reversed(range(len(received))):
        received[j] = swap(after(parts[2 * j + 1], *before), 1)
    return received


def collect_chips(parts, received):
    chips = len(received)

    def both(j, rows, extra=None, earlier=None):
        mine = parts[2 * j] if earlier is None else after(parts[2 * j], earlier)
        total = mine[rows].astype(F32) + received[j][rows].astype(F32)
        if extra is not None:
            total = total + extra.astype(F32)
        return total.astype(BF16)

    terms = [[parts[0]], [received[0]]]
    if chips != 4:
        return terms + [[swap(both(j, slice(None)), 2 * j)] for j in range(1, chips)], []
    half = parts[0].shape[0] // 2
    top, low = slice(0, half), slice(half, None)
    x_sum, y_sum = both(3, top), both(3, low)
    x_far, y_far = swap(x_sum, 2), swap(y_sum, 4)
    x_sum, y_sum = both(1, top, None, x_sum), both(2, low, None, y_sum)
    x_top, y_low = swap(x_sum, 2), swap(y_sum, 4)
    x_sum, y_sum = both(1, low, y_far, x_sum), both(2, top, x_far, y_sum)
    x_low, y_top = swap(x_sum, 2), swap(y_sum, 4)
    return terms + [[x_top, x_low], [y_top, y_low]], [x_sum, y_sum]


def merge_chips(parts, received, heads, between):
    chips = len(received)
    rows = parts[0].shape[0]
    half = rows // 2

    def merged(ins, plan):
        return pl.pallas_call(
            functools.partial(merge_kernel, plan, heads),
            out_shape=[
                jax.ShapeDtypeStruct((terms[0][2], ins[0].shape[1]), BF16) for terms in plan
            ],
            in_specs=[pl.BlockSpec(memory_space=pltpu.VMEM)] * len(ins),
            out_specs=[pl.BlockSpec(memory_space=pltpu.VMEM)] * len(plan),
            compiler_params=pltpu.CompilerParams(vmem_limit_bytes=SOME),
            name="merge",
        )(*ins)

    terms = [[parts[0]], [received[0]]]
    if chips != 4:
        for j in range(1, chips):
            (both,) = merged([parts[2 * j], received[j]], [[(0, 0, rows), (1, 0, rows)]])
            terms.append([swap(both, 2 * j)])
        return terms, between(received[0])
    top, low = (0, half), (half, half)
    x_far, y_far = merged(
        [parts[6], received[3]], [[(0, *top), (1, *top)], [(0, *low), (1, *low)]]
    )
    x_far, y_far = swap(x_far, 2), swap(y_far, 4)
    ins = [parts[2], received[1], parts[4], received[2]]
    x_top, y_low = merged(ins, [[(0, *top), (1, *top)], [(2, *low), (3, *low)]])
    x_top, y_low = swap(x_top, 2), swap(y_low, 4)
    x_low, y_top = merged(
        ins + [y_far, x_far],
        [[(0, *low), (1, *low), (4, *top)], [(2, *top), (3, *top), (5, *top)]],
    )
    done = between(x_low, y_top)
    x_low, y_top = swap(x_low, 2), swap(y_top, 4)
    return terms + [[x_top, x_low], [y_top, y_low]], done


def spread_line(x):
    lines = lax.axis_size("head")
    ups, downs = [x], [x]
    for d in range(1, lines):
        up = [(i, i + 1) for i in range(d - 1, lines - 1)]
        down = [(i, i - 1) for i in range(1, lines - d + 1)]
        if d == lines - 1 and lines > 2:
            last = jnp.where(lax.axis_index("head") == lines - 2, ups[-1], downs[-1])
            last = lax.ppermute(last, "head", up + down)
            ups.append(last)
            downs.append(last)
        else:
            ups.append(lax.ppermute(ups[-1], "head", up))
            downs.append(lax.ppermute(downs[-1], "head", down))
    return ups[1:], downs[1:]


def body(queries, key_rows, value_rows, selected, out_grad, out_weight):
    chunks = lax.axis_size("ctx")
    chips = chunks // 2
    lines = lax.axis_size("head")
    rows, width = queries.shape
    features = out_weight.shape[0]
    heads = width // HD
    block_count = key_rows.shape[0] // BLOCK
    block_total = block_count * chunks
    capacity = 2 * rows * TOPK // block_total
    span = max(1, 16 // capacity)
    cap = capacity * span
    groups = chunks // span
    slots = groups * cap
    index = lax.axis_index("ctx").astype(jnp.int32)
    me = index.reshape(1)
    keys = key_rows.reshape(block_count, BLOCK, width)
    values = value_rows.reshape(block_count, BLOCK, width)
    vmem = pl.BlockSpec(memory_space=pltpu.VMEM)
    smem = pl.BlockSpec(memory_space=pltpu.SMEM)
    anywhere = pl.BlockSpec(memory_space=pl.ANY)
    params = pltpu.CompilerParams(vmem_limit_bytes=MOST)
    small = pltpu.CompilerParams(vmem_limit_bytes=SOME)

    def shaped(shape, kind=BF16):
        return jax.ShapeDtypeStruct(shape, kind)

    ups, downs = spread_line(out_grad)
    packed = pl.pallas_call(
        pack_kernel,
        out_shape=shaped((rows + PAD, width)),
        in_specs=[vmem] * 2,
        out_specs=vmem,
        compiler_params=small,
        name="pack",
    )(selected.T, queries)
    query_chips = spread_chips(packed, rows // 2)
    query_all = with_cores(query_chips, ups[0], downs[0])

    outs = pl.pallas_call(
        functools.partial(forward_kernel, [len(pieces) for pieces in query_all], span, cap),
        out_shape=[shaped((rows, width + HD))] * chunks
        + [
            shaped((block_count, slots, width)),
            shaped((block_count, heads // 2, 2 * BLOCK, slots)),
            shaped((block_count, heads, slots), F32),
            shaped((groups, block_count * cap, rows * span)),
        ],
        in_specs=[smem, vmem] + [anywhere] * (2 + len(flat(query_all))),
        out_specs=[anywhere] * (chunks + 2) + [vmem, anywhere],
        scratch_shapes=[
            pltpu.VMEM((chunks, rows + PAD, width), BF16),
            pltpu.VMEM((chunks, rows, width + HD), BF16),
            pltpu.VMEM((block_count, BLOCK, width), BF16),
            pltpu.VMEM((block_count, BLOCK, width), BF16),
            pltpu.VMEM((block_count, slots, width), BF16),
            pltpu.VMEM((block_count, heads // 2, 2 * BLOCK, slots), BF16),
            pltpu.VMEM((groups, block_count * cap, rows * span), BF16),
            pltpu.VMEM((block_count, slots, HD), F32),
            pltpu.VMEM((block_count, slots, width), BF16),
            pltpu.SemaphoreType.DMA((len(flat(query_all)),)),
            pltpu.SemaphoreType.DMA((2,)),
            pltpu.SemaphoreType.DMA((chunks + 3,)),
        ],
        compiler_params=params,
        name="forward",
    )(me, keys[:, BLOCK - 1], keys, values, *flat(query_all))
    q_slots, probs, logits, hot = outs[chunks:]

    line = lax.axis_index("head").astype(jnp.int32).reshape(1)
    make_grad = pl.pallas_call(
        functools.partial(grad_kernel, lines),
        out_shape=[shaped((rows, width)), shaped((chunks, rows, features // chunks))],
        in_specs=[smem] + [anywhere] * (2 * lines),
        out_specs=[vmem] * 2,
        scratch_shapes=[
            pltpu.VMEM((lines, rows, width), BF16),
            pltpu.VMEM((lines, width, width), BF16),
            pltpu.SemaphoreType.DMA((lines,)),
            pltpu.SemaphoreType.DMA((lines,)),
        ],
        compiler_params=params,
        name="grad",
    )
    received = from_core(outs[:chunks], ups[1], downs[1])
    terms, (grad_attn, blocks) = merge_chips(
        outs[:chunks],
        received,
        heads,
        lambda *before: make_grad(after(line, *before), out_weight, out_grad, *ups, *downs),
    )
    attn_out, *extended = pl.pallas_call(
        functools.partial(finish_kernel, [len(pieces) for pieces in terms]),
        out_shape=[shaped((rows, width))] + [shaped((rows // 2, width + HD))] * 2,
        in_specs=[vmem] * (len(flat(terms)) + 1),
        out_specs=[vmem] * 3,
        compiler_params=small,
        name="finish",
    )(*flat(terms), grad_attn)
    grad_chips = spread_halves(*extended)
    grad_all = with_cores(grad_chips)
    attns = spread_near(after(attn_out, *flat(grad_chips[1:3])))
    columns = lax.all_to_all(
        after(blocks, *flat(attns[1:3]), *flat(grad_chips[3:])), "ctx", split_axis=0, concat_axis=0, tiled=True
    )

    outs = pl.pallas_call(
        functools.partial(backward_kernel, [len(pieces) for pieces in grad_all], span, cap),
        out_shape=[shaped((rows, width))] * chunks
        + [shaped((block_count, BLOCK, width), F32)] * 2,
        in_specs=[vmem] + [anywhere] * (5 + len(flat(grad_all))),
        out_specs=[anywhere] * (chunks + 2),
        scratch_shapes=[
            pltpu.VMEM((chunks, rows, width + HD), BF16),
            pltpu.VMEM((groups, block_count * cap, rows * span), BF16),
            pltpu.VMEM((block_count, slots, width), BF16),
            pltpu.VMEM((block_count, heads // 2, 2 * BLOCK, slots), BF16),
            pltpu.VMEM((block_count, BLOCK, width), BF16),
            pltpu.VMEM((block_count, BLOCK, width), BF16),
            pltpu.VMEM((block_count, slots, width + HD), BF16),
            pltpu.VMEM((block_count, slots, width), BF16),
            pltpu.VMEM((block_count, BLOCK, width), F32),
            pltpu.VMEM((block_count, BLOCK, width), F32),
            pltpu.SemaphoreType.DMA((len(flat(grad_all)),)),
            pltpu.SemaphoreType.DMA((1,)),
            pltpu.SemaphoreType.DMA((4, block_count)),
            pltpu.SemaphoreType.DMA((2, block_count)),
            pltpu.SemaphoreType.DMA((chunks,)),
        ],
        compiler_params=params,
        name="backward",
    )(logits, hot, q_slots, probs, keys, values, *flat(grad_all))
    key_grad, value_grad = outs[chunks:]
    received = from_core(outs[:chunks], columns)
    terms, last_sums = collect_chips(outs[:chunks], received)
    near = [[after(x, *last_sums) for x in pieces] for pieces in attns]
    attns = with_cores(spread_far(near, rows // 2, terms[2][-1], terms[-1][0]))

    def weight_part(chosen, first, when, *before):
        return pl.pallas_call(
            functools.partial(weight_kernel, [len(pieces) for pieces in chosen], first),
            out_shape=shaped((features // chunks, width), F32),
            in_specs=[smem] + [vmem] * (1 + len(flat(chosen)) + len(before)),
            out_specs=vmem,
            compiler_params=small,
            name="weight",
        )(when, columns, *flat(chosen), *before)

    weight_near = weight_part(attns[:-2], 0, after(me, terms[2][0]))
    query_grad = pl.pallas_call(
        functools.partial(total_kernel, [len(pieces) for pieces in terms]),
        out_shape=shaped((rows, width), F32),
        in_specs=[vmem] * len(flat(terms)),
        out_specs=vmem,
        compiler_params=small,
        name="total",
    )(after(terms[0][0], weight_near), *flat(terms[1:]))
    weight_grad = weight_part(attns[-2:], chunks - 2, after(me, query_grad), weight_near)
    return (
        query_grad,
        key_grad.reshape(-1, width),
        value_grad.reshape(-1, width),
        weight_grad,
    )


def solution(mesh):
    return jax.shard_map(
        body,
        mesh=mesh,
        in_specs=(
            P("ctx", "head"),
            P("ctx", "head"),
            P("ctx", "head"),
            P("ctx", None),
            P("ctx", "head"),
            P(None, "head"),
        ),
        out_specs=(P("ctx", "head"), P("ctx", "head"), P("ctx", "head"), P("ctx", "head")),
        check_vma=False,
    )
```

```python
import functools

import jax
import jax.numpy as jnp
from jax import lax
from jax.experimental import pallas as pl
from jax.experimental.pallas import tpu as pltpu
from jax.sharding import PartitionSpec as P

HD = 128
BLOCK = 64
TOPK = 4
F32 = jnp.float32
BF16 = jnp.bfloat16
MOST = 58 * 1024 * 1024
SOME = 20 * 1024 * 1024
PAD = 16
TOGETHER = 4
LOW = -(2.0**99)
NN = (((1,), (0,)), ((), ()))
NT = (((1,), (1,)), ((), ()))
TN = (((0,), (0,)), ((), ()))


def mm(a, b, dims=NN):
    return lax.dot_general(a, b, dims, preferred_element_type=F32)


def joined(items, axis):
    return items[0] if len(items) == 1 else jnp.concatenate(items, axis=axis)


def dealt(refs, counts):
    lists, at = [], 0
    for count in counts:
        lists.append(refs[at : at + count])
        at += count
    return lists, refs[at:]


def loads(lists, buf, sems):
    copies, at = [], 0
    for i, refs in enumerate(lists):
        mine, row = [], 0
        for ref in refs:
            rows = ref.shape[0]
            mine.append(
                pltpu.make_async_copy(ref, buf.at[i, pl.ds(row, rows)], sems.at[at])
            )
            row += rows
            at += 1
        copies.append(mine)
    return copies


def start(copies):
    for copy in copies:
        copy.start()


def wait(copies):
    for copy in copies:
        copy.wait()


def whole(refs):
    return joined([ref[...] for ref in refs], 0)


def added(terms, cols):
    total = None
    for refs in terms:
        term = joined([ref[:, cols].astype(F32) for ref in refs], 0)
        total = term if total is None else total + term
    return total


def diagonal(pair):
    zero = jnp.zeros((pair.shape[0], HD), pair.dtype)
    top = jnp.concatenate([pair[:, :HD], zero], axis=1)
    low = jnp.concatenate([zero, pair[:, HD:]], axis=1)
    return jnp.concatenate([top, low], axis=0)


def pack_kernel(sel_ref, q_ref, out_ref):
    rows, width = q_ref.shape
    out_ref[:rows] = q_ref[...]
    digits = [(sel_ref[...] >> 4).astype(F32), (sel_ref[...] & 15).astype(F32)]
    if width > 2 * rows:
        digits.append(jnp.zeros((TOPK, width - 2 * rows), F32))
    lines = [jnp.concatenate(digits, axis=1), jnp.zeros((PAD - TOPK, width), F32)]
    out_ref[rows:] = jnp.concatenate(lines, axis=0).astype(BF16)


def forward_kernel(counts, span, cap, me_ref, mark_ref, k_any, v_any, *refs):
    chunks = len(counts)
    q_refs, refs = dealt(refs, counts)
    part_any, refs = refs[:chunks], refs[chunks:]
    qg_any, p_any, logit_ref, hot_any = refs[:4]
    q_buf, part_refs, k_ref, v_ref, qg_ref, p_ref, hot_ref, topg_ref, out_ref = refs[4:13]
    in_sems, kv_sems, out_sems = refs[13:]
    q_copies = loads(q_refs, q_buf, in_sems)
    kv_copies = [
        pltpu.make_async_copy(k_any, k_ref, kv_sems.at[0]),
        pltpu.make_async_copy(v_any, v_ref, kv_sems.at[1]),
    ]
    out_copies = [
        pltpu.make_async_copy(qg_ref, qg_any, out_sems.at[chunks]),
        pltpu.make_async_copy(hot_ref, hot_any, out_sems.at[chunks + 1]),
        pltpu.make_async_copy(p_ref, p_any, out_sems.at[chunks + 2]),
    ]
    for copies in q_copies:
        start(copies)
    start(kv_copies)
    block_count, _, width = k_ref.shape
    heads = width // HD
    rows = part_any[0].shape[0]
    group_rows = rows * span
    groups = chunks // span
    scale = HD ** (-0.5)
    rate = scale * 1.4426950408889634
    base = me_ref[0] * block_count

    before = lax.broadcasted_iota(jnp.int32, (group_rows, group_rows), 0)
    later = lax.broadcasted_iota(jnp.int32, (group_rows, group_rows), 1)
    earlier = (before < later).astype(BF16)
    own_ids = (base + lax.broadcasted_iota(jnp.int32, (block_count, group_rows), 0)).astype(F32)
    place = lax.broadcasted_iota(jnp.int32, (cap, group_rows), 0).astype(F32)
    zero = jnp.zeros((block_count, HD), BF16)
    wide_marks = jnp.concatenate(
        [
            jnp.concatenate(
                [mark_ref[:, i * HD : (i + 1) * HD] if i == h else zero for i in range(heads)], axis=1
            )
            for h in range(heads)
        ],
        axis=0,
    )
    q_groups, owns = [], []
    for g in range(groups):
        for i in range(span):
            wait(q_copies[g * span + i])
        packs = [q_buf[g * span + i] for i in range(span)]
        digits = [pack[rows : rows + PAD].astype(F32)[:TOPK] for pack in packs]
        picked = joined([16.0 * d[:, :rows] + d[:, rows : 2 * rows] for d in digits], 1)
        own = picked[0:1, :] == own_ids
        for t in range(1, TOPK):
            own = own | (picked[t : t + 1, :] == own_ids)
        owns.append(jnp.where(own, 1.0, 0.0))
        q_groups.append(joined([pack[:rows] for pack in packs], 0))
    own_all = jnp.concatenate(owns, axis=0)
    rank_all = jnp.where(own_all > 0.5, mm(own_all.astype(BF16), earlier), -1.0)
    hots = []
    for g in range(groups):
        rank = rank_all[g * block_count : (g + 1) * block_count]
        hots.append(
            jnp.concatenate(
                [
                    jnp.where(rank[b : b + 1, :] == place, 1.0, 0.0).astype(BF16)
                    for b in range(block_count)
                ],
                axis=0,
            )
        )
        hot_ref[g] = hots[g]
    all_marks = [mm(wide_marks, q_groups[g], NT) for g in range(groups)]
    for g in range(groups):
        qg_ref[:, g * cap : (g + 1) * cap, :] = (
            mm(hots[g], q_groups[g]).astype(BF16).reshape(block_count, cap, width)
        )
    tails = []
    for g in range(groups):
        tops, sums = [], []
        for h in range(heads):
            mark = scale * all_marks[g][h * block_count : (h + 1) * block_count]
            mark = jnp.where(owns[g] > 0.5, mark, LOW)
            top = jnp.max(mark, axis=0, keepdims=True).astype(BF16).astype(F32)
            tops.append(top)
            sums.append(jnp.sum(owns[g] * jnp.exp(mark - top), axis=0, keepdims=True))
        tops, sums = jnp.concatenate(tops, axis=0), jnp.concatenate(sums, axis=0)
        upper = sums.astype(BF16).astype(F32)
        spare = jnp.zeros((HD - 3 * heads, group_rows), F32)
        tails.append(jnp.concatenate([tops, upper, sums - upper, spare], axis=0))
    for g in range(groups):
        topg_ref[:, g * cap : (g + 1) * cap, :] = mm(hots[g], tails[g].astype(BF16), NT).reshape(
            block_count, cap, HD
        )
    for g in range(groups):
        for i in range(span):
            part_refs[g * span + i, :, width:] = (
                tails[g][:, i * rows : (i + 1) * rows].T.astype(BF16)
            )
    start(out_copies[:2])
    wait(kv_copies)

    pairs = [slice(p * 2 * HD, (p + 1) * 2 * HD) for p in range(heads // 2)]

    def some_blocks(step, carry):
        blocks = [step * TOGETHER + u for u in range(TOGETHER)]
        logits = [
            [mm(diagonal(k_ref[b, :, cols]), qg_ref[b, :, cols], NT) for cols in pairs]
            for b in blocks
        ]
        probs, gated, kept = [], [], []
        for b, scores in zip(blocks, logits):
            tops = topg_ref[b].T[:heads]
            marks = scale * jnp.concatenate(
                [scores[h // 2][(h % 2 + 1) * BLOCK - 1 : (h % 2 + 1) * BLOCK] for h in range(heads)],
                axis=0,
            )
            gates = jnp.exp(marks - tops)
            kept.append(marks)
            for p in range(heads // 2):
                low, high = [], []
                for i in range(2):
                    part = scores[p][i * BLOCK : (i + 1) * BLOCK]
                    weight = jnp.exp2(rate * (part - jnp.max(part, axis=0, keepdims=True)))
                    inverse = 1.0 / jnp.sum(weight, axis=0, keepdims=True)
                    gate = gates[2 * p + i : 2 * p + i + 1, :]
                    low.append((weight * inverse).astype(BF16))
                    high.append((weight * (inverse * gate)).astype(BF16))
                probs.append(jnp.concatenate(low, axis=0))
                gated.append(jnp.concatenate(high, axis=0))
        outs = []
        for u, b in enumerate(blocks):
            for p, cols in enumerate(pairs):
                both = gated[u * len(pairs) + p]
                outs.append(mm(both, diagonal(v_ref[b, :, cols]), TN).astype(BF16))
        for u, b in enumerate(blocks):
            logit_ref[b] = kept[u]
            for p, cols in enumerate(pairs):
                p_ref[b, p] = probs[u * len(pairs) + p]
                out_ref[b, :, cols] = outs[u * len(pairs) + p]
        return carry

    lax.fori_loop(0, block_count // TOGETHER, some_blocks, 0)
    start(out_copies[2:])

    for g in range(groups):
        slots = out_ref[:, g * cap : (g + 1) * cap, :].reshape(block_count * cap, width)
        part = mm(hot_ref[g], slots, TN).astype(BF16)
        for i in range(span):
            m = g * span + i
            part_refs[m, :, :width] = part[i * rows : (i + 1) * rows]
            copy = pltpu.make_async_copy(part_refs.at[m], part_any[m], out_sems.at[m])
            copy.start()
            out_copies.append(copy)
    wait(out_copies)


def shift(heads, *moves):
    row = lax.broadcasted_iota(jnp.int32, (HD, HD), 0)
    col = lax.broadcasted_iota(jnp.int32, (HD, HD), 1)
    total = jnp.zeros((HD, HD), F32)
    for source, target in moves:
        inside = (row >= source * heads) & (row < (source + 1) * heads)
        hit = inside & (col - target * heads == row - source * heads)
        total = jnp.where(hit, 1.0, total)
    return total.astype(BF16)


def blend(terms, heads):
    width = heads * HD
    tails = [joined([ref[rows, width:] for ref, rows in term], 0) for term in terms]
    wide = [tail.astype(F32) for tail in tails]
    top = wide[0]
    for tail in wide[1:]:
        top = jnp.maximum(top, tail)
    gather = shift(heads, (1, 0), (2, 0))
    factors = [jnp.exp(tail - top) for tail in wide]
    total = None
    for tail, factor in zip(tails, factors):
        share = factor * mm(tail, gather)
        total = share if total is None else total + share
    columns = []
    for h in range(heads):
        cols = slice(h * HD, (h + 1) * HD)
        column = None
        for term, factor in zip(terms, factors):
            values = joined([ref[rows, cols] for ref, rows in term], 0).astype(F32)
            part = factor[:, h : h + 1] * values
            column = part if column is None else column + part
        columns.append(column)
    return top, total, columns


def digits_of(tile, count):
    digits = []
    for _ in range(count):
        upper = tile.astype(BF16)
        digits.append(upper)
        tile = tile - upper.astype(F32)
    return digits


def packed_tail(digits, heads):
    total = None
    for i, digit in enumerate(digits):
        part = mm(digit, shift(heads, (0, i)))
        total = part if total is None else total + part
    return total.astype(BF16)


def merge_kernel(plan, heads, *refs):
    ins, outs = refs[: len(refs) - len(plan)], refs[len(refs) - len(plan) :]
    for terms, out_ref in zip(plan, outs):
        top, total, columns = blend(
            [[(ins[i], pl.ds(first, count))] for i, first, count in terms], heads
        )
        for h in range(heads):
            out_ref[:, h * HD : (h + 1) * HD] = columns[h].astype(BF16)
        out_ref[:, heads * HD :] = packed_tail([top.astype(BF16)] + digits_of(total, 2), heads)


def grad_kernel(lines, line_ref, w_ref, *refs):
    own_ref, up_refs, down_refs = refs[0], refs[1:lines], refs[lines : 2 * lines - 1]
    ga_ref, blocks_ref, full_ref, w_buf, sems, piece_sems = refs[2 * lines - 1 :]
    width = own_ref.shape[1]
    chunks, _, share = blocks_ref.shape
    line = line_ref[0]
    copies = [
        pltpu.make_async_copy(w_ref.at[pl.ds(i * width, width)], w_buf.at[i], sems.at[i])
        for i in range(lines)
    ]
    start(copies)

    def placed(ref, i):
        return pltpu.make_async_copy(ref, full_ref.at[i], piece_sems.at[i])

    placed(own_ref, line).start()
    for d in range(1, lines):

        @pl.when(line >= d)
        def _():
            placed(up_refs[d - 1], line - d).start()

        @pl.when(line + d < lines)
        def _():
            placed(down_refs[d - 1], line + d).start()

    for i in range(lines):
        placed(own_ref, i).wait()
    for j in range(chunks):
        first = j * share
        blocks_ref[j] = full_ref[first // width, :, first % width : first % width + share]
    total = None
    for i in range(lines):
        copies[i].wait()
        term = mm(full_ref[i], w_buf[i])
        total = term if total is None else total + term
    ga_ref[...] = total.astype(BF16)


def finish_kernel(counts, *refs):
    terms, (ga_ref, attn_ref, *ext_refs) = dealt(refs, counts)
    rows, width = ga_ref.shape
    half = rows // len(ext_refs)
    heads = width // HD
    top, total, columns = blend(
        [[(ref, slice(None)) for ref in pieces] for pieces in terms], heads
    )
    lane = lax.broadcasted_iota(jnp.int32, (rows, HD), 1)
    total = jnp.where(lane < heads, total, 1.0)
    inverse = 1.0 / total
    dots = jnp.zeros((rows, HD), F32)
    for i, ext_ref in enumerate(ext_refs):
        ext_ref[:, :width] = ga_ref[i * half : (i + 1) * half]
    for h in range(heads):
        cols = slice(h * HD, (h + 1) * HD)
        attn = columns[h] * inverse[:, h : h + 1]
        attn_ref[:, cols] = attn.astype(BF16)
        dot = jnp.sum(attn * ga_ref[:, cols].astype(F32), axis=1, keepdims=True)
        dots = jnp.where(lane == h, dot, dots)
    level = jnp.where(lane < heads, top + jnp.log(total), 0.0)
    tail = packed_tail(digits_of(dots, 2) + digits_of(level, 3), heads)
    for i, ext_ref in enumerate(ext_refs):
        ext_ref[:, width:] = tail[i * half : (i + 1) * half]


def total_kernel(counts, *refs):
    terms, (out_ref,) = dealt(refs, counts)
    for h in range(out_ref.shape[1] // HD):
        cols = slice(h * HD, (h + 1) * HD)
        out_ref[:, cols] = added(terms, cols)


def backward_kernel(counts, span, cap, logit_ref, hot_any, qg_any, p_any, k_any, v_any, *refs):
    chunks = len(counts)
    ga_refs, refs = dealt(refs, counts)
    part_refs, refs = refs[:chunks], refs[chunks:]
    dk_any, dv_any = refs[:2]
    ga_buf, hot_ref, qg_ref, p_ref, k_ref, v_ref, gag_ref, dq_ref, dk_ref, dv_ref = refs[2:12]
    in_sems, hot_sem, block_sems, out_sems, part_sems = refs[12:]
    ga_copies = loads(ga_refs, ga_buf, in_sems)
    hot_copy = pltpu.make_async_copy(hot_any, hot_ref, hot_sem.at[0])
    hot_copy.start()
    for copies in ga_copies:
        start(copies)

    def block_loads(b):
        pairs = ((qg_any, qg_ref), (p_any, p_ref), (k_any, k_ref), (v_any, v_ref))
        return [
            pltpu.make_async_copy(far.at[b], near.at[b], block_sems.at[i, b])
            for i, (far, near) in enumerate(pairs)
        ]

    def block_stores(b):
        return [
            pltpu.make_async_copy(dk_ref.at[b], dk_any.at[b], out_sems.at[0, b]),
            pltpu.make_async_copy(dv_ref.at[b], dv_any.at[b], out_sems.at[1, b]),
        ]

    block_count, _, width = k_ref.shape
    heads = width // HD
    rows = part_refs[0].shape[0]
    groups = chunks // span
    scale = HD ** (-0.5)

    for b in range(block_count):
        start(block_loads(b))
    hot_copy.wait()
    for g in range(groups):
        for i in range(span):
            wait(ga_copies[g * span + i])
        ga_group = joined([ga_buf[g * span + i] for i in range(span)], 0)
        gag_ref[:, g * cap : (g + 1) * cap, :] = (
            mm(hot_ref[g], ga_group).astype(BF16).reshape(block_count, cap, width + HD)
        )
    last = lax.broadcasted_iota(jnp.int32, (BLOCK, groups * cap), 0) == BLOCK - 1

    pairs = [slice(p * 2 * HD, (p + 1) * 2 * HD) for p in range(heads // 2)]

    def some_blocks(step, carry):
        blocks = [step * TOGETHER + u for u in range(TOGETHER)]
        for b in blocks:
            wait(block_loads(b))
        grads = [
            [mm(diagonal(v_ref[b, :, cols]), gag_ref[b, :, cols], NT) for cols in pairs]
            for b in blocks
        ]
        gated, scores = [], []
        for b, grad_pairs in zip(blocks, grads):
            tail = gag_ref[b, :, width:].astype(F32).T
            tail = [tail[i * heads : (i + 1) * heads] for i in range(5)]
            dots = tail[0] + tail[1]
            gates = jnp.exp(jnp.minimum(logit_ref[b] - (tail[2] + tail[3] + tail[4]), 0.0))
            for p in range(heads // 2):
                both = p_ref[b, p].astype(F32)
                low, high = [], []
                for i in range(2):
                    at = slice(i * BLOCK, (i + 1) * BLOCK)
                    h = 2 * p + i
                    gate = gates[h : h + 1, :]
                    grad, probs = grad_pairs[p][at], both[at]
                    delta = jnp.sum(probs * grad, axis=0, keepdims=True)
                    weight = probs * gate
                    extra = jnp.where(last, scale * gate * (delta - dots[h : h + 1, :]), 0.0)
                    low.append((weight * (scale * (grad - delta)) + extra).astype(BF16))
                    high.append(weight.astype(BF16))
                scores.append(low)
                gated.append(high)
        for u, b in enumerate(blocks):
            for p, cols in enumerate(pairs):
                score, weight = scores[u * len(pairs) + p], gated[u * len(pairs) + p]
                for i in range(2):
                    head = slice((2 * p + i) * HD, (2 * p + i + 1) * HD)
                    dv_ref[b, :, head] = mm(weight[i], gag_ref[b, :, head])
                    dk_ref[b, :, head] = mm(score[i], qg_ref[b, :, head])
                both = jnp.concatenate(score, axis=0)
                dq_ref[b, :, cols] = mm(both, diagonal(k_ref[b, :, cols]), TN).astype(BF16)
        for b in blocks:
            start(block_stores(b))
        return carry

    lax.fori_loop(0, block_count // TOGETHER, some_blocks, 0)

    part_copies = []

    for g in range(groups):
        slots = dq_ref[:, g * cap : (g + 1) * cap, :].reshape(block_count * cap, width)
        part = mm(hot_ref[g], slots, TN).astype(BF16)
        for i in range(span):
            m = g * span + i
            ga_buf[m, :, :width] = part[i * rows : (i + 1) * rows]
            copy = pltpu.make_async_copy(
                ga_buf.at[m, :, pl.ds(0, width)], part_refs[m], part_sems.at[m]
            )
            copy.start()
            part_copies.append(copy)
    for b in range(block_count):
        wait(block_stores(b))
    wait(part_copies)


def weight_kernel(counts, me_ref, cols_ref, *refs):
    attns, (out_ref,) = dealt(refs, counts)
    me = me_ref[0]
    columns = joined([cols_ref[me ^ m] for m in range(len(counts))], 0)
    out_ref[...] = mm(columns, joined([whole(pieces) for pieces in attns], 0), TN)


def swap(x, bits):
    count = lax.axis_size("ctx")
    return lax.ppermute(x, "ctx", [(i, i ^ bits) for i in range(count)])


def after(x, *others):
    return lax.optimization_barrier((x, *others))[0]


def flat(lists):
    return [x for pieces in lists for x in pieces]


def spread_near(x):
    chips = lax.axis_size("ctx") // 2
    return [[x]] + [[swap(x, 2 * j)] for j in range(1, chips if chips != 4 else 3)]


def spread_far(near, half, *before):
    if len(near) != 3:
        return near
    (x_way,), (y_way,) = near[1:]
    far = [swap(after(x_way[:half], *before), 4), swap(after(y_way[half:], *before), 2)]
    return near + [far]


def spread_chips(x, half, *before):
    return spread_far(spread_near(x), half, *before)


def spread_halves(top, low):
    chips = lax.axis_size("ctx") // 2
    if chips != 4:
        return [[swap(x, 2 * j) if j else x for x in (top, low)] for j in range(chips)]
    x_top, y_low = swap(top, 2), swap(low, 4)
    x_low, y_top = swap(low, 2), swap(top, 4)
    return [[top, low], [x_top, x_low], [y_top, y_low], [swap(x_top, 4), swap(y_low, 2)]]


def with_cores(lists, *before):
    both = []
    for pieces in lists:
        if before and pieces is lists[-1]:
            pieces = [after(piece, *before) for piece in pieces]
        both += [pieces, [swap(piece, 1) for piece in pieces]]
    return both


def from_core(parts, *before):
    received = [None] * (len(parts) // 2)
    for j in reversed(range(len(received))):
        received[j] = swap(after(parts[2 * j + 1], *before), 1)
    return received


def collect_chips(parts, received):
    chips = len(received)

    def both(j, rows, extra=None, earlier=None):
        mine = parts[2 * j] if earlier is None else after(parts[2 * j], earlier)
        total = mine[rows].astype(F32) + received[j][rows].astype(F32)
        if extra is not None:
            total = total + extra.astype(F32)
        return total.astype(BF16)

    terms = [[parts[0]], [received[0]]]
    if chips != 4:
        return terms + [[swap(both(j, slice(None)), 2 * j)] for j in range(1, chips)], []
    half = parts[0].shape[0] // 2
    top, low = slice(0, half), slice(half, None)
    x_sum, y_sum = both(3, top), both(3, low)
    x_far, y_far = swap(x_sum, 2), swap(y_sum, 4)
    x_sum, y_sum = both(1, top, None, x_sum), both(2, low, None, y_sum)
    x_top, y_low = swap(x_sum, 2), swap(y_sum, 4)
    x_sum, y_sum = both(1, low, y_far, x_top), both(2, top, x_far, y_low)
    x_low, y_top = swap(x_sum, 2), swap(y_sum, 4)
    return terms + [[x_top, x_low], [y_top, y_low]], [x_sum, y_sum]


def merge_chips(parts, received, heads, between):
    chips = len(received)
    rows = parts[0].shape[0]
    half = rows // 2

    def merged(ins, plan):
        return pl.pallas_call(
            functools.partial(merge_kernel, plan, heads),
            out_shape=[
                jax.ShapeDtypeStruct((terms[0][2], ins[0].shape[1]), BF16) for terms in plan
            ],
            in_specs=[pl.BlockSpec(memory_space=pltpu.VMEM)] * len(ins),
            out_specs=[pl.BlockSpec(memory_space=pltpu.VMEM)] * len(plan),
            compiler_params=pltpu.CompilerParams(vmem_limit_bytes=SOME),
            name="merge",
        )(*ins)

    if chips != 4:
        terms = [[parts[0]], [swap(parts[1], 1)]]
        for j in range(1, chips):
            (both,) = merged([parts[2 * j], received[j]], [[(0, 0, rows), (1, 0, rows)]])
            terms.append([swap(both, 2 * j)])
        return terms, between(received[0])
    top, low = (0, half), (half, half)
    x_far, y_far = merged(
        [parts[6], received[3]], [[(0, *top), (1, *top)], [(0, *low), (1, *low)]]
    )
    x_far, y_far = swap(x_far, 2), swap(y_far, 4)
    ins = [parts[2], received[1], parts[4], received[2]]
    x_top, y_low = merged(ins, [[(0, *top), (1, *top)], [(2, *low), (3, *low)]])
    terms = [[parts[0]], [swap(after(parts[1], x_top), 1)]]
    x_top, y_low = swap(x_top, 2), swap(y_low, 4)
    x_low, y_top = merged(
        ins + [y_far, x_far],
        [[(0, *low), (1, *low), (4, *top)], [(2, *top), (3, *top), (5, *top)]],
    )
    done = between(x_low, y_top)
    x_low, y_top = swap(x_low, 2), swap(y_top, 4)
    return terms + [[x_top, x_low], [y_top, y_low]], done


def spread_line(x):
    lines = lax.axis_size("head")
    ups, downs = [x], [x]
    for d in range(1, lines):
        up = [(i, i + 1) for i in range(d - 1, lines - 1)]
        down = [(i, i - 1) for i in range(1, lines - d + 1)]
        if d == lines - 1 and lines > 2:
            last = jnp.where(lax.axis_index("head") == lines - 2, ups[-1], downs[-1])
            last = lax.ppermute(last, "head", up + down)
            ups.append(last)
            downs.append(last)
        else:
            ups.append(lax.ppermute(ups[-1], "head", up))
            downs.append(lax.ppermute(downs[-1], "head", down))
    return ups[1:], downs[1:]


def body(queries, key_rows, value_rows, selected, out_grad, out_weight):
    chunks = lax.axis_size("ctx")
    chips = chunks // 2
    lines = lax.axis_size("head")
    rows, width = queries.shape
    features = out_weight.shape[0]
    heads = width // HD
    block_count = key_rows.shape[0] // BLOCK
    block_total = block_count * chunks
    capacity = 2 * rows * TOPK // block_total
    span = max(1, 16 // capacity)
    cap = capacity * span
    groups = chunks // span
    slots = groups * cap
    index = lax.axis_index("ctx").astype(jnp.int32)
    me = index.reshape(1)
    keys = key_rows.reshape(block_count, BLOCK, width)
    values = value_rows.reshape(block_count, BLOCK, width)
    vmem = pl.BlockSpec(memory_space=pltpu.VMEM)
    smem = pl.BlockSpec(memory_space=pltpu.SMEM)
    anywhere = pl.BlockSpec(memory_space=pl.ANY)
    params = pltpu.CompilerParams(vmem_limit_bytes=MOST)
    small = pltpu.CompilerParams(vmem_limit_bytes=SOME)

    def shaped(shape, kind=BF16):
        return jax.ShapeDtypeStruct(shape, kind)

    ups, downs = spread_line(out_grad)
    packed = pl.pallas_call(
        pack_kernel,
        out_shape=shaped((rows + PAD, width)),
        in_specs=[vmem] * 2,
        out_specs=vmem,
        compiler_params=small,
        name="pack",
    )(selected.T, queries)
    query_chips = spread_chips(packed, rows // 2)
    query_all = with_cores(query_chips, ups[0], downs[0])

    outs = pl.pallas_call(
        functools.partial(forward_kernel, [len(pieces) for pieces in query_all], span, cap),
        out_shape=[shaped((rows, width + HD))] * chunks
        + [
            shaped((block_count, slots, width)),
            shaped((block_count, heads // 2, 2 * BLOCK, slots)),
            shaped((block_count, heads, slots), F32),
            shaped((groups, block_count * cap, rows * span)),
        ],
        in_specs=[smem, vmem] + [anywhere] * (2 + len(flat(query_all))),
        out_specs=[anywhere] * (chunks + 2) + [vmem, anywhere],
        scratch_shapes=[
            pltpu.VMEM((chunks, rows + PAD, width), BF16),
            pltpu.VMEM((chunks, rows, width + HD), BF16),
            pltpu.VMEM((block_count, BLOCK, width), BF16),
            pltpu.VMEM((block_count, BLOCK, width), BF16),
            pltpu.VMEM((block_count, slots, width), BF16),
            pltpu.VMEM((block_count, heads // 2, 2 * BLOCK, slots), BF16),
            pltpu.VMEM((groups, block_count * cap, rows * span), BF16),
            pltpu.VMEM((block_count, slots, HD), F32),
            pltpu.VMEM((block_count, slots, width), BF16),
            pltpu.SemaphoreType.DMA((len(flat(query_all)),)),
            pltpu.SemaphoreType.DMA((2,)),
            pltpu.SemaphoreType.DMA((chunks + 3,)),
        ],
        compiler_params=params,
        name="forward",
    )(me, keys[:, BLOCK - 1], keys, values, *flat(query_all))
    q_slots, probs, logits, hot = outs[chunks:]

    line = lax.axis_index("head").astype(jnp.int32).reshape(1)
    make_grad = pl.pallas_call(
        functools.partial(grad_kernel, lines),
        out_shape=[shaped((rows, width)), shaped((chunks, rows, features // chunks))],
        in_specs=[smem] + [anywhere] * (2 * lines),
        out_specs=[vmem] * 2,
        scratch_shapes=[
            pltpu.VMEM((lines, rows, width), BF16),
            pltpu.VMEM((lines, width, width), BF16),
            pltpu.SemaphoreType.DMA((lines,)),
            pltpu.SemaphoreType.DMA((lines,)),
        ],
        compiler_params=params,
        name="grad",
    )
    received = from_core(outs[:chunks], ups[1], downs[1])
    terms, (grad_attn, blocks) = merge_chips(
        outs[:chunks],
        received,
        heads,
        lambda *before: make_grad(after(line, *before), out_weight, out_grad, *ups, *downs),
    )
    attn_out, *extended = pl.pallas_call(
        functools.partial(finish_kernel, [len(pieces) for pieces in terms]),
        out_shape=[shaped((rows, width))] + [shaped((rows // 2, width + HD))] * 2,
        in_specs=[vmem] * (len(flat(terms)) + 1),
        out_specs=[vmem] * 3,
        compiler_params=small,
        name="finish",
    )(*flat(terms), grad_attn)
    grad_chips = spread_halves(*extended)
    grad_all = with_cores(grad_chips)
    arrived = flat(grad_chips[1:])
    near = after(attn_out, *flat(grad_chips[1:3]))
    attns = [[attn_out]] + [[swap(near, 2 * j)] for j in range(1, chips)]
    columns = lax.all_to_all(
        after(blocks, *arrived), "ctx", split_axis=0, concat_axis=0, tiled=True
    )

    outs = pl.pallas_call(
        functools.partial(backward_kernel, [len(pieces) for pieces in grad_all], span, cap),
        out_shape=[shaped((rows, width))] * chunks
        + [shaped((block_count, BLOCK, width), F32)] * 2,
        in_specs=[vmem] + [anywhere] * (5 + len(flat(grad_all))),
        out_specs=[anywhere] * (chunks + 2),
        scratch_shapes=[
            pltpu.VMEM((chunks, rows, width + HD), BF16),
            pltpu.VMEM((groups, block_count * cap, rows * span), BF16),
            pltpu.VMEM((block_count, slots, width), BF16),
            pltpu.VMEM((block_count, heads // 2, 2 * BLOCK, slots), BF16),
            pltpu.VMEM((block_count, BLOCK, width), BF16),
            pltpu.VMEM((block_count, BLOCK, width), BF16),
            pltpu.VMEM((block_count, slots, width + HD), BF16),
            pltpu.VMEM((block_count, slots, width), BF16),
            pltpu.VMEM((block_count, BLOCK, width), F32),
            pltpu.VMEM((block_count, BLOCK, width), F32),
            pltpu.SemaphoreType.DMA((len(flat(grad_all)),)),
            pltpu.SemaphoreType.DMA((1,)),
            pltpu.SemaphoreType.DMA((4, block_count)),
            pltpu.SemaphoreType.DMA((2, block_count)),
            pltpu.SemaphoreType.DMA((chunks,)),
        ],
        compiler_params=params,
        name="backward",
    )(logits, hot, q_slots, probs, keys, values, *flat(grad_all))
    key_grad, value_grad = outs[chunks:]
    received = from_core(outs[:chunks], columns, *flat(attns[1:]))
    terms, last_sums = collect_chips(outs[:chunks], received)
    attns = with_cores([[after(x, *last_sums) for x in pieces] for pieces in attns])
    weight_grad = pl.pallas_call(
        functools.partial(weight_kernel, [len(pieces) for pieces in attns]),
        out_shape=shaped((features // chunks, width), F32),
        in_specs=[smem] + [vmem] * (1 + len(flat(attns))),
        out_specs=vmem,
        compiler_params=small,
        name="weight",
    )(me, columns, *flat(attns))
    query_grad = pl.pallas_call(
        functools.partial(total_kernel, [len(pieces) for pieces in terms]),
        out_shape=shaped((rows, width), F32),
        in_specs=[vmem] * len(flat(terms)),
        out_specs=vmem,
        compiler_params=small,
        name="total",
    )(after(terms[0][0], weight_grad), *flat(terms[1:]))
    return (
        query_grad,
        key_grad.reshape(-1, width),
        value_grad.reshape(-1, width),
        weight_grad,
    )


def solution(mesh):
    return jax.shard_map(
        body,
        mesh=mesh,
        in_specs=(
            P("ctx", "head"),
            P("ctx", "head"),
            P("ctx", "head"),
            P("ctx", None),
            P("ctx", "head"),
            P(None, "head"),
        ),
        out_specs=(P("ctx", "head"), P("ctx", "head"), P("ctx", "head"), P("ctx", "head")),
        check_vma=False,
    )
```

```python
import functools

import jax
import jax.numpy as jnp
from jax import lax
from jax.experimental import pallas as pl
from jax.experimental.pallas import tpu as pltpu
from jax.sharding import PartitionSpec as P

HD = 128
BLOCK = 64
TOPK = 4
F32 = jnp.float32
BF16 = jnp.bfloat16
MOST = 58 * 1024 * 1024
SOME = 20 * 1024 * 1024
PAD = 16
TOGETHER = 4
LOW = -(2.0**99)
NN = (((1,), (0,)), ((), ()))
NT = (((1,), (1,)), ((), ()))
TN = (((0,), (0,)), ((), ()))


def mm(a, b, dims=NN):
    return lax.dot_general(a, b, dims, preferred_element_type=F32)


def joined(items, axis):
    return items[0] if len(items) == 1 else jnp.concatenate(items, axis=axis)


def dealt(refs, counts):
    lists, at = [], 0
    for count in counts:
        lists.append(refs[at : at + count])
        at += count
    return lists, refs[at:]


def loads(lists, buf, sems):
    copies, at = [], 0
    for i, refs in enumerate(lists):
        mine, row = [], 0
        for ref in refs:
            rows = ref.shape[0]
            mine.append(
                pltpu.make_async_copy(ref, buf.at[i, pl.ds(row, rows)], sems.at[at])
            )
            row += rows
            at += 1
        copies.append(mine)
    return copies


def start(copies):
    for copy in copies:
        copy.start()


def wait(copies):
    for copy in copies:
        copy.wait()


def whole(refs):
    return joined([ref[...] for ref in refs], 0)


def added(terms, cols):
    total = None
    for refs in terms:
        term = joined([ref[:, cols].astype(F32) for ref in refs], 0)
        total = term if total is None else total + term
    return total


def diagonal(pair):
    zero = jnp.zeros((pair.shape[0], HD), pair.dtype)
    top = jnp.concatenate([pair[:, :HD], zero], axis=1)
    low = jnp.concatenate([zero, pair[:, HD:]], axis=1)
    return jnp.concatenate([top, low], axis=0)


def pack_kernel(sel_ref, q_ref, out_ref):
    rows, width = q_ref.shape
    out_ref[:rows] = q_ref[...]
    digits = [(sel_ref[...] >> 4).astype(F32), (sel_ref[...] & 15).astype(F32)]
    if width > 2 * rows:
        digits.append(jnp.zeros((TOPK, width - 2 * rows), F32))
    lines = [jnp.concatenate(digits, axis=1), jnp.zeros((PAD - TOPK, width), F32)]
    out_ref[rows:] = jnp.concatenate(lines, axis=0).astype(BF16)


def forward_kernel(counts, span, cap, me_ref, mark_ref, k_any, v_any, *refs):
    chunks = len(counts)
    q_refs, refs = dealt(refs, counts)
    part_any, refs = refs[:chunks], refs[chunks:]
    qg_any, p_any, logit_ref, hot_any = refs[:4]
    q_buf, part_refs, k_ref, v_ref, qg_ref, p_ref, hot_ref, topg_ref, out_ref = refs[4:13]
    in_sems, kv_sems, out_sems = refs[13:]
    q_copies = loads(q_refs, q_buf, in_sems)
    kv_copies = [
        pltpu.make_async_copy(k_any, k_ref, kv_sems.at[0]),
        pltpu.make_async_copy(v_any, v_ref, kv_sems.at[1]),
    ]
    out_copies = [
        pltpu.make_async_copy(qg_ref, qg_any, out_sems.at[chunks]),
        pltpu.make_async_copy(hot_ref, hot_any, out_sems.at[chunks + 1]),
        pltpu.make_async_copy(p_ref, p_any, out_sems.at[chunks + 2]),
    ]
    for copies in q_copies:
        start(copies)
    start(kv_copies)
    block_count, _, width = k_ref.shape
    heads = width // HD
    rows = part_any[0].shape[0]
    group_rows = rows * span
    groups = chunks // span
    scale = HD ** (-0.5)
    rate = scale * 1.4426950408889634
    base = me_ref[0] * block_count

    before = lax.broadcasted_iota(jnp.int32, (group_rows, group_rows), 0)
    later = lax.broadcasted_iota(jnp.int32, (group_rows, group_rows), 1)
    earlier = (before < later).astype(BF16)
    own_ids = (base + lax.broadcasted_iota(jnp.int32, (block_count, group_rows), 0)).astype(F32)
    place = lax.broadcasted_iota(jnp.int32, (cap, group_rows), 0).astype(F32)
    zero = jnp.zeros((block_count, HD), BF16)
    wide_marks = jnp.concatenate(
        [
            jnp.concatenate(
                [mark_ref[:, i * HD : (i + 1) * HD] if i == h else zero for i in range(heads)], axis=1
            )
            for h in range(heads)
        ],
        axis=0,
    )
    q_groups, owns = [], []
    for g in range(groups):
        for i in range(span):
            wait(q_copies[g * span + i])
        packs = [q_buf[g * span + i] for i in range(span)]
        digits = [pack[rows : rows + PAD].astype(F32)[:TOPK] for pack in packs]
        picked = joined([16.0 * d[:, :rows] + d[:, rows : 2 * rows] for d in digits], 1)
        own = picked[0:1, :] == own_ids
        for t in range(1, TOPK):
            own = own | (picked[t : t + 1, :] == own_ids)
        owns.append(jnp.where(own, 1.0, 0.0))
        q_groups.append(joined([pack[:rows] for pack in packs], 0))
    own_all = jnp.concatenate(owns, axis=0)
    rank_all = jnp.where(own_all > 0.5, mm(own_all.astype(BF16), earlier), -1.0)
    hots = []
    for g in range(groups):
        rank = rank_all[g * block_count : (g + 1) * block_count]
        hots.append(
            jnp.concatenate(
                [
                    jnp.where(rank[b : b + 1, :] == place, 1.0, 0.0).astype(BF16)
                    for b in range(block_count)
                ],
                axis=0,
            )
        )
        hot_ref[g] = hots[g]
    all_marks = [mm(wide_marks, q_groups[g], NT) for g in range(groups)]
    for g in range(groups):
        qg_ref[:, g * cap : (g + 1) * cap, :] = (
            mm(hots[g], q_groups[g]).astype(BF16).reshape(block_count, cap, width)
        )
    tails = []
    for g in range(groups):
        tops, sums = [], []
        for h in range(heads):
            mark = scale * all_marks[g][h * block_count : (h + 1) * block_count]
            mark = jnp.where(owns[g] > 0.5, mark, LOW)
            top = jnp.max(mark, axis=0, keepdims=True).astype(BF16).astype(F32)
            tops.append(top)
            sums.append(jnp.sum(owns[g] * jnp.exp(mark - top), axis=0, keepdims=True))
        tops, sums = jnp.concatenate(tops, axis=0), jnp.concatenate(sums, axis=0)
        upper = sums.astype(BF16).astype(F32)
        spare = jnp.zeros((HD - 3 * heads, group_rows), F32)
        tails.append(jnp.concatenate([tops, upper, sums - upper, spare], axis=0))
    for g in range(groups):
        topg_ref[:, g * cap : (g + 1) * cap, :] = mm(hots[g], tails[g].astype(BF16), NT).reshape(
            block_count, cap, HD
        )
    for g in range(groups):
        for i in range(span):
            part_refs[g * span + i, :, width:] = (
                tails[g][:, i * rows : (i + 1) * rows].T.astype(BF16)
            )
    start(out_copies[:2])
    wait(kv_copies)

    pairs = [slice(p * 2 * HD, (p + 1) * 2 * HD) for p in range(heads // 2)]

    def some_blocks(step, carry):
        blocks = [step * TOGETHER + u for u in range(TOGETHER)]
        logits = [
            [mm(diagonal(k_ref[b, :, cols]), qg_ref[b, :, cols], NT) for cols in pairs]
            for b in blocks
        ]
        probs, gated, kept = [], [], []
        for b, scores in zip(blocks, logits):
            tops = topg_ref[b].T[:heads]
            marks = scale * jnp.concatenate(
                [scores[h // 2][(h % 2 + 1) * BLOCK - 1 : (h % 2 + 1) * BLOCK] for h in range(heads)],
                axis=0,
            )
            gates = jnp.exp(marks - tops)
            kept.append(marks)
            for p in range(heads // 2):
                low, high = [], []
                for i in range(2):
                    part = scores[p][i * BLOCK : (i + 1) * BLOCK]
                    weight = jnp.exp2(rate * (part - jnp.max(part, axis=0, keepdims=True)))
                    inverse = 1.0 / jnp.sum(weight, axis=0, keepdims=True)
                    gate = gates[2 * p + i : 2 * p + i + 1, :]
                    low.append((weight * inverse).astype(BF16))
                    high.append((weight * (inverse * gate)).astype(BF16))
                probs.append(jnp.concatenate(low, axis=0))
                gated.append(jnp.concatenate(high, axis=0))
        outs = []
        for u, b in enumerate(blocks):
            for p, cols in enumerate(pairs):
                both = gated[u * len(pairs) + p]
                outs.append(mm(both, diagonal(v_ref[b, :, cols]), TN).astype(BF16))
        for u, b in enumerate(blocks):
            logit_ref[b] = kept[u]
            for p, cols in enumerate(pairs):
                p_ref[b, p] = probs[u * len(pairs) + p]
                out_ref[b, :, cols] = outs[u * len(pairs) + p]
        return carry

    lax.fori_loop(0, block_count // TOGETHER, some_blocks, 0)
    start(out_copies[2:])

    for g in range(groups):
        slots = out_ref[:, g * cap : (g + 1) * cap, :].reshape(block_count * cap, width)
        part = mm(hot_ref[g], slots, TN).astype(BF16)
        for i in range(span):
            m = g * span + i
            part_refs[m, :, :width] = part[i * rows : (i + 1) * rows]
            copy = pltpu.make_async_copy(part_refs.at[m], part_any[m], out_sems.at[m])
            copy.start()
            out_copies.append(copy)
    wait(out_copies)


def shift(heads, *moves):
    row = lax.broadcasted_iota(jnp.int32, (HD, HD), 0)
    col = lax.broadcasted_iota(jnp.int32, (HD, HD), 1)
    total = jnp.zeros((HD, HD), F32)
    for source, target in moves:
        inside = (row >= source * heads) & (row < (source + 1) * heads)
        hit = inside & (col - target * heads == row - source * heads)
        total = jnp.where(hit, 1.0, total)
    return total.astype(BF16)


def blend(terms, heads):
    width = heads * HD
    tails = [joined([ref[rows, width:] for ref, rows in term], 0) for term in terms]
    wide = [tail.astype(F32) for tail in tails]
    top = wide[0]
    for tail in wide[1:]:
        top = jnp.maximum(top, tail)
    gather = shift(heads, (1, 0), (2, 0))
    factors = [jnp.exp(tail - top) for tail in wide]
    total = None
    for tail, factor in zip(tails, factors):
        share = factor * mm(tail, gather)
        total = share if total is None else total + share
    columns = []
    for h in range(heads):
        cols = slice(h * HD, (h + 1) * HD)
        column = None
        for term, factor in zip(terms, factors):
            values = joined([ref[rows, cols] for ref, rows in term], 0).astype(F32)
            part = factor[:, h : h + 1] * values
            column = part if column is None else column + part
        columns.append(column)
    return top, total, columns


def digits_of(tile, count):
    digits = []
    for _ in range(count):
        upper = tile.astype(BF16)
        digits.append(upper)
        tile = tile - upper.astype(F32)
    return digits


def packed_tail(digits, heads):
    total = None
    for i, digit in enumerate(digits):
        part = mm(digit, shift(heads, (0, i)))
        total = part if total is None else total + part
    return total.astype(BF16)


def merge_kernel(plan, heads, *refs):
    ins, outs = refs[: len(refs) - len(plan)], refs[len(refs) - len(plan) :]
    for terms, out_ref in zip(plan, outs):
        top, total, columns = blend(
            [[(ins[i], pl.ds(first, count))] for i, first, count in terms], heads
        )
        for h in range(heads):
            out_ref[:, h * HD : (h + 1) * HD] = columns[h].astype(BF16)
        out_ref[:, heads * HD :] = packed_tail([top.astype(BF16)] + digits_of(total, 2), heads)


def grad_kernel(lines, line_ref, w_ref, *refs):
    own_ref, up_refs, down_refs = refs[0], refs[1:lines], refs[lines : 2 * lines - 1]
    ga_ref, blocks_ref, full_ref, w_buf, sems, piece_sems = refs[2 * lines - 1 :]
    width = own_ref.shape[1]
    chunks, _, share = blocks_ref.shape
    line = line_ref[0]
    copies = [
        pltpu.make_async_copy(w_ref.at[pl.ds(i * width, width)], w_buf.at[i], sems.at[i])
        for i in range(lines)
    ]
    start(copies)

    def placed(ref, i):
        return pltpu.make_async_copy(ref, full_ref.at[i], piece_sems.at[i])

    placed(own_ref, line).start()
    for d in range(1, lines):

        @pl.when(line >= d)
        def _():
            placed(up_refs[d - 1], line - d).start()

        @pl.when(line + d < lines)
        def _():
            placed(down_refs[d - 1], line + d).start()

    for i in range(lines):
        placed(own_ref, i).wait()
    for j in range(chunks):
        first = j * share
        blocks_ref[j] = full_ref[first // width, :, first % width : first % width + share]
    total = None
    for i in range(lines):
        copies[i].wait()
        term = mm(full_ref[i], w_buf[i])
        total = term if total is None else total + term
    ga_ref[...] = total.astype(BF16)


def finish_kernel(counts, *refs):
    terms, (ga_ref, attn_ref, *ext_refs) = dealt(refs, counts)
    rows, width = ga_ref.shape
    half = rows // len(ext_refs)
    heads = width // HD
    top, total, columns = blend(
        [[(ref, slice(None)) for ref in pieces] for pieces in terms], heads
    )
    lane = lax.broadcasted_iota(jnp.int32, (rows, HD), 1)
    total = jnp.where(lane < heads, total, 1.0)
    inverse = 1.0 / total
    dots = jnp.zeros((rows, HD), F32)
    for i, ext_ref in enumerate(ext_refs):
        ext_ref[:, :width] = ga_ref[i * half : (i + 1) * half]
    for h in range(heads):
        cols = slice(h * HD, (h + 1) * HD)
        attn = columns[h] * inverse[:, h : h + 1]
        attn_ref[:, cols] = attn.astype(BF16)
        dot = jnp.sum(attn * ga_ref[:, cols].astype(F32), axis=1, keepdims=True)
        dots = jnp.where(lane == h, dot, dots)
    level = jnp.where(lane < heads, top + jnp.log(total), 0.0)
    tail = packed_tail(digits_of(dots, 2) + digits_of(level, 3), heads)
    for i, ext_ref in enumerate(ext_refs):
        ext_ref[:, width:] = tail[i * half : (i + 1) * half]


def total_kernel(counts, *refs):
    terms, (out_ref,) = dealt(refs, counts)
    for h in range(out_ref.shape[1] // HD):
        cols = slice(h * HD, (h + 1) * HD)
        out_ref[:, cols] = added(terms, cols)


def backward_kernel(counts, span, cap, logit_ref, hot_any, qg_any, p_any, k_any, v_any, *refs):
    chunks = len(counts)
    ga_refs, refs = dealt(refs, counts)
    part_refs, refs = refs[:chunks], refs[chunks:]
    dk_any, dv_any = refs[:2]
    ga_buf, hot_ref, qg_ref, p_ref, k_ref, v_ref, gag_ref, dq_ref, dk_ref, dv_ref = refs[2:12]
    in_sems, hot_sem, block_sems, out_sems, part_sems = refs[12:]
    ga_copies = loads(ga_refs, ga_buf, in_sems)
    hot_copy = pltpu.make_async_copy(hot_any, hot_ref, hot_sem.at[0])
    hot_copy.start()
    for copies in ga_copies:
        start(copies)

    def block_loads(b):
        pairs = ((qg_any, qg_ref), (p_any, p_ref), (k_any, k_ref), (v_any, v_ref))
        return [
            pltpu.make_async_copy(far.at[b], near.at[b], block_sems.at[i, b])
            for i, (far, near) in enumerate(pairs)
        ]

    def block_stores(b):
        return [
            pltpu.make_async_copy(dk_ref.at[b], dk_any.at[b], out_sems.at[0, b]),
            pltpu.make_async_copy(dv_ref.at[b], dv_any.at[b], out_sems.at[1, b]),
        ]

    block_count, _, width = k_ref.shape
    heads = width // HD
    rows = part_refs[0].shape[0]
    groups = chunks // span
    scale = HD ** (-0.5)

    for b in range(block_count):
        start(block_loads(b))
    hot_copy.wait()
    for g in range(groups):
        for i in range(span):
            wait(ga_copies[g * span + i])
        ga_group = joined([ga_buf[g * span + i] for i in range(span)], 0)
        gag_ref[:, g * cap : (g + 1) * cap, :] = (
            mm(hot_ref[g], ga_group).astype(BF16).reshape(block_count, cap, width + HD)
        )
    last = lax.broadcasted_iota(jnp.int32, (BLOCK, groups * cap), 0) == BLOCK - 1

    pairs = [slice(p * 2 * HD, (p + 1) * 2 * HD) for p in range(heads // 2)]

    def some_blocks(step, carry):
        blocks = [step * TOGETHER + u for u in range(TOGETHER)]
        for b in blocks:
            wait(block_loads(b))
        grads = [
            [mm(diagonal(v_ref[b, :, cols]), gag_ref[b, :, cols], NT) for cols in pairs]
            for b in blocks
        ]
        gated, scores = [], []
        for b, grad_pairs in zip(blocks, grads):
            tail = gag_ref[b, :, width:].astype(F32).T
            tail = [tail[i * heads : (i + 1) * heads] for i in range(5)]
            dots = tail[0] + tail[1]
            gates = jnp.exp(jnp.minimum(logit_ref[b] - (tail[2] + tail[3] + tail[4]), 0.0))
            for p in range(heads // 2):
                both = p_ref[b, p].astype(F32)
                low, high = [], []
                for i in range(2):
                    at = slice(i * BLOCK, (i + 1) * BLOCK)
                    h = 2 * p + i
                    gate = gates[h : h + 1, :]
                    grad, probs = grad_pairs[p][at], both[at]
                    delta = jnp.sum(probs * grad, axis=0, keepdims=True)
                    weight = probs * gate
                    extra = jnp.where(last, scale * gate * (delta - dots[h : h + 1, :]), 0.0)
                    low.append((weight * (scale * (grad - delta)) + extra).astype(BF16))
                    high.append(weight.astype(BF16))
                scores.append(low)
                gated.append(high)
        for u, b in enumerate(blocks):
            for p, cols in enumerate(pairs):
                score, weight = scores[u * len(pairs) + p], gated[u * len(pairs) + p]
                for i in range(2):
                    head = slice((2 * p + i) * HD, (2 * p + i + 1) * HD)
                    dv_ref[b, :, head] = mm(weight[i], gag_ref[b, :, head])
                    dk_ref[b, :, head] = mm(score[i], qg_ref[b, :, head])
                both = jnp.concatenate(score, axis=0)
                dq_ref[b, :, cols] = mm(both, diagonal(k_ref[b, :, cols]), TN).astype(BF16)
        for b in blocks:
            start(block_stores(b))
        return carry

    lax.fori_loop(0, block_count // TOGETHER, some_blocks, 0)

    part_copies = []

    for g in range(groups):
        slots = dq_ref[:, g * cap : (g + 1) * cap, :].reshape(block_count * cap, width)
        part = mm(hot_ref[g], slots, TN).astype(BF16)
        for i in range(span):
            m = g * span + i
            ga_buf[m, :, :width] = part[i * rows : (i + 1) * rows]
            copy = pltpu.make_async_copy(
                ga_buf.at[m, :, pl.ds(0, width)], part_refs[m], part_sems.at[m]
            )
            copy.start()
            part_copies.append(copy)
    for b in range(block_count):
        wait(block_stores(b))
    wait(part_copies)


def weight_kernel(counts, first, me_ref, cols_ref, *refs):
    attns, (*before, out_ref) = dealt(refs, counts)
    me = me_ref[0]
    columns = joined([cols_ref[me ^ (first + m)] for m in range(len(counts))], 0)
    total = mm(columns, joined([whole(pieces) for pieces in attns], 0), TN)
    for ref in before:
        total = total + ref[...]
    out_ref[...] = total


def swap(x, bits):
    count = lax.axis_size("ctx")
    return lax.ppermute(x, "ctx", [(i, i ^ bits) for i in range(count)])


def after(x, *others):
    return lax.optimization_barrier((x, *others))[0]


def flat(lists):
    return [x for pieces in lists for x in pieces]


def spread_near(x):
    chips = lax.axis_size("ctx") // 2
    return [[x]] + [[swap(x, 2 * j)] for j in range(1, chips if chips != 4 else 3)]


def spread_far(near, half, *before):
    if len(near) != 3:
        return near
    (x_way,), (y_way,) = near[1:]
    far = [swap(after(x_way[:half], *before), 4), swap(after(y_way[half:], *before), 2)]
    return near + [far]


def spread_chips(x, half, *before):
    return spread_far(spread_near(x), half, *before)


def spread_halves(top, low):
    chips = lax.axis_size("ctx") // 2
    if chips != 4:
        return [[swap(x, 2 * j) if j else x for x in (top, low)] for j in range(chips)]
    x_top, y_low = swap(top, 2), swap(low, 4)
    x_low, y_top = swap(low, 2), swap(top, 4)
    return [[top, low], [x_top, x_low], [y_top, y_low], [swap(x_top, 4), swap(y_low, 2)]]


def with_cores(lists, *before):
    both = []
    for pieces in lists:
        if before and pieces is lists[-1]:
            pieces = [after(piece, *before) for piece in pieces]
        both += [pieces, [swap(piece, 1) for piece in pieces]]
    return both


def from_core(parts, *before):
    received = [None] * (len(parts) // 2)
    for j in reversed(range(len(received))):
        received[j] = swap(after(parts[2 * j + 1], *before), 1)
    return received


def collect_chips(parts, received):
    chips = len(received)

    def both(j, rows, extra=None, earlier=None):
        mine = parts[2 * j] if earlier is None else after(parts[2 * j], earlier)
        total = mine[rows].astype(F32) + received[j][rows].astype(F32)
        if extra is not None:
            total = total + extra.astype(F32)
        return total.astype(BF16)

    terms = [[parts[0]], [received[0]]]
    if chips != 4:
        return terms + [[swap(both(j, slice(None)), 2 * j)] for j in range(1, chips)], []
    half = parts[0].shape[0] // 2
    top, low = slice(0, half), slice(half, None)
    x_sum, y_sum = both(3, top), both(3, low)
    x_far, y_far = swap(x_sum, 2), swap(y_sum, 4)
    x_sum, y_sum = both(1, top, None, x_sum), both(2, low, None, y_sum)
    near_sums = [x_sum, y_sum]
    x_top, y_low = swap(x_sum, 2), swap(y_sum, 4)
    x_sum, y_sum = both(1, low, y_far, x_sum), both(2, top, x_far, y_sum)
    x_low, y_top = swap(x_sum, 2), swap(y_sum, 4)
    return terms + [[x_top, x_low], [y_top, y_low]], near_sums


def merge_chips(parts, received, heads, between):
    chips = len(received)
    rows = parts[0].shape[0]
    half = rows // 2

    def merged(ins, plan):
        return pl.pallas_call(
            functools.partial(merge_kernel, plan, heads),
            out_shape=[
                jax.ShapeDtypeStruct((terms[0][2], ins[0].shape[1]), BF16) for terms in plan
            ],
            in_specs=[pl.BlockSpec(memory_space=pltpu.VMEM)] * len(ins),
            out_specs=[pl.BlockSpec(memory_space=pltpu.VMEM)] * len(plan),
            compiler_params=pltpu.CompilerParams(vmem_limit_bytes=SOME),
            name="merge",
        )(*ins)

    terms = [[parts[0]], [received[0]]]
    if chips != 4:
        for j in range(1, chips):
            (both,) = merged([parts[2 * j], received[j]], [[(0, 0, rows), (1, 0, rows)]])
            terms.append([swap(both, 2 * j)])
        return terms, between(received[0])
    top, low = (0, half), (half, half)
    x_far, y_far = merged(
        [parts[6], received[3]], [[(0, *top), (1, *top)], [(0, *low), (1, *low)]]
    )
    x_far, y_far = swap(x_far, 2), swap(y_far, 4)
    ins = [parts[2], received[1], parts[4], received[2]]
    x_top, y_low = merged(ins, [[(0, *top), (1, *top)], [(2, *low), (3, *low)]])
    x_top, y_low = swap(x_top, 2), swap(y_low, 4)
    x_low, y_top = merged(
        ins + [y_far, x_far],
        [[(0, *low), (1, *low), (4, *top)], [(2, *top), (3, *top), (5, *top)]],
    )
    done = between(x_low, y_top)
    x_low, y_top = swap(x_low, 2), swap(y_top, 4)
    return terms + [[x_top, x_low], [y_top, y_low]], done


def spread_line(x):
    lines = lax.axis_size("head")
    ups, downs = [x], [x]
    for d in range(1, lines):
        up = [(i, i + 1) for i in range(d - 1, lines - 1)]
        down = [(i, i - 1) for i in range(1, lines - d + 1)]
        if d == lines - 1 and lines > 2:
            last = jnp.where(lax.axis_index("head") == lines - 2, ups[-1], downs[-1])
            last = lax.ppermute(last, "head", up + down)
            ups.append(last)
            downs.append(last)
        else:
            ups.append(lax.ppermute(ups[-1], "head", up))
            downs.append(lax.ppermute(downs[-1], "head", down))
    return ups[1:], downs[1:]


def body(queries, key_rows, value_rows, selected, out_grad, out_weight):
    chunks = lax.axis_size("ctx")
    chips = chunks // 2
    lines = lax.axis_size("head")
    rows, width = queries.shape
    features = out_weight.shape[0]
    heads = width // HD
    block_count = key_rows.shape[0] // BLOCK
    block_total = block_count * chunks
    capacity = 2 * rows * TOPK // block_total
    span = max(1, 16 // capacity)
    cap = capacity * span
    groups = chunks // span
    slots = groups * cap
    index = lax.axis_index("ctx").astype(jnp.int32)
    me = index.reshape(1)
    keys = key_rows.reshape(block_count, BLOCK, width)
    values = value_rows.reshape(block_count, BLOCK, width)
    vmem = pl.BlockSpec(memory_space=pltpu.VMEM)
    smem = pl.BlockSpec(memory_space=pltpu.SMEM)
    anywhere = pl.BlockSpec(memory_space=pl.ANY)
    params = pltpu.CompilerParams(vmem_limit_bytes=MOST)
    small = pltpu.CompilerParams(vmem_limit_bytes=SOME)

    def shaped(shape, kind=BF16):
        return jax.ShapeDtypeStruct(shape, kind)

    ups, downs = spread_line(out_grad)
    packed = pl.pallas_call(
        pack_kernel,
        out_shape=shaped((rows + PAD, width)),
        in_specs=[vmem] * 2,
        out_specs=vmem,
        compiler_params=small,
        name="pack",
    )(selected.T, queries)
    query_chips = spread_chips(packed, rows // 2)
    query_all = with_cores(query_chips, ups[0], downs[0])

    outs = pl.pallas_call(
        functools.partial(forward_kernel, [len(pieces) for pieces in query_all], span, cap),
        out_shape=[shaped((rows, width + HD))] * chunks
        + [
            shaped((block_count, slots, width)),
            shaped((block_count, heads // 2, 2 * BLOCK, slots)),
            shaped((block_count, heads, slots), F32),
            shaped((groups, block_count * cap, rows * span)),
        ],
        in_specs=[smem, vmem] + [anywhere] * (2 + len(flat(query_all))),
        out_specs=[anywhere] * (chunks + 2) + [vmem, anywhere],
        scratch_shapes=[
            pltpu.VMEM((chunks, rows + PAD, width), BF16),
            pltpu.VMEM((chunks, rows, width + HD), BF16),
            pltpu.VMEM((block_count, BLOCK, width), BF16),
            pltpu.VMEM((block_count, BLOCK, width), BF16),
            pltpu.VMEM((block_count, slots, width), BF16),
            pltpu.VMEM((block_count, heads // 2, 2 * BLOCK, slots), BF16),
            pltpu.VMEM((groups, block_count * cap, rows * span), BF16),
            pltpu.VMEM((block_count, slots, HD), F32),
            pltpu.VMEM((block_count, slots, width), BF16),
            pltpu.SemaphoreType.DMA((len(flat(query_all)),)),
            pltpu.SemaphoreType.DMA((2,)),
            pltpu.SemaphoreType.DMA((chunks + 3,)),
        ],
        compiler_params=params,
        name="forward",
    )(me, keys[:, BLOCK - 1], keys, values, *flat(query_all))
    q_slots, probs, logits, hot = outs[chunks:]

    line = lax.axis_index("head").astype(jnp.int32).reshape(1)
    make_grad = pl.pallas_call(
        functools.partial(grad_kernel, lines),
        out_shape=[shaped((rows, width)), shaped((chunks, rows, features // chunks))],
        in_specs=[smem] + [anywhere] * (2 * lines),
        out_specs=[vmem] * 2,
        scratch_shapes=[
            pltpu.VMEM((lines, rows, width), BF16),
            pltpu.VMEM((lines, width, width), BF16),
            pltpu.SemaphoreType.DMA((lines,)),
            pltpu.SemaphoreType.DMA((lines,)),
        ],
        compiler_params=params,
        name="grad",
    )
    received = from_core(outs[:chunks], ups[1], downs[1])
    terms, (grad_attn, blocks) = merge_chips(
        outs[:chunks],
        received,
        heads,
        lambda *before: make_grad(after(line, *before), out_weight, out_grad, *ups, *downs),
    )
    attn_out, *extended = pl.pallas_call(
        functools.partial(finish_kernel, [len(pieces) for pieces in terms]),
        out_shape=[shaped((rows, width))] + [shaped((rows // 2, width + HD))] * 2,
        in_specs=[vmem] * (len(flat(terms)) + 1),
        out_specs=[vmem] * 3,
        compiler_params=small,
        name="finish",
    )(*flat(terms), grad_attn)
    grad_chips = spread_halves(*extended)
    grad_all = with_cores(grad_chips)
    arrived = flat(grad_chips[1:])
    columns = lax.all_to_all(
        after(blocks, *arrived), "ctx", split_axis=0, concat_axis=0, tiled=True
    )

    outs = pl.pallas_call(
        functools.partial(backward_kernel, [len(pieces) for pieces in grad_all], span, cap),
        out_shape=[shaped((rows, width))] * chunks
        + [shaped((block_count, BLOCK, width), F32)] * 2,
        in_specs=[vmem] + [anywhere] * (5 + len(flat(grad_all))),
        out_specs=[anywhere] * (chunks + 2),
        scratch_shapes=[
            pltpu.VMEM((chunks, rows, width + HD), BF16),
            pltpu.VMEM((groups, block_count * cap, rows * span), BF16),
            pltpu.VMEM((block_count, slots, width), BF16),
            pltpu.VMEM((block_count, heads // 2, 2 * BLOCK, slots), BF16),
            pltpu.VMEM((block_count, BLOCK, width), BF16),
            pltpu.VMEM((block_count, BLOCK, width), BF16),
            pltpu.VMEM((block_count, slots, width + HD), BF16),
            pltpu.VMEM((block_count, slots, width), BF16),
            pltpu.VMEM((block_count, BLOCK, width), F32),
            pltpu.VMEM((block_count, BLOCK, width), F32),
            pltpu.SemaphoreType.DMA((len(flat(grad_all)),)),
            pltpu.SemaphoreType.DMA((1,)),
            pltpu.SemaphoreType.DMA((4, block_count)),
            pltpu.SemaphoreType.DMA((2, block_count)),
            pltpu.SemaphoreType.DMA((chunks,)),
        ],
        compiler_params=params,
        name="backward",
    )(logits, hot, q_slots, probs, keys, values, *flat(grad_all))
    key_grad, value_grad = outs[chunks:]
    received = from_core(outs[:chunks], columns)
    terms, near_sums = collect_chips(outs[:chunks], received)
    attns = with_cores(spread_chips(after(attn_out, *near_sums), rows // 2))

    def weight_part(chosen, first, when, *before):
        return pl.pallas_call(
            functools.partial(weight_kernel, [len(pieces) for pieces in chosen], first),
            out_shape=shaped((features // chunks, width), F32),
            in_specs=[smem] + [vmem] * (1 + len(flat(chosen)) + len(before)),
            out_specs=vmem,
            compiler_params=small,
            name="weight",
        )(when, columns, *flat(chosen), *before)

    weight_near = weight_part(attns[:-2], 0, me)
    query_grad = pl.pallas_call(
        functools.partial(total_kernel, [len(pieces) for pieces in terms]),
        out_shape=shaped((rows, width), F32),
        in_specs=[vmem] * len(flat(terms)),
        out_specs=vmem,
        compiler_params=small,
        name="total",
    )(*flat(terms))
    weight_grad = weight_part(attns[-2:], chunks - 2, me, weight_near)
    return (
        query_grad,
        key_grad.reshape(-1, width),
        value_grad.reshape(-1, width),
        weight_grad,
    )


def solution(mesh):
    return jax.shard_map(
        body,
        mesh=mesh,
        in_specs=(
            P("ctx", "head"),
            P("ctx", "head"),
            P("ctx", "head"),
            P("ctx", None),
            P("ctx", "head"),
            P(None, "head"),
        ),
        out_specs=(P("ctx", "head"), P("ctx", "head"), P("ctx", "head"), P("ctx", "head")),
        check_vma=False,
    )
```

```python
import functools

import jax
import jax.numpy as jnp
from jax import lax
from jax.experimental import pallas as pl
from jax.experimental.pallas import tpu as pltpu
from jax.sharding import PartitionSpec as P

HD = 128
BLOCK = 64
TOPK = 4
F32 = jnp.float32
BF16 = jnp.bfloat16
MOST = 58 * 1024 * 1024
SOME = 20 * 1024 * 1024
PAD = 16
TOGETHER = 4
LOW = -(2.0**99)
NN = (((1,), (0,)), ((), ()))
NT = (((1,), (1,)), ((), ()))
TN = (((0,), (0,)), ((), ()))


def mm(a, b, dims=NN):
    return lax.dot_general(a, b, dims, preferred_element_type=F32)


def joined(items, axis):
    return items[0] if len(items) == 1 else jnp.concatenate(items, axis=axis)


def dealt(refs, counts):
    lists, at = [], 0
    for count in counts:
        lists.append(refs[at : at + count])
        at += count
    return lists, refs[at:]


def loads(lists, buf, sems):
    copies, at = [], 0
    for i, refs in enumerate(lists):
        mine, row = [], 0
        for ref in refs:
            rows = ref.shape[0]
            mine.append(
                pltpu.make_async_copy(ref, buf.at[i, pl.ds(row, rows)], sems.at[at])
            )
            row += rows
            at += 1
        copies.append(mine)
    return copies


def start(copies):
    for copy in copies:
        copy.start()


def wait(copies):
    for copy in copies:
        copy.wait()


def whole(refs):
    return joined([ref[...] for ref in refs], 0)


def added(terms, cols):
    total = None
    for refs in terms:
        term = joined([ref[:, cols].astype(F32) for ref in refs], 0)
        total = term if total is None else total + term
    return total


def diagonal(pair):
    zero = jnp.zeros((pair.shape[0], HD), pair.dtype)
    top = jnp.concatenate([pair[:, :HD], zero], axis=1)
    low = jnp.concatenate([zero, pair[:, HD:]], axis=1)
    return jnp.concatenate([top, low], axis=0)


def pack_kernel(sel_ref, q_ref, out_ref):
    rows, width = q_ref.shape
    out_ref[:rows] = q_ref[...]
    digits = [(sel_ref[...] >> 4).astype(F32), (sel_ref[...] & 15).astype(F32)]
    if width > 2 * rows:
        digits.append(jnp.zeros((TOPK, width - 2 * rows), F32))
    lines = [jnp.concatenate(digits, axis=1), jnp.zeros((PAD - TOPK, width), F32)]
    out_ref[rows:] = jnp.concatenate(lines, axis=0).astype(BF16)


def forward_kernel(counts, span, cap, me_ref, mark_ref, k_any, v_any, *refs):
    chunks = len(counts)
    q_refs, refs = dealt(refs, counts)
    part_any, refs = refs[:chunks], refs[chunks:]
    qg_any, p_any, logit_ref, hot_any = refs[:4]
    q_buf, part_refs, k_ref, v_ref, qg_ref, p_ref, hot_ref, topg_ref, out_ref = refs[4:13]
    in_sems, kv_sems, out_sems = refs[13:]
    q_copies = loads(q_refs, q_buf, in_sems)
    kv_copies = [
        pltpu.make_async_copy(k_any, k_ref, kv_sems.at[0]),
        pltpu.make_async_copy(v_any, v_ref, kv_sems.at[1]),
    ]
    out_copies = [
        pltpu.make_async_copy(qg_ref, qg_any, out_sems.at[chunks]),
        pltpu.make_async_copy(hot_ref, hot_any, out_sems.at[chunks + 1]),
        pltpu.make_async_copy(p_ref, p_any, out_sems.at[chunks + 2]),
    ]
    for copies in q_copies:
        start(copies)
    start(kv_copies)
    block_count, _, width = k_ref.shape
    heads = width // HD
    rows = part_any[0].shape[0]
    group_rows = rows * span
    groups = chunks // span
    scale = HD ** (-0.5)
    rate = scale * 1.4426950408889634
    base = me_ref[0] * block_count

    before = lax.broadcasted_iota(jnp.int32, (group_rows, group_rows), 0)
    later = lax.broadcasted_iota(jnp.int32, (group_rows, group_rows), 1)
    earlier = (before < later).astype(BF16)
    own_ids = (base + lax.broadcasted_iota(jnp.int32, (block_count, group_rows), 0)).astype(F32)
    place = lax.broadcasted_iota(jnp.int32, (cap, group_rows), 0).astype(F32)
    zero = jnp.zeros((block_count, HD), BF16)
    wide_marks = jnp.concatenate(
        [
            jnp.concatenate(
                [mark_ref[:, i * HD : (i + 1) * HD] if i == h else zero for i in range(heads)], axis=1
            )
            for h in range(heads)
        ],
        axis=0,
    )
    q_groups, owns = [], []
    for g in range(groups):
        for i in range(span):
            wait(q_copies[g * span + i])
        packs = [q_buf[g * span + i] for i in range(span)]
        digits = [pack[rows : rows + PAD].astype(F32)[:TOPK] for pack in packs]
        picked = joined([16.0 * d[:, :rows] + d[:, rows : 2 * rows] for d in digits], 1)
        own = picked[0:1, :] == own_ids
        for t in range(1, TOPK):
            own = own | (picked[t : t + 1, :] == own_ids)
        owns.append(jnp.where(own, 1.0, 0.0))
        q_groups.append(joined([pack[:rows] for pack in packs], 0))
    own_all = jnp.concatenate(owns, axis=0)
    rank_all = jnp.where(own_all > 0.5, mm(own_all.astype(BF16), earlier), -1.0)
    hots = []
    for g in range(groups):
        rank = rank_all[g * block_count : (g + 1) * block_count]
        hots.append(
            jnp.concatenate(
                [
                    jnp.where(rank[b : b + 1, :] == place, 1.0, 0.0).astype(BF16)
                    for b in range(block_count)
                ],
                axis=0,
            )
        )
        hot_ref[g] = hots[g]
    all_marks = [mm(wide_marks, q_groups[g], NT) for g in range(groups)]
    for g in range(groups):
        qg_ref[:, g * cap : (g + 1) * cap, :] = (
            mm(hots[g], q_groups[g]).astype(BF16).reshape(block_count, cap, width)
        )
    tails = []
    for g in range(groups):
        tops, sums = [], []
        for h in range(heads):
            mark = scale * all_marks[g][h * block_count : (h + 1) * block_count]
            mark = jnp.where(owns[g] > 0.5, mark, LOW)
            top = jnp.max(mark, axis=0, keepdims=True).astype(BF16).astype(F32)
            tops.append(top)
            sums.append(jnp.sum(owns[g] * jnp.exp(mark - top), axis=0, keepdims=True))
        tops, sums = jnp.concatenate(tops, axis=0), jnp.concatenate(sums, axis=0)
        upper = sums.astype(BF16).astype(F32)
        spare = jnp.zeros((HD - 3 * heads, group_rows), F32)
        tails.append(jnp.concatenate([tops, upper, sums - upper, spare], axis=0))
    for g in range(groups):
        topg_ref[:, g * cap : (g + 1) * cap, :] = mm(hots[g], tails[g].astype(BF16), NT).reshape(
            block_count, cap, HD
        )
    for g in range(groups):
        for i in range(span):
            part_refs[g * span + i, :, width:] = (
                tails[g][:, i * rows : (i + 1) * rows].T.astype(BF16)
            )
    start(out_copies[:2])
    wait(kv_copies)

    pairs = [slice(p * 2 * HD, (p + 1) * 2 * HD) for p in range(heads // 2)]

    def some_blocks(step, carry):
        blocks = [step * TOGETHER + u for u in range(TOGETHER)]
        logits = [
            [mm(diagonal(k_ref[b, :, cols]), qg_ref[b, :, cols], NT) for cols in pairs]
            for b in blocks
        ]
        probs, gated, kept = [], [], []
        for b, scores in zip(blocks, logits):
            tops = topg_ref[b].T[:heads]
            marks = scale * jnp.concatenate(
                [scores[h // 2][(h % 2 + 1) * BLOCK - 1 : (h % 2 + 1) * BLOCK] for h in range(heads)],
                axis=0,
            )
            gates = jnp.exp(marks - tops)
            kept.append(marks)
            for p in range(heads // 2):
                low, high = [], []
                for i in range(2):
                    part = scores[p][i * BLOCK : (i + 1) * BLOCK]
                    weight = jnp.exp2(rate * (part - jnp.max(part, axis=0, keepdims=True)))
                    inverse = 1.0 / jnp.sum(weight, axis=0, keepdims=True)
                    gate = gates[2 * p + i : 2 * p + i + 1, :]
                    low.append((weight * inverse).astype(BF16))
                    high.append((weight * (inverse * gate)).astype(BF16))
                probs.append(jnp.concatenate(low, axis=0))
                gated.append(jnp.concatenate(high, axis=0))
        outs = []
        for u, b in enumerate(blocks):
            for p, cols in enumerate(pairs):
                both = gated[u * len(pairs) + p]
                outs.append(mm(both, diagonal(v_ref[b, :, cols]), TN).astype(BF16))
        for u, b in enumerate(blocks):
            logit_ref[b] = kept[u]
            for p, cols in enumerate(pairs):
                p_ref[b, p] = probs[u * len(pairs) + p]
                out_ref[b, :, cols] = outs[u * len(pairs) + p]
        return carry

    lax.fori_loop(0, block_count // TOGETHER, some_blocks, 0)
    start(out_copies[2:])

    for g in range(groups):
        slots = out_ref[:, g * cap : (g + 1) * cap, :].reshape(block_count * cap, width)
        part = mm(hot_ref[g], slots, TN).astype(BF16)
        for i in range(span):
            m = g * span + i
            part_refs[m, :, :width] = part[i * rows : (i + 1) * rows]
            copy = pltpu.make_async_copy(part_refs.at[m], part_any[m], out_sems.at[m])
            copy.start()
            out_copies.append(copy)
    wait(out_copies)


def shift(heads, *moves):
    row = lax.broadcasted_iota(jnp.int32, (HD, HD), 0)
    col = lax.broadcasted_iota(jnp.int32, (HD, HD), 1)
    total = jnp.zeros((HD, HD), F32)
    for source, target in moves:
        inside = (row >= source * heads) & (row < (source + 1) * heads)
        hit = inside & (col - target * heads == row - source * heads)
        total = jnp.where(hit, 1.0, total)
    return total.astype(BF16)


def blend(terms, heads):
    width = heads * HD
    tails = [joined([ref[rows, width:] for ref, rows in term], 0) for term in terms]
    wide = [tail.astype(F32) for tail in tails]
    top = wide[0]
    for tail in wide[1:]:
        top = jnp.maximum(top, tail)
    gather = shift(heads, (1, 0), (2, 0))
    factors = [jnp.exp(tail - top) for tail in wide]
    total = None
    for tail, factor in zip(tails, factors):
        share = factor * mm(tail, gather)
        total = share if total is None else total + share
    columns = []
    for h in range(heads):
        cols = slice(h * HD, (h + 1) * HD)
        column = None
        for term, factor in zip(terms, factors):
            values = joined([ref[rows, cols] for ref, rows in term], 0).astype(F32)
            part = factor[:, h : h + 1] * values
            column = part if column is None else column + part
        columns.append(column)
    return top, total, columns


def digits_of(tile, count):
    digits = []
    for _ in range(count):
        upper = tile.astype(BF16)
        digits.append(upper)
        tile = tile - upper.astype(F32)
    return digits


def packed_tail(digits, heads):
    total = None
    for i, digit in enumerate(digits):
        part = mm(digit, shift(heads, (0, i)))
        total = part if total is None else total + part
    return total.astype(BF16)


def merge_kernel(plan, heads, *refs):
    ins, outs = refs[: len(refs) - len(plan)], refs[len(refs) - len(plan) :]
    for terms, out_ref in zip(plan, outs):
        top, total, columns = blend(
            [[(ins[i], pl.ds(first, count))] for i, first, count in terms], heads
        )
        for h in range(heads):
            out_ref[:, h * HD : (h + 1) * HD] = columns[h].astype(BF16)
        out_ref[:, heads * HD :] = packed_tail([top.astype(BF16)] + digits_of(total, 2), heads)


def grad_kernel(lines, line_ref, w_ref, *refs):
    own_ref, up_refs, down_refs = refs[0], refs[1:lines], refs[lines : 2 * lines - 1]
    ga_ref, blocks_ref, full_ref, w_buf, sems, piece_sems = refs[2 * lines - 1 :]
    width = own_ref.shape[1]
    chunks, _, share = blocks_ref.shape
    line = line_ref[0]
    copies = [
        pltpu.make_async_copy(w_ref.at[pl.ds(i * width, width)], w_buf.at[i], sems.at[i])
        for i in range(lines)
    ]
    start(copies)

    def placed(ref, i):
        return pltpu.make_async_copy(ref, full_ref.at[i], piece_sems.at[i])

    placed(own_ref, line).start()
    for d in range(1, lines):

        @pl.when(line >= d)
        def _():
            placed(up_refs[d - 1], line - d).start()

        @pl.when(line + d < lines)
        def _():
            placed(down_refs[d - 1], line + d).start()

    for i in range(lines):
        placed(own_ref, i).wait()
    for j in range(chunks):
        first = j * share
        blocks_ref[j] = full_ref[first // width, :, first % width : first % width + share]
    total = None
    for i in range(lines):
        copies[i].wait()
        term = mm(full_ref[i], w_buf[i])
        total = term if total is None else total + term
    ga_ref[...] = total.astype(BF16)


def finish_kernel(counts, *refs):
    terms, (ga_ref, attn_ref, *ext_refs) = dealt(refs, counts)
    rows, width = ga_ref.shape
    half = rows // len(ext_refs)
    heads = width // HD
    top, total, columns = blend(
        [[(ref, slice(None)) for ref in pieces] for pieces in terms], heads
    )
    lane = lax.broadcasted_iota(jnp.int32, (rows, HD), 1)
    total = jnp.where(lane < heads, total, 1.0)
    inverse = 1.0 / total
    dots = jnp.zeros((rows, HD), F32)
    for i, ext_ref in enumerate(ext_refs):
        ext_ref[:, :width] = ga_ref[i * half : (i + 1) * half]
    for h in range(heads):
        cols = slice(h * HD, (h + 1) * HD)
        attn = columns[h] * inverse[:, h : h + 1]
        attn_ref[:, cols] = attn.astype(BF16)
        dot = jnp.sum(attn * ga_ref[:, cols].astype(F32), axis=1, keepdims=True)
        dots = jnp.where(lane == h, dot, dots)
    level = jnp.where(lane < heads, top + jnp.log(total), 0.0)
    tail = packed_tail(digits_of(dots, 2) + digits_of(level, 3), heads)
    for i, ext_ref in enumerate(ext_refs):
        ext_ref[:, width:] = tail[i * half : (i + 1) * half]


def total_kernel(counts, *refs):
    terms, (out_ref,) = dealt(refs, counts)
    for h in range(out_ref.shape[1] // HD):
        cols = slice(h * HD, (h + 1) * HD)
        out_ref[:, cols] = added(terms, cols)


def backward_kernel(counts, span, cap, logit_ref, hot_any, qg_any, p_any, k_any, v_any, *refs):
    chunks = len(counts)
    ga_refs, refs = dealt(refs, counts)
    part_refs, refs = refs[:chunks], refs[chunks:]
    dk_any, dv_any = refs[:2]
    ga_buf, hot_ref, qg_ref, p_ref, k_ref, v_ref, gag_ref, dq_ref, dk_ref, dv_ref = refs[2:12]
    in_sems, hot_sem, block_sems, out_sems, part_sems = refs[12:]
    ga_copies = loads(ga_refs, ga_buf, in_sems)
    hot_copy = pltpu.make_async_copy(hot_any, hot_ref, hot_sem.at[0])
    hot_copy.start()
    for copies in ga_copies:
        start(copies)

    def block_loads(b):
        pairs = ((qg_any, qg_ref), (p_any, p_ref), (k_any, k_ref), (v_any, v_ref))
        return [
            pltpu.make_async_copy(far.at[b], near.at[b], block_sems.at[i, b])
            for i, (far, near) in enumerate(pairs)
        ]

    def block_stores(b):
        return [
            pltpu.make_async_copy(dk_ref.at[b], dk_any.at[b], out_sems.at[0, b]),
            pltpu.make_async_copy(dv_ref.at[b], dv_any.at[b], out_sems.at[1, b]),
        ]

    block_count, _, width = k_ref.shape
    heads = width // HD
    rows = part_refs[0].shape[0]
    groups = chunks // span
    scale = HD ** (-0.5)

    for b in range(block_count):
        start(block_loads(b))
    hot_copy.wait()
    for g in range(groups):
        for i in range(span):
            wait(ga_copies[g * span + i])
        ga_group = joined([ga_buf[g * span + i] for i in range(span)], 0)
        gag_ref[:, g * cap : (g + 1) * cap, :] = (
            mm(hot_ref[g], ga_group).astype(BF16).reshape(block_count, cap, width + HD)
        )
    last = lax.broadcasted_iota(jnp.int32, (BLOCK, groups * cap), 0) == BLOCK - 1

    pairs = [slice(p * 2 * HD, (p + 1) * 2 * HD) for p in range(heads // 2)]

    def some_blocks(step, carry):
        blocks = [step * TOGETHER + u for u in range(TOGETHER)]
        for b in blocks:
            wait(block_loads(b))
        grads = [
            [mm(diagonal(v_ref[b, :, cols]), gag_ref[b, :, cols], NT) for cols in pairs]
            for b in blocks
        ]
        gated, scores = [], []
        for b, grad_pairs in zip(blocks, grads):
            tail = gag_ref[b, :, width:].astype(F32).T
            tail = [tail[i * heads : (i + 1) * heads] for i in range(5)]
            dots = tail[0] + tail[1]
            gates = jnp.exp(jnp.minimum(logit_ref[b] - (tail[2] + tail[3] + tail[4]), 0.0))
            for p in range(heads // 2):
                both = p_ref[b, p].astype(F32)
                low, high = [], []
                for i in range(2):
                    at = slice(i * BLOCK, (i + 1) * BLOCK)
                    h = 2 * p + i
                    gate = gates[h : h + 1, :]
                    grad, probs = grad_pairs[p][at], both[at]
                    delta = jnp.sum(probs * grad, axis=0, keepdims=True)
                    weight = probs * gate
                    extra = jnp.where(last, scale * gate * (delta - dots[h : h + 1, :]), 0.0)
                    low.append((weight * (scale * (grad - delta)) + extra).astype(BF16))
                    high.append(weight.astype(BF16))
                scores.append(low)
                gated.append(high)
        for u, b in enumerate(blocks):
            for p, cols in enumerate(pairs):
                score, weight = scores[u * len(pairs) + p], gated[u * len(pairs) + p]
                for i in range(2):
                    head = slice((2 * p + i) * HD, (2 * p + i + 1) * HD)
                    dv_ref[b, :, head] = mm(weight[i], gag_ref[b, :, head])
                    dk_ref[b, :, head] = mm(score[i], qg_ref[b, :, head])
                both = jnp.concatenate(score, axis=0)
                dq_ref[b, :, cols] = mm(both, diagonal(k_ref[b, :, cols]), TN).astype(BF16)
        for b in blocks:
            start(block_stores(b))
        return carry

    lax.fori_loop(0, block_count // TOGETHER, some_blocks, 0)

    part_copies = []

    for g in range(groups):
        slots = dq_ref[:, g * cap : (g + 1) * cap, :].reshape(block_count * cap, width)
        part = mm(hot_ref[g], slots, TN).astype(BF16)
        for i in range(span):
            m = g * span + i
            ga_buf[m, :, :width] = part[i * rows : (i + 1) * rows]
            copy = pltpu.make_async_copy(
                ga_buf.at[m, :, pl.ds(0, width)], part_refs[m], part_sems.at[m]
            )
            copy.start()
            part_copies.append(copy)
    for b in range(block_count):
        wait(block_stores(b))
    wait(part_copies)


def weight_kernel(counts, first, me_ref, cols_ref, *refs):
    attns, (*before, out_ref) = dealt(refs, counts)
    me = me_ref[0]
    columns = joined([cols_ref[me ^ (first + m)] for m in range(len(counts))], 0)
    total = mm(columns, joined([whole(pieces) for pieces in attns], 0), TN)
    for ref in before:
        total = total + ref[...]
    out_ref[...] = total


def swap(x, bits):
    count = lax.axis_size("ctx")
    return lax.ppermute(x, "ctx", [(i, i ^ bits) for i in range(count)])


def after(x, *others):
    return lax.optimization_barrier((x, *others))[0]


def flat(lists):
    return [x for pieces in lists for x in pieces]


def spread_near(x):
    chips = lax.axis_size("ctx") // 2
    return [[x]] + [[swap(x, 2 * j)] for j in range(1, chips if chips != 4 else 3)]


def spread_far(near, half, *before):
    if len(near) != 3:
        return near
    (x_way,), (y_way,) = near[1:]
    far = [swap(after(x_way[:half], *before), 4), swap(after(y_way[half:], *before), 2)]
    return near + [far]


def spread_chips(x, half, *before):
    return spread_far(spread_near(x), half, *before)


def spread_halves(top, low):
    chips = lax.axis_size("ctx") // 2
    if chips != 4:
        return [[swap(x, 2 * j) if j else x for x in (top, low)] for j in range(chips)]
    x_top, y_low = swap(top, 2), swap(low, 4)
    x_low, y_top = swap(low, 2), swap(top, 4)
    return [[top, low], [x_top, x_low], [y_top, y_low], [swap(x_top, 4), swap(y_low, 2)]]


def with_cores(lists, *before):
    both = []
    for pieces in lists:
        if before and pieces is lists[-1]:
            pieces = [after(piece, *before) for piece in pieces]
        both += [pieces, [swap(piece, 1) for piece in pieces]]
    return both


def from_core(parts, *before):
    received = [None] * (len(parts) // 2)
    for j in reversed(range(len(received))):
        received[j] = swap(after(parts[2 * j + 1], *before), 1)
    return received


def collect_chips(parts, received):
    chips = len(received)

    def both(j, rows, extra=None, earlier=None):
        mine = parts[2 * j] if earlier is None else after(parts[2 * j], earlier)
        total = mine[rows].astype(F32) + received[j][rows].astype(F32)
        if extra is not None:
            total = total + extra.astype(F32)
        return total.astype(BF16)

    terms = [[parts[0]], [received[0]]]
    if chips != 4:
        return terms + [[swap(both(j, slice(None)), 2 * j)] for j in range(1, chips)], []
    half = parts[0].shape[0] // 2
    top, low = slice(0, half), slice(half, None)
    x_sum, y_sum = both(3, top), both(3, low)
    x_far, y_far = swap(x_sum, 2), swap(y_sum, 4)
    x_sum, y_sum = both(1, top, None, x_sum), both(2, low, None, y_sum)
    x_top, y_low = swap(x_sum, 2), swap(y_sum, 4)
    x_sum, y_sum = both(1, low, y_far, x_sum), both(2, top, x_far, y_sum)
    x_low, y_top = swap(x_sum, 2), swap(y_sum, 4)
    return terms + [[x_top, x_low], [y_top, y_low]], [x_top, y_low]


def merge_chips(parts, received, heads, between):
    chips = len(received)
    rows = parts[0].shape[0]
    half = rows // 2

    def merged(ins, plan):
        return pl.pallas_call(
            functools.partial(merge_kernel, plan, heads),
            out_shape=[
                jax.ShapeDtypeStruct((terms[0][2], ins[0].shape[1]), BF16) for terms in plan
            ],
            in_specs=[pl.BlockSpec(memory_space=pltpu.VMEM)] * len(ins),
            out_specs=[pl.BlockSpec(memory_space=pltpu.VMEM)] * len(plan),
            compiler_params=pltpu.CompilerParams(vmem_limit_bytes=SOME),
            name="merge",
        )(*ins)

    terms = [[parts[0]], [received[0]]]
    if chips != 4:
        for j in range(1, chips):
            (both,) = merged([parts[2 * j], received[j]], [[(0, 0, rows), (1, 0, rows)]])
            terms.append([swap(both, 2 * j)])
        return terms, between(received[0])
    top, low = (0, half), (half, half)
    x_far, y_far = merged(
        [parts[6], received[3]], [[(0, *top), (1, *top)], [(0, *low), (1, *low)]]
    )
    x_far, y_far = swap(x_far, 2), swap(y_far, 4)
    ins = [parts[2], received[1], parts[4], received[2]]
    x_top, y_low = merged(ins, [[(0, *top), (1, *top)], [(2, *low), (3, *low)]])
    x_top, y_low = swap(x_top, 2), swap(y_low, 4)
    x_low, y_top = merged(
        ins + [y_far, x_far],
        [[(0, *low), (1, *low), (4, *top)], [(2, *top), (3, *top), (5, *top)]],
    )
    done = between(x_low, y_top)
    x_low, y_top = swap(x_low, 2), swap(y_top, 4)
    return terms + [[x_top, x_low], [y_top, y_low]], done


def spread_line(x):
    lines = lax.axis_size("head")
    ups, downs = [x], [x]
    for d in range(1, lines):
        up = [(i, i + 1) for i in range(d - 1, lines - 1)]
        down = [(i, i - 1) for i in range(1, lines - d + 1)]
        if d == lines - 1 and lines > 2:
            last = jnp.where(lax.axis_index("head") == lines - 2, ups[-1], downs[-1])
            last = lax.ppermute(last, "head", up + down)
            ups.append(last)
            downs.append(last)
        else:
            ups.append(lax.ppermute(ups[-1], "head", up))
            downs.append(lax.ppermute(downs[-1], "head", down))
    return ups[1:], downs[1:]


def body(queries, key_rows, value_rows, selected, out_grad, out_weight):
    chunks = lax.axis_size("ctx")
    chips = chunks // 2
    lines = lax.axis_size("head")
    rows, width = queries.shape
    features = out_weight.shape[0]
    heads = width // HD
    block_count = key_rows.shape[0] // BLOCK
    block_total = block_count * chunks
    capacity = 2 * rows * TOPK // block_total
    span = max(1, 16 // capacity)
    cap = capacity * span
    groups = chunks // span
    slots = groups * cap
    index = lax.axis_index("ctx").astype(jnp.int32)
    me = index.reshape(1)
    keys = key_rows.reshape(block_count, BLOCK, width)
    values = value_rows.reshape(block_count, BLOCK, width)
    vmem = pl.BlockSpec(memory_space=pltpu.VMEM)
    smem = pl.BlockSpec(memory_space=pltpu.SMEM)
    anywhere = pl.BlockSpec(memory_space=pl.ANY)
    params = pltpu.CompilerParams(vmem_limit_bytes=MOST)
    small = pltpu.CompilerParams(vmem_limit_bytes=SOME)

    def shaped(shape, kind=BF16):
        return jax.ShapeDtypeStruct(shape, kind)

    ups, downs = spread_line(out_grad)
    packed = pl.pallas_call(
        pack_kernel,
        out_shape=shaped((rows + PAD, width)),
        in_specs=[vmem] * 2,
        out_specs=vmem,
        compiler_params=small,
        name="pack",
    )(selected.T, queries)
    query_chips = spread_chips(packed, rows // 2)
    query_all = with_cores(query_chips, ups[0], downs[0])

    outs = pl.pallas_call(
        functools.partial(forward_kernel, [len(pieces) for pieces in query_all], span, cap),
        out_shape=[shaped((rows, width + HD))] * chunks
        + [
            shaped((block_count, slots, width)),
            shaped((block_count, heads // 2, 2 * BLOCK, slots)),
            shaped((block_count, heads, slots), F32),
            shaped((groups, block_count * cap, rows * span)),
        ],
        in_specs=[smem, vmem] + [anywhere] * (2 + len(flat(query_all))),
        out_specs=[anywhere] * (chunks + 2) + [vmem, anywhere],
        scratch_shapes=[
            pltpu.VMEM((chunks, rows + PAD, width), BF16),
            pltpu.VMEM((chunks, rows, width + HD), BF16),
            pltpu.VMEM((block_count, BLOCK, width), BF16),
            pltpu.VMEM((block_count, BLOCK, width), BF16),
            pltpu.VMEM((block_count, slots, width), BF16),
            pltpu.VMEM((block_count, heads // 2, 2 * BLOCK, slots), BF16),
            pltpu.VMEM((groups, block_count * cap, rows * span), BF16),
            pltpu.VMEM((block_count, slots, HD), F32),
            pltpu.VMEM((block_count, slots, width), BF16),
            pltpu.SemaphoreType.DMA((len(flat(query_all)),)),
            pltpu.SemaphoreType.DMA((2,)),
            pltpu.SemaphoreType.DMA((chunks + 3,)),
        ],
        compiler_params=params,
        name="forward",
    )(me, keys[:, BLOCK - 1], keys, values, *flat(query_all))
    q_slots, probs, logits, hot = outs[chunks:]

    line = lax.axis_index("head").astype(jnp.int32).reshape(1)
    make_grad = pl.pallas_call(
        functools.partial(grad_kernel, lines),
        out_shape=[shaped((rows, width)), shaped((chunks, rows, features // chunks))],
        in_specs=[smem] + [anywhere] * (2 * lines),
        out_specs=[vmem] * 2,
        scratch_shapes=[
            pltpu.VMEM((lines, rows, width), BF16),
            pltpu.VMEM((lines, width, width), BF16),
            pltpu.SemaphoreType.DMA((lines,)),
            pltpu.SemaphoreType.DMA((lines,)),
        ],
        compiler_params=params,
        name="grad",
    )
    received = from_core(outs[:chunks], ups[1], downs[1])
    terms, (grad_attn, blocks) = merge_chips(
        outs[:chunks],
        received,
        heads,
        lambda *before: make_grad(after(line, *before), out_weight, out_grad, *ups, *downs),
    )
    attn_out, *extended = pl.pallas_call(
        functools.partial(finish_kernel, [len(pieces) for pieces in terms]),
        out_shape=[shaped((rows, width))] + [shaped((rows // 2, width + HD))] * 2,
        in_specs=[vmem] * (len(flat(terms)) + 1),
        out_specs=[vmem] * 3,
        compiler_params=small,
        name="finish",
    )(*flat(terms), grad_attn)
    grad_chips = spread_halves(*extended)
    grad_all = with_cores(grad_chips)
    arrived = flat(grad_chips[1:])
    columns = lax.all_to_all(
        after(blocks, *arrived), "ctx", split_axis=0, concat_axis=0, tiled=True
    )

    outs = pl.pallas_call(
        functools.partial(backward_kernel, [len(pieces) for pieces in grad_all], span, cap),
        out_shape=[shaped((rows, width))] * chunks
        + [shaped((block_count, BLOCK, width), F32)] * 2,
        in_specs=[vmem] + [anywhere] * (5 + len(flat(grad_all))),
        out_specs=[anywhere] * (chunks + 2),
        scratch_shapes=[
            pltpu.VMEM((chunks, rows, width + HD), BF16),
            pltpu.VMEM((groups, block_count * cap, rows * span), BF16),
            pltpu.VMEM((block_count, slots, width), BF16),
            pltpu.VMEM((block_count, heads // 2, 2 * BLOCK, slots), BF16),
            pltpu.VMEM((block_count, BLOCK, width), BF16),
            pltpu.VMEM((block_count, BLOCK, width), BF16),
            pltpu.VMEM((block_count, slots, width + HD), BF16),
            pltpu.VMEM((block_count, slots, width), BF16),
            pltpu.VMEM((block_count, BLOCK, width), F32),
            pltpu.VMEM((block_count, BLOCK, width), F32),
            pltpu.SemaphoreType.DMA((len(flat(grad_all)),)),
            pltpu.SemaphoreType.DMA((1,)),
            pltpu.SemaphoreType.DMA((4, block_count)),
            pltpu.SemaphoreType.DMA((2, block_count)),
            pltpu.SemaphoreType.DMA((chunks,)),
        ],
        compiler_params=params,
        name="backward",
    )(logits, hot, q_slots, probs, keys, values, *flat(grad_all))
    key_grad, value_grad = outs[chunks:]
    received = from_core(outs[:chunks], columns)
    terms, arrived = collect_chips(outs[:chunks], received)
    attns = with_cores(spread_chips(after(attn_out, *arrived), rows // 2))

    def weight_part(chosen, first, when, *before):
        return pl.pallas_call(
            functools.partial(weight_kernel, [len(pieces) for pieces in chosen], first),
            out_shape=shaped((features // chunks, width), F32),
            in_specs=[smem] + [vmem] * (1 + len(flat(chosen)) + len(before)),
            out_specs=vmem,
            compiler_params=small,
            name="weight",
        )(when, columns, *flat(chosen), *before)

    weight_near = weight_part(attns[:-2], 0, me)
    query_grad = pl.pallas_call(
        functools.partial(total_kernel, [len(pieces) for pieces in terms]),
        out_shape=shaped((rows, width), F32),
        in_specs=[vmem] * len(flat(terms)),
        out_specs=vmem,
        compiler_params=small,
        name="total",
    )(*flat(terms))
    weight_grad = weight_part(attns[-2:], chunks - 2, me, weight_near)
    return (
        query_grad,
        key_grad.reshape(-1, width),
        value_grad.reshape(-1, width),
        weight_grad,
    )


def solution(mesh):
    return jax.shard_map(
        body,
        mesh=mesh,
        in_specs=(
            P("ctx", "head"),
            P("ctx", "head"),
            P("ctx", "head"),
            P("ctx", None),
            P("ctx", "head"),
            P(None, "head"),
        ),
        out_specs=(P("ctx", "head"), P("ctx", "head"), P("ctx", "head"), P("ctx", "head")),
        check_vma=False,
    )
```

```python
import functools

import jax
import jax.numpy as jnp
from jax import lax
from jax.experimental import pallas as pl
from jax.experimental.pallas import tpu as pltpu
from jax.sharding import PartitionSpec as P

HD = 128
BLOCK = 64
TOPK = 4
F32 = jnp.float32
BF16 = jnp.bfloat16
MOST = 58 * 1024 * 1024
SOME = 20 * 1024 * 1024
PAD = 16
TOGETHER = 4
LOW = -(2.0**99)
NN = (((1,), (0,)), ((), ()))
NT = (((1,), (1,)), ((), ()))
TN = (((0,), (0,)), ((), ()))


def mm(a, b, dims=NN):
    return lax.dot_general(a, b, dims, preferred_element_type=F32)


def joined(items, axis):
    return items[0] if len(items) == 1 else jnp.concatenate(items, axis=axis)


def dealt(refs, counts):
    lists, at = [], 0
    for count in counts:
        lists.append(refs[at : at + count])
        at += count
    return lists, refs[at:]


def loads(lists, buf, sems):
    copies, at = [], 0
    for i, refs in enumerate(lists):
        mine, row = [], 0
        for ref in refs:
            rows = ref.shape[0]
            mine.append(
                pltpu.make_async_copy(ref, buf.at[i, pl.ds(row, rows)], sems.at[at])
            )
            row += rows
            at += 1
        copies.append(mine)
    return copies


def start(copies):
    for copy in copies:
        copy.start()


def wait(copies):
    for copy in copies:
        copy.wait()


def whole(refs):
    return joined([ref[...] for ref in refs], 0)


def added(terms, cols):
    total = None
    for refs in terms:
        term = joined([ref[:, cols].astype(F32) for ref in refs], 0)
        total = term if total is None else total + term
    return total


def diagonal(pair):
    zero = jnp.zeros((pair.shape[0], HD), pair.dtype)
    top = jnp.concatenate([pair[:, :HD], zero], axis=1)
    low = jnp.concatenate([zero, pair[:, HD:]], axis=1)
    return jnp.concatenate([top, low], axis=0)


def pack_kernel(sel_ref, q_ref, out_ref):
    rows, width = q_ref.shape
    out_ref[:rows] = q_ref[...]
    digits = [(sel_ref[...] >> 4).astype(F32), (sel_ref[...] & 15).astype(F32)]
    if width > 2 * rows:
        digits.append(jnp.zeros((TOPK, width - 2 * rows), F32))
    lines = [jnp.concatenate(digits, axis=1), jnp.zeros((PAD - TOPK, width), F32)]
    out_ref[rows:] = jnp.concatenate(lines, axis=0).astype(BF16)


def forward_kernel(counts, span, cap, me_ref, mark_ref, k_any, v_any, *refs):
    chunks = len(counts)
    q_refs, refs = dealt(refs, counts)
    part_any, refs = refs[:chunks], refs[chunks:]
    qg_any, p_any, logit_ref, hot_any = refs[:4]
    q_buf, part_refs, k_ref, v_ref, qg_ref, p_ref, hot_ref, topg_ref, out_ref = refs[4:13]
    in_sems, kv_sems, out_sems = refs[13:]
    q_copies = loads(q_refs, q_buf, in_sems)
    kv_copies = [
        pltpu.make_async_copy(k_any, k_ref, kv_sems.at[0]),
        pltpu.make_async_copy(v_any, v_ref, kv_sems.at[1]),
    ]
    out_copies = [
        pltpu.make_async_copy(qg_ref, qg_any, out_sems.at[chunks]),
        pltpu.make_async_copy(hot_ref, hot_any, out_sems.at[chunks + 1]),
        pltpu.make_async_copy(p_ref, p_any, out_sems.at[chunks + 2]),
    ]
    for copies in q_copies:
        start(copies)
    start(kv_copies)
    block_count, _, width = k_ref.shape
    heads = width // HD
    rows = part_any[0].shape[0]
    group_rows = rows * span
    groups = chunks // span
    scale = HD ** (-0.5)
    rate = scale * 1.4426950408889634
    base = me_ref[0] * block_count

    before = lax.broadcasted_iota(jnp.int32, (group_rows, group_rows), 0)
    later = lax.broadcasted_iota(jnp.int32, (group_rows, group_rows), 1)
    earlier = (before < later).astype(BF16)
    own_ids = (base + lax.broadcasted_iota(jnp.int32, (block_count, group_rows), 0)).astype(F32)
    place = lax.broadcasted_iota(jnp.int32, (cap, group_rows), 0).astype(F32)
    zero = jnp.zeros((block_count, HD), BF16)
    wide_marks = jnp.concatenate(
        [
            jnp.concatenate(
                [mark_ref[:, i * HD : (i + 1) * HD] if i == h else zero for i in range(heads)], axis=1
            )
            for h in range(heads)
        ],
        axis=0,
    )
    q_groups, owns = [], []
    for g in range(groups):
        for i in range(span):
            wait(q_copies[g * span + i])
        packs = [q_buf[g * span + i] for i in range(span)]
        digits = [pack[rows : rows + PAD].astype(F32)[:TOPK] for pack in packs]
        picked = joined([16.0 * d[:, :rows] + d[:, rows : 2 * rows] for d in digits], 1)
        own = picked[0:1, :] == own_ids
        for t in range(1, TOPK):
            own = own | (picked[t : t + 1, :] == own_ids)
        owns.append(jnp.where(own, 1.0, 0.0))
        q_groups.append(joined([pack[:rows] for pack in packs], 0))
    own_all = jnp.concatenate(owns, axis=0)
    rank_all = jnp.where(own_all > 0.5, mm(own_all.astype(BF16), earlier), -1.0)
    hots = []
    for g in range(groups):
        rank = rank_all[g * block_count : (g + 1) * block_count]
        hots.append(
            jnp.concatenate(
                [
                    jnp.where(rank[b : b + 1, :] == place, 1.0, 0.0).astype(BF16)
                    for b in range(block_count)
                ],
                axis=0,
            )
        )
        hot_ref[g] = hots[g]
    all_marks = [mm(wide_marks, q_groups[g], NT) for g in range(groups)]
    for g in range(groups):
        qg_ref[:, g * cap : (g + 1) * cap, :] = (
            mm(hots[g], q_groups[g]).astype(BF16).reshape(block_count, cap, width)
        )
    tails = []
    for g in range(groups):
        tops, sums = [], []
        for h in range(heads):
            mark = scale * all_marks[g][h * block_count : (h + 1) * block_count]
            mark = jnp.where(owns[g] > 0.5, mark, LOW)
            top = jnp.max(mark, axis=0, keepdims=True).astype(BF16).astype(F32)
            tops.append(top)
            sums.append(jnp.sum(owns[g] * jnp.exp(mark - top), axis=0, keepdims=True))
        tops, sums = jnp.concatenate(tops, axis=0), jnp.concatenate(sums, axis=0)
        upper = sums.astype(BF16).astype(F32)
        spare = jnp.zeros((HD - 3 * heads, group_rows), F32)
        tails.append(jnp.concatenate([tops, upper, sums - upper, spare], axis=0))
    for g in range(groups):
        topg_ref[:, g * cap : (g + 1) * cap, :] = mm(hots[g], tails[g].astype(BF16), NT).reshape(
            block_count, cap, HD
        )
    for g in range(groups):
        for i in range(span):
            part_refs[g * span + i, :, width:] = (
                tails[g][:, i * rows : (i + 1) * rows].T.astype(BF16)
            )
    start(out_copies[:2])
    wait(kv_copies)

    pairs = [slice(p * 2 * HD, (p + 1) * 2 * HD) for p in range(heads // 2)]

    def some_blocks(step, carry):
        blocks = [step * TOGETHER + u for u in range(TOGETHER)]
        logits = [
            [mm(diagonal(k_ref[b, :, cols]), qg_ref[b, :, cols], NT) for cols in pairs]
            for b in blocks
        ]
        probs, gated, kept = [], [], []
        for b, scores in zip(blocks, logits):
            tops = topg_ref[b].T[:heads]
            marks = scale * jnp.concatenate(
                [scores[h // 2][(h % 2 + 1) * BLOCK - 1 : (h % 2 + 1) * BLOCK] for h in range(heads)],
                axis=0,
            )
            gates = jnp.exp(marks - tops)
            kept.append(marks)
            for p in range(heads // 2):
                low, high = [], []
                for i in range(2):
                    part = scores[p][i * BLOCK : (i + 1) * BLOCK]
                    weight = jnp.exp2(rate * (part - jnp.max(part, axis=0, keepdims=True)))
                    inverse = 1.0 / jnp.sum(weight, axis=0, keepdims=True)
                    gate = gates[2 * p + i : 2 * p + i + 1, :]
                    low.append((weight * inverse).astype(BF16))
                    high.append((weight * (inverse * gate)).astype(BF16))
                probs.append(jnp.concatenate(low, axis=0))
                gated.append(jnp.concatenate(high, axis=0))
        outs = []
        for u, b in enumerate(blocks):
            for p, cols in enumerate(pairs):
                both = gated[u * len(pairs) + p]
                outs.append(mm(both, diagonal(v_ref[b, :, cols]), TN).astype(BF16))
        for u, b in enumerate(blocks):
            logit_ref[b] = kept[u]
            for p, cols in enumerate(pairs):
                p_ref[b, p] = probs[u * len(pairs) + p]
                out_ref[b, :, cols] = outs[u * len(pairs) + p]
        return carry

    lax.fori_loop(0, block_count // TOGETHER, some_blocks, 0)
    start(out_copies[2:])

    for g in range(groups):
        slots = out_ref[:, g * cap : (g + 1) * cap, :].reshape(block_count * cap, width)
        part = mm(hot_ref[g], slots, TN).astype(BF16)
        for i in range(span):
            m = g * span + i
            part_refs[m, :, :width] = part[i * rows : (i + 1) * rows]
            copy = pltpu.make_async_copy(part_refs.at[m], part_any[m], out_sems.at[m])
            copy.start()
            out_copies.append(copy)
    wait(out_copies)


def shift(heads, *moves):
    row = lax.broadcasted_iota(jnp.int32, (HD, HD), 0)
    col = lax.broadcasted_iota(jnp.int32, (HD, HD), 1)
    total = jnp.zeros((HD, HD), F32)
    for source, target in moves:
        inside = (row >= source * heads) & (row < (source + 1) * heads)
        hit = inside & (col - target * heads == row - source * heads)
        total = jnp.where(hit, 1.0, total)
    return total.astype(BF16)


def blend(terms, heads):
    width = heads * HD
    tails = [joined([ref[rows, width:] for ref, rows in term], 0) for term in terms]
    wide = [tail.astype(F32) for tail in tails]
    top = wide[0]
    for tail in wide[1:]:
        top = jnp.maximum(top, tail)
    gather = shift(heads, (1, 0), (2, 0))
    factors = [jnp.exp(tail - top) for tail in wide]
    total = None
    for tail, factor in zip(tails, factors):
        share = factor * mm(tail, gather)
        total = share if total is None else total + share
    columns = []
    for h in range(heads):
        cols = slice(h * HD, (h + 1) * HD)
        column = None
        for term, factor in zip(terms, factors):
            values = joined([ref[rows, cols] for ref, rows in term], 0).astype(F32)
            part = factor[:, h : h + 1] * values
            column = part if column is None else column + part
        columns.append(column)
    return top, total, columns


def digits_of(tile, count):
    digits = []
    for _ in range(count):
        upper = tile.astype(BF16)
        digits.append(upper)
        tile = tile - upper.astype(F32)
    return digits


def packed_tail(digits, heads):
    total = None
    for i, digit in enumerate(digits):
        part = mm(digit, shift(heads, (0, i)))
        total = part if total is None else total + part
    return total.astype(BF16)


def merge_kernel(plan, heads, *refs):
    ins, outs = refs[: len(refs) - len(plan)], refs[len(refs) - len(plan) :]
    for terms, out_ref in zip(plan, outs):
        top, total, columns = blend(
            [[(ins[i], pl.ds(first, count))] for i, first, count in terms], heads
        )
        for h in range(heads):
            out_ref[:, h * HD : (h + 1) * HD] = columns[h].astype(BF16)
        out_ref[:, heads * HD :] = packed_tail([top.astype(BF16)] + digits_of(total, 2), heads)


def grad_kernel(lines, line_ref, w_ref, *refs):
    own_ref, up_refs, down_refs = refs[0], refs[1:lines], refs[lines : 2 * lines - 1]
    ga_ref, blocks_ref, full_ref, w_buf, sems, piece_sems = refs[2 * lines - 1 :]
    width = own_ref.shape[1]
    chunks, _, share = blocks_ref.shape
    line = line_ref[0]
    copies = [
        pltpu.make_async_copy(w_ref.at[pl.ds(i * width, width)], w_buf.at[i], sems.at[i])
        for i in range(lines)
    ]
    start(copies)

    def placed(ref, i):
        return pltpu.make_async_copy(ref, full_ref.at[i], piece_sems.at[i])

    placed(own_ref, line).start()
    for d in range(1, lines):

        @pl.when(line >= d)
        def _():
            placed(up_refs[d - 1], line - d).start()

        @pl.when(line + d < lines)
        def _():
            placed(down_refs[d - 1], line + d).start()

    for i in range(lines):
        placed(own_ref, i).wait()
    for j in range(chunks):
        first = j * share
        blocks_ref[j] = full_ref[first // width, :, first % width : first % width + share]
    total = None
    for i in range(lines):
        copies[i].wait()
        term = mm(full_ref[i], w_buf[i])
        total = term if total is None else total + term
    ga_ref[...] = total.astype(BF16)


def finish_kernel(counts, *refs):
    terms, (ga_ref, attn_ref, *ext_refs) = dealt(refs, counts)
    rows, width = ga_ref.shape
    half = rows // len(ext_refs)
    heads = width // HD
    top, total, columns = blend(
        [[(ref, slice(None)) for ref in pieces] for pieces in terms], heads
    )
    lane = lax.broadcasted_iota(jnp.int32, (rows, HD), 1)
    total = jnp.where(lane < heads, total, 1.0)
    inverse = 1.0 / total
    dots = jnp.zeros((rows, HD), F32)
    for i, ext_ref in enumerate(ext_refs):
        ext_ref[:, :width] = ga_ref[i * half : (i + 1) * half]
    for h in range(heads):
        cols = slice(h * HD, (h + 1) * HD)
        attn = columns[h] * inverse[:, h : h + 1]
        attn_ref[:, cols] = attn.astype(BF16)
        dot = jnp.sum(attn * ga_ref[:, cols].astype(F32), axis=1, keepdims=True)
        dots = jnp.where(lane == h, dot, dots)
    level = jnp.where(lane < heads, top + jnp.log(total), 0.0)
    tail = packed_tail(digits_of(dots, 2) + digits_of(level, 3), heads)
    for i, ext_ref in enumerate(ext_refs):
        ext_ref[:, width:] = tail[i * half : (i + 1) * half]


def total_kernel(counts, *refs):
    terms, (out_ref,) = dealt(refs, counts)
    for h in range(out_ref.shape[1] // HD):
        cols = slice(h * HD, (h + 1) * HD)
        out_ref[:, cols] = added(terms, cols)


def backward_kernel(counts, span, cap, logit_ref, hot_any, qg_any, p_any, k_any, v_any, *refs):
    chunks = len(counts)
    ga_refs, refs = dealt(refs, counts)
    part_refs, refs = refs[:chunks], refs[chunks:]
    dk_any, dv_any = refs[:2]
    ga_buf, hot_ref, qg_ref, p_ref, k_ref, v_ref, gag_ref, dq_ref, dk_ref, dv_ref = refs[2:12]
    in_sems, hot_sem, block_sems, out_sems, part_sems = refs[12:]
    ga_copies = loads(ga_refs, ga_buf, in_sems)
    hot_copy = pltpu.make_async_copy(hot_any, hot_ref, hot_sem.at[0])
    hot_copy.start()
    for copies in ga_copies:
        start(copies)

    def block_loads(b):
        pairs = ((qg_any, qg_ref), (p_any, p_ref), (k_any, k_ref), (v_any, v_ref))
        return [
            pltpu.make_async_copy(far.at[b], near.at[b], block_sems.at[i, b])
            for i, (far, near) in enumerate(pairs)
        ]

    def block_stores(b):
        return [
            pltpu.make_async_copy(dk_ref.at[b], dk_any.at[b], out_sems.at[0, b]),
            pltpu.make_async_copy(dv_ref.at[b], dv_any.at[b], out_sems.at[1, b]),
        ]

    block_count, _, width = k_ref.shape
    heads = width // HD
    rows = part_refs[0].shape[0]
    groups = chunks // span
    scale = HD ** (-0.5)

    for b in range(block_count):
        start(block_loads(b))
    hot_copy.wait()
    for g in range(groups):
        for i in range(span):
            wait(ga_copies[g * span + i])
        ga_group = joined([ga_buf[g * span + i] for i in range(span)], 0)
        gag_ref[:, g * cap : (g + 1) * cap, :] = (
            mm(hot_ref[g], ga_group).astype(BF16).reshape(block_count, cap, width + HD)
        )
    last = lax.broadcasted_iota(jnp.int32, (BLOCK, groups * cap), 0) == BLOCK - 1

    pairs = [slice(p * 2 * HD, (p + 1) * 2 * HD) for p in range(heads // 2)]

    def some_blocks(step, carry):
        blocks = [step * TOGETHER + u for u in range(TOGETHER)]
        for b in blocks:
            wait(block_loads(b))
        grads = [
            [mm(diagonal(v_ref[b, :, cols]), gag_ref[b, :, cols], NT) for cols in pairs]
            for b in blocks
        ]
        gated, scores = [], []
        for b, grad_pairs in zip(blocks, grads):
            tail = gag_ref[b, :, width:].astype(F32).T
            tail = [tail[i * heads : (i + 1) * heads] for i in range(5)]
            dots = tail[0] + tail[1]
            gates = jnp.exp(jnp.minimum(logit_ref[b] - (tail[2] + tail[3] + tail[4]), 0.0))
            for p in range(heads // 2):
                both = p_ref[b, p].astype(F32)
                low, high = [], []
                for i in range(2):
                    at = slice(i * BLOCK, (i + 1) * BLOCK)
                    h = 2 * p + i
                    gate = gates[h : h + 1, :]
                    grad, probs = grad_pairs[p][at], both[at]
                    delta = jnp.sum(probs * grad, axis=0, keepdims=True)
                    weight = probs * gate
                    extra = jnp.where(last, scale * gate * (delta - dots[h : h + 1, :]), 0.0)
                    low.append((weight * (scale * (grad - delta)) + extra).astype(BF16))
                    high.append(weight.astype(BF16))
                scores.append(low)
                gated.append(high)
        for u, b in enumerate(blocks):
            for p, cols in enumerate(pairs):
                score, weight = scores[u * len(pairs) + p], gated[u * len(pairs) + p]
                for i in range(2):
                    head = slice((2 * p + i) * HD, (2 * p + i + 1) * HD)
                    dv_ref[b, :, head] = mm(weight[i], gag_ref[b, :, head])
                    dk_ref[b, :, head] = mm(score[i], qg_ref[b, :, head])
                both = jnp.concatenate(score, axis=0)
                dq_ref[b, :, cols] = mm(both, diagonal(k_ref[b, :, cols]), TN).astype(BF16)
        for b in blocks:
            start(block_stores(b))
        return carry

    lax.fori_loop(0, block_count // TOGETHER, some_blocks, 0)

    part_copies = []

    for g in range(groups):
        slots = dq_ref[:, g * cap : (g + 1) * cap, :].reshape(block_count * cap, width)
        part = mm(hot_ref[g], slots, TN).astype(BF16)
        for i in range(span):
            m = g * span + i
            ga_buf[m, :, :width] = part[i * rows : (i + 1) * rows]
            copy = pltpu.make_async_copy(
                ga_buf.at[m, :, pl.ds(0, width)], part_refs[m], part_sems.at[m]
            )
            copy.start()
            part_copies.append(copy)
    for b in range(block_count):
        wait(block_stores(b))
    wait(part_copies)


def weight_kernel(counts, first, me_ref, cols_ref, *refs):
    attns, (*before, out_ref) = dealt(refs, counts)
    me = me_ref[0]
    columns = joined([cols_ref[me ^ (first + m)] for m in range(len(counts))], 0)
    total = mm(columns, joined([whole(pieces) for pieces in attns], 0), TN)
    for ref in before:
        total = total + ref[...]
    out_ref[...] = total


def swap(x, bits):
    count = lax.axis_size("ctx")
    return lax.ppermute(x, "ctx", [(i, i ^ bits) for i in range(count)])


def after(x, *others):
    return lax.optimization_barrier((x, *others))[0]


def flat(lists):
    return [x for pieces in lists for x in pieces]


def spread_near(x):
    chips = lax.axis_size("ctx") // 2
    return [[x]] + [[swap(x, 2 * j)] for j in range(1, chips if chips != 4 else 3)]


def spread_far(near, half, *before):
    if len(near) != 3:
        return near
    (x_way,), (y_way,) = near[1:]
    far = [swap(after(x_way[:half], *before), 4), swap(after(y_way[half:], *before), 2)]
    return near + [far]


def spread_chips(x, half, *before):
    return spread_far(spread_near(x), half, *before)


def spread_halves(top, low):
    chips = lax.axis_size("ctx") // 2
    if chips != 4:
        return [[swap(x, 2 * j) if j else x for x in (top, low)] for j in range(chips)]
    x_top, y_low = swap(top, 2), swap(low, 4)
    x_low, y_top = swap(low, 2), swap(top, 4)
    return [[top, low], [x_top, x_low], [y_top, y_low], [swap(x_top, 4), swap(y_low, 2)]]


def with_cores(lists, *before):
    both = []
    for pieces in lists:
        if before and pieces is lists[-1]:
            pieces = [after(piece, *before) for piece in pieces]
        both += [pieces, [swap(piece, 1) for piece in pieces]]
    return both


def from_core(parts, *before):
    received = [None] * (len(parts) // 2)
    for j in reversed(range(len(received))):
        received[j] = swap(after(parts[2 * j + 1], *before), 1)
    return received


def collect_chips(parts, received):
    chips = len(received)

    def both(j, rows, extra=None, earlier=None):
        mine = parts[2 * j] if earlier is None else after(parts[2 * j], earlier)
        total = mine[rows].astype(F32) + received[j][rows].astype(F32)
        if extra is not None:
            total = total + extra.astype(F32)
        return total.astype(BF16)

    terms = [[parts[0]], [received[0]]]
    if chips != 4:
        return terms + [[swap(both(j, slice(None)), 2 * j)] for j in range(1, chips)], []
    half = parts[0].shape[0] // 2
    top, low = slice(0, half), slice(half, None)
    x_sum, y_sum = both(3, top), both(3, low)
    x_far, y_far = swap(x_sum, 2), swap(y_sum, 4)
    x_sum, y_sum = both(1, top, None, x_sum), both(2, low, None, y_sum)
    x_top, y_low = swap(x_sum, 2), swap(y_sum, 4)
    x_sum, y_sum = both(1, low, y_far, x_sum), both(2, top, x_far, y_sum)
    x_low, y_top = swap(x_sum, 2), swap(y_sum, 4)
    return terms + [[x_top, x_low], [y_top, y_low]], [x_sum, y_sum]


def merge_chips(parts, received, heads, between):
    chips = len(received)
    rows = parts[0].shape[0]
    half = rows // 2

    def merged(ins, plan):
        return pl.pallas_call(
            functools.partial(merge_kernel, plan, heads),
            out_shape=[
                jax.ShapeDtypeStruct((terms[0][2], ins[0].shape[1]), BF16) for terms in plan
            ],
            in_specs=[pl.BlockSpec(memory_space=pltpu.VMEM)] * len(ins),
            out_specs=[pl.BlockSpec(memory_space=pltpu.VMEM)] * len(plan),
            compiler_params=pltpu.CompilerParams(vmem_limit_bytes=SOME),
            name="merge",
        )(*ins)

    terms = [[parts[0]], [received[0]]]
    if chips != 4:
        for j in range(1, chips):
            (both,) = merged([parts[2 * j], received[j]], [[(0, 0, rows), (1, 0, rows)]])
            terms.append([swap(both, 2 * j)])
        return terms, between(received[0])
    top, low = (0, half), (half, half)
    x_far, y_far = merged(
        [parts[6], received[3]], [[(0, *top), (1, *top)], [(0, *low), (1, *low)]]
    )
    x_far, y_far = swap(x_far, 2), swap(y_far, 4)
    ins = [parts[2], received[1], parts[4], received[2]]
    x_top, y_low = merged(ins, [[(0, *top), (1, *top)], [(2, *low), (3, *low)]])
    x_top, y_low = swap(x_top, 2), swap(y_low, 4)
    x_low, y_top = merged(
        ins + [y_far, x_far],
        [[(0, *low), (1, *low), (4, *top)], [(2, *top), (3, *top), (5, *top)]],
    )
    done = between(x_low, y_top)
    x_low, y_top = swap(x_low, 2), swap(y_top, 4)
    return terms + [[x_top, x_low], [y_top, y_low]], done


def spread_line(x):
    lines = lax.axis_size("head")
    ups, downs = [x], [x]
    for d in range(1, lines):
        up = [(i, i + 1) for i in range(d - 1, lines - 1)]
        down = [(i, i - 1) for i in range(1, lines - d + 1)]
        if d == lines - 1 and lines > 2:
            last = jnp.where(lax.axis_index("head") == lines - 2, ups[-1], downs[-1])
            last = lax.ppermute(last, "head", up + down)
            ups.append(last)
            downs.append(last)
        else:
            ups.append(lax.ppermute(ups[-1], "head", up))
            downs.append(lax.ppermute(downs[-1], "head", down))
    return ups[1:], downs[1:]


def body(queries, key_rows, value_rows, selected, out_grad, out_weight):
    chunks = lax.axis_size("ctx")
    chips = chunks // 2
    lines = lax.axis_size("head")
    rows, width = queries.shape
    features = out_weight.shape[0]
    heads = width // HD
    block_count = key_rows.shape[0] // BLOCK
    block_total = block_count * chunks
    capacity = 2 * rows * TOPK // block_total
    span = max(1, 16 // capacity)
    cap = capacity * span
    groups = chunks // span
    slots = groups * cap
    index = lax.axis_index("ctx").astype(jnp.int32)
    me = index.reshape(1)
    keys = key_rows.reshape(block_count, BLOCK, width)
    values = value_rows.reshape(block_count, BLOCK, width)
    vmem = pl.BlockSpec(memory_space=pltpu.VMEM)
    smem = pl.BlockSpec(memory_space=pltpu.SMEM)
    anywhere = pl.BlockSpec(memory_space=pl.ANY)
    params = pltpu.CompilerParams(vmem_limit_bytes=MOST)
    small = pltpu.CompilerParams(vmem_limit_bytes=SOME)

    def shaped(shape, kind=BF16):
        return jax.ShapeDtypeStruct(shape, kind)

    ups, downs = spread_line(out_grad)
    packed = pl.pallas_call(
        pack_kernel,
        out_shape=shaped((rows + PAD, width)),
        in_specs=[vmem] * 2,
        out_specs=vmem,
        compiler_params=small,
        name="pack",
    )(selected.T, queries)
    query_chips = spread_chips(packed, rows // 2)
    query_all = with_cores(query_chips, ups[0], downs[0])

    outs = pl.pallas_call(
        functools.partial(forward_kernel, [len(pieces) for pieces in query_all], span, cap),
        out_shape=[shaped((rows, width + HD))] * chunks
        + [
            shaped((block_count, slots, width)),
            shaped((block_count, heads // 2, 2 * BLOCK, slots)),
            shaped((block_count, heads, slots), F32),
            shaped((groups, block_count * cap, rows * span)),
        ],
        in_specs=[smem, vmem] + [anywhere] * (2 + len(flat(query_all))),
        out_specs=[anywhere] * (chunks + 2) + [vmem, anywhere],
        scratch_shapes=[
            pltpu.VMEM((chunks, rows + PAD, width), BF16),
            pltpu.VMEM((chunks, rows, width + HD), BF16),
            pltpu.VMEM((block_count, BLOCK, width), BF16),
            pltpu.VMEM((block_count, BLOCK, width), BF16),
            pltpu.VMEM((block_count, slots, width), BF16),
            pltpu.VMEM((block_count, heads // 2, 2 * BLOCK, slots), BF16),
            pltpu.VMEM((groups, block_count * cap, rows * span), BF16),
            pltpu.VMEM((block_count, slots, HD), F32),
            pltpu.VMEM((block_count, slots, width), BF16),
            pltpu.SemaphoreType.DMA((len(flat(query_all)),)),
            pltpu.SemaphoreType.DMA((2,)),
            pltpu.SemaphoreType.DMA((chunks + 3,)),
        ],
        compiler_params=params,
        name="forward",
    )(me, keys[:, BLOCK - 1], keys, values, *flat(query_all))
    q_slots, probs, logits, hot = outs[chunks:]

    line = lax.axis_index("head").astype(jnp.int32).reshape(1)
    make_grad = pl.pallas_call(
        functools.partial(grad_kernel, lines),
        out_shape=[shaped((rows, width)), shaped((chunks, rows, features // chunks))],
        in_specs=[smem] + [anywhere] * (2 * lines),
        out_specs=[vmem] * 2,
        scratch_shapes=[
            pltpu.VMEM((lines, rows, width), BF16),
            pltpu.VMEM((lines, width, width), BF16),
            pltpu.SemaphoreType.DMA((lines,)),
            pltpu.SemaphoreType.DMA((lines,)),
        ],
        compiler_params=params,
        name="grad",
    )
    received = from_core(outs[:chunks], ups[1], downs[1])
    terms, (grad_attn, blocks) = merge_chips(
        outs[:chunks],
        received,
        heads,
        lambda *before: make_grad(after(line, *before), out_weight, out_grad, *ups, *downs),
    )
    attn_out, *extended = pl.pallas_call(
        functools.partial(finish_kernel, [len(pieces) for pieces in terms]),
        out_shape=[shaped((rows, width))] + [shaped((rows // 2, width + HD))] * 2,
        in_specs=[vmem] * (len(flat(terms)) + 1),
        out_specs=[vmem] * 3,
        compiler_params=small,
        name="finish",
    )(*flat(terms), grad_attn)
    grad_chips = spread_halves(*extended)
    grad_all = with_cores(grad_chips)
    arrived = flat(grad_chips[1:])
    attns = spread_near(after(attn_out, *arrived))
    columns = lax.all_to_all(
        after(blocks, *arrived), "ctx", split_axis=0, concat_axis=0, tiled=True
    )

    outs = pl.pallas_call(
        functools.partial(backward_kernel, [len(pieces) for pieces in grad_all], span, cap),
        out_shape=[shaped((rows, width))] * chunks
        + [shaped((block_count, BLOCK, width), F32)] * 2,
        in_specs=[vmem] + [anywhere] * (5 + len(flat(grad_all))),
        out_specs=[anywhere] * (chunks + 2),
        scratch_shapes=[
            pltpu.VMEM((chunks, rows, width + HD), BF16),
            pltpu.VMEM((groups, block_count * cap, rows * span), BF16),
            pltpu.VMEM((block_count, slots, width), BF16),
            pltpu.VMEM((block_count, heads // 2, 2 * BLOCK, slots), BF16),
            pltpu.VMEM((block_count, BLOCK, width), BF16),
            pltpu.VMEM((block_count, BLOCK, width), BF16),
            pltpu.VMEM((block_count, slots, width + HD), BF16),
            pltpu.VMEM((block_count, slots, width), BF16),
            pltpu.VMEM((block_count, BLOCK, width), F32),
            pltpu.VMEM((block_count, BLOCK, width), F32),
            pltpu.SemaphoreType.DMA((len(flat(grad_all)),)),
            pltpu.SemaphoreType.DMA((1,)),
            pltpu.SemaphoreType.DMA((4, block_count)),
            pltpu.SemaphoreType.DMA((2, block_count)),
            pltpu.SemaphoreType.DMA((chunks,)),
        ],
        compiler_params=params,
        name="backward",
    )(logits, hot, q_slots, probs, keys, values, *flat(grad_all))
    key_grad, value_grad = outs[chunks:]
    received = from_core(outs[:chunks], columns, *flat(attns[1:3]))
    terms, last_sums = collect_chips(outs[:chunks], received)
    attns = with_cores(spread_far(attns, rows // 2, *last_sums))

    def weight_part(chosen, first, when, *before):
        return pl.pallas_call(
            functools.partial(weight_kernel, [len(pieces) for pieces in chosen], first),
            out_shape=shaped((features // chunks, width), F32),
            in_specs=[smem] + [vmem] * (1 + len(flat(chosen)) + len(before)),
            out_specs=vmem,
            compiler_params=small,
            name="weight",
        )(when, columns, *flat(chosen), *before)

    weight_near = weight_part(attns[:-2], 0, after(me, terms[2][0]))
    query_grad = pl.pallas_call(
        functools.partial(total_kernel, [len(pieces) for pieces in terms]),
        out_shape=shaped((rows, width), F32),
        in_specs=[vmem] * len(flat(terms)),
        out_specs=vmem,
        compiler_params=small,
        name="total",
    )(after(terms[0][0], weight_near), *flat(terms[1:]))
    weight_grad = weight_part(attns[-2:], chunks - 2, after(me, query_grad), weight_near)
    return (
        query_grad,
        key_grad.reshape(-1, width),
        value_grad.reshape(-1, width),
        weight_grad,
    )


def solution(mesh):
    return jax.shard_map(
        body,
        mesh=mesh,
        in_specs=(
            P("ctx", "head"),
            P("ctx", "head"),
            P("ctx", "head"),
            P("ctx", None),
            P("ctx", "head"),
            P(None, "head"),
        ),
        out_specs=(P("ctx", "head"), P("ctx", "head"), P("ctx", "head"), P("ctx", "head")),
        check_vma=False,
    )
```

```python
import functools

import jax
import jax.numpy as jnp
from jax import lax
from jax.experimental import pallas as pl
from jax.experimental.pallas import tpu as pltpu
from jax.sharding import PartitionSpec as P

HD = 128
BLOCK = 64
TOPK = 4
F32 = jnp.float32
BF16 = jnp.bfloat16
MOST = 58 * 1024 * 1024
SOME = 20 * 1024 * 1024
PAD = 16
TOGETHER = 4
LOW = -(2.0**99)
NN = (((1,), (0,)), ((), ()))
NT = (((1,), (1,)), ((), ()))
TN = (((0,), (0,)), ((), ()))


def mm(a, b, dims=NN):
    return lax.dot_general(a, b, dims, preferred_element_type=F32)


def joined(items, axis):
    return items[0] if len(items) == 1 else jnp.concatenate(items, axis=axis)


def dealt(refs, counts):
    lists, at = [], 0
    for count in counts:
        lists.append(refs[at : at + count])
        at += count
    return lists, refs[at:]


def loads(lists, buf, sems):
    copies, at = [], 0
    for i, refs in enumerate(lists):
        mine, row = [], 0
        for ref in refs:
            rows = ref.shape[0]
            mine.append(
                pltpu.make_async_copy(ref, buf.at[i, pl.ds(row, rows)], sems.at[at])
            )
            row += rows
            at += 1
        copies.append(mine)
    return copies


def start(copies):
    for copy in copies:
        copy.start()


def wait(copies):
    for copy in copies:
        copy.wait()


def whole(refs):
    return joined([ref[...] for ref in refs], 0)


def added(terms, cols):
    total = None
    for refs in terms:
        term = joined([ref[:, cols].astype(F32) for ref in refs], 0)
        total = term if total is None else total + term
    return total


def diagonal(pair):
    zero = jnp.zeros((pair.shape[0], HD), pair.dtype)
    top = jnp.concatenate([pair[:, :HD], zero], axis=1)
    low = jnp.concatenate([zero, pair[:, HD:]], axis=1)
    return jnp.concatenate([top, low], axis=0)


def pack_kernel(sel_ref, q_ref, out_ref):
    rows, width = q_ref.shape
    out_ref[:rows] = q_ref[...]
    digits = [(sel_ref[...] >> 4).astype(F32), (sel_ref[...] & 15).astype(F32)]
    if width > 2 * rows:
        digits.append(jnp.zeros((TOPK, width - 2 * rows), F32))
    lines = [jnp.concatenate(digits, axis=1), jnp.zeros((PAD - TOPK, width), F32)]
    out_ref[rows:] = jnp.concatenate(lines, axis=0).astype(BF16)


def forward_kernel(counts, span, cap, me_ref, mark_ref, k_any, v_any, *refs):
    chunks = len(counts)
    q_refs, refs = dealt(refs, counts)
    part_any, refs = refs[:chunks], refs[chunks:]
    qg_any, p_any, logit_ref, hot_any = refs[:4]
    q_buf, part_refs, k_ref, v_ref, qg_ref, p_ref, hot_ref, topg_ref, out_ref = refs[4:13]
    in_sems, kv_sems, out_sems = refs[13:]
    q_copies = loads(q_refs, q_buf, in_sems)
    kv_copies = [
        pltpu.make_async_copy(k_any, k_ref, kv_sems.at[0]),
        pltpu.make_async_copy(v_any, v_ref, kv_sems.at[1]),
    ]
    out_copies = [
        pltpu.make_async_copy(qg_ref, qg_any, out_sems.at[chunks]),
        pltpu.make_async_copy(hot_ref, hot_any, out_sems.at[chunks + 1]),
        pltpu.make_async_copy(p_ref, p_any, out_sems.at[chunks + 2]),
    ]
    for copies in q_copies:
        start(copies)
    start(kv_copies)
    block_count, _, width = k_ref.shape
    heads = width // HD
    rows = part_any[0].shape[0]
    group_rows = rows * span
    groups = chunks // span
    scale = HD ** (-0.5)
    rate = scale * 1.4426950408889634
    base = me_ref[0] * block_count

    before = lax.broadcasted_iota(jnp.int32, (group_rows, group_rows), 0)
    later = lax.broadcasted_iota(jnp.int32, (group_rows, group_rows), 1)
    earlier = (before < later).astype(BF16)
    own_ids = (base + lax.broadcasted_iota(jnp.int32, (block_count, group_rows), 0)).astype(F32)
    place = lax.broadcasted_iota(jnp.int32, (cap, group_rows), 0).astype(F32)
    zero = jnp.zeros((block_count, HD), BF16)
    wide_marks = jnp.concatenate(
        [
            jnp.concatenate(
                [mark_ref[:, i * HD : (i + 1) * HD] if i == h else zero for i in range(heads)], axis=1
            )
            for h in range(heads)
        ],
        axis=0,
    )
    q_groups, owns = [], []
    for g in range(groups):
        for i in range(span):
            wait(q_copies[g * span + i])
        packs = [q_buf[g * span + i] for i in range(span)]
        digits = [pack[rows : rows + PAD].astype(F32)[:TOPK] for pack in packs]
        picked = joined([16.0 * d[:, :rows] + d[:, rows : 2 * rows] for d in digits], 1)
        own = picked[0:1, :] == own_ids
        for t in range(1, TOPK):
            own = own | (picked[t : t + 1, :] == own_ids)
        owns.append(jnp.where(own, 1.0, 0.0))
        q_groups.append(joined([pack[:rows] for pack in packs], 0))
    own_all = jnp.concatenate(owns, axis=0)
    rank_all = jnp.where(own_all > 0.5, mm(own_all.astype(BF16), earlier), -1.0)
    hots = []
    for g in range(groups):
        rank = rank_all[g * block_count : (g + 1) * block_count]
        hots.append(
            jnp.concatenate(
                [
                    jnp.where(rank[b : b + 1, :] == place, 1.0, 0.0).astype(BF16)
                    for b in range(block_count)
                ],
                axis=0,
            )
        )
        hot_ref[g] = hots[g]
    all_marks = [mm(wide_marks, q_groups[g], NT) for g in range(groups)]
    for g in range(groups):
        qg_ref[:, g * cap : (g + 1) * cap, :] = (
            mm(hots[g], q_groups[g]).astype(BF16).reshape(block_count, cap, width)
        )
    tails = []
    for g in range(groups):
        tops, sums = [], []
        for h in range(heads):
            mark = scale * all_marks[g][h * block_count : (h + 1) * block_count]
            mark = jnp.where(owns[g] > 0.5, mark, LOW)
            top = jnp.max(mark, axis=0, keepdims=True).astype(BF16).astype(F32)
            tops.append(top)
            sums.append(jnp.sum(owns[g] * jnp.exp(mark - top), axis=0, keepdims=True))
        tops, sums = jnp.concatenate(tops, axis=0), jnp.concatenate(sums, axis=0)
        upper = sums.astype(BF16).astype(F32)
        spare = jnp.zeros((HD - 3 * heads, group_rows), F32)
        tails.append(jnp.concatenate([tops, upper, sums - upper, spare], axis=0))
    for g in range(groups):
        topg_ref[:, g * cap : (g + 1) * cap, :] = mm(hots[g], tails[g].astype(BF16), NT).reshape(
            block_count, cap, HD
        )
    for g in range(groups):
        for i in range(span):
            part_refs[g * span + i, :, width:] = (
                tails[g][:, i * rows : (i + 1) * rows].T.astype(BF16)
            )
    start(out_copies[:2])
    wait(kv_copies)

    pairs = [slice(p * 2 * HD, (p + 1) * 2 * HD) for p in range(heads // 2)]

    def some_blocks(step, carry):
        blocks = [step * TOGETHER + u for u in range(TOGETHER)]
        logits = [
            [mm(diagonal(k_ref[b, :, cols]), qg_ref[b, :, cols], NT) for cols in pairs]
            for b in blocks
        ]
        probs, gated, kept = [], [], []
        for b, scores in zip(blocks, logits):
            tops = topg_ref[b].T[:heads]
            marks = scale * jnp.concatenate(
                [scores[h // 2][(h % 2 + 1) * BLOCK - 1 : (h % 2 + 1) * BLOCK] for h in range(heads)],
                axis=0,
            )
            gates = jnp.exp(marks - tops)
            kept.append(marks)
            for p in range(heads // 2):
                low, high = [], []
                for i in range(2):
                    part = scores[p][i * BLOCK : (i + 1) * BLOCK]
                    weight = jnp.exp2(rate * (part - jnp.max(part, axis=0, keepdims=True)))
                    inverse = 1.0 / jnp.sum(weight, axis=0, keepdims=True)
                    gate = gates[2 * p + i : 2 * p + i + 1, :]
                    low.append((weight * inverse).astype(BF16))
                    high.append((weight * (inverse * gate)).astype(BF16))
                probs.append(jnp.concatenate(low, axis=0))
                gated.append(jnp.concatenate(high, axis=0))
        outs = []
        for u, b in enumerate(blocks):
            for p, cols in enumerate(pairs):
                both = gated[u * len(pairs) + p]
                outs.append(mm(both, diagonal(v_ref[b, :, cols]), TN).astype(BF16))
        for u, b in enumerate(blocks):
            logit_ref[b] = kept[u]
            for p, cols in enumerate(pairs):
                p_ref[b, p] = probs[u * len(pairs) + p]
                out_ref[b, :, cols] = outs[u * len(pairs) + p]
        return carry

    lax.fori_loop(0, block_count // TOGETHER, some_blocks, 0)
    start(out_copies[2:])

    for g in range(groups):
        slots = out_ref[:, g * cap : (g + 1) * cap, :].reshape(block_count * cap, width)
        part = mm(hot_ref[g], slots, TN).astype(BF16)
        for i in range(span):
            m = g * span + i
            part_refs[m, :, :width] = part[i * rows : (i + 1) * rows]
            copy = pltpu.make_async_copy(part_refs.at[m], part_any[m], out_sems.at[m])
            copy.start()
            out_copies.append(copy)
    wait(out_copies)


def shift(heads, *moves):
    row = lax.broadcasted_iota(jnp.int32, (HD, HD), 0)
    col = lax.broadcasted_iota(jnp.int32, (HD, HD), 1)
    total = jnp.zeros((HD, HD), F32)
    for source, target in moves:
        inside = (row >= source * heads) & (row < (source + 1) * heads)
        hit = inside & (col - target * heads == row - source * heads)
        total = jnp.where(hit, 1.0, total)
    return total.astype(BF16)


def blend(terms, heads):
    width = heads * HD
    tails = [joined([ref[rows, width:] for ref, rows in term], 0) for term in terms]
    wide = [tail.astype(F32) for tail in tails]
    top = wide[0]
    for tail in wide[1:]:
        top = jnp.maximum(top, tail)
    gather = shift(heads, (1, 0), (2, 0))
    factors = [jnp.exp(tail - top) for tail in wide]
    total = None
    for tail, factor in zip(tails, factors):
        share = factor * mm(tail, gather)
        total = share if total is None else total + share
    columns = []
    for h in range(heads):
        cols = slice(h * HD, (h + 1) * HD)
        column = None
        for term, factor in zip(terms, factors):
            values = joined([ref[rows, cols] for ref, rows in term], 0).astype(F32)
            part = factor[:, h : h + 1] * values
            column = part if column is None else column + part
        columns.append(column)
    return top, total, columns


def digits_of(tile, count):
    digits = []
    for _ in range(count):
        upper = tile.astype(BF16)
        digits.append(upper)
        tile = tile - upper.astype(F32)
    return digits


def packed_tail(digits, heads):
    total = None
    for i, digit in enumerate(digits):
        part = mm(digit, shift(heads, (0, i)))
        total = part if total is None else total + part
    return total.astype(BF16)


def merge_kernel(plan, heads, *refs):
    ins, outs = refs[: len(refs) - len(plan)], refs[len(refs) - len(plan) :]
    for terms, out_ref in zip(plan, outs):
        top, total, columns = blend(
            [[(ins[i], pl.ds(first, count))] for i, first, count in terms], heads
        )
        for h in range(heads):
            out_ref[:, h * HD : (h + 1) * HD] = columns[h].astype(BF16)
        out_ref[:, heads * HD :] = packed_tail([top.astype(BF16)] + digits_of(total, 2), heads)


def grad_kernel(lines, line_ref, w_ref, *refs):
    own_ref, up_refs, down_refs = refs[0], refs[1:lines], refs[lines : 2 * lines - 1]
    ga_ref, blocks_ref, full_ref, w_buf, sems, piece_sems = refs[2 * lines - 1 :]
    width = own_ref.shape[1]
    chunks, _, share = blocks_ref.shape
    line = line_ref[0]
    copies = [
        pltpu.make_async_copy(w_ref.at[pl.ds(i * width, width)], w_buf.at[i], sems.at[i])
        for i in range(lines)
    ]
    start(copies)

    def placed(ref, i):
        return pltpu.make_async_copy(ref, full_ref.at[i], piece_sems.at[i])

    placed(own_ref, line).start()
    for d in range(1, lines):

        @pl.when(line >= d)
        def _():
            placed(up_refs[d - 1], line - d).start()

        @pl.when(line + d < lines)
        def _():
            placed(down_refs[d - 1], line + d).start()

    for i in range(lines):
        placed(own_ref, i).wait()
    for j in range(chunks):
        first = j * share
        blocks_ref[j] = full_ref[first // width, :, first % width : first % width + share]
    total = None
    for i in range(lines):
        copies[i].wait()
        term = mm(full_ref[i], w_buf[i])
        total = term if total is None else total + term
    ga_ref[...] = total.astype(BF16)


def finish_kernel(counts, *refs):
    terms, (ga_ref, attn_ref, *ext_refs) = dealt(refs, counts)
    rows, width = ga_ref.shape
    half = rows // len(ext_refs)
    heads = width // HD
    top, total, columns = blend(
        [[(ref, slice(None)) for ref in pieces] for pieces in terms], heads
    )
    lane = lax.broadcasted_iota(jnp.int32, (rows, HD), 1)
    total = jnp.where(lane < heads, total, 1.0)
    inverse = 1.0 / total
    dots = jnp.zeros((rows, HD), F32)
    for i, ext_ref in enumerate(ext_refs):
        ext_ref[:, :width] = ga_ref[i * half : (i + 1) * half]
    for h in range(heads):
        cols = slice(h * HD, (h + 1) * HD)
        attn = columns[h] * inverse[:, h : h + 1]
        attn_ref[:, cols] = attn.astype(BF16)
        dot = jnp.sum(attn * ga_ref[:, cols].astype(F32), axis=1, keepdims=True)
        dots = jnp.where(lane == h, dot, dots)
    level = jnp.where(lane < heads, top + jnp.log(total), 0.0)
    tail = packed_tail(digits_of(dots, 2) + digits_of(level, 3), heads)
    for i, ext_ref in enumerate(ext_refs):
        ext_ref[:, width:] = tail[i * half : (i + 1) * half]


def total_kernel(counts, *refs):
    terms, (out_ref,) = dealt(refs, counts)
    for h in range(out_ref.shape[1] // HD):
        cols = slice(h * HD, (h + 1) * HD)
        out_ref[:, cols] = added(terms, cols)


def backward_kernel(counts, span, cap, logit_ref, hot_any, qg_any, p_any, k_any, v_any, *refs):
    chunks = len(counts)
    ga_refs, refs = dealt(refs, counts)
    part_refs, refs = refs[:chunks], refs[chunks:]
    dk_any, dv_any = refs[:2]
    ga_buf, hot_ref, qg_ref, p_ref, k_ref, v_ref, gag_ref, dq_ref, dk_ref, dv_ref = refs[2:12]
    in_sems, hot_sem, block_sems, out_sems, part_sems = refs[12:]
    ga_copies = loads(ga_refs, ga_buf, in_sems)
    hot_copy = pltpu.make_async_copy(hot_any, hot_ref, hot_sem.at[0])
    hot_copy.start()
    for copies in ga_copies:
        start(copies)

    def block_loads(b):
        pairs = ((qg_any, qg_ref), (p_any, p_ref), (k_any, k_ref), (v_any, v_ref))
        return [
            pltpu.make_async_copy(far.at[b], near.at[b], block_sems.at[i, b])
            for i, (far, near) in enumerate(pairs)
        ]

    def block_stores(b):
        return [
            pltpu.make_async_copy(dk_ref.at[b], dk_any.at[b], out_sems.at[0, b]),
            pltpu.make_async_copy(dv_ref.at[b], dv_any.at[b], out_sems.at[1, b]),
        ]

    block_count, _, width = k_ref.shape
    heads = width // HD
    rows = part_refs[0].shape[0]
    groups = chunks // span
    scale = HD ** (-0.5)

    for b in range(block_count):
        start(block_loads(b))
    hot_copy.wait()
    for g in range(groups):
        for i in range(span):
            wait(ga_copies[g * span + i])
        ga_group = joined([ga_buf[g * span + i] for i in range(span)], 0)
        gag_ref[:, g * cap : (g + 1) * cap, :] = (
            mm(hot_ref[g], ga_group).astype(BF16).reshape(block_count, cap, width + HD)
        )
    last = lax.broadcasted_iota(jnp.int32, (BLOCK, groups * cap), 0) == BLOCK - 1

    pairs = [slice(p * 2 * HD, (p + 1) * 2 * HD) for p in range(heads // 2)]

    def some_blocks(step, carry):
        blocks = [step * TOGETHER + u for u in range(TOGETHER)]
        for b in blocks:
            wait(block_loads(b))
        grads = [
            [mm(diagonal(v_ref[b, :, cols]), gag_ref[b, :, cols], NT) for cols in pairs]
            for b in blocks
        ]
        gated, scores = [], []
        for b, grad_pairs in zip(blocks, grads):
            tail = gag_ref[b, :, width:].astype(F32).T
            tail = [tail[i * heads : (i + 1) * heads] for i in range(5)]
            dots = tail[0] + tail[1]
            gates = jnp.exp(jnp.minimum(logit_ref[b] - (tail[2] + tail[3] + tail[4]), 0.0))
            for p in range(heads // 2):
                both = p_ref[b, p].astype(F32)
                low, high = [], []
                for i in range(2):
                    at = slice(i * BLOCK, (i + 1) * BLOCK)
                    h = 2 * p + i
                    gate = gates[h : h + 1, :]
                    grad, probs = grad_pairs[p][at], both[at]
                    delta = jnp.sum(probs * grad, axis=0, keepdims=True)
                    weight = probs * gate
                    extra = jnp.where(last, scale * gate * (delta - dots[h : h + 1, :]), 0.0)
                    low.append((weight * (scale * (grad - delta)) + extra).astype(BF16))
                    high.append(weight.astype(BF16))
                scores.append(low)
                gated.append(high)
        for u, b in enumerate(blocks):
            for p, cols in enumerate(pairs):
                score, weight = scores[u * len(pairs) + p], gated[u * len(pairs) + p]
                for i in range(2):
                    head = slice((2 * p + i) * HD, (2 * p + i + 1) * HD)
                    dv_ref[b, :, head] = mm(weight[i], gag_ref[b, :, head])
                    dk_ref[b, :, head] = mm(score[i], qg_ref[b, :, head])
                both = jnp.concatenate(score, axis=0)
                dq_ref[b, :, cols] = mm(both, diagonal(k_ref[b, :, cols]), TN).astype(BF16)
        for b in blocks:
            start(block_stores(b))
        return carry

    lax.fori_loop(0, block_count // TOGETHER, some_blocks, 0)

    part_copies = []

    for g in range(groups):
        slots = dq_ref[:, g * cap : (g + 1) * cap, :].reshape(block_count * cap, width)
        part = mm(hot_ref[g], slots, TN).astype(BF16)
        for i in range(span):
            m = g * span + i
            ga_buf[m, :, :width] = part[i * rows : (i + 1) * rows]
            copy = pltpu.make_async_copy(
                ga_buf.at[m, :, pl.ds(0, width)], part_refs[m], part_sems.at[m]
            )
            copy.start()
            part_copies.append(copy)
    for b in range(block_count):
        wait(block_stores(b))
    wait(part_copies)


def weight_kernel(counts, first, me_ref, cols_ref, *refs):
    attns, (*before, out_ref) = dealt(refs, counts)
    me = me_ref[0]
    columns = joined([cols_ref[me ^ (first + m)] for m in range(len(counts))], 0)
    total = mm(columns, joined([whole(pieces) for pieces in attns], 0), TN)
    for ref in before:
        total = total + ref[...]
    out_ref[...] = total


def swap(x, bits):
    count = lax.axis_size("ctx")
    return lax.ppermute(x, "ctx", [(i, i ^ bits) for i in range(count)])


def after(x, *others):
    return lax.optimization_barrier((x, *others))[0]


def flat(lists):
    return [x for pieces in lists for x in pieces]


def spread_near(x):
    chips = lax.axis_size("ctx") // 2
    return [[x]] + [[swap(x, 2 * j)] for j in range(1, chips if chips != 4 else 3)]


def spread_far(near, half, *before):
    if len(near) != 3:
        return near
    (x_way,), (y_way,) = near[1:]
    far = [swap(after(x_way[:half], *before), 4), swap(after(y_way[half:], *before), 2)]
    return near + [far]


def spread_chips(x, half, *before):
    return spread_far(spread_near(x), half, *before)


def spread_halves(top, low):
    chips = lax.axis_size("ctx") // 2
    if chips != 4:
        return [[swap(x, 2 * j) if j else x for x in (top, low)] for j in range(chips)]
    x_top, y_low = swap(top, 2), swap(low, 4)
    x_low, y_top = swap(low, 2), swap(top, 4)
    return [[top, low], [x_top, x_low], [y_top, y_low], [swap(x_top, 4), swap(y_low, 2)]]


def with_cores(lists, *before):
    both = []
    for pieces in lists:
        if before and pieces is lists[-1]:
            pieces = [after(piece, *before) for piece in pieces]
        both += [pieces, [swap(piece, 1) for piece in pieces]]
    return both


def from_core(parts, *before):
    received = [None] * (len(parts) // 2)
    for j in reversed(range(len(received))):
        received[j] = swap(after(parts[2 * j + 1], *before), 1)
    return received


def collect_chips(parts, received):
    chips = len(received)

    def both(j, rows, extra=None, earlier=None):
        mine = parts[2 * j] if earlier is None else after(parts[2 * j], earlier)
        total = mine[rows].astype(F32) + received[j][rows].astype(F32)
        if extra is not None:
            total = total + extra.astype(F32)
        return total.astype(BF16)

    terms = [[parts[0]], [received[0]]]
    if chips != 4:
        return terms + [[swap(both(j, slice(None)), 2 * j)] for j in range(1, chips)], []
    half = parts[0].shape[0] // 2
    top, low = slice(0, half), slice(half, None)
    x_sum, y_sum = both(3, top), both(3, low)
    x_far, y_far = swap(x_sum, 2), swap(y_sum, 4)
    x_sum, y_sum = both(1, top, None, x_sum), both(2, low, None, y_sum)
    x_top, y_low = swap(x_sum, 2), swap(y_sum, 4)
    x_sum, y_sum = both(1, low, y_far, x_sum), both(2, top, x_far, y_sum)
    x_low, y_top = swap(x_sum, 2), swap(y_sum, 4)
    return terms + [[x_top, x_low], [y_top, y_low]], [x_sum, y_sum]


def merge_chips(parts, received, heads, between):
    chips = len(received)
    rows = parts[0].shape[0]
    half = rows // 2

    def merged(ins, plan):
        return pl.pallas_call(
            functools.partial(merge_kernel, plan, heads),
            out_shape=[
                jax.ShapeDtypeStruct((terms[0][2], ins[0].shape[1]), BF16) for terms in plan
            ],
            in_specs=[pl.BlockSpec(memory_space=pltpu.VMEM)] * len(ins),
            out_specs=[pl.BlockSpec(memory_space=pltpu.VMEM)] * len(plan),
            compiler_params=pltpu.CompilerParams(vmem_limit_bytes=SOME),
            name="merge",
        )(*ins)

    terms = [[parts[0]], [received[0]]]
    if chips != 4:
        for j in range(1, chips):
            (both,) = merged([parts[2 * j], received[j]], [[(0, 0, rows), (1, 0, rows)]])
            terms.append([swap(both, 2 * j)])
        return terms, between(received[0])
    top, low = (0, half), (half, half)
    x_far, y_far = merged(
        [parts[6], received[3]], [[(0, *top), (1, *top)], [(0, *low), (1, *low)]]
    )
    x_far, y_far = swap(x_far, 2), swap(y_far, 4)
    ins = [parts[2], received[1], parts[4], received[2]]
    x_top, y_low = merged(ins, [[(0, *top), (1, *top)], [(2, *low), (3, *low)]])
    x_top, y_low = swap(x_top, 2), swap(y_low, 4)
    x_low, y_top = merged(
        ins + [y_far, x_far],
        [[(0, *low), (1, *low), (4, *top)], [(2, *top), (3, *top), (5, *top)]],
    )
    done = between(x_low, y_top)
    x_low, y_top = swap(x_low, 2), swap(y_top, 4)
    return terms + [[x_top, x_low], [y_top, y_low]], done


def spread_line(x):
    lines = lax.axis_size("head")
    ups, downs = [x], [x]
    for d in range(1, lines):
        up = [(i, i + 1) for i in range(d - 1, lines - 1)]
        down = [(i, i - 1) for i in range(1, lines - d + 1)]
        if d == lines - 1 and lines > 2:
            last = jnp.where(lax.axis_index("head") == lines - 2, ups[-1], downs[-1])
            last = lax.ppermute(last, "head", up + down)
            ups.append(last)
            downs.append(last)
        else:
            ups.append(lax.ppermute(ups[-1], "head", up))
            downs.append(lax.ppermute(downs[-1], "head", down))
    return ups[1:], downs[1:]


def body(queries, key_rows, value_rows, selected, out_grad, out_weight):
    chunks = lax.axis_size("ctx")
    chips = chunks // 2
    lines = lax.axis_size("head")
    rows, width = queries.shape
    features = out_weight.shape[0]
    heads = width // HD
    block_count = key_rows.shape[0] // BLOCK
    block_total = block_count * chunks
    capacity = 2 * rows * TOPK // block_total
    span = max(1, 16 // capacity)
    cap = capacity * span
    groups = chunks // span
    slots = groups * cap
    index = lax.axis_index("ctx").astype(jnp.int32)
    me = index.reshape(1)
    keys = key_rows.reshape(block_count, BLOCK, width)
    values = value_rows.reshape(block_count, BLOCK, width)
    vmem = pl.BlockSpec(memory_space=pltpu.VMEM)
    smem = pl.BlockSpec(memory_space=pltpu.SMEM)
    anywhere = pl.BlockSpec(memory_space=pl.ANY)
    params = pltpu.CompilerParams(vmem_limit_bytes=MOST)
    small = pltpu.CompilerParams(vmem_limit_bytes=SOME)

    def shaped(shape, kind=BF16):
        return jax.ShapeDtypeStruct(shape, kind)

    ups, downs = spread_line(out_grad)
    packed = pl.pallas_call(
        pack_kernel,
        out_shape=shaped((rows + PAD, width)),
        in_specs=[vmem] * 2,
        out_specs=vmem,
        compiler_params=small,
        name="pack",
    )(selected.T, queries)
    query_chips = spread_chips(packed, rows // 2)
    query_all = with_cores(query_chips, ups[0], downs[0])

    outs = pl.pallas_call(
        functools.partial(forward_kernel, [len(pieces) for pieces in query_all], span, cap),
        out_shape=[shaped((rows, width + HD))] * chunks
        + [
            shaped((block_count, slots, width)),
            shaped((block_count, heads // 2, 2 * BLOCK, slots)),
            shaped((block_count, heads, slots), F32),
            shaped((groups, block_count * cap, rows * span)),
        ],
        in_specs=[smem, vmem] + [anywhere] * (2 + len(flat(query_all))),
        out_specs=[anywhere] * (chunks + 2) + [vmem, anywhere],
        scratch_shapes=[
            pltpu.VMEM((chunks, rows + PAD, width), BF16),
            pltpu.VMEM((chunks, rows, width + HD), BF16),
            pltpu.VMEM((block_count, BLOCK, width), BF16),
            pltpu.VMEM((block_count, BLOCK, width), BF16),
            pltpu.VMEM((block_count, slots, width), BF16),
            pltpu.VMEM((block_count, heads // 2, 2 * BLOCK, slots), BF16),
            pltpu.VMEM((groups, block_count * cap, rows * span), BF16),
            pltpu.VMEM((block_count, slots, HD), F32),
            pltpu.VMEM((block_count, slots, width), BF16),
            pltpu.SemaphoreType.DMA((len(flat(query_all)),)),
            pltpu.SemaphoreType.DMA((2,)),
            pltpu.SemaphoreType.DMA((chunks + 3,)),
        ],
        compiler_params=params,
        name="forward",
    )(me, keys[:, BLOCK - 1], keys, values, *flat(query_all))
    q_slots, probs, logits, hot = outs[chunks:]

    line = lax.axis_index("head").astype(jnp.int32).reshape(1)
    make_grad = pl.pallas_call(
        functools.partial(grad_kernel, lines),
        out_shape=[shaped((rows, width)), shaped((chunks, rows, features // chunks))],
        in_specs=[smem] + [anywhere] * (2 * lines),
        out_specs=[vmem] * 2,
        scratch_shapes=[
            pltpu.VMEM((lines, rows, width), BF16),
            pltpu.VMEM((lines, width, width), BF16),
            pltpu.SemaphoreType.DMA((lines,)),
            pltpu.SemaphoreType.DMA((lines,)),
        ],
        compiler_params=params,
        name="grad",
    )
    received = from_core(outs[:chunks], ups[1], downs[1])
    terms, (grad_attn, blocks) = merge_chips(
        outs[:chunks],
        received,
        heads,
        lambda *before: make_grad(after(line, *before), out_weight, out_grad, *ups, *downs),
    )
    attn_out, *extended = pl.pallas_call(
        functools.partial(finish_kernel, [len(pieces) for pieces in terms]),
        out_shape=[shaped((rows, width))] + [shaped((rows // 2, width + HD))] * 2,
        in_specs=[vmem] * (len(flat(terms)) + 1),
        out_specs=[vmem] * 3,
        compiler_params=small,
        name="finish",
    )(*flat(terms), grad_attn)
    grad_chips = spread_halves(*extended)
    grad_all = with_cores(grad_chips)
    arrived = flat(grad_chips[1:])
    attns = spread_near(after(attn_out, *arrived))
    columns = lax.all_to_all(
        after(blocks, *arrived), "ctx", split_axis=0, concat_axis=0, tiled=True
    )

    outs = pl.pallas_call(
        functools.partial(backward_kernel, [len(pieces) for pieces in grad_all], span, cap),
        out_shape=[shaped((rows, width))] * chunks
        + [shaped((block_count, BLOCK, width), F32)] * 2,
        in_specs=[vmem] + [anywhere] * (5 + len(flat(grad_all))),
        out_specs=[anywhere] * (chunks + 2),
        scratch_shapes=[
            pltpu.VMEM((chunks, rows, width + HD), BF16),
            pltpu.VMEM((groups, block_count * cap, rows * span), BF16),
            pltpu.VMEM((block_count, slots, width), BF16),
            pltpu.VMEM((block_count, heads // 2, 2 * BLOCK, slots), BF16),
            pltpu.VMEM((block_count, BLOCK, width), BF16),
            pltpu.VMEM((block_count, BLOCK, width), BF16),
            pltpu.VMEM((block_count, slots, width + HD), BF16),
            pltpu.VMEM((block_count, slots, width), BF16),
            pltpu.VMEM((block_count, BLOCK, width), F32),
            pltpu.VMEM((block_count, BLOCK, width), F32),
            pltpu.SemaphoreType.DMA((len(flat(grad_all)),)),
            pltpu.SemaphoreType.DMA((1,)),
            pltpu.SemaphoreType.DMA((4, block_count)),
            pltpu.SemaphoreType.DMA((2, block_count)),
            pltpu.SemaphoreType.DMA((chunks,)),
        ],
        compiler_params=params,
        name="backward",
    )(logits, hot, q_slots, probs, keys, values, *flat(grad_all))
    key_grad, value_grad = outs[chunks:]
    received = from_core(outs[:chunks], columns, *flat(attns[1:3]))
    terms, last_sums = collect_chips(outs[:chunks], received)
    near = [[after(x, *last_sums) for x in pieces] for pieces in attns]
    attns = with_cores(spread_far(near, rows // 2))

    def weight_part(chosen, first, when, *before):
        return pl.pallas_call(
            functools.partial(weight_kernel, [len(pieces) for pieces in chosen], first),
            out_shape=shaped((features // chunks, width), F32),
            in_specs=[smem] + [vmem] * (1 + len(flat(chosen)) + len(before)),
            out_specs=vmem,
            compiler_params=small,
            name="weight",
        )(when, columns, *flat(chosen), *before)

    weight_near = weight_part(attns[:-2], 0, after(me, terms[2][0]))
    query_grad = pl.pallas_call(
        functools.partial(total_kernel, [len(pieces) for pieces in terms]),
        out_shape=shaped((rows, width), F32),
        in_specs=[vmem] * len(flat(terms)),
        out_specs=vmem,
        compiler_params=small,
        name="total",
    )(after(terms[0][0], weight_near), *flat(terms[1:]))
    weight_grad = weight_part(attns[-2:], chunks - 2, after(me, query_grad), weight_near)
    return (
        query_grad,
        key_grad.reshape(-1, width),
        value_grad.reshape(-1, width),
        weight_grad,
    )


def solution(mesh):
    return jax.shard_map(
        body,
        mesh=mesh,
        in_specs=(
            P("ctx", "head"),
            P("ctx", "head"),
            P("ctx", "head"),
            P("ctx", None),
            P("ctx", "head"),
            P(None, "head"),
        ),
        out_specs=(P("ctx", "head"), P("ctx", "head"), P("ctx", "head"), P("ctx", "head")),
        check_vma=False,
    )
```
